32 devices in a mesh: dp: 16 (over z, y, core), seq: 2 (over x).
Axes of the slice: x: 2, y: 2, z: 4, core: 2. Of those that a mesh axis runs over, the one named last changes fastest.
Arguments:
- tokens: bfloat16 [32, 1024, 1152], P('dp', 'seq'), may hold values from -6 to 6
- cotangent: bfloat16 [32, 1024, 1152], P('dp', 'seq'), may hold values from -6 to 6
- lengths: int32 [32, 10], P('dp'), may hold values from 0 to 1024, as said below
- adapter_ids: int32 [32, 10], P('dp'), may hold values from 0 to 7
- w_query: bfloat16 [1152, 1152], P('dp', 'seq'), may hold values from -0.1875 to 0.1875
- w_key: bfloat16 [1152, 1152], P('dp', 'seq'), may hold values from -0.1875 to 0.1875
- w_value: bfloat16 [1152, 1152], P('dp', 'seq'), may hold values from -0.1875 to 0.1875
- w_out: bfloat16 [1152, 1152], P('dp', 'seq'), may hold values from -2 to 2
- w_up: bfloat16 [1152, 4304], P('dp', 'seq'), may hold values from -0.1875 to 0.1875
- w_down: bfloat16 [4304, 1152], P('seq', 'dp'), may hold values from -0.09375 to 0.09375
- b_query: bfloat16 [1152], P('seq'), may hold values from -3 to 3
- b_value: bfloat16 [1152], P('seq'), may hold values from -0.29882812 to 0.29882812
- b_out: bfloat16 [1152], P('seq'), may hold values from -1.796875 to 1.796875
- b_up: bfloat16 [4304], P('seq'), may hold values from -3 to 3
- b_down: bfloat16 [1152], P('seq'), may hold values from -1.796875 to 1.796875
- gain_one: bfloat16 [1152], P('seq'), may hold values from 0.5 to 1.5
- shift_one: bfloat16 [1152], P('seq'), may hold values from -1.796875 to 1.796875
- gain_two: bfloat16 [1152], P('seq'), may hold values from 0.5 to 1.5
- shift_two: bfloat16 [1152], P('seq'), may hold values from -1.796875 to 1.796875
- qkv_a: bfloat16 [3, 8, 1152, 16], P(None, 'seq'), may hold values from -0.1875 to 0.1875
- out_a: bfloat16 [8, 1152, 16], P('seq'), may hold values from -2 to 2
- attn_b: bfloat16 [4, 8, 16, 1152], P(None, 'seq'), may hold values from -1.5 to 1.5
- up_a: bfloat16 [8, 1152, 16], P('seq'), may hold values from -0.1875 to 0.1875
- up_b: bfloat16 [8, 16, 4304], P('seq'), may hold values from -1.5 to 1.5
- down_a: bfloat16 [8, 4304, 16], P('seq'), may hold values from -0.09375 to 0.09375
- down_b: bfloat16 [8, 16, 1152], P('seq'), may hold values from -1.5 to 1.5
Outputs:
- mixed: bfloat16 [32, 1024, 1152], P('dp', 'seq')
- input_grad: float32 [32, 1024, 1152], P('dp', 'seq')
- grad_qkv_a: float32 [3, 8, 1152, 16], P(None, 'seq')
- grad_out_a: float32 [8, 1152, 16], P('seq')
- grad_attn_b: float32 [4, 8, 16, 1152], P(None, 'seq')
- grad_up_a: float32 [8, 1152, 16], P('seq')
- grad_up_b: float32 [8, 16, 4304], P('seq')
- grad_down_a: float32 [8, 4304, 16], P('seq')
- grad_down_b: float32 [8, 16, 1152], P('seq')
The draws below stay inside these ranges and needn't reach their ends.
Inputs may be any that keep to these rules, and one draw needn't show every extreme that they name: `lengths`: each row lists the patch counts of its pictures in order, each 100 to 1024, then zeros; the counts sum to at most 1024 and the rest of the row is padding. In each aligned group of 2 rows one row holds a single picture of 1024 patches. `adapter_ids`: slots after a row's last picture are unused.
All inputs are finite; a program needn't handle non-finite values.
Results may differ from the reference program's by a relative error of at most 0.019.
Values may be sent and summed in bfloat16 or wider, within the bound.
A program may use at most 320 MiB of HBM per device.

```python
import math
import jax
import jax.numpy as jnp
from jax import lax

D = 1152
HEADS = 16
HEAD_DIM = 72
FF = 4304
RANK = 16
ADAPTERS = 8
LEN = 1024
MIN_PATCHES = 100
MAX_PATCHES = 1024
ROWS_DEV = 2
PICS = 10
ROWS = 32


def draw_lengths(key, part):
    key_one, key_two = jax.random.split(key)
    drawn_len = jax.random.randint(key_one, (ROWS, PICS), MIN_PATCHES, MAX_PATCHES + 1)
    pic_ends = jnp.cumsum(drawn_len, axis=1)
    packed = jnp.where(pic_ends <= LEN, drawn_len, 0)
    chosen = jax.random.randint(key_two, (ROWS // ROWS_DEV, 1), 0, ROWS_DEV)
    row_pos = jnp.arange(ROWS_DEV)[None, :]
    single_row = (row_pos == chosen).reshape(ROWS, 1)
    single = jnp.where(jnp.arange(PICS)[None, :] == 0, LEN, 0)
    return jnp.where(single_row, single, packed).astype(jnp.int32)


def with_ends(values, key, low, largest):
    index_at = [jax.random.randint(jax.random.fold_in(key, axis), (), 0, length) for axis, length in enumerate(values.shape)]
    longest = values.shape.index(max(values.shape))
    neighbour = index_at[:longest] + [(index_at[longest] + 1) % values.shape[longest]] + index_at[longest + 1:]
    return values.at[tuple(index_at)].set(low).at[tuple(neighbour)].set(largest)


def block_scale(own_key, dims, shards, smallest, top_value):
    def one(dim, shards_of):
        heights = jax.random.uniform(jax.random.fold_in(jax.random.fold_in(own_key, 6), dim), (shards_of,), jnp.float32, smallest / len(shards), top_value / len(shards))
        return jnp.repeat(jnp.exp(heights), dims[dim] // shards_of).reshape((-1,) + (1,) * (len(dims) - dim - 1))

    loudness = one(*shards[0])
    for cut in shards[1:]:
        loudness = loudness * one(*cut)
    return loudness


def normal_values(own_key, dims, spread, most, cuts=(), held_as=jnp.bfloat16):
    factor_of = block_scale(own_key, dims, cuts, -0.22, 0.18) if cuts else 1.0
    array = jax.random.normal(own_key, dims, jnp.float32) * spread * factor_of
    return jnp.minimum(jnp.maximum(array, -most), most).astype(held_as)


def setup_inputs(seed: int = 0) -> dict:
    key_of = jax.random.split(jax.random.key(seed), 27)
    return {
        "tokens": normal_values(key_of[0], (ROWS, LEN, D), 1.0, 6.0, ((0, 16), (1, 2))),
        "cotangent": normal_values(key_of[1], (ROWS, LEN, D), 1.0, 6.0, ((0, 16), (1, 2))),
        "lengths": draw_lengths(jax.random.fold_in(key_of[26], 71), 0),
        "adapter_ids": with_ends(jax.random.randint(key_of[3], (ROWS, PICS), 0, ADAPTERS), jax.random.fold_in(key_of[3], 1), 0, ADAPTERS - 1).astype(jnp.int32),
        "w_query": normal_values(key_of[4], (D, D), D ** -0.5, 0.1875, ((0, 16), (1, 2))),
        "w_key": normal_values(key_of[5], (D, D), D ** -0.5, 0.1875, ((0, 16), (1, 2))),
        "w_value": normal_values(key_of[6], (D, D), D ** -0.5, 0.1875, ((0, 16), (1, 2))),
        "w_out": normal_values(key_of[7], (D, D), (max(D // 128, 1)) ** -0.5, 2.0, ((0, 16), (1, 2))),
        "w_up": normal_values(key_of[8], (D, FF), D ** -0.5, 0.1875, ((0, 16), (1, 2))),
        "w_down": normal_values(key_of[9], (FF, D), FF ** -0.5, 0.09375, ((0, 2), (1, 16))),
        "b_query": normal_values(key_of[10], (D,), 0.5, 3.0, ((0, 2),)),
        "b_value": normal_values(key_of[11], (D,), 0.05, 0.29882812, ((0, 2),)),
        "b_out": normal_values(key_of[12], (D,), 0.3, 1.796875, ((0, 2),)),
        "b_up": normal_values(key_of[13], (FF,), 0.5, 3.0, ((0, 2),)),
        "b_down": normal_values(key_of[14], (D,), 0.3, 1.796875, ((0, 2),)),
        "gain_one": jnp.clip(1.0 + 0.1 * jax.random.normal(key_of[15], (D,), jnp.float32), 0.5, 1.5).astype(jnp.bfloat16),
        "shift_one": normal_values(key_of[16], (D,), 0.3, 1.796875, ((0, 2),)),
        "gain_two": jnp.clip(1.0 + 0.1 * jax.random.normal(key_of[17], (D,), jnp.float32), 0.5, 1.5).astype(jnp.bfloat16),
        "shift_two": normal_values(key_of[18], (D,), 0.3, 1.796875, ((0, 2),)),
        "qkv_a": normal_values(key_of[19], (3, ADAPTERS, D, RANK), D ** -0.5, 0.1875, ((1, 2),)),
        "out_a": normal_values(key_of[20], (ADAPTERS, D, RANK), (max(D // 128, 1)) ** -0.5, 2.0, ((0, 2),)),
        "attn_b": normal_values(key_of[21], (4, ADAPTERS, RANK, D), RANK ** -0.5, 1.5, ((1, 2),)),
        "up_a": normal_values(key_of[22], (ADAPTERS, D, RANK), D ** -0.5, 0.1875, ((0, 2),)),
        "up_b": normal_values(key_of[23], (ADAPTERS, RANK, FF), RANK ** -0.5, 1.5, ((0, 2),)),
        "down_a": normal_values(key_of[24], (ADAPTERS, FF, RANK), FF ** -0.5, 0.09375, ((0, 2),)),
        "down_b": normal_values(key_of[25], (ADAPTERS, RANK, D), RANK ** -0.5, 1.5, ((0, 2),)),
    }


adapter_scale = 0.5
norm_eps = 1e-06
masked_score = -1e+30

@jax.custom_vjp
def low(v):
    return lax.optimization_barrier(v.astype(jnp.bfloat16)).astype(jnp.float32)

@jax.custom_vjp
def low_back(v):
    return v

def low_keep(v):
    return (low(v), None)

def low_pass(kept, grad):
    return (grad,)

def back_keep(v):
    return (v, None)

def back_low(kept, grad):
    return (low(grad),)
low.defvjp(low_keep, low_pass)
low_back.defvjp(back_keep, back_low)

def product_highest(left_op, right_op):
    return jnp.dot(left_op, right_op, precision=lax.Precision.HIGHEST, preferred_element_type=jnp.float32)

def layer_norm(values, gain_vec, shift_vec):
    center = lax.optimization_barrier(jnp.mean(values, axis=-1, keepdims=True))
    centered = values - center
    variance = lax.optimization_barrier(jnp.mean(centered * centered, axis=-1, keepdims=True))
    return centered * lax.rsqrt(variance + norm_eps) * gain_vec + shift_vec

def gelu_tanh(values):
    return jax.nn.gelu(values, approximate=True)

def flat_down(matrix):
    return jnp.transpose(matrix, (1, 0, 2)).reshape(matrix.shape[1], matrix.shape[0] * matrix.shape[2])

def flattened_up_factor(matrix):
    return matrix.reshape(matrix.shape[0] * matrix.shape[1], matrix.shape[2])

def adapter_term(inputs, column_mask, down_mat, up_factor_matrix):
    hidden_state = low(low_back(product_highest(inputs, flat_down(down_mat)) * column_mask))
    return adapter_scale * product_highest(hidden_state, flattened_up_factor(up_factor_matrix))

def token_info(length_row, adapter_row, positions):
    pic_ends = jnp.cumsum(length_row, dtype=jnp.int32)
    picture = lax.optimization_barrier(jnp.sum((positions[:, None] >= pic_ends[None, :]).astype(jnp.int32), axis=1, dtype=jnp.int32))
    is_live = positions < pic_ends[-1]
    slot_ids = jnp.arange(length_row.shape[0], dtype=jnp.int32)
    adapter = lax.optimization_barrier(jnp.sum(jnp.where(picture[:, None] == slot_ids[None, :], adapter_row[None, :], 0), axis=1, dtype=jnp.int32))
    chosen = (adapter[:, None] == jnp.arange(ADAPTERS, dtype=jnp.int32)[None, :]) & is_live[:, None]
    column_mask = jnp.repeat(chosen.astype(jnp.float32), RANK, axis=1)
    return (picture, is_live, column_mask)

def attend_block(query_blk, pic_blk, key_all, value_all, pic_all):
    scores = jnp.einsum('qhd,khd->hqk', query_blk, key_all, precision=lax.Precision.HIGHEST) * HEAD_DIM ** (-0.5)
    scores = low_back(scores)
    allowed = pic_blk[:, None] == pic_all[None, :]
    scores = jnp.where(allowed[None, :, :], scores, masked_score)
    top_score = lax.optimization_barrier(jnp.max(scores, axis=-1, keepdims=True))
    weights = jnp.exp(scores - top_score)
    attn_probs = low(weights / lax.optimization_barrier(jnp.sum(weights, axis=-1, keepdims=True)))
    return jnp.einsum('hqk,khd->qhd', attn_probs, value_all, precision=lax.Precision.HIGHEST)

def row_forward(row_in, adapter_set, frozen, picture, column_mask):
    w_query, w_key, w_value, w_out, w_up, w_down, b_query, b_value, b_out, b_up, b_down, gain_one, shift_one, gain_two, shift_two = frozen
    qkv_a, out_a, attn_b, up_a, up_b, down_a, down_b = adapter_set
    normed = low(layer_norm(row_in, gain_one, shift_one))
    query = low(low_back(product_highest(normed, w_query) + b_query + adapter_term(normed, column_mask, qkv_a[0], attn_b[0])))
    key_proj = low(low_back(product_highest(normed, w_key) + adapter_term(normed, column_mask, qkv_a[1], attn_b[1])))
    value_proj = low(low_back(product_highest(normed, w_value) + b_value + adapter_term(normed, column_mask, qkv_a[2], attn_b[2])))
    length = row_in.shape[0]
    block_rows = math.gcd(length, 512)
    block_count = length // block_rows
    query_blocks = query.reshape(block_count, block_rows, HEADS, HEAD_DIM)
    pic_blocks = picture.reshape(block_count, block_rows)
    key_heads = key_proj.reshape(length, HEADS, HEAD_DIM)
    value_heads = value_proj.reshape(length, HEADS, HEAD_DIM)

    def one_block(packed):
        return attend_block(packed[0], packed[1], key_heads, value_heads, picture)
    attended = lax.map(jax.checkpoint(one_block), (query_blocks, pic_blocks))
    attended = low(low_back(attended.reshape(length, HEADS * HEAD_DIM)))
    branch = low_back(product_highest(attended, w_out) + b_out + adapter_term(attended, column_mask, out_a, attn_b[3]))
    middle_activation = row_in + branch
    normed_two = low(layer_norm(middle_activation, gain_two, shift_two))
    preactivation = low_back(product_highest(normed_two, w_up) + b_up + adapter_term(normed_two, column_mask, up_a, up_b))
    activated = low(low_back(gelu_tanh(preactivation)))
    return middle_activation + product_highest(activated, w_down) + b_down + adapter_term(activated, column_mask, down_a, down_b)

def reference(tokens, cotangent, lengths, adapter_ids, w_query, w_key, w_value, w_out, w_up, w_down, b_query, b_value, b_out, b_up, b_down, gain_one, shift_one, gain_two, shift_two, qkv_a, out_a, attn_b, up_a, up_b, down_a, down_b):
    frozen = tuple((member.astype(jnp.float32) for member in (w_query, w_key, w_value, w_out, w_up, w_down, b_query, b_value, b_out, b_up, b_down, gain_one, shift_one, gain_two, shift_two)))
    adapters = tuple((member.astype(jnp.float32) for member in (qkv_a, out_a, attn_b, up_a, up_b, down_a, down_b)))
    positions = jnp.arange(LEN, dtype=jnp.int32)

    def one_row(running, packed):
        row_in, row_cot, length_row, adapter_row = packed
        picture, is_live, column_mask = token_info(length_row, adapter_row, positions)

        def forward(row_val, adapter_set):
            return row_forward(row_val, adapter_set, frozen, picture, column_mask)
        row_out, back_fn = jax.vjp(forward, row_in.astype(jnp.float32), adapters)
        grad_row, grad_set = back_fn(row_cot.astype(jnp.float32) * is_live[:, None].astype(jnp.float32))
        running = tuple((summed + update for summed, update in zip(running, grad_set)))
        return (running, (row_out.astype(jnp.bfloat16), grad_row))
    start_sum = tuple((jnp.zeros_like(member) for member in adapters))
    totals, (outputs, grads_in) = lax.scan(one_row, start_sum, (tokens, cotangent, lengths, adapter_ids))
    return (outputs, grads_in, totals[0], totals[1], totals[2], totals[3], totals[4], totals[5], totals[6])
```

```python
from functools import partial

import jax
import jax.numpy as jnp
from jax import lax
from jax.experimental import pallas as pl
from jax.experimental.pallas import tpu as pltpu
from jax.sharding import PartitionSpec as P

HEADS = 16
HEAD_DIM = 72
RANK = 16
ADAPTERS = 8
LORA = RANK * ADAPTERS
LANES = 128
EPS = 1e-06
SCALE = HEAD_DIM ** (-0.5)
BIG = 1e30
LOG2E = 1.4426950408889634
VMEM = 60 * 1024 * 1024

bf16 = jnp.bfloat16
f32 = jnp.float32


def nn(a, b):
    return jnp.dot(a, b, preferred_element_type=f32)


def nt(a, b):
    return lax.dot_general(a, b, (((1,), (1,)), ((), ())), preferred_element_type=f32)


def tn(a, b):
    return lax.dot_general(a, b, (((0,), (0,)), ((), ())), preferred_element_type=f32)


def up128(n):
    return -(-n // LANES) * LANES


def lane_ids(rows):
    return lax.broadcasted_iota(jnp.int32, (rows, LANES), 1)


def norm_parts(x):
    center = jnp.mean(x, axis=-1, keepdims=True)
    xc = x - center
    r = lax.rsqrt(jnp.mean(xc * xc, axis=-1, keepdims=True) + EPS)
    return xc * r, r


def norm_back(dn, gain, nh, r):
    gh = dn * gain
    a = jnp.mean(gh, axis=-1, keepdims=True)
    b = jnp.mean(gh * nh, axis=-1, keepdims=True)
    return r * (gh - a - nh * b)


def column_mask(aid):
    return (lane_ids(aid.shape[0]) // RANK == aid).astype(f32)


def qkv_kernel(nh, tm, x_ref, w_ref, at_ref, b_ref, bias_ref, vec_ref, aid_ref, pic_ref,
               out_ref, n1_ref, h_ref):
    p = pl.program_id(0)
    j = pl.program_id(1)
    tokens = x_ref.shape[0]
    width = nh * HEAD_DIM

    @pl.when((p == 0) & (j == 0))
    def _():
        def norm_step(i, c):
            rows = pl.ds(i * tm, tm)
            nhat, _ = norm_parts(x_ref[rows, :].astype(f32))
            n1_ref[rows, :] = (nhat * vec_ref[4:5, :] + vec_ref[5:6, :]).astype(bf16)
            return c
        lax.fori_loop(0, tokens // tm, norm_step, 0)

    @pl.when(j == 0)
    def _():
        def hidden_step(i, c):
            rows = pl.ds(i * tm, tm)
            h = nt(n1_ref[rows, :], at_ref[0]) * column_mask(aid_ref[rows, :])
            h_ref[0, rows, :] = h.astype(bf16)
            return c
        lax.fori_loop(0, tokens // tm, hidden_step, 0)

    def step(i, c):
        rows = pl.ds(i * tm, tm)
        y = nn(n1_ref[rows, :], w_ref[0])[:, :width]
        y = y + 0.5 * nn(h_ref[0, rows, :], b_ref[0, 0]) + bias_ref[0, 0]
        slot = lane_ids(tm) - HEAD_DIM
        pic = pic_ref[rows, :]
        same = slot == pic
        in_slots = (slot >= 0) & (slot < 16)
        q_aug = jnp.where(same, 1.0, 0.0)
        k_aug = jnp.where(in_slots & jnp.logical_not(same), -BIG, 0.0)
        v_aug = jnp.where((slot == 0) | (slot == 1), 1.0, 0.0)
        aug = jnp.where(p == 0, q_aug, jnp.where(p == 1, k_aug, v_aug))[:, HEAD_DIM:]
        for h in range(nh):
            head = y[:, h * HEAD_DIM:(h + 1) * HEAD_DIM]
            out_ref[0, h, rows, :HEAD_DIM] = head.astype(bf16)
            out_ref[0, h, rows, HEAD_DIM:] = aug.astype(bf16)
        return c
    lax.fori_loop(0, tokens // tm, step, 0)


def qkv_call(x, wa, at, bq, bias, vec, aid, pic):
    tokens, d = x.shape
    s = wa.shape[0]
    nh = HEADS // s
    slot = wa.shape[2] // 4
    tm = min(256, tokens)
    return pl.pallas_call(
        partial(qkv_kernel, nh, tm),
        grid=(3, s),
        in_specs=[
            pl.BlockSpec((tokens, d), lambda p, j: (0, 0)),
            pl.BlockSpec((1, d, slot), lambda p, j: (j, 0, p)),
            pl.BlockSpec((1, LORA, d), lambda p, j: (p, 0, 0)),
            pl.BlockSpec((1, 1, LORA, nh * HEAD_DIM), lambda p, j: (p, j, 0, 0)),
            pl.BlockSpec((1, 1, 1, nh * HEAD_DIM), lambda p, j: (p, j, 0, 0)),
            pl.BlockSpec(vec.shape, lambda p, j: (0, 0)),
            pl.BlockSpec((tokens, 1), lambda p, j: (0, 0)),
            pl.BlockSpec((tokens, 1), lambda p, j: (0, 0)),
        ],
        out_specs=[
            pl.BlockSpec((1, nh, tokens, LANES), lambda p, j: (p, j, 0, 0)),
            pl.BlockSpec((tokens, d), lambda p, j: (0, 0)),
            pl.BlockSpec((1, tokens, LORA), lambda p, j: (p, 0, 0)),
        ],
        out_shape=[
            jax.ShapeDtypeStruct((3, HEADS, tokens, LANES), bf16),
            jax.ShapeDtypeStruct((tokens, d), bf16),
            jax.ShapeDtypeStruct((3, tokens, LORA), bf16),
        ],
        compiler_params=pltpu.CompilerParams(vmem_limit_bytes=VMEM),
        name="qkv",
    )(x, wa, at, bq, bias, vec, aid, pic)


def attn_fwd_kernel(tq, q_ref, k_ref, v_ref, p_ref, o_ref):
    def step(i, c):
        rows = pl.ds(i * tq, tq)
        s = nt(q_ref[0, 0, rows, :], k_ref[0, 0])
        top = jnp.max(s, axis=-1, keepdims=True)
        p = jnp.exp2((s - top) * (SCALE * LOG2E)).astype(bf16)
        p_ref[0, rows, :] = p
        o = nn(p, v_ref[0, 0])
        inv = 1.0 / o[:, HEAD_DIM:HEAD_DIM + 1]
        one = inv.astype(bf16).astype(f32)
        two = (inv - one).astype(bf16).astype(f32)
        lane = lane_ids(tq)
        tail = jnp.where(lane == HEAD_DIM, one, jnp.where(lane == HEAD_DIM + 1, two, inv - one - two))
        o_ref[0, rows, :] = jnp.where(lane < HEAD_DIM, o * inv, tail).astype(bf16)
        return c
    lax.fori_loop(0, q_ref.shape[2] // tq, step, 0)


def attn_fwd_call(qkv, kv, off):
    tokens, keys = qkv.shape[2], kv.shape[2]
    tq = min(256, tokens)
    return pl.pallas_call(
        partial(attn_fwd_kernel, tq),
        grid=(HEADS,),
        in_specs=[
            pl.BlockSpec((1, 1, tokens, LANES), lambda h: (0, h, 0, 0)),
            pl.BlockSpec((1, 1, keys, LANES), lambda h: (off, h, 0, 0)),
            pl.BlockSpec((1, 1, keys, LANES), lambda h: (off + 1, h, 0, 0)),
        ],
        out_specs=[
            pl.BlockSpec((1, tokens, keys), lambda h: (h, 0, 0)),
            pl.BlockSpec((1, tokens, LANES), lambda h: (h, 0, 0)),
        ],
        out_shape=[
            jax.ShapeDtypeStruct((HEADS, tokens, keys), bf16),
            jax.ShapeDtypeStruct((HEADS, tokens, LANES), bf16),
        ],
        compiler_params=pltpu.CompilerParams(vmem_limit_bytes=VMEM),
        name="attn_fwd",
    )(qkv, kv, kv)


def attn_bwd_kernel(tq, q_ref, k_ref, v_ref, p_ref, do_ref, dq_ref, dk_ref, dv_ref, ds_ref):
    def step(i, c):
        rows = pl.ds(i * tq, tq)
        dp = nt(do_ref[0, rows, :], v_ref[0, 0])
        ds = (p_ref[0, rows, :].astype(f32) * dp).astype(bf16)
        ds_ref[rows, :] = ds
        dq_ref[0, rows, :] = (nn(ds, k_ref[0, 0]) * SCALE).astype(bf16)
        return c
    lax.fori_loop(0, q_ref.shape[2] // tq, step, 0)
    keys = k_ref.shape[2]
    tk = min(256, keys)

    def key_step(i, c):
        cols = pl.ds(i * tk, tk)
        dv_ref[0, cols, :] = tn(p_ref[0, :, cols], do_ref[0]).astype(bf16)
        dk_ref[0, cols, :] = (tn(ds_ref[:, cols], q_ref[0, 0]) * SCALE).astype(bf16)
        return c
    for i in range(keys // tk):
        key_step(i, 0)


def attn_bwd_call(qkv, kv, off, probs, do_aug):
    tokens, keys = qkv.shape[2], kv.shape[2]
    tq = min(256, tokens)
    return pl.pallas_call(
        partial(attn_bwd_kernel, tq),
        grid=(HEADS,),
        in_specs=[
            pl.BlockSpec((1, 1, tokens, LANES), lambda h: (0, h, 0, 0)),
            pl.BlockSpec((1, 1, keys, LANES), lambda h: (off, h, 0, 0)),
            pl.BlockSpec((1, 1, keys, LANES), lambda h: (off + 1, h, 0, 0)),
            pl.BlockSpec((1, tokens, keys), lambda h: (h, 0, 0)),
            pl.BlockSpec((1, tokens, LANES), lambda h: (h, 0, 0)),
        ],
        out_specs=[
            pl.BlockSpec((1, tokens, LANES), lambda h: (h, 0, 0)),
            pl.BlockSpec((1, keys, LANES), lambda h: (h, 0, 0)),
            pl.BlockSpec((1, keys, LANES), lambda h: (h, 0, 0)),
        ],
        out_shape=[
            jax.ShapeDtypeStruct((HEADS, tokens, LANES), bf16),
            jax.ShapeDtypeStruct((HEADS, keys, LANES), bf16),
            jax.ShapeDtypeStruct((HEADS, keys, LANES), bf16),
        ],
        scratch_shapes=[pltpu.VMEM((tokens, keys), bf16)],
        compiler_params=pltpu.CompilerParams(vmem_limit_bytes=VMEM),
        name="attn_bwd",
    )(qkv, kv, kv, probs, do_aug)


def gelu_parts(z):
    c = 0.7978845608028654
    z2 = z * z
    t = jnp.tanh(z * (c + (c * 0.044715) * z2))
    half = 0.5 * (1.0 + t)
    g = z * half
    dg = half + 0.5 * z * (1.0 - t * t) * (c + (3 * c * 0.044715) * z2)
    return g, dg


def ff_pieces(s, width):
    parts = max(width // 1024, 1)
    step = width // parts // LANES * LANES
    cuts = [k * step for k in range(parts)] + [width]
    return [(j, slice(a, b)) for j in range(s) for a, b in zip(cuts, cuts[1:])]


def mid_kernel(s, slot, oaug_ref, x_ref, cot_ref, aid_ref, wa_ref, wu_ref, wd_ref,
               at_ref, b_ref, ff_ref, bup_ref, vec_ref,
               mixed_ref, dmid_ref, do_ref, go_ref, gff_ref,
               wo_ref, ocat_ref, do_scr, g_ref, dgelu_ref):
    i = pl.program_id(0)
    tm, d = x_ref.shape
    ds = d // s
    pieces = ff_pieces(s, wu_ref.shape[2])
    mask = column_mask(aid_ref[...])
    live = aid_ref[...] >= 0
    bo, bd, gain2, shift2 = vec_ref[2:3, :], vec_ref[3:4, :], vec_ref[6:7, :], vec_ref[7:8, :]
    at_o, at_u, b_o, b_d = at_ref[3], at_ref[4], b_ref[3], b_ref[4]

    @pl.when(i == 0)
    def _():
        for j in range(s):
            wo_ref[:, j * ds:(j + 1) * ds] = wa_ref[j][:, :ds]
        go_ref[...] = jnp.zeros_like(go_ref)
        gff_ref[...] = jnp.zeros_like(gff_ref)

    for h in range(HEADS):
        ocat_ref[:, h * HEAD_DIM:(h + 1) * HEAD_DIM] = oaug_ref[h, :, :HEAD_DIM]
    ocat = ocat_ref[...]
    h_o = (nt(ocat, at_o) * mask).astype(bf16)
    mid = x_ref[...].astype(f32) + nn(ocat, wo_ref[...]) + 0.5 * nn(h_o, b_o) + bo
    nh2, r2 = norm_parts(mid)
    n2 = (nh2 * gain2 + shift2).astype(bf16)
    h_u = (nt(n2, at_u) * mask).astype(bf16)
    h_d = jnp.zeros((tm, LORA), f32)
    out = mid + bd
    for j, cols in pieces:
        z = nn(n2, wu_ref[j, :, cols]) + 0.5 * nn(h_u, ff_ref[1, j, :, cols]) + bup_ref[j, :, cols]
        g, dgelu = gelu_parts(z)
        g = g.astype(bf16)
        g_ref[j, :, cols] = g
        dgelu_ref[j, :, cols] = dgelu.astype(bf16)
        h_d = h_d + nt(g, ff_ref[0, j, :, cols])
        out = out + nt(g, wd_ref[j, :, cols])
    h_d = (h_d * mask).astype(bf16)
    mixed_ref[...] = (out + 0.5 * nn(h_d, b_d)).astype(bf16)

    dy = jnp.where(live, cot_ref[...], jnp.zeros_like(cot_ref))
    dh_d = (0.5 * nt(dy, b_d) * mask).astype(bf16)
    dh_u = jnp.zeros((tm, LORA), f32)
    dn2 = jnp.zeros((tm, d), f32)
    for j, cols in pieces:
        dg = (nn(dy, wd_ref[j, :, cols]) + nn(dh_d, ff_ref[0, j, :, cols])).astype(bf16)
        dz = (dg.astype(f32) * dgelu_ref[j, :, cols].astype(f32)).astype(bf16)
        dh_u = dh_u + nt(dz, ff_ref[1, j, :, cols])
        dn2 = dn2 + nt(dz, wu_ref[j, :, cols])
        gff_ref[0, j, :, cols] += tn(dh_d, g_ref[j, :, cols])
        gff_ref[1, j, :, cols] += 0.5 * tn(h_u, dz)
    dh_u = (0.5 * dh_u * mask).astype(bf16)
    dn2 = dn2 + nn(dh_u, at_u)
    dmid = dy.astype(f32) + norm_back(dn2, gain2, nh2, r2)
    dmid_ref[...] = dmid
    db = dmid.astype(bf16)
    dh_o = (0.5 * nt(db, b_o) * mask).astype(bf16)
    do_scr[...] = (nt(db, wo_ref[...]) + nn(dh_o, at_o)).astype(bf16)
    go_ref[0] += tn(dh_o, ocat)
    go_ref[1] += 0.5 * tn(h_o, db)
    go_ref[2] += tn(dh_u, n2)
    go_ref[3] += 0.5 * tn(h_d, dy)
    lane = lane_ids(tm)[:, HEAD_DIM:]
    for h in range(HEADS):
        parts = oaug_ref[h].astype(f32)
        inv = sum(parts[:, HEAD_DIM + k:HEAD_DIM + k + 1] for k in range(3))
        sl = slice(h * HEAD_DIM, (h + 1) * HEAD_DIM)
        dh = (do_scr[:, sl].astype(f32) * inv).astype(bf16)
        delta = jnp.sum(dh.astype(f32) * ocat_ref[:, sl].astype(f32), axis=-1, keepdims=True)
        hi = delta.astype(bf16).astype(f32)
        lo = delta - hi
        tail = jnp.where(lane == HEAD_DIM, -hi, jnp.where(lane == HEAD_DIM + 1, -lo, 0.0))
        do_ref[h, :, :HEAD_DIM] = dh
        do_ref[h, :, HEAD_DIM:] = tail.astype(bf16)


def mid_call(oaug, x, cot, aid, wa, wu, wd, at, b, ff, bup, vec):
    tokens, d = x.shape
    s = wa.shape[0]
    slot = wa.shape[2] // 4
    fs = wu.shape[2]
    tm = min(256, tokens)
    full = pl.BlockSpec(memory_space=pltpu.VMEM)
    tile = pl.BlockSpec((tm, d), lambda i: (i, 0))
    return pl.pallas_call(
        partial(mid_kernel, s, slot),
        grid=(tokens // tm,),
        in_specs=[
            pl.BlockSpec((HEADS, tm, LANES), lambda i: (0, i, 0)),
            tile, tile,
            pl.BlockSpec((tm, 1), lambda i: (i, 0)),
            pl.BlockSpec((s, d, slot), lambda i: (0, 0, 3), pipeline_mode=pl.Buffered(1)),
            full, full, full, full, full, full, full,
        ],
        out_specs=[
            tile, tile,
            pl.BlockSpec((HEADS, tm, LANES), lambda i: (0, i, 0)),
            full, full,
        ],
        out_shape=[
            jax.ShapeDtypeStruct((tokens, d), bf16),
            jax.ShapeDtypeStruct((tokens, d), f32),
            jax.ShapeDtypeStruct((HEADS, tokens, LANES), bf16),
            jax.ShapeDtypeStruct((4, LORA, d), f32),
            jax.ShapeDtypeStruct((2, s, LORA, fs), f32),
        ],
        scratch_shapes=[
            pltpu.VMEM((d, d), bf16),
            pltpu.VMEM((tm, d), bf16),
            pltpu.VMEM((tm, d), bf16),
            pltpu.VMEM((s, tm, fs), bf16),
            pltpu.VMEM((s, tm, fs), bf16),
        ],
        compiler_params=pltpu.CompilerParams(vmem_limit_bytes=VMEM),
        name="mid",
    )(oaug, x, cot, aid, wa, wu, wd, at, b, ff, bup, vec)


def tail_kernel(s, slot, dq_ref, dk_ref, dv_ref, x_ref, n1_ref, h_ref, dmid_ref, aid_ref,
                w_ref, at_ref, b_ref, vec_ref, out_ref, ga_ref, gb_ref, dy_ref):
    i = pl.program_id(0)
    tm, d = x_ref.shape
    nh = HEADS // s
    ds = d // s
    mask = column_mask(aid_ref[...])

    @pl.when(i == 0)
    def _():
        ga_ref[...] = jnp.zeros_like(ga_ref)
        gb_ref[...] = jnp.zeros_like(gb_ref)

    n1 = n1_ref[...]
    dn = jnp.zeros((tm, d), f32)
    for p, src in enumerate((dq_ref, dk_ref, dv_ref)):
        dh = jnp.zeros((tm, LORA), f32)
        for j in range(s):
            for h in range(nh):
                dy_ref[p, j, :, h * HEAD_DIM:(h + 1) * HEAD_DIM] = src[j * nh + h, :, :HEAD_DIM]
            dy = dy_ref[p, j]
            dh = dh + nt(dy, b_ref[p, j])
            dn = dn + nt(dy, w_ref[j, :, p * slot:p * slot + ds])
            gb_ref[p, j] += 0.5 * tn(h_ref[p], dy)
        dh = (0.5 * dh * mask).astype(bf16)
        dn = dn + nn(dh, at_ref[p])
        ga_ref[p] += tn(dh, n1)
    nhat, r = norm_parts(x_ref[...].astype(f32))
    out_ref[...] = dmid_ref[...] + norm_back(dn, vec_ref[4:5, :], nhat, r)


def tail_call(dq, dk, dv, x, n1, hid, dmid, aid, wa, at, bq, vec):
    tokens, d = x.shape
    s = wa.shape[0]
    slot = wa.shape[2] // 4
    tm = min(256, tokens)
    full = pl.BlockSpec(memory_space=pltpu.VMEM)
    tile = pl.BlockSpec((tm, d), lambda i: (i, 0))
    heads = pl.BlockSpec((HEADS, tm, LANES), lambda i: (0, i, 0))
    return pl.pallas_call(
        partial(tail_kernel, s, slot),
        grid=(tokens // tm,),
        in_specs=[
            heads, heads, heads, tile, tile,
            pl.BlockSpec((3, tm, LORA), lambda i: (0, i, 0)),
            tile,
            pl.BlockSpec((tm, 1), lambda i: (i, 0)),
            full, full, full, full,
        ],
        out_specs=[tile, full, full],
        out_shape=[
            jax.ShapeDtypeStruct((tokens, d), f32),
            jax.ShapeDtypeStruct((3, LORA, d), f32),
            jax.ShapeDtypeStruct((3, s, LORA, d // s), f32),
        ],
        scratch_shapes=[pltpu.VMEM((3, s, tm, d // s), bf16)],
        compiler_params=pltpu.CompilerParams(vmem_limit_bytes=VMEM),
        name="tail",
    )(dq, dk, dv, x, n1, hid, dmid, aid, wa, at, bq, vec)


def rows_of_adapters(a):
    t = jnp.swapaxes(a, -1, -2)
    return t.reshape(*t.shape[:-3], t.shape[-3] * t.shape[-2], t.shape[-1])


def local(tokens, cotangent, lengths, adapter_ids, w_query, w_key, w_value, w_out, w_up, w_down,
          b_query, b_value, b_out, b_up, b_down, gain_one, shift_one, gain_two, shift_two,
          qkv_a, out_a, attn_b, up_a, up_b, down_a, down_b):
    seq = lax.axis_size("seq")
    rows, part_len, d = tokens.shape
    group = seq // rows
    count = rows * part_len
    ds, fs = w_query.shape[1], w_up.shape[1]
    me = lax.axis_index("seq")
    row, chunk = me // group, me % group

    def moves(j):
        return [(a, (a % rows + j) % rows * group + a // rows) for a in range(seq)]

    def send(piece, pairs):
        return piece if all(a == b for a, b in pairs) else lax.ppermute(piece, "seq", pairs)

    def to_row(t):
        out = jnp.zeros((rows, part_len, d), t.dtype)
        for j in range(rows):
            piece = lax.dynamic_index_in_dim(t, (me + j) % rows, 0, False)
            out = lax.dynamic_update_index_in_dim(out, send(piece, moves(j)), (row - j) % rows, 0)
        return out.reshape(count, d)

    def from_row(t, dtype):
        t = t.reshape(rows, part_len, d)
        out = jnp.zeros((rows, part_len, d), dtype)
        for j in range(rows):
            piece = lax.dynamic_index_in_dim(t, (row - j) % rows, 0, False)
            pairs = [(b, a) for a, b in moves(j)]
            if not all(a == b for a, b in pairs):
                piece = piece.astype(bf16)
            got = send(piece, pairs).astype(dtype)
            out = lax.dynamic_update_index_in_dim(out, got, (me + j) % rows, 0)
        return out

    def gather_all(shard):
        full = lax.all_gather(shard, ("seq", "dp"), axis=0, tiled=True)
        return full.reshape(seq, d, shard.shape[1])

    slot = up128(ds)
    pad = ((0, 0), (0, slot - ds))
    wa = gather_all(jnp.concatenate([jnp.pad(w, pad) for w in (w_query, w_key, w_value, w_out)], axis=1))
    wu = gather_all(w_up)
    wd = gather_all(w_down.T)

    vec = jnp.stack([b_query, b_value, b_out, b_down, gain_one, shift_one, gain_two, shift_two])
    vec = lax.all_gather(vec, "seq", axis=1, tiled=True).astype(f32)
    bup = lax.all_gather(b_up[None], "seq", axis=0, tiled=True).astype(f32)[:, None]

    narrow = jnp.concatenate([
        rows_of_adapters(qkv_a), rows_of_adapters(out_a)[None], rows_of_adapters(up_a)[None],
        attn_b.reshape(4, -1, d), down_b.reshape(1, -1, d)])
    wide = jnp.stack([rows_of_adapters(down_a), up_b.reshape(-1, up_b.shape[-1])])
    narrow = lax.all_gather(narrow, "seq", axis=1, tiled=True)
    wide = lax.all_gather(wide, "seq", axis=1, tiled=True)
    at, b = narrow[:5], narrow[5:]
    bq = jnp.swapaxes(b[:3].reshape(3, LORA, seq, ds), 1, 2)
    ff = jnp.swapaxes(wide.reshape(2, LORA, seq, fs), 1, 2)

    my_len = lax.dynamic_index_in_dim(lengths, row, 0, False)
    my_ids = lax.dynamic_index_in_dim(adapter_ids, row, 0, False)
    slots = jnp.arange(my_len.shape[0], dtype=jnp.int32)
    ends = jnp.sum(jnp.where(slots[None, :] <= slots[:, None], my_len[None, :], 0), axis=1)
    pos = chunk * count + jnp.arange(count, dtype=jnp.int32)
    pic = jnp.sum((pos[:, None] >= ends[None, :]).astype(jnp.int32), axis=1, keepdims=True)
    aid = jnp.sum(jnp.where(pic == slots[None, :], my_ids[None, :], 0), axis=1, keepdims=True)
    aid = jnp.where(pos[:, None] < ends[-1], aid, -1)

    x = to_row(tokens)
    cot = to_row(cotangent)
    bias = jnp.stack([vec[0], jnp.zeros_like(vec[0]), vec[1]]).reshape(3, seq, 1, ds)
    qkv, n1, hid = qkv_call(x, wa, at, bq, bias, vec, aid, pic)
    teams = [[g * group + c for c in range(group)] for g in range(rows)]
    if group == 1:
        kv, off = qkv, 1
    else:
        kv = lax.all_gather(qkv[1:], "seq", axis=2, tiled=True, axis_index_groups=teams)
        off = 0
    probs, oaug = attn_fwd_call(qkv, kv, off)
    mixed, dmid, do_aug, g_out, g_ff = mid_call(oaug, x, cot, aid, wa, wu, wd, at, b, ff, bup, vec)
    dq, dk, dv = attn_bwd_call(qkv, kv, off, probs, do_aug)
    if group > 1:
        dk, dv = (lax.psum_scatter(t, "seq", scatter_dimension=1, axis_index_groups=teams, tiled=True)
                  for t in (dk, dv))
    d_in, g_a, g_b = tail_call(dq, dk, dv, x, n1, hid, dmid, aid, wa, at, bq, vec)

    mixed = from_row(mixed, bf16)
    d_in = from_row(d_in, f32)

    def total(t):
        t = lax.psum_scatter(t.astype(bf16), "seq", scatter_dimension=t.ndim - 2, tiled=True)
        return lax.psum(t, "dp").astype(f32)

    g_out, g_ff = total(g_out), total(g_ff)
    g_b = jnp.swapaxes(g_b, 1, 2).reshape(3, LORA, d)
    g_qkv = total(jnp.concatenate([g_a, g_b]))
    g_ff = jnp.swapaxes(g_ff, 1, 2)

    def down_form(t):
        t = t.reshape(*t.shape[:-2], -1, RANK, t.shape[-1])
        return jnp.swapaxes(t, -1, -2)

    def up_form(t):
        return t.reshape(*t.shape[:-2], -1, RANK, t.shape[-1])

    ff_rows = g_ff.reshape(2, -1, seq * fs)
    return (
        mixed,
        d_in,
        down_form(g_qkv[:3]),
        down_form(g_out[0]),
        up_form(jnp.concatenate([g_qkv[3:], g_out[1:2]])),
        down_form(g_out[2]),
        up_form(ff_rows[1]),
        down_form(ff_rows[0]),
        up_form(g_out[3]),
    )


def solution(mesh):
    both = P("dp", "seq", None)
    lead = P("seq", None, None)
    second = P(None, "seq", None, None)
    return jax.shard_map(
        local,
        mesh=mesh,
        in_specs=(both, both, P("dp", None), P("dp", None))
        + (P("dp", "seq"),) * 5 + (P("seq", "dp"),) + (P("seq"),) * 9
        + (second, lead, second, lead, lead, lead, lead),
        out_specs=(both, both, second, lead, second, lead, lead, lead, lead),
        check_vma=False,
    )
```

```python
from functools import partial

import jax
import jax.numpy as jnp
from jax import lax
from jax.experimental import pallas as pl
from jax.experimental.pallas import tpu as pltpu
from jax.sharding import PartitionSpec as P

HEADS = 16
HEAD_DIM = 72
RANK = 16
ADAPTERS = 8
LORA = RANK * ADAPTERS
LANES = 128
EPS = 1e-06
SCALE = HEAD_DIM ** (-0.5)
BIG = 1e30
LOG2E = 1.4426950408889634
VMEM = 61 * 1024 * 1024

MESH = pl.DeviceIdType.MESH
bf16 = jnp.bfloat16
f32 = jnp.float32


def nn(a, b):
    return jnp.dot(a, b, preferred_element_type=f32)


def nt(a, b):
    return lax.dot_general(a, b, (((1,), (1,)), ((), ())), preferred_element_type=f32)


def tn(a, b):
    return lax.dot_general(a, b, (((0,), (0,)), ((), ())), preferred_element_type=f32)


def up128(n):
    return -(-n // LANES) * LANES


def lane_ids(rows):
    return lax.broadcasted_iota(jnp.int32, (rows, LANES), 1)


def norm_parts(x):
    center = jnp.mean(x, axis=-1, keepdims=True)
    xc = x - center
    r = lax.rsqrt(jnp.mean(xc * xc, axis=-1, keepdims=True) + EPS)
    return xc * r, r


def norm_back(dn, gain, nh, r):
    gh = dn * gain
    a = jnp.mean(gh, axis=-1, keepdims=True)
    b = jnp.mean(gh * nh, axis=-1, keepdims=True)
    return r * (gh - a - nh * b)


def column_mask(aid):
    return (lane_ids(aid.shape[0]) // RANK == aid).astype(f32)


class Spot:
    def __init__(self, nz):
        dp = lax.axis_index("dp")
        self.nz = nz
        self.x = lax.axis_index("seq")
        self.z, self.y, self.c = dp // 4, (dp // 2) % 2, dp % 2
        self.xn = self.device(1 - self.x, self.y, self.z, self.c)
        self.yn = self.device(self.x, 1 - self.y, self.z, self.c)
        self.sib = self.device(self.x, self.y, self.z, 1 - self.c)
        self.zs = [None] + [self.device(self.x, self.y, self.zk(k), self.c) for k in range(1, nz)]

    def device(self, x, y, z, c):
        return ((z * 2 + y) * 2 + c, x)

    def shard(self, x, y, z):
        return (x * self.nz + z) * 4 + y * 2 + self.c

    def zk(self, k):
        return (self.z + k) % self.nz

    def barrier(self):
        peers = [self.xn, self.yn, self.sib] + self.zs[1:]
        sem = pltpu.get_barrier_semaphore()
        for peer in peers:
            pl.semaphore_signal(sem, inc=1, device_id=peer, device_id_type=MESH)
        pl.semaphore_wait(sem, len(peers))


def remote(src, dst, send, recv, device):
    return pltpu.make_async_remote_copy(
        src_ref=src, dst_ref=dst, send_sem=send, recv_sem=recv, device_id=device, device_id_type=MESH
    )


class Gather:
    def __init__(self, spot, parts, ins, outs, send, recv, core, own):
        self.s, self.parts, self.ins, self.outs = spot, parts, ins, outs
        self.send, self.recv, self.core, self.own = send, recv, core, own
        nz = spot.nz
        self.slot = {}
        for k in range(nz):
            for kind in "zxyd":
                for to in self.targets(kind, k):
                    self.slot[kind, k, to] = len(self.slot)

    @staticmethod
    def sends(nz):
        return nz - 1 + 3 * nz + 2 * nz + nz + nz + 4

    @staticmethod
    def scratch(nz, count):
        dma = pltpu.SemaphoreType.DMA
        return [dma((count, Gather.sends(nz))), dma((count, 4 * nz)), dma((count,)), dma((count,))]

    def targets(self, kind, k):
        nz = self.s.nz
        if kind == "z":
            return (["z%d" % i for i in range(1, nz)] if k == 0 else []) + ["x", "y", "s"]
        if kind == "x":
            return (["y"] if k < nz // 2 else []) + ["s"]
        if kind == "y":
            return (["x"] if k >= nz // 2 else []) + ["s"]
        return ["s"]

    def index(self, kind, k):
        s = self.s
        x = 1 - s.x if kind in "xd" else s.x
        y = 1 - s.y if kind in "yd" else s.y
        return s.shard(x, y, s.zk(k))

    def place(self, g, index):
        a, start, size = self.parts[g]
        return self.outs[a].at[index, :, pl.ds(start, size)]

    def source(self, g, kind, k):
        if kind == "z" and k == 0:
            a, start, size = self.parts[g]
            return self.ins[a].at[:, pl.ds(start, size)]
        return self.place(g, self.index(kind, k))

    def copy(self, g, kind, k, to):
        s, nz = self.s, self.s.nz
        index = self.index(kind, k)
        if to == "s":
            recv, device = self.core.at[g], s.sib
        elif to[0] == "z":
            i = int(to[1:])
            recv, device = self.recv.at[g, nz - i - 1], s.zs[i]
        elif to == "x":
            recv, device = self.recv.at[g, (nz - 1 if kind == "z" else 3 * nz - 1) + k], s.xn
        else:
            recv, device = self.recv.at[g, (2 * nz - 1 if kind == "z" else 3 * nz - 1) + k], s.yn
        return remote(self.source(g, kind, k), self.place(g, index), self.send.at[g, self.slot[kind, k, to]], recv, device)

    def local(self, g):
        return pltpu.make_async_copy(self.source(g, "z", 0), self.place(g, self.index("z", 0)), self.own.at[g])

    def arrive(self, g, kind, k):
        nz = self.s.nz
        if kind == "z" and k == 0:
            self.local(g).start()
        else:
            base = {"z": -1, "x": nz - 1, "y": 2 * nz - 1, "d": 3 * nz - 1}[kind]
            ref = self.place(g, self.index(kind, k))
            remote(ref, ref, self.send.at[g, 0], self.recv.at[g, base + k], self.s.xn).wait_recv()
        for to in self.targets(kind, k):
            self.copy(g, kind, k, to).start()

    def end(self, g):
        nz = self.s.nz
        a, start, size = self.parts[g]
        ref = self.outs[a].at[pl.ds(0, 4 * nz), :, pl.ds(start, size)]
        remote(ref, ref, self.send.at[g, 0], self.core.at[g], self.s.sib).wait_recv()
        self.local(g).wait()
        for kind, k, to in self.slot:
            self.copy(g, kind, k, to).wait_send()

    def actions(self):
        nz, n = self.s.nz, len(self.parts)
        out = []
        for t in range(n + 3):
            if t < n:
                out.append((self.arrive, t, "z", 0))
            if 0 <= t - 1 < n:
                out += [(self.arrive, t - 1, "z", k) for k in range(1, nz)]
            if 0 <= t - 2 < n:
                out += [(self.arrive, t - 2, kind, k) for k in range(nz) for kind in "xy"]
            if 0 <= t - 3 < n:
                out += [(self.arrive, t - 3, "d", k) for k in range(nz)]
        out += [(self.end, g) for g in range(n)]
        return out


class Swap:
    def __init__(self, spot, mine, got, sems, slot=None):
        self.s, self.mine, self.got, self.sems = spot, mine, got, sems
        self.slot = spot.x if slot is None else slot

    def copies(self):
        s = self.s
        here = pltpu.make_async_copy(self.mine.at[s.x], self.got.at[s.x], self.sems.at[0])
        there = remote(self.mine.at[1 - s.x], self.got.at[self.slot], self.sems.at[1], self.sems.at[2], s.xn)
        return here, there

    def start(self):
        for copy in self.copies():
            copy.start()

    def end(self):
        here, there = self.copies()
        here.wait()
        ref = self.got.at[1 - self.s.x]
        remote(ref, ref, self.sems.at[1], self.sems.at[2], self.s.xn).wait_recv()
        there.wait_send()


def run_actions(actions, step, steps):
    for t in range(steps):
        a, b = len(actions) * t // steps, len(actions) * (t + 1) // steps
        if a == b:
            continue

        @pl.when(step == t)
        def _(a=a, b=b):
            for action in actions[a:b]:
                action[0](*action[1:])


class Reduce:
    def __init__(self, spot, data, result, refs):
        self.s, self.data, self.result = spot, data, result
        self.r1, self.s1, self.r2, self.s2, self.r3, self.s3, self.r4, self.total = refs[:8]
        self.send, self.recv, self.out = refs[8:]

    @staticmethod
    def scratch(nz, width):
        def v(*dims):
            return pltpu.VMEM((*dims, 8, width), bf16)
        dma = pltpu.SemaphoreType.DMA
        n = 5 + 2 * (nz - 1)
        return [v(2, 2 * nz), v(2, 2 * nz), v(2 * nz), v(2 * nz), v(nz), v(nz), v(nz), v(2, 2 * nz),
                dma((n,)), dma((n,)), dma((1,))]

    def pair(self, i, src, dst, device):
        return remote(src, dst, self.send.at[i], self.recv.at[i], device)

    def to_core(self):
        return self.pair(0, self.data.at[1 - self.s.c], self.r1, self.s.sib)

    def to_x(self):
        return self.pair(1, self.s1.at[1 - self.s.x], self.r2, self.s.xn)

    def to_y(self):
        nz = self.s.nz
        return self.pair(2, self.s2.at[pl.ds((1 - self.s.y) * nz, nz)], self.r3, self.s.yn)

    def to_z(self, k):
        s = self.s
        return self.pair(4 + k, self.s3.at[s.zk(k)], self.r4.at[s.z], s.zs[k])

    def from_z(self, k):
        s = self.s
        ref = self.r4.at[s.zk(k)]
        return remote(ref, ref, self.send.at[4 + s.nz - k], self.recv.at[4 + s.nz - k], s.zs[k])

    def back_z(self, k):
        s = self.s
        ref = self.total.at[s.c, s.y * s.nz + s.z]
        return self.pair(4 + s.nz - 1 + k, ref, ref, s.zs[k])

    def from_back_z(self, k):
        s = self.s
        i = 4 + s.nz - 1 + s.nz - k
        ref = self.total.at[s.c, s.y * s.nz + s.zk(k)]
        return remote(ref, ref, self.send.at[i], self.recv.at[i], s.zs[k])

    def back_y(self, y):
        s = self.s
        ref = self.total.at[s.c, pl.ds(y * s.nz, s.nz)]
        return self.pair(3, ref, ref, s.yn)

    def back_core(self, c):
        ref = self.total.at[c]
        return self.pair(4, ref, ref, self.s.sib)

    def one(self):
        self.to_core().start()

    def two(self):
        s, nz = self.s, self.s.nz
        self.to_core().wait_recv()

        def add(i, c):
            x, b = i // (2 * nz), i % (2 * nz)
            self.s1[x, b] = (self.data[s.c, x, b].astype(f32) + self.r1[x, b].astype(f32)).astype(bf16)
            return c
        lax.fori_loop(0, 4 * nz, add, 0)
        self.to_x().start()

    def three(self):
        s, nz = self.s, self.s.nz
        self.to_x().wait_recv()

        def add(b, c):
            self.s2[b] = (self.s1[s.x, b].astype(f32) + self.r2[b].astype(f32)).astype(bf16)
            return c
        lax.fori_loop(0, 2 * nz, add, 0)
        self.to_y().start()

    def four(self):
        s, nz = self.s, self.s.nz
        self.to_y().wait_recv()

        def add(b, c):
            self.s3[b] = (self.s2[s.y * nz + b].astype(f32) + self.r3[b].astype(f32)).astype(bf16)
            return c
        lax.fori_loop(0, nz, add, 0)
        for k in range(1, nz):
            self.to_z(k).start()

    def five(self):
        s, nz = self.s, self.s.nz
        for k in range(1, nz):
            self.from_z(k).wait_recv()
        v = self.s3[s.z].astype(f32)
        for k in range(1, nz):
            v = v + self.r4[s.zk(k)].astype(f32)
        self.total[s.c, s.y * nz + s.z] = v.astype(bf16)
        for k in range(1, nz):
            self.back_z(k).start()

    def six(self):
        for k in range(1, self.s.nz):
            self.from_back_z(k).wait_recv()
        self.back_y(self.s.y).start()

    def seven(self):
        self.back_y(1 - self.s.y).wait_recv()
        self.back_core(self.s.c).start()

    def end(self):
        s = self.s
        self.back_core(1 - s.c).wait_recv()
        out = pltpu.make_async_copy(self.total, self.result, self.out.at[0])
        out.start()
        out.wait()
        self.to_core().wait_send()
        self.to_x().wait_send()
        self.to_y().wait_send()
        for k in range(1, s.nz):
            self.to_z(k).wait_send()
            self.back_z(k).wait_send()
        self.back_y(s.y).wait_send()
        self.back_core(s.c).wait_send()

    def actions(self):
        return [(f,) for f in (self.one, self.two, self.three, self.four, self.five, self.six, self.seven, self.end)]


def start_kernel(nz, parts, na, *refs):
    ins, (tokens, vec), refs = refs[:na], refs[na:na + 2], refs[na + 2:]
    outs, (row, vecs), refs = refs[:na], refs[na:na + 2], refs[na + 2:]
    spot = Spot(nz)
    spot.barrier()
    gather = Gather(spot, parts, ins, outs, *refs[:4])
    swap = Swap(spot, tokens, row, refs[4])
    vsems = refs[5]
    here = pltpu.make_async_copy(vec, vecs.at[spot.x], vsems.at[0])
    there = remote(vec, vecs.at[spot.x], vsems.at[1], vsems.at[2], spot.xn)
    here.start()
    there.start()
    swap.start()
    for action in gather.actions():
        action[0](*action[1:])
    swap.end()
    here.wait()
    there.wait_send()
    ref = vecs.at[1 - spot.x]
    remote(ref, ref, vsems.at[1], vsems.at[2], spot.xn).wait_recv()


def any_specs(n):
    return [pl.BlockSpec(memory_space=pl.ANY)] * n


def gathered(nz, arrays):
    return [jax.ShapeDtypeStruct((8 * nz,) + a.shape, a.dtype) for a in arrays]


def start_call(nz, shards, parts, tokens, vec):
    na = len(shards)
    dma = pltpu.SemaphoreType.DMA
    return pl.pallas_call(
        partial(start_kernel, nz, parts, na),
        in_specs=any_specs(na + 2),
        out_specs=any_specs(na + 2),
        out_shape=gathered(nz, shards) + [
            jax.ShapeDtypeStruct(tokens.shape, bf16), jax.ShapeDtypeStruct((2,) + vec.shape, bf16)],
        scratch_shapes=Gather.scratch(nz, len(parts)) + [dma((3,)), dma((3,))],
        compiler_params=pltpu.CompilerParams(collective_id=1, has_side_effects=True, vmem_limit_bytes=8 * 2**20),
        name="start",
    )(*shards, tokens, vec)


def finish_kernel(nz, g_ref, d_ref, total_ref, got_ref, *refs):
    spot = Spot(nz)
    spot.barrier()
    reduce = Reduce(spot, g_ref, total_ref, refs[:-1])
    sems = refs[-1]
    there = remote(d_ref.at[1 - spot.x], got_ref, sems.at[0], sems.at[1], spot.xn)
    reduce.one()
    there.start()
    for f in reduce.actions()[1:]:
        f[0]()
    there.wait()


def finish_call(nz, g, d):
    width = g.shape[-1]
    dma = pltpu.SemaphoreType.DMA
    return pl.pallas_call(
        partial(finish_kernel, nz),
        in_specs=[pl.BlockSpec(memory_space=pltpu.VMEM), pl.BlockSpec(memory_space=pl.ANY)],
        out_specs=any_specs(2),
        out_shape=[
            jax.ShapeDtypeStruct((2,) + g.shape[2:], bf16), jax.ShapeDtypeStruct(d.shape[1:], bf16)],
        scratch_shapes=Reduce.scratch(nz, width) + [dma((2,))],
        compiler_params=pltpu.CompilerParams(collective_id=5, has_side_effects=True, vmem_limit_bytes=40 * 2**20),
        name="finish",
    )(g, d)


class Quiet:
    args = ()
    outs = ()
    steps = 1

    def split(self, refs, own):
        a, b = len(self.args), len(self.outs)
        return refs[:a], refs[a:a + own], refs[a + own:a + own + b], refs[a + own + b:]

    def in_specs(self):
        return any_specs(len(self.args))

    def out_specs(self):
        return any_specs(len(self.outs))

    def out_shape(self):
        return list(self.outs)

    def scratch(self):
        return []

    def params(self):
        return pltpu.CompilerParams(vmem_limit_bytes=VMEM)

    def run(self, step, ins, outs, refs):
        pass

    def close(self, step, ins, outs, refs):
        pass


class Fetch(Quiet):
    def __init__(self, nz, shards, parts, cid, halves=None):
        self.nz, self.parts, self.cid, self.na = nz, parts, cid, len(shards)
        self.args = tuple(shards) + (() if halves is None else (halves,))
        self.outs = gathered(nz, shards) + ([] if halves is None else [jax.ShapeDtypeStruct(halves.shape, halves.dtype)])

    def scratch(self):
        return Gather.scratch(self.nz, len(self.parts)) + [pltpu.SemaphoreType.DMA((3,))]

    def params(self):
        return pltpu.CompilerParams(vmem_limit_bytes=VMEM, collective_id=self.cid, has_side_effects=True)

    def make(self, ins, outs, refs):
        spot = Spot(self.nz)
        gather = Gather(spot, self.parts, ins[:self.na], outs[:self.na], *refs[-5:-1])
        swap = Swap(spot, ins[-1], outs[-1], refs[-1]) if len(ins) > self.na else None
        return spot, gather, swap

    def run(self, step, ins, outs, refs):
        spot, gather, swap = self.make(ins, outs, refs)

        @pl.when(step == 0)
        def _():
            spot.barrier()
            if swap:
                swap.start()
        run_actions(gather.actions()[:-len(self.parts)], step, self.steps)

    def close(self, step, ins, outs, refs):
        _, gather, swap = self.make(ins, outs, refs)

        @pl.when(step == self.steps - 1)
        def _():
            for action in gather.actions()[-len(self.parts):]:
                action[0](*action[1:])
            if swap:
                swap.end()


class Settle(Quiet):
    def __init__(self, nz, g, halves, cid):
        self.nz, self.width, self.cid = nz, g.shape[-1], cid
        self.args = (g, halves)
        self.outs = [jax.ShapeDtypeStruct((2,) + g.shape[2:], bf16), jax.ShapeDtypeStruct(halves.shape, halves.dtype)]

    def in_specs(self):
        return [pl.BlockSpec(memory_space=pltpu.VMEM), pl.BlockSpec(memory_space=pl.ANY)]

    def scratch(self):
        return Reduce.scratch(self.nz, self.width) + [pltpu.SemaphoreType.DMA((3,))]

    def params(self):
        return pltpu.CompilerParams(vmem_limit_bytes=VMEM, collective_id=self.cid, has_side_effects=True)

    def make(self, ins, outs, refs):
        spot = Spot(self.nz)
        refs = refs[-12:]
        return spot, Reduce(spot, ins[0], outs[0], refs[:-1]), Swap(spot, ins[1], outs[1], refs[-1])

    def run(self, step, ins, outs, refs):
        spot, reduce, swap = self.make(ins, outs, refs)
        when = [0, 1, 4, 7, 9, 11, 13]

        @pl.when(step == 0)
        def _():
            spot.barrier()
        for (f,), t in zip(reduce.actions(), when):
            pl.when(step == t)(f)

        @pl.when(step == 4)
        def _():
            swap.start()

    def close(self, step, ins, outs, refs):
        _, reduce, swap = self.make(ins, outs, refs)

        @pl.when(step == self.steps - 1)
        def _():
            reduce.end()
            swap.end()


def qkv_kernel(nh, tm, comm, x_ref, w_ref, at_ref, b_ref, bias_ref, vec_ref, aid_ref, pic_ref, *refs):
    p = pl.program_id(0)
    j = pl.program_id(1)
    ins, (out_ref, n1_ref, h_ref), outs, refs = comm.split(refs, 3)
    comm.run(p * pl.num_programs(1) + j, ins, outs, refs)
    tokens = x_ref.shape[0]
    width = nh * HEAD_DIM

    @pl.when((p == 0) & (j == 0))
    def _():
        def norm_step(i, c):
            rows = pl.ds(i * tm, tm)
            nhat, _ = norm_parts(x_ref[rows, :].astype(f32))
            n1_ref[rows, :] = (nhat * vec_ref[4:5, :] + vec_ref[5:6, :]).astype(bf16)
            return c
        lax.fori_loop(0, tokens // tm, norm_step, 0)

    @pl.when(j == 0)
    def _():
        def hidden_step(i, c):
            rows = pl.ds(i * tm, tm)
            h = nt(n1_ref[rows, :], at_ref[0]) * column_mask(aid_ref[rows, :])
            h_ref[0, rows, :] = h.astype(bf16)
            return c
        lax.fori_loop(0, tokens // tm, hidden_step, 0)

    def step(i, c):
        rows = pl.ds(i * tm, tm)
        y = nn(n1_ref[rows, :], w_ref[0])[:, :width]
        y = y + 0.5 * nn(h_ref[0, rows, :], b_ref[0, 0]) + bias_ref[0, 0]
        slot = lane_ids(tm) - HEAD_DIM
        pic = pic_ref[rows, :]
        same = slot == pic
        in_slots = (slot >= 0) & (slot < 16)
        q_aug = jnp.where(same, 1.0, 0.0)
        k_aug = jnp.where(in_slots & jnp.logical_not(same), -BIG, 0.0)
        v_aug = jnp.where((slot == 0) | (slot == 1), 1.0, 0.0)
        aug = jnp.where(p == 0, q_aug, jnp.where(p == 1, k_aug, v_aug))[:, HEAD_DIM:]
        for h in range(nh):
            head = y[:, h * HEAD_DIM:(h + 1) * HEAD_DIM]
            out_ref[0, h, rows, :HEAD_DIM] = head.astype(bf16)
            out_ref[0, h, rows, HEAD_DIM:] = aug.astype(bf16)
        return c
    lax.fori_loop(0, tokens // tm, step, 0)
    comm.close(p * pl.num_programs(1) + j, ins, outs, refs)


def qkv_call(x, wa, at, bq, bias, vec, aid, pic, comm):
    tokens, d = x.shape
    s = wa.shape[0]
    nh = HEADS // s
    slot = up128(d // s)
    tm = min(256, tokens)
    comm.steps = 3 * s
    return pl.pallas_call(
        partial(qkv_kernel, nh, tm, comm),
        grid=(3, s),
        in_specs=[
            pl.BlockSpec((tokens, d), lambda p, j: (0, 0)),
            pl.BlockSpec((1, d, slot), lambda p, j: (j, 0, p)),
            pl.BlockSpec((1, LORA, d), lambda p, j: (p, 0, 0)),
            pl.BlockSpec((1, 1, LORA, nh * HEAD_DIM), lambda p, j: (p, j, 0, 0)),
            pl.BlockSpec((1, 1, 1, nh * HEAD_DIM), lambda p, j: (p, j, 0, 0)),
            pl.BlockSpec(vec.shape, lambda p, j: (0, 0)),
            pl.BlockSpec((tokens, 1), lambda p, j: (0, 0)),
            pl.BlockSpec((tokens, 1), lambda p, j: (0, 0)),
        ] + comm.in_specs(),
        out_specs=[
            pl.BlockSpec((1, nh, tokens, LANES), lambda p, j: (p, j, 0, 0)),
            pl.BlockSpec((tokens, d), lambda p, j: (0, 0)),
            pl.BlockSpec((1, tokens, LORA), lambda p, j: (p, 0, 0)),
        ] + comm.out_specs(),
        out_shape=[
            jax.ShapeDtypeStruct((3, HEADS, tokens, LANES), bf16),
            jax.ShapeDtypeStruct((tokens, d), bf16),
            jax.ShapeDtypeStruct((3, tokens, LORA), bf16),
        ] + comm.out_shape(),
        scratch_shapes=comm.scratch(),
        compiler_params=comm.params(),
        name="qkv",
    )(x, wa, at, bq, bias, vec, aid, pic, *comm.args)


def attn_fwd_kernel(tq, comm, q_ref, k_ref, v_ref, *refs):
    ins, (p_ref, o_ref), outs, refs = comm.split(refs, 2)
    comm.run(pl.program_id(0), ins, outs, refs)

    def step(i, c):
        rows = pl.ds(i * tq, tq)
        s = nt(q_ref[0, 0, rows, :], k_ref[0, 0])
        top = jnp.max(s, axis=-1, keepdims=True)
        p = jnp.exp2((s - top) * (SCALE * LOG2E)).astype(bf16)
        p_ref[0, rows, :] = p
        o = nn(p, v_ref[0, 0])
        inv = 1.0 / o[:, HEAD_DIM:HEAD_DIM + 1]
        one = inv.astype(bf16).astype(f32)
        two = (inv - one).astype(bf16).astype(f32)
        lane = lane_ids(tq)
        tail = jnp.where(lane == HEAD_DIM, one, jnp.where(lane == HEAD_DIM + 1, two, inv - one - two))
        o_ref[0, rows, :] = jnp.where(lane < HEAD_DIM, o * inv, tail).astype(bf16)
        return c
    lax.fori_loop(0, q_ref.shape[2] // tq, step, 0)
    comm.close(pl.program_id(0), ins, outs, refs)


def attn_fwd_call(qkv, kv, off, comm):
    tokens, keys = qkv.shape[2], kv.shape[2]
    tq = min(256, tokens)
    comm.steps = HEADS
    return pl.pallas_call(
        partial(attn_fwd_kernel, tq, comm),
        grid=(HEADS,),
        in_specs=[
            pl.BlockSpec((1, 1, tokens, LANES), lambda h: (0, h, 0, 0)),
            pl.BlockSpec((1, 1, keys, LANES), lambda h: (off, h, 0, 0)),
            pl.BlockSpec((1, 1, keys, LANES), lambda h: (off + 1, h, 0, 0)),
        ] + comm.in_specs(),
        out_specs=[
            pl.BlockSpec((1, tokens, keys), lambda h: (h, 0, 0)),
            pl.BlockSpec((1, tokens, LANES), lambda h: (h, 0, 0)),
        ] + comm.out_specs(),
        out_shape=[
            jax.ShapeDtypeStruct((HEADS, tokens, keys), bf16),
            jax.ShapeDtypeStruct((HEADS, tokens, LANES), bf16),
        ] + comm.out_shape(),
        scratch_shapes=comm.scratch(),
        compiler_params=comm.params(),
        name="attn_fwd",
    )(qkv, kv, kv, *comm.args)


def attn_bwd_kernel(tq, comm, q_ref, k_ref, v_ref, p_ref, do_ref, *refs):
    ins, (dq_ref, dk_ref, dv_ref), outs, (ds_ref, *refs) = comm.split(refs, 3)
    comm.run(pl.program_id(0), ins, outs, refs)

    def step(i, c):
        rows = pl.ds(i * tq, tq)
        dp = nt(do_ref[0, rows, :], v_ref[0, 0])
        ds = (p_ref[0, rows, :].astype(f32) * dp).astype(bf16)
        ds_ref[rows, :] = ds
        dq_ref[0, rows, :] = (nn(ds, k_ref[0, 0]) * SCALE).astype(bf16)
        return c
    lax.fori_loop(0, q_ref.shape[2] // tq, step, 0)
    keys = k_ref.shape[2]
    tk = min(256, keys)

    def key_step(i, c):
        cols = pl.ds(i * tk, tk)
        dv_ref[0, cols, :] = tn(p_ref[0, :, cols], do_ref[0]).astype(bf16)
        dk_ref[0, cols, :] = (tn(ds_ref[:, cols], q_ref[0, 0]) * SCALE).astype(bf16)
        return c
    for i in range(keys // tk):
        key_step(i, 0)
    comm.close(pl.program_id(0), ins, outs, refs)


def attn_bwd_call(qkv, kv, off, probs, do_aug, comm):
    tokens, keys = qkv.shape[2], kv.shape[2]
    tq = min(256, tokens)
    comm.steps = HEADS
    return pl.pallas_call(
        partial(attn_bwd_kernel, tq, comm),
        grid=(HEADS,),
        in_specs=[
            pl.BlockSpec((1, 1, tokens, LANES), lambda h: (0, h, 0, 0)),
            pl.BlockSpec((1, 1, keys, LANES), lambda h: (off, h, 0, 0)),
            pl.BlockSpec((1, 1, keys, LANES), lambda h: (off + 1, h, 0, 0)),
            pl.BlockSpec((1, tokens, keys), lambda h: (h, 0, 0)),
            pl.BlockSpec((1, tokens, LANES), lambda h: (h, 0, 0)),
        ] + comm.in_specs(),
        out_specs=[
            pl.BlockSpec((1, tokens, LANES), lambda h: (h, 0, 0)),
            pl.BlockSpec((1, keys, LANES), lambda h: (h, 0, 0)),
            pl.BlockSpec((1, keys, LANES), lambda h: (h, 0, 0)),
        ] + comm.out_specs(),
        out_shape=[
            jax.ShapeDtypeStruct((HEADS, tokens, LANES), bf16),
            jax.ShapeDtypeStruct((HEADS, keys, LANES), bf16),
            jax.ShapeDtypeStruct((HEADS, keys, LANES), bf16),
        ] + comm.out_shape(),
        scratch_shapes=[pltpu.VMEM((tokens, keys), bf16)] + comm.scratch(),
        compiler_params=comm.params(),
        name="attn_bwd",
    )(qkv, kv, kv, probs, do_aug, *comm.args)


def gelu_parts(z):
    c = 0.7978845608028654
    z2 = z * z
    t = jnp.tanh(z * (c + (c * 0.044715) * z2))
    half = 0.5 * (1.0 + t)
    g = z * half
    dg = half + 0.5 * z * (1.0 - t * t) * (c + (3 * c * 0.044715) * z2)
    return g, dg


def ff_pieces(s, width):
    parts = max(width // 1024, 1)
    step = width // parts // LANES * LANES
    cuts = [k * step for k in range(parts)] + [width]
    return [(j, slice(a, b)) for j in range(s) for a, b in zip(cuts, cuts[1:])]


def mid_kernel(s, oaug_ref, x_ref, cot_ref, aid_ref, wa_ref, wu_ref, wd_ref,
               ab_ref, ff_ref, bup_ref, vec_ref,
               mixed_ref, dmid_ref, do_ref, pack_ref,
               wo_ref, ocat_ref, do_scr, g_ref, dgelu_ref, go_ref, gff_ref):
    i = pl.program_id(0)
    tm, d = x_ref.shape
    ds = d // s
    pieces = ff_pieces(s, ff_ref.shape[3])
    mask = column_mask(aid_ref[...])
    live = aid_ref[...] >= 0
    bo, bd, gain2, shift2 = vec_ref[2:3, :], vec_ref[3:4, :], vec_ref[6:7, :], vec_ref[7:8, :]
    at_o, at_u, b_o, b_d = ab_ref[0], ab_ref[1], ab_ref[2], ab_ref[3]

    @pl.when(i == 0)
    def _():
        for j in range(s):
            wo_ref[:, j * ds:(j + 1) * ds] = wa_ref[j][:, :ds]
        go_ref[...] = jnp.zeros_like(go_ref)
        gff_ref[...] = jnp.zeros_like(gff_ref)

    for h in range(HEADS):
        ocat_ref[:, h * HEAD_DIM:(h + 1) * HEAD_DIM] = oaug_ref[h, :, :HEAD_DIM]
    ocat = ocat_ref[...]
    h_o = (nt(ocat, at_o) * mask).astype(bf16)
    mid = x_ref[...].astype(f32) + nn(ocat, wo_ref[...]) + 0.5 * nn(h_o, b_o) + bo
    nh2, r2 = norm_parts(mid)
    n2 = (nh2 * gain2 + shift2).astype(bf16)
    h_u = (nt(n2, at_u) * mask).astype(bf16)
    h_d = jnp.zeros((tm, LORA), f32)
    out = mid + bd
    for j, cols in pieces:
        z = nn(n2, wu_ref[j, :, cols]) + 0.5 * nn(h_u, ff_ref[1, j, :, cols]) + bup_ref[j, :, cols]
        g, dgelu = gelu_parts(z)
        g = g.astype(bf16)
        g_ref[j, :, cols] = g
        dgelu_ref[j, :, cols] = dgelu.astype(bf16)
        h_d = h_d + nt(g, ff_ref[0, j, :, cols])
        out = out + nt(g, wd_ref[j, :, cols])
    h_d = (h_d * mask).astype(bf16)
    mixed_ref[...] = (out + 0.5 * nn(h_d, b_d)).astype(bf16)

    dy = jnp.where(live, cot_ref[...], jnp.zeros_like(cot_ref))
    dh_d = (0.5 * nt(dy, b_d) * mask).astype(bf16)
    dh_u = jnp.zeros((tm, LORA), f32)
    dn2 = jnp.zeros((tm, d), f32)
    for j, cols in pieces:
        dg = (nn(dy, wd_ref[j, :, cols]) + nn(dh_d, ff_ref[0, j, :, cols])).astype(bf16)
        dz = (dg.astype(f32) * dgelu_ref[j, :, cols].astype(f32)).astype(bf16)
        dh_u = dh_u + nt(dz, ff_ref[1, j, :, cols])
        dn2 = dn2 + nt(dz, wu_ref[j, :, cols])
        gff_ref[0, j, :, cols] += tn(dh_d, g_ref[j, :, cols])
        gff_ref[1, j, :, cols] += 0.5 * tn(h_u, dz)
    dh_u = (0.5 * dh_u * mask).astype(bf16)
    dn2 = dn2 + nn(dh_u, at_u)
    dmid = dy.astype(f32) + norm_back(dn2, gain2, nh2, r2)
    dmid_ref[...] = dmid
    db = dmid.astype(bf16)
    dh_o = (0.5 * nt(db, b_o) * mask).astype(bf16)
    do_scr[...] = (nt(db, wo_ref[...]) + nn(dh_o, at_o)).astype(bf16)
    go_ref[0] += tn(dh_o, ocat)
    go_ref[1] += 0.5 * tn(h_o, db)
    go_ref[2] += tn(dh_u, n2)
    go_ref[3] += 0.5 * tn(h_d, dy)
    lane = lane_ids(tm)[:, HEAD_DIM:]
    for h in range(HEADS):
        parts = oaug_ref[h].astype(f32)
        inv = sum(parts[:, HEAD_DIM + k:HEAD_DIM + k + 1] for k in range(3))
        sl = slice(h * HEAD_DIM, (h + 1) * HEAD_DIM)
        dh = (do_scr[:, sl].astype(f32) * inv).astype(bf16)
        delta = jnp.sum(dh.astype(f32) * ocat_ref[:, sl].astype(f32), axis=-1, keepdims=True)
        hi = delta.astype(bf16).astype(f32)
        lo = delta - hi
        tail = jnp.where(lane == HEAD_DIM, -hi, jnp.where(lane == HEAD_DIM + 1, -lo, 0.0))
        do_ref[h, :, :HEAD_DIM] = dh
        do_ref[h, :, HEAD_DIM:] = tail.astype(bf16)

    @pl.when(i == pl.num_programs(0) - 1)
    def _():
        fs = ff_ref.shape[3]
        for c, order in enumerate(((0, 2), (1, 3))):
            for k, which in enumerate(order):
                pack_ref[c, :, k * d:(k + 1) * d] = go_ref[which].astype(bf16)
            for j in range(s):
                at = 2 * d + j * up128(fs)
                pack_ref[c, :, at:at + fs] = gff_ref[c, j].astype(bf16)
                if up128(fs) > fs:
                    pack_ref[c, :, at + fs:at + up128(fs)] = jnp.zeros((LORA, up128(fs) - fs), bf16)


def mid_call(oaug, x, cot, aid, wo, wu, wd, ab, ff, bup, vec):
    tokens, d = x.shape
    s = wo.shape[0]
    fs = ff.shape[3]
    tm = min(256, tokens)
    full = pl.BlockSpec(memory_space=pltpu.VMEM)
    tile = pl.BlockSpec((tm, d), lambda i: (i, 0))
    return pl.pallas_call(
        partial(mid_kernel, s),
        grid=(tokens // tm,),
        in_specs=[
            pl.BlockSpec((HEADS, tm, LANES), lambda i: (0, i, 0)),
            tile, tile,
            pl.BlockSpec((tm, 1), lambda i: (i, 0)),
            full, full, full, full, full, full, full,
        ],
        out_specs=[
            tile, tile,
            pl.BlockSpec((HEADS, tm, LANES), lambda i: (0, i, 0)),
            full,
        ],
        out_shape=[
            jax.ShapeDtypeStruct((tokens, d), bf16),
            jax.ShapeDtypeStruct((tokens, d), f32),
            jax.ShapeDtypeStruct((HEADS, tokens, LANES), bf16),
            jax.ShapeDtypeStruct((2, LORA, 2 * d + s * up128(fs)), bf16),
        ],
        scratch_shapes=[
            pltpu.VMEM((d, d), bf16),
            pltpu.VMEM((tm, d), bf16),
            pltpu.VMEM((tm, d), bf16),
            pltpu.VMEM((s, tm, fs), bf16),
            pltpu.VMEM((s, tm, fs), bf16),
            pltpu.VMEM((4, LORA, d), f32),
            pltpu.VMEM((2, s, LORA, fs), f32),
        ],
        compiler_params=pltpu.CompilerParams(vmem_limit_bytes=VMEM),
        name="mid",
    )(oaug, x, cot, aid, wo, wu, wd, ab, ff, bup, vec)


def tail_kernel(s, slot, dq_ref, dk_ref, dv_ref, x_ref, n1_ref, h_ref, dmid_ref, aid_ref,
                w_ref, at_ref, b_ref, vec_ref, out_ref, low_ref, pack_ref, dy_ref, ga_ref, gb_ref):
    i = pl.program_id(0)
    tm, d = x_ref.shape
    nh = HEADS // s
    ds = d // s
    mask = column_mask(aid_ref[...])

    @pl.when(i == 0)
    def _():
        ga_ref[...] = jnp.zeros_like(ga_ref)
        gb_ref[...] = jnp.zeros_like(gb_ref)

    n1 = n1_ref[...]
    dn = jnp.zeros((tm, d), f32)
    for p, src in enumerate((dq_ref, dk_ref, dv_ref)):
        dh = jnp.zeros((tm, LORA), f32)
        for j in range(s):
            for h in range(nh):
                dy_ref[p, j, :, h * HEAD_DIM:(h + 1) * HEAD_DIM] = src[j * nh + h, :, :HEAD_DIM]
            dy = dy_ref[p, j]
            dh = dh + nt(dy, b_ref[p, j])
            dn = dn + nt(dy, w_ref[j, :, p * slot:p * slot + ds])
            gb_ref[p, j] += 0.5 * tn(h_ref[p], dy)
        dh = (0.5 * dh * mask).astype(bf16)
        dn = dn + nn(dh, at_ref[p])
        ga_ref[p] += tn(dh, n1)
    nhat, r = norm_parts(x_ref[...].astype(f32))
    out = dmid_ref[...] + norm_back(dn, vec_ref[4:5, :], nhat, r)
    out_ref[...] = out
    low_ref[...] = out.astype(bf16)

    @pl.when(i == pl.num_programs(0) - 1)
    def _():
        for p in range(3):
            pack_ref[0, :, p * d:(p + 1) * d] = ga_ref[p].astype(bf16)
            for j in range(s):
                at = p * d + j * ds
                pack_ref[1, :, at:at + ds] = gb_ref[p, j].astype(bf16)


def tail_call(dq, dk, dv, x, n1, hid, dmid, aid, wa, at, bq, vec):
    tokens, d = x.shape
    s = wa.shape[0]
    slot = up128(d // s)
    tm = min(256, tokens)
    full = pl.BlockSpec(memory_space=pltpu.VMEM)
    tile = pl.BlockSpec((tm, d), lambda i: (i, 0))
    heads = pl.BlockSpec((HEADS, tm, LANES), lambda i: (0, i, 0))
    return pl.pallas_call(
        partial(tail_kernel, s, slot),
        grid=(tokens // tm,),
        in_specs=[
            heads, heads, heads, tile, tile,
            pl.BlockSpec((3, tm, LORA), lambda i: (0, i, 0)),
            tile,
            pl.BlockSpec((tm, 1), lambda i: (i, 0)),
            full, full, full, full,
        ],
        out_specs=[tile, tile, full],
        out_shape=[
            jax.ShapeDtypeStruct((tokens, d), f32),
            jax.ShapeDtypeStruct((tokens, d), bf16),
            jax.ShapeDtypeStruct((2, LORA, 3 * d), bf16),
        ],
        scratch_shapes=[
            pltpu.VMEM((3, s, tm, d // s), bf16),
            pltpu.VMEM((3, LORA, d), f32),
            pltpu.VMEM((3, s, LORA, d // s), f32),
        ],
        compiler_params=pltpu.CompilerParams(vmem_limit_bytes=VMEM),
        name="tail",
    )(dq, dk, dv, x, n1, hid, dmid, aid, wa, at, bq, vec)


def rows_of_adapters(a):
    t = jnp.swapaxes(a, -1, -2)
    return t.reshape(*t.shape[:-3], t.shape[-3] * t.shape[-2], t.shape[-1])


def local(tokens, cotangent, lengths, adapter_ids, w_query, w_key, w_value, w_out, w_up, w_down,
          b_query, b_value, b_out, b_up, b_down, gain_one, shift_one, gain_two, shift_two,
          qkv_a, out_a, attn_b, up_a, up_b, down_a, down_b):
    seq = lax.axis_size("seq")
    rows, part_len, d = tokens.shape
    group = seq // rows
    count = rows * part_len
    ds, fs = w_query.shape[1], w_up.shape[1]
    me = lax.axis_index("seq")
    row, chunk = me // group, me % group

    def moves(j):
        return [(a, (a % rows + j) % rows * group + a // rows) for a in range(seq)]

    def send(piece, pairs):
        return piece if all(a == b for a, b in pairs) else lax.ppermute(piece, "seq", pairs)

    def to_row(t):
        out = jnp.zeros((rows, part_len, d), t.dtype)
        for j in range(rows):
            piece = lax.dynamic_index_in_dim(t, (me + j) % rows, 0, False)
            out = lax.dynamic_update_index_in_dim(out, send(piece, moves(j)), (row - j) % rows, 0)
        return out.reshape(count, d)

    def from_row(t, dtype):
        t = t.reshape(rows, part_len, d)
        out = jnp.zeros((rows, part_len, d), dtype)
        for j in range(rows):
            piece = lax.dynamic_index_in_dim(t, (row - j) % rows, 0, False)
            pairs = [(b, a) for a, b in moves(j)]
            if not all(a == b for a, b in pairs):
                piece = piece.astype(bf16)
            got = send(piece, pairs).astype(dtype)
            out = lax.dynamic_update_index_in_dim(out, got, (me + j) % rows, 0)
        return out

    dps = lax.axis_size("dp")
    nz = dps // 4
    fast = seq == 2 and rows == 2 and nz == 4
    slot, fslot = up128(ds), up128(fs)

    def wide_to(t, n):
        return jnp.pad(t, ((0, 0), (0, n - t.shape[1])))

    wq_part = jnp.concatenate([wide_to(w, slot) for w in (w_query, w_key, w_value)], axis=1)
    wo_part, wu_part, wd_part = wide_to(w_out, slot), wide_to(w_up, fslot), wide_to(w_down.T, fslot)
    narrow = jnp.concatenate([
        rows_of_adapters(qkv_a), rows_of_adapters(out_a)[None], rows_of_adapters(up_a)[None],
        attn_b.reshape(4, -1, d), down_b.reshape(1, -1, d)])
    wide = jnp.stack([rows_of_adapters(down_a), up_b.reshape(-1, up_b.shape[-1])])
    vec_part = jnp.stack([b_query, b_value, b_out, b_down, gain_one, shift_one, gain_two, shift_two])
    teams = [[g * group + c for c in range(group)] for g in range(rows)]

    my_len = lax.dynamic_index_in_dim(lengths, row, 0, False)
    my_ids = lax.dynamic_index_in_dim(adapter_ids, row, 0, False)
    slots = jnp.arange(my_len.shape[0], dtype=jnp.int32)
    ends = jnp.sum(jnp.where(slots[None, :] <= slots[:, None], my_len[None, :], 0), axis=1)
    pos = chunk * count + jnp.arange(count, dtype=jnp.int32)
    pic = jnp.sum((pos[:, None] >= ends[None, :]).astype(jnp.int32), axis=1, keepdims=True)
    aid = jnp.sum(jnp.where(pic == slots[None, :], my_ids[None, :], 0), axis=1, keepdims=True)
    aid = jnp.where(pos[:, None] < ends[-1], aid, -1)

    def from_halves(t):
        return jnp.swapaxes(t, 0, 1).reshape(t.shape[1], -1, t.shape[3])

    if fast:
        me_dp = lax.axis_index("dp")

        def share(t):
            flat = t.reshape(-1, t.shape[-1])
            n = flat.shape[0] // dps
            return lax.dynamic_slice_in_dim(flat, me_dp * n, n, 0)

        def whole(t):
            return t.reshape(seq, d, t.shape[2])

        small = jnp.concatenate([wide_to(vec_part, fslot), wide_to(b_up[None], fslot), jnp.zeros((7, fslot), bf16)])
        parts = [(0, 0, d)] + [(1, p * slot, slot) for p in range(3)]
        narrow, wq, x, small = start_call(nz, [share(narrow), wq_part], parts, tokens, small)
        x = x.reshape(count, d)
        narrow = from_halves(narrow.reshape(seq, 10, LORA // seq, d))
        vec = jnp.concatenate([small[k, :8, :ds] for k in range(seq)], axis=1).astype(f32)
        bup = small[:, 8:9, :fs].astype(f32)
        wq = whole(wq)
        third = fslot // LANES // 3 * LANES
        cuts = [(0, third), (third, third), (2 * third, fslot - 2 * third)]
        first = Fetch(nz, [wo_part, share(wide), wu_part],
                      [(0, 0, slot), (1, 0, wide.shape[-1])] + [(2, a, n) for a, n in cuts], 2)
        second = Fetch(nz, [wd_part], [(0, a, n) for a, n in cuts], 3, cotangent)
    else:
        def gather_all(shard):
            full = lax.all_gather(shard, ("seq", "dp"), axis=0, tiled=True)
            return full.reshape(seq, d, shard.shape[1])

        wq, wo, wu, wd = (gather_all(t) for t in (wq_part, wo_part, wu_part, wd_part))
        narrow = lax.all_gather(narrow, "seq", axis=1, tiled=True)
        wide = lax.all_gather(wide, "seq", axis=1, tiled=True)
        vec = lax.all_gather(vec_part, "seq", axis=1, tiled=True).astype(f32)
        bup = lax.all_gather(b_up[None], "seq", axis=0, tiled=True).astype(f32)[:, None]
        x = to_row(tokens)
        cot = to_row(cotangent)
        first = second = Quiet()

    at, b = narrow[:5], narrow[5:]
    bq = jnp.swapaxes(b[:3].reshape(3, LORA, seq, ds), 1, 2)
    bias = jnp.stack([vec[0], jnp.zeros_like(vec[0]), vec[1]]).reshape(3, seq, 1, ds)
    qkv, n1, hid, *got = qkv_call(x, wq, at, bq, bias, vec, aid, pic, first)
    if fast:
        wo, wide, wu = whole(got[0]), from_halves(got[1].reshape(seq, 2, LORA // seq, -1)), whole(got[2])
    if group == 1:
        kv, off = qkv, 1
    else:
        kv = lax.all_gather(qkv[1:], "seq", axis=2, tiled=True, axis_index_groups=teams)
        off = 0
    probs, oaug, *got = attn_fwd_call(qkv, kv, off, second)
    if fast:
        wd, cot = whole(got[0]), got[1].reshape(count, d)
    ff = jnp.swapaxes(wide.reshape(2, LORA, seq, fs), 1, 2)
    mixed, dmid, do_aug, g_mid = mid_call(
        oaug, x, cot, aid, wo, wu, wd, jnp.concatenate([at[3:], b[3:]]), ff, bup, vec)

    def blocks(t):
        return t.reshape(2, 2, 2 * nz, 8, t.shape[2])

    third_comm = Settle(nz, blocks(g_mid), mixed.reshape(rows, part_len, d), 4) if fast else Quiet()
    dq, dk, dv, *got = attn_bwd_call(qkv, kv, off, probs, do_aug, third_comm)
    if fast:
        g_mid, mixed = got[0].reshape(2, LORA // seq, -1), got[1]
    if group > 1:
        dk, dv = (lax.psum_scatter(t, "seq", scatter_dimension=1, axis_index_groups=teams, tiled=True)
                  for t in (dk, dv))
    d_in, d_low, g_qkv = tail_call(dq, dk, dv, x, n1, hid, dmid, aid, wq, at, bq, vec)
    if fast:
        g_qkv, other = finish_call(nz, blocks(g_qkv), d_low.reshape(rows, part_len, d))
        g_qkv = g_qkv.reshape(2, LORA // seq, -1)
        mine = lax.dynamic_index_in_dim(d_in.reshape(rows, part_len, d), me, 0, False)
        other = other.astype(f32)
        d_in = jnp.where(me == 0, jnp.stack([mine, other]), jnp.stack([other, mine]))
    else:
        def total(t):
            return lax.psum(lax.psum_scatter(t, "seq", scatter_dimension=1, tiled=True), "dp")

        g_mid, g_qkv = total(g_mid), total(g_qkv)
        mixed = from_row(mixed, bf16)
        d_in = from_row(d_in, f32)

    def down_form(t):
        return jnp.swapaxes(t.astype(f32).reshape(-1, RANK, t.shape[-1]), -1, -2)

    def up_form(t):
        return t.astype(f32).reshape(-1, RANK, t.shape[-1])

    def cut(t, k):
        return t[:, k * d:(k + 1) * d]

    def ff_of(t):
        return jnp.concatenate([t[:, 2 * d + j * fslot:2 * d + j * fslot + fs] for j in range(seq)], axis=1)

    a_mid, b_mid = g_mid
    a_qkv, b_qkv = g_qkv
    return (
        mixed,
        d_in,
        jnp.stack([down_form(cut(a_qkv, p)) for p in range(3)]),
        down_form(cut(a_mid, 0)),
        jnp.stack([up_form(cut(b_qkv, p)) for p in range(3)] + [up_form(cut(b_mid, 0))]),
        down_form(cut(a_mid, 1)),
        up_form(ff_of(b_mid)),
        down_form(ff_of(a_mid)),
        up_form(cut(b_mid, 1)),
    )


def solution(mesh):
    both = P("dp", "seq", None)
    lead = P("seq", None, None)
    second = P(None, "seq", None, None)
    return jax.shard_map(
        local,
        mesh=mesh,
        in_specs=(both, both, P("dp", None), P("dp", None))
        + (P("dp", "seq"),) * 5 + (P("seq", "dp"),) + (P("seq"),) * 9
        + (second, lead, second, lead, lead, lead, lead),
        out_specs=(both, both, second, lead, second, lead, lead, lead, lead),
        check_vma=False,
    )
```

```python
from functools import partial

import jax
import jax.numpy as jnp
from jax import lax
from jax.experimental import pallas as pl
from jax.experimental.pallas import tpu as pltpu
from jax.sharding import PartitionSpec as P

HEADS = 16
HEAD_DIM = 72
RANK = 16
ADAPTERS = 8
LORA = RANK * ADAPTERS
LANES = 128
EPS = 1e-06
SCALE = HEAD_DIM ** (-0.5)
BIG = 1e30
LOG2E = 1.4426950408889634
VMEM = 61 * 1024 * 1024

MESH = pl.DeviceIdType.MESH
bf16 = jnp.bfloat16
f32 = jnp.float32


def nn(a, b):
    return jnp.dot(a, b, preferred_element_type=f32)


def nt(a, b):
    return lax.dot_general(a, b, (((1,), (1,)), ((), ())), preferred_element_type=f32)


def tn(a, b):
    return lax.dot_general(a, b, (((0,), (0,)), ((), ())), preferred_element_type=f32)


def up128(n):
    return -(-n // LANES) * LANES


def lane_ids(rows):
    return lax.broadcasted_iota(jnp.int32, (rows, LANES), 1)


def norm_parts(x):
    center = jnp.mean(x, axis=-1, keepdims=True)
    xc = x - center
    r = lax.rsqrt(jnp.mean(xc * xc, axis=-1, keepdims=True) + EPS)
    return xc * r, r


def norm_back(dn, gain, nh, r):
    gh = dn * gain
    a = jnp.mean(gh, axis=-1, keepdims=True)
    b = jnp.mean(gh * nh, axis=-1, keepdims=True)
    return r * (gh - a - nh * b)


def column_mask(aid):
    return (lane_ids(aid.shape[0]) // RANK == aid).astype(f32)


class Spot:
    def __init__(self, nz):
        dp = lax.axis_index("dp")
        self.nz = nz
        self.x = lax.axis_index("seq")
        self.z, self.y, self.c = dp // 4, (dp // 2) % 2, dp % 2
        self.xn = self.device(1 - self.x, self.y, self.z, self.c)
        self.yn = self.device(self.x, 1 - self.y, self.z, self.c)
        self.sib = self.device(self.x, self.y, self.z, 1 - self.c)
        self.zs = [None] + [self.device(self.x, self.y, self.zk(k), self.c) for k in range(1, nz)]
        flip = self.z // 2
        self.inner = self.z + flip * (3 - 2 * self.z)
        self.zr = [m + flip * (3 - 2 * m) for m in (self.inner, 1 - self.inner, 2, 3)]
        self.zp = [self.device(self.x, self.y, z, self.c) for z in self.zr]

    def device(self, x, y, z, c):
        return ((z * 2 + y) * 2 + c, x)

    def shard(self, x, y, z):
        return (x * self.nz + z) * 4 + y * 2 + self.c

    def zk(self, k):
        return (self.z + k) % self.nz

    def barrier(self):
        peers = [self.xn, self.yn, self.sib] + self.zs[1:]
        sem = pltpu.get_barrier_semaphore()
        for peer in peers:
            pl.semaphore_signal(sem, inc=1, device_id=peer, device_id_type=MESH)
        pl.semaphore_wait(sem, len(peers))


def remote(src, dst, send, recv, device):
    return pltpu.make_async_remote_copy(
        src_ref=src, dst_ref=dst, send_sem=send, recv_sem=recv, device_id=device, device_id_type=MESH
    )


class Gather:
    kinds = [(kind, r) for r in range(4) for kind in "zxyd"]

    def __init__(self, spot, parts, ins, outs, send, recv, core, own):
        self.s, self.parts, self.ins, self.outs = spot, parts, ins, outs
        self.send, self.recv, self.core, self.own = send, recv, core, own
        self.slot = {}
        for kind, r in self.kinds:
            for to in self.targets(kind, r):
                self.slot[kind, r, to] = len(self.slot)

    @staticmethod
    def scratch(nz, count):
        dma = pltpu.SemaphoreType.DMA
        return [dma((count, 36)), dma((count, 4 * nz)), dma((count,)), dma((count,))]

    def targets(self, kind, r):
        if kind == "z":
            return (["z1", "z2", "z3"] if r == 0 else []) + ["x", "y", "s"]
        if kind == "x":
            return (["y"] if r in (0, 3) else []) + ["s"]
        if kind == "d":
            return {0: ["z1", "iz2"], 2: ["iz1"]}.get(r, []) + ["s"]
        return ["s"]

    def index(self, kind, r):
        s = self.s
        x = 1 - s.x if kind in "xd" else s.x
        y = 1 - s.y if kind in "yd" else s.y
        return s.shard(x, y, s.zr[r])

    def place(self, g, index):
        a, start, size = self.parts[g]
        if size == self.outs[a].shape[2]:
            return self.outs[a].at[index]
        return self.outs[a].at[index, :, pl.ds(start, size)]

    def source(self, g, kind, r):
        if (kind, r) != ("z", 0):
            return self.place(g, self.index(kind, r))
        a, start, size = self.parts[g]
        if size == self.ins[a].shape[1]:
            return self.ins[a]
        return self.ins[a].at[:, pl.ds(start, size)]

    def arrival(self, g, kind, r):
        return self.recv.at[g, "zxyd".index(kind) * 4 + r]

    def copy(self, g, kind, r, to):
        s = self.s
        if to == "s":
            recv, device = self.core.at[g], s.sib
        elif to == "x":
            recv, device = self.arrival(g, "x", r), s.xn
        elif to == "y":
            recv, device = self.arrival(g, "y" if kind == "z" else "d", r), s.yn
        else:
            i = int(to[-1])
            if kind == "z":
                there = i if i < 2 else 3 - s.inner
            else:
                there = 1 if to == "z1" else 2
            recv, device = self.arrival(g, kind, there), s.zp[i]
        send = self.send.at[g, self.slot[kind, r, to]]
        return remote(self.source(g, kind, r), self.place(g, self.index(kind, r)), send, recv, device)

    def each(self, g, kind, r, act):
        for to in self.targets(kind, r):
            if to[0] == "i":
                @pl.when(self.s.inner == 1)
                def _(to=to):
                    act(self.copy(g, kind, r, to))
            else:
                act(self.copy(g, kind, r, to))

    def local(self, g):
        return pltpu.make_async_copy(self.source(g, "z", 0), self.place(g, self.index("z", 0)), self.own.at[g])

    def arrive(self, g, kind, r):
        if (kind, r) == ("z", 0):
            self.local(g).start()
        else:
            ref = self.place(g, self.index(kind, r))
            remote(ref, ref, self.send.at[g, 0], self.arrival(g, kind, r), self.s.xn).wait_recv()
        self.each(g, kind, r, lambda copy: copy.start())

    def end(self, g):
        a, start, size = self.parts[g]
        n = self.outs[a].shape[0] // 2
        ref = self.outs[a].at[pl.ds(0, n), :, pl.ds(start, size)]
        if size == self.outs[a].shape[2]:
            ref = self.outs[a].at[pl.ds(0, n)]
        remote(ref, ref, self.send.at[g, 0], self.core.at[g], self.s.sib).wait_recv()
        self.local(g).wait()
        for kind, r in self.kinds:
            self.each(g, kind, r, lambda copy: copy.wait_send())

    def actions(self):
        n = len(self.parts)
        out = []
        for t in range(n + 4):
            if t < n:
                out.append((self.arrive, t, "z", 0))
            if 0 <= t - 1 < n:
                out += [(self.arrive, t - 1, "z", r) for r in (1, 2, 3)]
            if 0 <= t - 2 < n:
                out += [(self.arrive, t - 2, kind, r) for r in (0, 3, 1, 2) for kind in "xy"]
            if 0 <= t - 3 < n:
                out += [(self.arrive, t - 3, "d", r) for r in (0, 3, 2, 1)]
            if 0 <= t - 4 < n:
                out.append((self.end, t - 4))
        return out


class Swap:
    def __init__(self, spot, mine, got, sems, slot=None):
        self.s, self.mine, self.got, self.sems = spot, mine, got, sems
        self.slot = spot.x if slot is None else slot

    def copies(self):
        s = self.s
        here = pltpu.make_async_copy(self.mine.at[s.x], self.got.at[s.x], self.sems.at[0])
        there = remote(self.mine.at[1 - s.x], self.got.at[self.slot], self.sems.at[1], self.sems.at[2], s.xn)
        return here, there

    def start(self):
        for copy in self.copies():
            copy.start()

    def end(self):
        here, there = self.copies()
        here.wait()
        ref = self.got.at[1 - self.s.x]
        remote(ref, ref, self.sems.at[1], self.sems.at[2], self.s.xn).wait_recv()
        there.wait_send()


def run_actions(actions, step, steps):
    for t in range(steps):
        a, b = len(actions) * t // steps, len(actions) * (t + 1) // steps
        if a == b:
            continue

        @pl.when(step == t)
        def _(a=a, b=b):
            for action in actions[a:b]:
                action[0](*action[1:])


class Reduce:
    def __init__(self, spot, data, result, refs):
        self.s, self.data, self.result = spot, data, result
        self.r1, self.s1, self.r2, self.s2, self.r3, self.s3, self.r4, self.total = refs[:8]
        self.send, self.recv, self.out = refs[8:]

    @staticmethod
    def scratch(nz, width):
        def v(*dims):
            return pltpu.VMEM((*dims, 8, width), bf16)
        dma = pltpu.SemaphoreType.DMA
        n = 5 + 2 * (nz - 1)
        return [v(2, 2 * nz), v(2, 2 * nz), v(2, nz), v(2, nz), v(nz, 2), v(2), v(1), v(2, 2 * nz),
                dma((n,)), dma((n,)), dma((1,))]

    def pair(self, i, src, dst, device):
        return remote(src, dst, self.send.at[i], self.recv.at[i], device)

    def to_core(self):
        return self.pair(0, self.data.at[1 - self.s.c], self.r1, self.s.sib)

    def to_y(self):
        nz = self.s.nz
        return self.pair(1, self.s1.at[:, pl.ds((1 - self.s.y) * nz, nz)], self.r2, self.s.yn)

    def to_x(self):
        return self.pair(2, self.s3.at[1 - self.s.x], self.r4.at[0], self.s.xn)

    def to_z(self, k):
        s = self.s
        return self.pair(4 + k, self.s2.at[:, s.zk(k)], self.r3.at[s.z], s.zs[k])

    def from_z(self, k):
        s = self.s
        ref = self.r3.at[s.zk(k)]
        return remote(ref, ref, self.send.at[4 + s.nz - k], self.recv.at[4 + s.nz - k], s.zs[k])

    def back_z(self, k):
        s = self.s
        ref = self.total.at[s.c, s.y * s.nz + s.z]
        return self.pair(4 + s.nz - 1 + k, ref, ref, s.zs[k])

    def from_back_z(self, k):
        s = self.s
        i = 4 + s.nz - 1 + s.nz - k
        ref = self.total.at[s.c, s.y * s.nz + s.zk(k)]
        return remote(ref, ref, self.send.at[i], self.recv.at[i], s.zs[k])

    def back_y(self, y):
        s = self.s
        ref = self.total.at[s.c, pl.ds(y * s.nz, s.nz)]
        return self.pair(3, ref, ref, s.yn)

    def back_core(self, c):
        ref = self.total.at[c]
        return self.pair(4, ref, ref, self.s.sib)

    def one(self):
        self.to_core().start()

    def two(self):
        s, nz = self.s, self.s.nz
        self.to_core().wait_recv()

        def add(i, c):
            x, b = i // (2 * nz), i % (2 * nz)
            self.s1[x, b] = (self.data[s.c, x, b].astype(f32) + self.r1[x, b].astype(f32)).astype(bf16)
            return c
        lax.fori_loop(0, 4 * nz, add, 0)
        self.to_y().start()

    def three(self):
        s, nz = self.s, self.s.nz
        self.to_y().wait_recv()

        def add(i, c):
            x, b = i // nz, i % nz
            self.s2[x, b] = (self.s1[x, s.y * nz + b].astype(f32) + self.r2[x, b].astype(f32)).astype(bf16)
            return c
        lax.fori_loop(0, 2 * nz, add, 0)
        for k in range(1, nz):
            self.to_z(k).start()

    def four(self):
        s, nz = self.s, self.s.nz
        for k in range(1, nz):
            self.from_z(k).wait_recv()
        for x in range(2):
            v = self.s2[x, s.z].astype(f32)
            for k in range(1, nz):
                v = v + self.r3[s.zk(k), x].astype(f32)
            self.s3[x] = v.astype(bf16)
        self.to_x().start()

    def five(self):
        s, nz = self.s, self.s.nz
        self.to_x().wait_recv()
        v = self.s3[s.x].astype(f32) + self.r4[0].astype(f32)
        self.total[s.c, s.y * s.nz + s.z] = v.astype(bf16)
        for k in range(1, nz):
            self.back_z(k).start()

    def six(self):
        for k in range(1, self.s.nz):
            self.from_back_z(k).wait_recv()
        self.back_y(self.s.y).start()

    def seven(self):
        self.back_y(1 - self.s.y).wait_recv()
        self.back_core(self.s.c).start()

    def end(self):
        s = self.s
        self.back_core(1 - s.c).wait_recv()
        out = pltpu.make_async_copy(self.total, self.result, self.out.at[0])
        out.start()
        out.wait()
        self.to_core().wait_send()
        self.to_x().wait_send()
        self.to_y().wait_send()
        for k in range(1, s.nz):
            self.to_z(k).wait_send()
            self.back_z(k).wait_send()
        self.back_y(s.y).wait_send()
        self.back_core(s.c).wait_send()

    def actions(self):
        return [(f,) for f in (self.one, self.two, self.three, self.four, self.five, self.six, self.seven, self.end)]


def front_kernel(nz, na, *refs):
    shards, (tokens, vec, aid_ref, pic_ref), refs = refs[:na], refs[na:na + 4], refs[na + 4:]
    wholes, (x_out, vec_out, qkv_out, n1_out, h_out), refs = refs[:na], refs[na:na + 5], refs[na + 5:]
    (xbuf, vbuf, nbuf, wbuf, abuf, bbuf, n1, hbuf, heads, sems, wsem, osem, *refs) = refs
    n, d = nz * 4, xbuf.shape[2]
    count, tm = 2 * xbuf.shape[1], 512
    ds = wbuf.shape[3]
    nh = ds // HEAD_DIM
    spot = Spot(nz)
    spot.barrier()
    gather = Gather(spot, [(k, 0, a.shape[1]) for k, a in enumerate(shards)], shards, wholes, *refs)
    run = Steps(gather.actions())
    vec_here = pltpu.make_async_copy(vec, vbuf.at[spot.x], sems.at[0])
    vec_there = remote(vec, vbuf.at[spot.x], sems.at[1], sems.at[2], spot.xn)
    row_here = pltpu.make_async_copy(tokens.at[spot.x], xbuf.at[spot.x], sems.at[3])
    row_there = remote(tokens.at[1 - spot.x], xbuf.at[spot.x], sems.at[4], sems.at[5], spot.xn)
    vec_here.start()
    vec_there.start()
    run.step(2)
    row_here.start()
    row_there.start()
    run.step(13)

    vec_here.wait()
    got = vbuf.at[1 - spot.x]
    remote(got, got, sems.at[1], sems.at[2], spot.xn).wait_recv()
    row_here.wait()
    got = xbuf.at[1 - spot.x]
    remote(got, got, sems.at[4], sems.at[5], spot.xn).wait_recv()
    gain, shift = (jnp.concatenate([vbuf[j, k:k + 1, :ds] for j in range(2)], axis=1).astype(f32) for k in (4, 5))
    keep = [pltpu.make_async_copy(xbuf, x_out, osem.at[0]), pltpu.make_async_copy(vbuf, vec_out, osem.at[1])]
    for copy in keep:
        copy.start()
    for half in range(2):
        def norm_step(i, carry, half=half):
            nhat, _ = norm_parts(xbuf[half, pl.ds(i * 256, 256), :].astype(f32))
            n1[pl.ds(half * (count // 2) + i * 256, 256), :d] = (nhat * gain + shift).astype(bf16)
            return carry
        lax.fori_loop(0, count // 512, norm_step, 0)
        run.step(4)
    keep.append(pltpu.make_async_copy(n1.at[:, pl.ds(0, d)], n1_out, osem.at[2]))
    keep[-1].start()

    run.until(0)
    small = pltpu.make_async_copy(wholes[0], nbuf, sems.at[6])
    small.start()
    small.wait()
    each = LORA // 2
    for m in range(3):
        for j in range(2):
            rows = slice(j * each, (j + 1) * each)
            one = nbuf[j * n:(j + 1) * n].reshape(10 * each, d)
            abuf[m, rows, :] = one[m * each:(m + 1) * each]
            for i in range(2):
                bbuf[m, i, rows, :] = one[(5 + m) * each:(6 + m) * each, i * ds:(i + 1) * ds]

    def fetch(p, j):
        return pltpu.make_async_copy(wholes[1 + p].at[pl.ds(j * n, n)], wbuf.at[j], wsem.at[j])

    blocks = []
    for p in range(3):
        run.until(1 + p)
        for j in range(2):
            fetch(p, j).start()
        for i in range(count // tm):
            rows = pl.ds(i * tm, tm)
            h = (nt(n1[rows, :d], abuf[p]) * column_mask(aid_ref[rows, :])).astype(bf16)
            hbuf[p, rows, :] = h
            n1[rows, d:] = (0.5 * h.astype(f32)).astype(bf16)
        for j in range(2):
            fetch(p, j).wait()
            bias = vbuf[j, p // 2:p // 2 + 1, :ds].astype(f32) if p != 1 else 0.0

            def step(i, carry, p=p, j=j, bias=bias):
                rows = pl.ds(i * tm, tm)
                run.within(i, 1, count // tm, 3)
                w = jnp.concatenate([wbuf[j].reshape(d, ds), bbuf[p, j]])
                y = (nn(n1[rows, :], w) + bias).astype(bf16)
                place = lax.broadcasted_iota(jnp.int32, (tm, LANES), 1) - HEAD_DIM
                same = place == pic_ref[rows, :]
                if p == 0:
                    extra = jnp.where(same, 1.0, 0.0)
                elif p == 1:
                    extra = jnp.where((place >= 0) & (place < 16) & jnp.logical_not(same), -BIG, 0.0)
                else:
                    extra = jnp.where((place == 0) | (place == 1), 1.0, 0.0)
                extra = extra.astype(bf16)[:, HEAD_DIM:]
                for h in range(nh):
                    heads[p, j * nh + h, rows, :HEAD_DIM] = y[:, h * HEAD_DIM:(h + 1) * HEAD_DIM]
                    heads[p, j * nh + h, rows, HEAD_DIM:] = extra
                return carry
            lax.fori_loop(0, count // tm, step, 0)
            which = pl.ds(j * nh, nh)
            blocks.append(pltpu.make_async_copy(heads.at[p, which], qkv_out.at[p, which], osem.at[4 + 2 * p + j]))
            blocks[-1].start()
            run.step(3)
    keep.append(pltpu.make_async_copy(hbuf, h_out, osem.at[3]))
    keep[-1].start()
    run.rest()
    for copy in keep + blocks:
        copy.wait()
    vec_there.wait_send()
    row_there.wait_send()


def front_call(nz, shards, tokens, vec, aid, pic):
    na = len(shards)
    dma = pltpu.SemaphoreType.DMA
    count, d = 2 * tokens.shape[1], tokens.shape[2]
    ds = shards[1].shape[1]
    full = pl.BlockSpec(memory_space=pltpu.VMEM)

    def v(*shape):
        return pltpu.VMEM(shape, bf16)

    def out(*shape):
        return jax.ShapeDtypeStruct(shape, bf16)

    return pl.pallas_call(
        partial(front_kernel, nz, na),
        in_specs=any_specs(na + 2) + [full, full],
        out_specs=any_specs(na + 5),
        out_shape=gathered(nz, shards) + [
            out(*tokens.shape), out(2, *vec.shape), out(3, HEADS, count, LANES), out(count, d), out(3, count, LORA)],
        scratch_shapes=[
            v(*tokens.shape), v(2, *vec.shape), v(8 * nz, *shards[0].shape), v(2, 4 * nz, *shards[1].shape),
            v(3, LORA, d), v(3, 2, LORA, ds), v(count, d + LORA), v(3, count, LORA), v(3, HEADS, count, LANES),
            dma((7,)), dma((2,)), dma((10,))] + Gather.scratch(nz, na),
        compiler_params=pltpu.CompilerParams(collective_id=1, has_side_effects=True, vmem_limit_bytes=VMEM),
        name="front",
    )(*shards, tokens, vec, aid, pic)


def any_specs(n):
    return [pl.BlockSpec(memory_space=pl.ANY)] * n


def gathered(nz, arrays):
    return [jax.ShapeDtypeStruct((8 * nz,) + a.shape, a.dtype) for a in arrays]


def finish_kernel(nz, g_ref, d_ref, total_ref, got_ref, *refs):
    spot = Spot(nz)
    spot.barrier()
    reduce = Reduce(spot, g_ref, total_ref, refs[:-1])
    sems = refs[-1]
    there = remote(d_ref.at[1 - spot.x], got_ref, sems.at[0], sems.at[1], spot.xn)
    reduce.one()
    there.start()
    for f in reduce.actions()[1:]:
        f[0]()
    there.wait()


def finish_call(nz, g, d):
    width = g.shape[-1]
    dma = pltpu.SemaphoreType.DMA
    return pl.pallas_call(
        partial(finish_kernel, nz),
        in_specs=[pl.BlockSpec(memory_space=pltpu.VMEM), pl.BlockSpec(memory_space=pl.ANY)],
        out_specs=any_specs(2),
        out_shape=[
            jax.ShapeDtypeStruct((2,) + g.shape[2:], bf16), jax.ShapeDtypeStruct(d.shape[1:], bf16)],
        scratch_shapes=Reduce.scratch(nz, width) + [dma((2,))],
        compiler_params=pltpu.CompilerParams(collective_id=5, has_side_effects=True, vmem_limit_bytes=40 * 2**20),
        name="finish",
    )(g, d)


class Steps:
    def __init__(self, actions):
        self.actions = list(actions)

    def step(self, count):
        for action in self.actions[:count]:
            action[0](*action[1:])
        del self.actions[:count]

    def rest(self):
        self.step(len(self.actions))

    def until(self, part):
        ends = [k for k, action in enumerate(self.actions) if action[0].__name__ == "end" and action[1] == part]
        if ends:
            self.step(ends[0] + 1)

    def within(self, i, first, last, count):
        for t in range(first, last):
            pl.when(i == t)(partial(self.step, count))


class Quiet:
    args = ()
    outs = ()
    steps = 1

    def split(self, refs, own):
        a, b = len(self.args), len(self.outs)
        return refs[:a], refs[a:a + own], refs[a + own:a + own + b], refs[a + own + b:]

    def in_specs(self):
        return any_specs(len(self.args))

    def out_specs(self):
        return any_specs(len(self.outs))

    def out_shape(self):
        return list(self.outs)

    def scratch(self):
        return []

    def params(self):
        return pltpu.CompilerParams(vmem_limit_bytes=VMEM)

    def run(self, step, ins, outs, refs):
        pass

    def close(self, step, ins, outs, refs):
        pass

    def begin(self, ins, outs, refs):
        return Steps([])


class Fetch(Quiet):
    def __init__(self, nz, shards, parts, cid, halves=None):
        self.nz, self.parts, self.cid, self.na = nz, parts, cid, len(shards)
        self.args = tuple(shards) + (() if halves is None else (halves,))
        self.outs = gathered(nz, shards) + ([] if halves is None else [jax.ShapeDtypeStruct(halves.shape, halves.dtype)])

    def scratch(self):
        return Gather.scratch(self.nz, len(self.parts)) + [pltpu.SemaphoreType.DMA((3,))]

    def params(self):
        return pltpu.CompilerParams(vmem_limit_bytes=VMEM, collective_id=self.cid, has_side_effects=True)

    def make(self, ins, outs, refs):
        spot = Spot(self.nz)
        gather = Gather(spot, self.parts, ins[:self.na], outs[:self.na], *refs[-5:-1])
        swap = Swap(spot, ins[-1], outs[-1], refs[-1]) if len(ins) > self.na else None
        return spot, gather, swap

    def begin(self, ins, outs, refs):
        spot, gather, _ = self.make(ins, outs, refs)
        spot.barrier()
        return Steps(gather.actions())

    def run(self, step, ins, outs, refs):
        spot, gather, swap = self.make(ins, outs, refs)

        @pl.when(step == 0)
        def _():
            spot.barrier()
            if swap:
                swap.start()
        run_actions(gather.actions()[:-4], step, self.steps)

    def close(self, step, ins, outs, refs):
        _, gather, swap = self.make(ins, outs, refs)

        @pl.when(step == self.steps - 1)
        def _():
            for action in gather.actions()[-4:]:
                action[0](*action[1:])
            if swap:
                swap.end()


class Settle(Quiet):
    def __init__(self, nz, g, halves, cid):
        self.nz, self.width, self.cid = nz, g.shape[-1], cid
        self.args = (g, halves)
        self.outs = [jax.ShapeDtypeStruct((2,) + g.shape[2:], bf16), jax.ShapeDtypeStruct(halves.shape, halves.dtype)]

    def in_specs(self):
        return [pl.BlockSpec(memory_space=pltpu.VMEM), pl.BlockSpec(memory_space=pl.ANY)]

    def scratch(self):
        return Reduce.scratch(self.nz, self.width) + [pltpu.SemaphoreType.DMA((3,))]

    def params(self):
        return pltpu.CompilerParams(vmem_limit_bytes=VMEM, collective_id=self.cid, has_side_effects=True)

    def make(self, ins, outs, refs):
        spot = Spot(self.nz)
        refs = refs[-12:]
        return spot, Reduce(spot, ins[0], outs[0], refs[:-1]), Swap(spot, ins[1], outs[1], refs[-1])

    def run(self, step, ins, outs, refs):
        spot, reduce, swap = self.make(ins, outs, refs)
        when = [0, 1, 4, 7, 9, 11, 13]

        @pl.when(step == 0)
        def _():
            spot.barrier()
        for (f,), t in zip(reduce.actions(), when):
            pl.when(step == t)(f)

        @pl.when(step == 4)
        def _():
            swap.start()

    def close(self, step, ins, outs, refs):
        _, reduce, swap = self.make(ins, outs, refs)

        @pl.when(step == self.steps - 1)
        def _():
            reduce.end()
            swap.end()


def qkv_kernel(nh, tm, x_ref, w_ref, at_ref, b_ref, bias_ref, vec_ref, aid_ref, pic_ref, out_ref, n1_ref, h_ref):
    p = pl.program_id(0)
    j = pl.program_id(1)
    tokens = x_ref.shape[0]

    @pl.when((p == 0) & (j == 0))
    def _():
        def norm_step(i, c):
            rows = pl.ds(i * tm, tm)
            nhat, _ = norm_parts(x_ref[rows, :].astype(f32))
            n1_ref[rows, :] = (nhat * vec_ref[4:5, :] + vec_ref[5:6, :]).astype(bf16)
            return c
        lax.fori_loop(0, tokens // tm, norm_step, 0)

    @pl.when(j == 0)
    def _():
        def hidden_step(i, c):
            rows = pl.ds(i * tm, tm)
            h = nt(n1_ref[rows, :], at_ref[0]) * column_mask(aid_ref[rows, :])
            h_ref[0, rows, :] = h.astype(bf16)
            return c
        lax.fori_loop(0, tokens // tm, hidden_step, 0)

    def step(i, c):
        rows = pl.ds(i * tm, tm)
        y = nn(n1_ref[rows, :], w_ref[0, 0])
        y = y + 0.5 * nn(h_ref[0, rows, :], b_ref[0, 0]) + bias_ref[0, 0]
        slot = lane_ids(tm) - HEAD_DIM
        pic = pic_ref[rows, :]
        same = slot == pic
        in_slots = (slot >= 0) & (slot < 16)
        q_aug = jnp.where(same, 1.0, 0.0)
        k_aug = jnp.where(in_slots & jnp.logical_not(same), -BIG, 0.0)
        v_aug = jnp.where((slot == 0) | (slot == 1), 1.0, 0.0)
        aug = jnp.where(p == 0, q_aug, jnp.where(p == 1, k_aug, v_aug))[:, HEAD_DIM:]
        for h in range(nh):
            head = y[:, h * HEAD_DIM:(h + 1) * HEAD_DIM]
            out_ref[0, h, rows, :HEAD_DIM] = head.astype(bf16)
            out_ref[0, h, rows, HEAD_DIM:] = aug.astype(bf16)
        return c
    lax.fori_loop(0, tokens // tm, step, 0)


def qkv_call(x, w, at, bq, bias, vec, aid, pic):
    tokens, d = x.shape
    s = w.shape[1]
    nh = HEADS // s
    tm = min(256, tokens)
    return pl.pallas_call(
        partial(qkv_kernel, nh, tm),
        grid=(3, s),
        in_specs=[
            pl.BlockSpec((tokens, d), lambda p, j: (0, 0)),
            pl.BlockSpec((1, 1, d, d // s), lambda p, j: (p, j, 0, 0)),
            pl.BlockSpec((1, LORA, d), lambda p, j: (p, 0, 0)),
            pl.BlockSpec((1, 1, LORA, nh * HEAD_DIM), lambda p, j: (p, j, 0, 0)),
            pl.BlockSpec((1, 1, 1, nh * HEAD_DIM), lambda p, j: (p, j, 0, 0)),
            pl.BlockSpec(vec.shape, lambda p, j: (0, 0)),
            pl.BlockSpec((tokens, 1), lambda p, j: (0, 0)),
            pl.BlockSpec((tokens, 1), lambda p, j: (0, 0)),
        ],
        out_specs=[
            pl.BlockSpec((1, nh, tokens, LANES), lambda p, j: (p, j, 0, 0)),
            pl.BlockSpec((tokens, d), lambda p, j: (0, 0)),
            pl.BlockSpec((1, tokens, LORA), lambda p, j: (p, 0, 0)),
        ],
        out_shape=[
            jax.ShapeDtypeStruct((3, HEADS, tokens, LANES), bf16),
            jax.ShapeDtypeStruct((tokens, d), bf16),
            jax.ShapeDtypeStruct((3, tokens, LORA), bf16),
        ],
        compiler_params=pltpu.CompilerParams(vmem_limit_bytes=VMEM),
        name="qkv",
    )(x, w, at, bq, bias, vec, aid, pic)


def attn_fwd_kernel(tq, comm, q_ref, k_ref, v_ref, *refs):
    ins, (p_ref, o_ref), outs, refs = comm.split(refs, 2)
    comm.run(pl.program_id(0), ins, outs, refs)

    for i in range(q_ref.shape[2] // tq):
        rows = pl.ds(i * tq, tq)
        s = nt(q_ref[0, 0, rows, :], k_ref[0, 0])
        top = jnp.max(s, axis=-1, keepdims=True)
        p = jnp.exp2((s - top) * (SCALE * LOG2E)).astype(bf16)
        o = nn(p, v_ref[0, 0])
        inv = 1.0 / o[:, HEAD_DIM:HEAD_DIM + 1]
        p_ref[0, rows, :] = (p.astype(f32) * inv).astype(bf16)
        o_ref[0, rows, :] = (o * inv).astype(bf16)
    comm.close(pl.program_id(0), ins, outs, refs)


def attn_fwd_call(qkv, kv, off, comm):
    tokens, keys = qkv.shape[2], kv.shape[2]
    tq = min(512, tokens)
    comm.steps = HEADS
    return pl.pallas_call(
        partial(attn_fwd_kernel, tq, comm),
        grid=(HEADS,),
        in_specs=[
            pl.BlockSpec((1, 1, tokens, LANES), lambda h: (0, h, 0, 0)),
            pl.BlockSpec((1, 1, keys, LANES), lambda h: (off, h, 0, 0)),
            pl.BlockSpec((1, 1, keys, LANES), lambda h: (off + 1, h, 0, 0)),
        ] + comm.in_specs(),
        out_specs=[
            pl.BlockSpec((1, tokens, keys), lambda h: (h, 0, 0)),
            pl.BlockSpec((1, tokens, LANES), lambda h: (h, 0, 0)),
        ] + comm.out_specs(),
        out_shape=[
            jax.ShapeDtypeStruct((HEADS, tokens, keys), bf16),
            jax.ShapeDtypeStruct((HEADS, tokens, LANES), bf16),
        ] + comm.out_shape(),
        scratch_shapes=comm.scratch(),
        compiler_params=comm.params(),
        name="attn_fwd",
    )(qkv, kv, kv, *comm.args)


def attn_bwd_kernel(tq, comm, q_ref, k_ref, v_ref, p_ref, o_ref, do_ref, *refs):
    ins, (dq_ref, dk_ref, dv_ref), outs, (ds_ref, da_ref, *refs) = comm.split(refs, 3)
    comm.run(pl.program_id(0), ins, outs, refs)

    for i in range(q_ref.shape[2] // tq):
        rows = pl.ds(i * tq, tq)
        lane = lane_ids(tq)
        do = jnp.where(lane < HEAD_DIM, do_ref[0, rows, :].astype(f32), 0.0)
        delta = jnp.sum(do * o_ref[0, rows, :].astype(f32), axis=-1, keepdims=True)
        hi = delta.astype(bf16).astype(f32)
        do = jnp.where(lane == HEAD_DIM, -hi, jnp.where(lane == HEAD_DIM + 1, hi - delta, do)).astype(bf16)
        da_ref[rows, :] = do
        dp = nt(do, v_ref[0, 0])
        ds = (p_ref[0, rows, :].astype(f32) * dp).astype(bf16)
        ds_ref[rows, :] = ds
        dq_ref[0, rows, :] = (nn(ds, k_ref[0, 0]) * SCALE).astype(bf16)
    dv_ref[0] = nn(da_ref[...].T, p_ref[0]).T.astype(bf16)
    dk_ref[0] = (nn(q_ref[0, 0].T, ds_ref[...]).T * SCALE).astype(bf16)
    comm.close(pl.program_id(0), ins, outs, refs)


def attn_bwd_call(qkv, kv, off, probs, out, d_out, comm):
    tokens, keys = qkv.shape[2], kv.shape[2]
    tq = min(256, tokens)
    comm.steps = HEADS
    return pl.pallas_call(
        partial(attn_bwd_kernel, tq, comm),
        grid=(HEADS,),
        in_specs=[
            pl.BlockSpec((1, 1, tokens, LANES), lambda h: (0, h, 0, 0)),
            pl.BlockSpec((1, 1, keys, LANES), lambda h: (off, h, 0, 0)),
            pl.BlockSpec((1, 1, keys, LANES), lambda h: (off + 1, h, 0, 0)),
            pl.BlockSpec((1, tokens, keys), lambda h: (h, 0, 0)),
            pl.BlockSpec((1, tokens, LANES), lambda h: (h, 0, 0)),
            pl.BlockSpec((1, tokens, LANES), lambda h: (h, 0, 0)),
        ] + comm.in_specs(),
        out_specs=[
            pl.BlockSpec((1, tokens, LANES), lambda h: (h, 0, 0)),
            pl.BlockSpec((1, keys, LANES), lambda h: (h, 0, 0)),
            pl.BlockSpec((1, keys, LANES), lambda h: (h, 0, 0)),
        ] + comm.out_specs(),
        out_shape=[
            jax.ShapeDtypeStruct((HEADS, tokens, LANES), bf16),
            jax.ShapeDtypeStruct((HEADS, keys, LANES), bf16),
            jax.ShapeDtypeStruct((HEADS, keys, LANES), bf16),
        ] + comm.out_shape(),
        scratch_shapes=[pltpu.VMEM((tokens, keys), bf16), pltpu.VMEM((tokens, LANES), bf16)] + comm.scratch(),
        compiler_params=comm.params(),
        name="attn_bwd",
    )(qkv, kv, kv, probs, out, d_out, *comm.args)


def gelu_parts(z):
    c = 0.7978845608028654
    z2 = z * z
    t = jnp.tanh(z * (c + (c * 0.044715) * z2))
    half = 0.5 * (1.0 + t)
    g = z * half
    dg = half + 0.5 * z * (1.0 - t * t) * (c + (3 * c * 0.044715) * z2)
    return g, dg


def mid_kernel(s, n, cuts, comm, *refs):
    own, refs = refs[:9 + 2 * comm.ready], refs[9 + 2 * comm.ready:]
    oaug_ref, x_ref, cot_ref, aid_ref, wo_ref, ab_ref, ff_ref, bup_ref, vec_ref = own[:9]
    weights = list(own[9:])
    ins, (mixed_ref, dmid_ref, do_ref, pack_ref), outs, refs = comm.split(refs, 4)
    (obuf, xbuf, dybuf, wobuf, ocat, n2buf, mid, acc, dn2, hidden, wofull, ubuf, dbuf, ga, gb, isem, wsem, osem,
     go, cotbuf, lsem, *comm_refs) = refs
    weights += list(outs[:2 * (len(cuts) - comm.ready)])
    tokens, d = xbuf.shape
    ds = d // s
    bo, bd, gain2, shift2 = vec_ref[2:3, :], vec_ref[3:4, :], vec_ref[6:7, :], vec_ref[7:8, :]
    at_o, at_u, b_o, b_d = (ab_ref.at[k] for k in range(4))
    ta, tm = min(256, tokens), min(512, tokens)
    chunks = [(c, j) for c in range(len(cuts)) for j in range(s)]

    def load(i):
        rows = pl.ds(i * ta, ta)
        for k, (src, dst) in enumerate(((oaug_ref.at[:, rows], obuf.at[:, rows]), (x_ref.at[rows], xbuf.at[rows]),
                                        (cot_ref.at[rows], cotbuf.at[rows]))):
            yield pltpu.make_async_copy(src, dst, isem.at[i, k])

    def save(i):
        rows = pl.ds(i * ta, ta)
        for k, (src, dst) in enumerate(((xbuf.at[rows], mixed_ref.at[rows]), (mid.at[rows], dmid_ref.at[rows]),
                                        (obuf.at[:, rows], do_ref.at[:, rows]))):
            yield pltpu.make_async_copy(src, dst, osem.at[i, k])

    wo_load = pltpu.make_async_copy(wo_ref, wobuf, lsem.at[0])
    def fetch(k):
        c, j = chunks[k]
        w = cuts[c][1]
        for m, (ref, buf) in enumerate(((weights[2 * c], ubuf), (weights[2 * c + 1], dbuf))):
            dst = buf.at[k % 2] if w == buf.shape[3] else buf.at[k % 2, :, :, pl.ds(0, w)]
            yield pltpu.make_async_copy(ref.at[pl.ds(j * n, n)], dst, wsem.at[k % 2, m])

    wo_load.start()
    for i in range(tokens // ta):
        for copy in load(i):
            copy.start()
    run = comm.begin(ins, outs, comm_refs)
    for copy in fetch(0):
        copy.start()
    wo_load.wait()
    run.step(4)

    wo = jnp.concatenate([wobuf[j][:, :ds] for j in range(s)], axis=1) if s > 1 else wobuf[0]
    wofull[...] = wo

    def before(i, carry):
        rows = pl.ds(i * ta, ta)
        run.within(i, 1, tokens // ta, 4)
        for copy in load(i):
            copy.wait()
        mask = column_mask(aid_ref[rows, :])
        for h in range(HEADS):
            ocat[rows, h * HEAD_DIM:(h + 1) * HEAD_DIM] = obuf[h, rows, :HEAD_DIM]
        o = ocat[rows, :]
        h_o = (nt(o, at_o[...]) * mask).astype(bf16)
        value = xbuf[rows, :].astype(f32) + nn(o, wofull[...]) + 0.5 * nn(h_o, b_o[...]) + bo
        mid[rows, :] = value
        nh2, _ = norm_parts(value)
        n2 = (nh2 * gain2 + shift2).astype(bf16)
        n2buf[rows, :d] = n2
        dy = jnp.where(aid_ref[rows, :] >= 0, cotbuf[rows, :], jnp.zeros((ta, d), bf16))
        dybuf[rows, :d] = dy
        hidden[rows, :] = h_o
        n2buf[rows, d:] = (0.5 * (nt(n2, at_u[...]) * mask).astype(bf16).astype(f32)).astype(bf16)
        dybuf[rows, d:] = (0.5 * nt(dy, b_d[...]) * mask).astype(bf16)
        return carry
    lax.fori_loop(0, tokens // ta, before, 0)

    for k, (c, j) in enumerate(chunks):
        start, w = cuts[c]
        late = k + 1 < len(chunks) and chunks[k + 1][0] >= comm.ready and chunks[k + 1][1] == 0
        if k + 1 < len(chunks) and not late:
            for copy in fetch(k + 1):
                copy.start()
        for copy in fetch(k):
            copy.wait()
        cols = slice(start, start + w)

        def chunk(i, carry, k=k, j=j, w=w, cols=cols, slot=k % 2):
            rows = pl.ds(i * tm, tm)
            run.within(i, 1, tokens // tm, 8)
            wu = jnp.concatenate([ubuf[slot, :, :, :w].reshape(d, w), ff_ref[1, j, :, cols]])
            wd = jnp.concatenate([dbuf[slot, :, :, :w].reshape(d, w), ff_ref[0, j, :, cols]])
            z = nn(n2buf[rows, :], wu) + bup_ref[j, :, cols]
            g, dgelu = gelu_parts(z)
            g = g.astype(bf16)
            dg = nn(dybuf[rows, :], wd).astype(bf16)
            dz = (dg.astype(f32) * dgelu).astype(bf16)
            if k == 0:
                acc[rows, :] = nt(g, wd)
                dn2[rows, :] = nt(dz, wu)
            else:
                acc[rows, :] += nt(g, wd)
                dn2[rows, :] += nt(dz, wu)
            more_a, more_b = tn(dybuf[rows, d:], g), tn(n2buf[rows, d:], dz)

            @pl.when(i == 0)
            def _():
                ga[:, :w] = more_a
                gb[:, :w] = more_b

            @pl.when(i > 0)
            def _():
                ga[:, :w] += more_a
                gb[:, :w] += more_b
            return carry
        lax.fori_loop(0, tokens // tm, chunk, 0)
        at = 2 * d + j * ff_ref.shape[3] + start
        pack_ref[0, :, at:at + w] = ga[:, :w].astype(bf16)
        pack_ref[1, :, at:at + w] = gb[:, :w].astype(bf16)
        run.step(8)
        if late:
            run.until(2 * (chunks[k + 1][0] - comm.ready) + 1)
            for copy in fetch(k + 1):
                copy.start()

    run.rest()

    go[...] = jnp.zeros_like(go)

    def after(i, carry):
        rows = pl.ds(i * ta, ta)
        mask = column_mask(aid_ref[rows, :])
        h_d = (acc[rows, d:] * mask).astype(bf16)
        xbuf[rows, :] = (mid[rows, :] + bd + acc[rows, :d] + 0.5 * nn(h_d, b_d[...])).astype(bf16)
        dh_u = (0.5 * dn2[rows, d:] * mask).astype(bf16)
        nh2, r2 = norm_parts(mid[rows, :])
        dy = dybuf[rows, :d]
        dmid = dy.astype(f32) + norm_back(dn2[rows, :d] + nn(dh_u, at_u[...]), gain2, nh2, r2)
        mid[rows, :] = dmid
        db = dmid.astype(bf16)
        dh_o = (0.5 * nt(db, b_o[...]) * mask).astype(bf16)
        do = (nt(db, wofull[...]) + nn(dh_o, at_o[...])).astype(bf16)
        go[0] += tn(dh_o, ocat[rows, :])
        go[1] += 0.5 * tn(hidden[rows, :], db)
        go[2] += tn(dh_u, n2buf[rows, :d])
        go[3] += 0.5 * tn(h_d, dy)
        for h in range(HEADS):
            obuf[h, rows, :HEAD_DIM] = do[:, h * HEAD_DIM:(h + 1) * HEAD_DIM]
        for copy in save(i):
            copy.start()
        return carry
    lax.fori_loop(0, tokens // ta, after, 0)
    for c, order in enumerate(((0, 2), (1, 3))):
        for k, which in enumerate(order):
            pack_ref[c, :, k * d:(k + 1) * d] = go[which].astype(bf16)
    for i in range(tokens // ta):
        for copy in save(i):
            copy.wait()


def mid_call(oaug, x, cot, aid, wo, weights, cuts, ab, ff, bup, vec, comm):
    tokens, d = x.shape
    s, ds = wo.shape[0], wo.shape[2]
    pieces = weights[0].shape[0] // s
    widest = max(w for _, w in cuts)
    fslot = ff.shape[3]
    full = pl.BlockSpec(memory_space=pltpu.VMEM)
    dma = pltpu.SemaphoreType.DMA
    comm.ready = len(weights) // 2
    tiles = tokens // min(256, tokens)

    def v(*shape, dtype=bf16):
        return pltpu.VMEM(shape, dtype)

    return pl.pallas_call(
        partial(mid_kernel, s, pieces, cuts, comm),
        in_specs=any_specs(3) + [full] + any_specs(1) + [full] * 4 + any_specs(len(weights)) + comm.in_specs(),
        out_specs=any_specs(3) + [full] + comm.out_specs(),
        out_shape=[
            jax.ShapeDtypeStruct((tokens, d), bf16),
            jax.ShapeDtypeStruct((tokens, d), f32),
            jax.ShapeDtypeStruct((HEADS, tokens, LANES), bf16),
            jax.ShapeDtypeStruct((2, LORA, 2 * d + s * fslot), bf16),
        ] + comm.out_shape(),
        scratch_shapes=[
            v(HEADS, tokens, LANES), v(tokens, d), v(tokens, d + LORA), v(s, d, ds), v(tokens, d), v(tokens, d + LORA),
            v(tokens, d, dtype=f32), v(tokens, d + LORA, dtype=f32), v(tokens, d + LORA, dtype=f32),
            v(tokens, LORA), v(d, d), v(2, pieces, d // pieces, widest), v(2, pieces, d // pieces, widest),
            v(LORA, widest, dtype=f32), v(LORA, widest, dtype=f32),
            dma((tiles, 3)), dma((2, 2)), dma((tiles, 3)), v(4, LORA, d, dtype=f32), v(tokens, d), dma((1,)),
        ] + comm.scratch(),
        compiler_params=comm.params(),
        name="mid",
    )(oaug, x, cot, aid, wo, ab, ff, bup, vec, *weights, *comm.args)


def tail_kernel(s, dq_ref, dk_ref, dv_ref, x_ref, n1_ref, h_ref, dmid_ref, aid_ref,
                wq_ref, wk_ref, wv_ref, at_ref, b_ref, vec_ref, out_ref, low_ref, pack_ref, dy_ref, ga_ref, gb_ref):
    i = pl.program_id(0)
    tm, d = x_ref.shape
    nh = HEADS // s
    ds = d // s
    mask = column_mask(aid_ref[...])

    @pl.when(i == 0)
    def _():
        ga_ref[...] = jnp.zeros_like(ga_ref)
        gb_ref[...] = jnp.zeros_like(gb_ref)

    n1 = n1_ref[...]
    dn = jnp.zeros((tm, d), f32)
    for p, (src, w_ref) in enumerate(((dq_ref, wq_ref), (dk_ref, wk_ref), (dv_ref, wv_ref))):
        dh = jnp.zeros((tm, LORA), f32)
        for j in range(s):
            for h in range(nh):
                dy_ref[p, j, :, h * HEAD_DIM:(h + 1) * HEAD_DIM] = src[j * nh + h, :, :HEAD_DIM]
            dy = dy_ref[p, j]
            dh = dh + nt(dy, b_ref[p, j])
            dn = dn + nt(dy, w_ref[j])
            gb_ref[p, j] += 0.5 * tn(h_ref[p], dy)
        dh = (0.5 * dh * mask).astype(bf16)
        dn = dn + nn(dh, at_ref[p])
        ga_ref[p] += tn(dh, n1)
    nhat, r = norm_parts(x_ref[...].astype(f32))
    out = dmid_ref[...] + norm_back(dn, vec_ref[4:5, :], nhat, r)
    out_ref[...] = out
    low_ref[...] = out.astype(bf16)

    @pl.when(i == pl.num_programs(0) - 1)
    def _():
        for p in range(3):
            pack_ref[0, :, p * d:(p + 1) * d] = ga_ref[p].astype(bf16)
            for j in range(s):
                at = p * d + j * ds
                pack_ref[1, :, at:at + ds] = gb_ref[p, j].astype(bf16)


def tail_call(dq, dk, dv, x, n1, hid, dmid, aid, wq, wk, wv, at, bq, vec):
    tokens, d = x.shape
    s = wq.shape[0]
    tm = min(256, tokens)
    full = pl.BlockSpec(memory_space=pltpu.VMEM)
    tile = pl.BlockSpec((tm, d), lambda i: (i, 0))
    heads = pl.BlockSpec((HEADS, tm, LANES), lambda i: (0, i, 0))
    return pl.pallas_call(
        partial(tail_kernel, s),
        grid=(tokens // tm,),
        in_specs=[
            heads, heads, heads, tile, tile,
            pl.BlockSpec((3, tm, LORA), lambda i: (0, i, 0)),
            tile,
            pl.BlockSpec((tm, 1), lambda i: (i, 0)),
            full, full, full, full, full, full,
        ],
        out_specs=[tile, tile, full],
        out_shape=[
            jax.ShapeDtypeStruct((tokens, d), f32),
            jax.ShapeDtypeStruct((tokens, d), bf16),
            jax.ShapeDtypeStruct((2, LORA, 3 * d), bf16),
        ],
        scratch_shapes=[
            pltpu.VMEM((3, s, tm, d // s), bf16),
            pltpu.VMEM((3, LORA, d), f32),
            pltpu.VMEM((3, s, LORA, d // s), f32),
        ],
        compiler_params=pltpu.CompilerParams(vmem_limit_bytes=VMEM),
        name="tail",
    )(dq, dk, dv, x, n1, hid, dmid, aid, wq, wk, wv, at, bq, vec)


def rows_of_adapters(a):
    t = jnp.swapaxes(a, -1, -2)
    return t.reshape(*t.shape[:-3], t.shape[-3] * t.shape[-2], t.shape[-1])


def local(tokens, cotangent, lengths, adapter_ids, w_query, w_key, w_value, w_out, w_up, w_down,
          b_query, b_value, b_out, b_up, b_down, gain_one, shift_one, gain_two, shift_two,
          qkv_a, out_a, attn_b, up_a, up_b, down_a, down_b):
    seq = lax.axis_size("seq")
    rows, part_len, d = tokens.shape
    group = seq // rows
    count = rows * part_len
    ds, fs = w_query.shape[1], w_up.shape[1]
    me = lax.axis_index("seq")
    row, chunk = me // group, me % group

    def moves(j):
        return [(a, (a % rows + j) % rows * group + a // rows) for a in range(seq)]

    def send(piece, pairs):
        return piece if all(a == b for a, b in pairs) else lax.ppermute(piece, "seq", pairs)

    def to_row(t):
        out = jnp.zeros((rows, part_len, d), t.dtype)
        for j in range(rows):
            piece = lax.dynamic_index_in_dim(t, (me + j) % rows, 0, False)
            out = lax.dynamic_update_index_in_dim(out, send(piece, moves(j)), (row - j) % rows, 0)
        return out.reshape(count, d)

    def from_row(t, dtype):
        t = t.reshape(rows, part_len, d)
        out = jnp.zeros((rows, part_len, d), dtype)
        for j in range(rows):
            piece = lax.dynamic_index_in_dim(t, (row - j) % rows, 0, False)
            pairs = [(b, a) for a, b in moves(j)]
            if not all(a == b for a, b in pairs):
                piece = piece.astype(bf16)
            got = send(piece, pairs).astype(dtype)
            out = lax.dynamic_update_index_in_dim(out, got, (me + j) % rows, 0)
        return out

    dps = lax.axis_size("dp")
    nz = dps // 4
    fast = seq == 2 and rows == 2 and nz == 4
    slot, fslot = up128(ds), up128(fs)
    step = up128(-(-fslot // max(round(fslot / 768), 1)))
    cuts = [(a, min(step, fslot - a)) for a in range(0, fslot, step)]

    def wide_to(t, n):
        return jnp.pad(t, ((0, 0), (0, n - t.shape[1])))

    wu_part, wd_part = wide_to(w_up, fslot), wide_to(w_down.T, fslot)
    ff_parts = [t[:, a:a + n] for a, n in cuts for t in (wu_part, wd_part)]
    narrow = jnp.concatenate([
        rows_of_adapters(qkv_a), rows_of_adapters(out_a)[None], rows_of_adapters(up_a)[None],
        attn_b.reshape(4, -1, d), down_b.reshape(1, -1, d)])
    wide = jnp.stack([rows_of_adapters(down_a), up_b.reshape(-1, up_b.shape[-1])])
    vec_part = jnp.stack([b_query, b_value, b_out, b_down, gain_one, shift_one, gain_two, shift_two])
    teams = [[g * group + c for c in range(group)] for g in range(rows)]

    my_len = lax.dynamic_index_in_dim(lengths, row, 0, False)
    my_ids = lax.dynamic_index_in_dim(adapter_ids, row, 0, False)
    slots = jnp.arange(my_len.shape[0], dtype=jnp.int32)
    ends = jnp.sum(jnp.where(slots[None, :] <= slots[:, None], my_len[None, :], 0), axis=1)
    pos = chunk * count + jnp.arange(count, dtype=jnp.int32)
    pic = jnp.sum((pos[:, None] >= ends[None, :]).astype(jnp.int32), axis=1, keepdims=True)
    aid = jnp.sum(jnp.where(pic == slots[None, :], my_ids[None, :], 0), axis=1, keepdims=True)
    aid = jnp.where(pos[:, None] < ends[-1], aid, -1)

    def from_halves(t):
        return jnp.swapaxes(t, 0, 1).reshape(t.shape[1], -1, t.shape[3])

    if fast:
        me_dp = lax.axis_index("dp")

        def share(t):
            flat = t.reshape(-1, t.shape[-1])
            n = flat.shape[0] // dps
            return lax.dynamic_slice_in_dim(flat, me_dp * n, n, 0)

        def whole(t):
            return t.reshape(seq, d, t.shape[2])

        small = jnp.concatenate([wide_to(vec_part, fslot), wide_to(b_up[None], fslot), jnp.zeros((7, fslot), bf16)])
        narrow, wq, wk, wv, wo, wide, x, small, qkv, n1, hid = front_call(
            nz, [share(narrow), w_query, w_key, w_value, w_out, share(wide)], tokens, small, aid, pic)
        x = x.reshape(count, d)
        narrow = from_halves(narrow.reshape(seq, 10, LORA // seq, d))
        vec = jnp.concatenate([small[k, :8, :ds] for k in range(seq)], axis=1).astype(f32)
        bup = small[:, 8:9, :fs].astype(f32)
        wq, wk, wv, wo = whole(wq), whole(wk), whole(wv), whole(wo)
        wide = from_halves(wide.reshape(seq, 2, LORA // seq, -1))

        def fetch(shards, cid, halves=None):
            return Fetch(nz, shards, [(k, 0, t.shape[1]) for k, t in enumerate(shards)], cid, halves)

        second = fetch(ff_parts[:2], 3, cotangent)
        last = fetch(ff_parts[2:], 6)
    else:
        def gather_all(shard):
            full = lax.all_gather(shard, ("seq", "dp"), axis=0, tiled=True)
            return full.reshape(seq, d, shard.shape[1])

        wq, wk, wv, wo, *weights = (gather_all(t) for t in [w_query, w_key, w_value, w_out] + ff_parts)
        narrow = lax.all_gather(narrow, "seq", axis=1, tiled=True)
        wide = lax.all_gather(wide, "seq", axis=1, tiled=True)
        vec = lax.all_gather(vec_part, "seq", axis=1, tiled=True).astype(f32)
        bup = lax.all_gather(b_up[None], "seq", axis=0, tiled=True).astype(f32)[:, None]
        x = to_row(tokens)
        cot = to_row(cotangent)
        second = last = Quiet()

    at, b = narrow[:5], narrow[5:]
    bq = jnp.swapaxes(b[:3].reshape(3, LORA, seq, ds), 1, 2)
    bias = jnp.stack([vec[0], jnp.zeros_like(vec[0]), vec[1]]).reshape(3, seq, 1, ds)
    if not fast:
        wqkv = jnp.stack([wq, wk, wv])
        qkv, n1, hid = qkv_call(x, wqkv, at, bq, bias, vec, aid, pic)
    if group == 1:
        kv, off = qkv, 1
    else:
        kv = lax.all_gather(qkv[1:], "seq", axis=2, tiled=True, axis_index_groups=teams)
        off = 0
    probs, oaug, *got = attn_fwd_call(qkv, kv, off, second)
    if fast:
        weights, cot = got[:2], got[2].reshape(count, d)
    more = ((0, 0), (0, 0), (0, 0), (0, fslot - fs))
    ff = jnp.pad(jnp.swapaxes(wide.reshape(2, LORA, seq, fs), 1, 2), more)
    bup = jnp.pad(bup, more[1:])
    mixed, dmid, d_out, g_mid, *got = mid_call(
        oaug, x, cot, aid, wo, weights, cuts, jnp.concatenate([at[3:], b[3:]]), ff, bup, vec, last)

    def blocks(t):
        return t.reshape(2, 2, 2 * nz, 8, t.shape[2])

    third_comm = Settle(nz, blocks(g_mid), mixed.reshape(rows, part_len, d), 4) if fast else Quiet()
    dq, dk, dv, *got = attn_bwd_call(qkv, kv, off, probs, oaug, d_out, third_comm)
    if fast:
        g_mid, mixed = got[0].reshape(2, LORA // seq, -1), got[1]
    if group > 1:
        dk, dv = (lax.psum_scatter(t, "seq", scatter_dimension=1, axis_index_groups=teams, tiled=True)
                  for t in (dk, dv))
    d_in, d_low, g_qkv = tail_call(dq, dk, dv, x, n1, hid, dmid, aid, wq, wk, wv, at, bq, vec)
    if fast:
        g_qkv, other = finish_call(nz, blocks(g_qkv), d_low.reshape(rows, part_len, d))
        g_qkv = g_qkv.reshape(2, LORA // seq, -1)
        mine = lax.dynamic_index_in_dim(d_in.reshape(rows, part_len, d), me, 0, False)
        other = other.astype(f32)
        d_in = jnp.where(me == 0, jnp.stack([mine, other]), jnp.stack([other, mine]))
    else:
        def total(t):
            return lax.psum(lax.psum_scatter(t, "seq", scatter_dimension=1, tiled=True), "dp")

        g_mid, g_qkv = total(g_mid), total(g_qkv)
        mixed = from_row(mixed, bf16)
        d_in = from_row(d_in, f32)

    def down_form(t):
        return jnp.swapaxes(t.astype(f32).reshape(-1, RANK, t.shape[-1]), -1, -2)

    def up_form(t):
        return t.astype(f32).reshape(-1, RANK, t.shape[-1])

    def cut(t, k):
        return t[:, k * d:(k + 1) * d]

    def ff_of(t):
        return jnp.concatenate([t[:, 2 * d + j * fslot:2 * d + j * fslot + fs] for j in range(seq)], axis=1)

    a_mid, b_mid = g_mid
    a_qkv, b_qkv = g_qkv
    return (
        mixed,
        d_in,
        jnp.stack([down_form(cut(a_qkv, p)) for p in range(3)]),
        down_form(cut(a_mid, 0)),
        jnp.stack([up_form(cut(b_qkv, p)) for p in range(3)] + [up_form(cut(b_mid, 0))]),
        down_form(cut(a_mid, 1)),
        up_form(ff_of(b_mid)),
        down_form(ff_of(a_mid)),
        up_form(cut(b_mid, 1)),
    )


def solution(mesh):
    both = P("dp", "seq", None)
    lead = P("seq", None, None)
    second = P(None, "seq", None, None)
    return jax.shard_map(
        local,
        mesh=mesh,
        in_specs=(both, both, P("dp", None), P("dp", None))
        + (P("dp", "seq"),) * 5 + (P("seq", "dp"),) + (P("seq"),) * 9
        + (second, lead, second, lead, lead, lead, lead),
        out_specs=(both, both, second, lead, second, lead, lead, lead, lead),
        check_vma=False,
    )
```

```python
from functools import partial

import jax
import jax.numpy as jnp
from jax import lax
from jax.experimental import pallas as pl
from jax.experimental.pallas import tpu as pltpu
from jax.sharding import PartitionSpec as P

HEADS = 16
HEAD_DIM = 72
RANK = 16
ADAPTERS = 8
LORA = RANK * ADAPTERS
LANES = 128
EPS = 1e-06
SCALE = HEAD_DIM ** (-0.5)
BIG = 1e30
LOG2E = 1.4426950408889634
VMEM = 61 * 1024 * 1024

MESH = pl.DeviceIdType.MESH
bf16 = jnp.bfloat16
f32 = jnp.float32


def nn(a, b):
    return jnp.dot(a, b, preferred_element_type=f32)


def nt(a, b):
    return lax.dot_general(a, b, (((1,), (1,)), ((), ())), preferred_element_type=f32)


def tn(a, b):
    return lax.dot_general(a, b, (((0,), (0,)), ((), ())), preferred_element_type=f32)


def up128(n):
    return -(-n // LANES) * LANES


def lane_ids(rows):
    return lax.broadcasted_iota(jnp.int32, (rows, LANES), 1)


def norm_parts(x):
    center = jnp.mean(x, axis=-1, keepdims=True)
    xc = x - center
    r = lax.rsqrt(jnp.mean(xc * xc, axis=-1, keepdims=True) + EPS)
    return xc * r, r


def norm_back(dn, gain, nh, r):
    gh = dn * gain
    a = jnp.mean(gh, axis=-1, keepdims=True)
    b = jnp.mean(gh * nh, axis=-1, keepdims=True)
    return r * (gh - a - nh * b)


def column_mask(aid):
    return (lane_ids(aid.shape[0]) // RANK == aid).astype(f32)


class Spot:
    def __init__(self, nz):
        dp = lax.axis_index("dp")
        self.nz = nz
        self.x = lax.axis_index("seq")
        self.z, self.y, self.c = dp // 4, (dp // 2) % 2, dp % 2
        self.xn = self.device(1 - self.x, self.y, self.z, self.c)
        self.yn = self.device(self.x, 1 - self.y, self.z, self.c)
        self.sib = self.device(self.x, self.y, self.z, 1 - self.c)
        self.zs = [None] + [self.device(self.x, self.y, self.zk(k), self.c) for k in range(1, nz)]
        flip = self.z // 2
        self.inner = self.z + flip * (3 - 2 * self.z)
        self.zr = [m + flip * (3 - 2 * m) for m in (self.inner, 1 - self.inner, 2, 3)]
        self.zp = [self.device(self.x, self.y, z, self.c) for z in self.zr]

    def device(self, x, y, z, c):
        return ((z * 2 + y) * 2 + c, x)

    def shard(self, x, y, z):
        return (x * self.nz + z) * 4 + y * 2 + self.c

    def zk(self, k):
        return (self.z + k) % self.nz

    def barrier(self):
        peers = [self.xn, self.yn, self.sib] + self.zs[1:]
        sem = pltpu.get_barrier_semaphore()
        for peer in peers:
            pl.semaphore_signal(sem, inc=1, device_id=peer, device_id_type=MESH)
        pl.semaphore_wait(sem, len(peers))


def remote(src, dst, send, recv, device):
    return pltpu.make_async_remote_copy(
        src_ref=src, dst_ref=dst, send_sem=send, recv_sem=recv, device_id=device, device_id_type=MESH
    )


class Gather:
    kinds = [(kind, r) for r in range(4) for kind in "zxyd"]

    def __init__(self, spot, parts, ins, outs, send, recv, core, own):
        self.s, self.parts, self.ins, self.outs = spot, parts, ins, outs
        self.send, self.recv, self.core, self.own = send, recv, core, own
        every = [to for kind, r in self.kinds for to in self.targets(kind, r)]
        self.counts = sum(to[0] != "i" for to in every), sum(to[0] == "i" for to in every)

    @staticmethod
    def scratch(nz, count):
        dma = pltpu.SemaphoreType.DMA
        return [dma((count, 2)), dma((count, 4 * nz)), dma((count,)), dma((count,))]

    def targets(self, kind, r):
        if kind == "z":
            return (["z1", "z2", "z3"] if r == 0 else []) + ["x", "y", "s"]
        if kind == "x":
            return (["y"] if r in (0, 3) else []) + ["s"]
        if kind == "d":
            return {0: ["z1", "iz2"], 2: ["iz1"]}.get(r, []) + ["s"]
        return ["s"]

    def index(self, kind, r):
        s = self.s
        x = 1 - s.x if kind in "xd" else s.x
        y = 1 - s.y if kind in "yd" else s.y
        return s.shard(x, y, s.zr[r])

    def place(self, g, index):
        a, start, size = self.parts[g]
        if size == self.outs[a].shape[2]:
            return self.outs[a].at[index]
        return self.outs[a].at[index, :, pl.ds(start, size)]

    def source(self, g, kind, r):
        if (kind, r) != ("z", 0):
            return self.place(g, self.index(kind, r))
        a, start, size = self.parts[g]
        if size == self.ins[a].shape[1]:
            return self.ins[a]
        return self.ins[a].at[:, pl.ds(start, size)]

    def arrival(self, g, kind, r):
        return self.recv.at[g, "zxyd".index(kind) * 4 + r]

    def copy(self, g, kind, r, to):
        s = self.s
        if to == "s":
            recv, device = self.core.at[g], s.sib
        elif to == "x":
            recv, device = self.arrival(g, "x", r), s.xn
        elif to == "y":
            recv, device = self.arrival(g, "y" if kind == "z" else "d", r), s.yn
        else:
            i = int(to[-1])
            if kind == "z":
                there = i if i < 2 else 3 - s.inner
            else:
                there = 1 if to == "z1" else 2
            recv, device = self.arrival(g, kind, there), s.zp[i]
        send = self.send.at[g, int(to[0] == "i")]
        return remote(self.source(g, kind, r), self.place(g, self.index(kind, r)), send, recv, device)

    def local(self, g):
        return pltpu.make_async_copy(self.source(g, "z", 0), self.place(g, self.index("z", 0)), self.own.at[g])

    def arrive(self, g, kind, r):
        if (kind, r) == ("z", 0):
            self.local(g).start()
        else:
            ref = self.place(g, self.index(kind, r))
            remote(ref, ref, self.send.at[g, 0], self.arrival(g, kind, r), self.s.xn).wait_recv()
        for to in self.targets(kind, r):
            if to[0] == "i":
                pl.when(self.s.inner == 1)(self.copy(g, kind, r, to).start)
            else:
                self.copy(g, kind, r, to).start()

    def several(self, g, n, which=0):
        a, start, size = self.parts[g]
        ref = self.outs[a].at[pl.ds(0, n)]
        if size < self.outs[a].shape[2]:
            ref = self.outs[a].at[pl.ds(0, n), :, pl.ds(start, size)]
        return remote(ref, ref, self.send.at[g, which], self.core.at[g], self.s.sib)

    def end(self, g):
        self.several(g, self.outs[self.parts[g][0]].shape[0] // 2).wait_recv()
        self.local(g).wait()
        self.several(g, self.counts[0]).wait_send()

        @pl.when(self.s.inner == 1)
        def _():
            self.several(g, self.counts[1], 1).wait_send()

    def actions(self):
        n = len(self.parts)
        out = []
        for t in range(n + 4):
            if t < n:
                out.append((self.arrive, t, "z", 0))
            if 0 <= t - 1 < n:
                out += [(self.arrive, t - 1, "z", r) for r in (1, 2, 3)]
            if 0 <= t - 2 < n:
                out += [(self.arrive, t - 2, kind, r) for r in (0, 3, 1, 2) for kind in "xy"]
            if 0 <= t - 3 < n:
                out += [(self.arrive, t - 3, "d", r) for r in (0, 3, 2, 1)]
            if 0 <= t - 4 < n:
                out.append((self.end, t - 4))
        return out


class Swap:
    def __init__(self, spot, mine, got, sems, slot=None):
        self.s, self.mine, self.got, self.sems = spot, mine, got, sems
        self.slot = spot.x if slot is None else slot

    def copies(self):
        s = self.s
        here = pltpu.make_async_copy(self.mine.at[s.x], self.got.at[s.x], self.sems.at[0])
        there = remote(self.mine.at[1 - s.x], self.got.at[self.slot], self.sems.at[1], self.sems.at[2], s.xn)
        return here, there

    def start(self):
        for copy in self.copies():
            copy.start()

    def end(self):
        here, there = self.copies()
        here.wait()
        ref = self.got.at[1 - self.s.x]
        remote(ref, ref, self.sems.at[1], self.sems.at[2], self.s.xn).wait_recv()
        there.wait_send()


def run_actions(actions, step, steps):
    for t in range(steps):
        a, b = len(actions) * t // steps, len(actions) * (t + 1) // steps
        if a == b:
            continue

        @pl.when(step == t)
        def _(a=a, b=b):
            for action in actions[a:b]:
                action[0](*action[1:])


class Reduce:
    def __init__(self, spot, data, result, refs):
        self.s, self.data, self.result = spot, data, result
        self.r1, self.s1, self.r2, self.s2, self.r3, self.s3, self.r4, self.total = refs[:8]
        self.send, self.recv, self.out = refs[8:]

    @staticmethod
    def scratch(nz, width):
        def v(*dims):
            return pltpu.VMEM((*dims, 8, width), bf16)
        dma = pltpu.SemaphoreType.DMA
        n = 5 + 2 * (nz - 1)
        return [v(2, 2 * nz), v(2, 2 * nz), v(2, nz), v(2, nz), v(nz, 2), v(2), v(1), v(2, 2 * nz),
                dma((n,)), dma((n,)), dma((1,))]

    def pair(self, i, src, dst, device):
        return remote(src, dst, self.send.at[i], self.recv.at[i], device)

    def to_core(self):
        return self.pair(0, self.data.at[1 - self.s.c], self.r1, self.s.sib)

    def to_y(self):
        nz = self.s.nz
        return self.pair(1, self.s1.at[:, pl.ds((1 - self.s.y) * nz, nz)], self.r2, self.s.yn)

    def to_x(self):
        return self.pair(2, self.s3.at[1 - self.s.x], self.r4.at[0], self.s.xn)

    def to_z(self, k):
        s = self.s
        return self.pair(4 + k, self.s2.at[:, s.zk(k)], self.r3.at[s.z], s.zs[k])

    def from_z(self, k):
        s = self.s
        ref = self.r3.at[s.zk(k)]
        return remote(ref, ref, self.send.at[4 + s.nz - k], self.recv.at[4 + s.nz - k], s.zs[k])

    def back_z(self, k):
        s = self.s
        ref = self.total.at[s.c, s.y * s.nz + s.z]
        return self.pair(4 + s.nz - 1 + k, ref, ref, s.zs[k])

    def from_back_z(self, k):
        s = self.s
        i = 4 + s.nz - 1 + s.nz - k
        ref = self.total.at[s.c, s.y * s.nz + s.zk(k)]
        return remote(ref, ref, self.send.at[i], self.recv.at[i], s.zs[k])

    def back_y(self, y):
        s = self.s
        ref = self.total.at[s.c, pl.ds(y * s.nz, s.nz)]
        return self.pair(3, ref, ref, s.yn)

    def back_core(self, c):
        ref = self.total.at[c]
        return self.pair(4, ref, ref, self.s.sib)

    def one(self):
        self.to_core().start()

    def two(self):
        s, nz = self.s, self.s.nz
        self.to_core().wait_recv()

        def add(i, c):
            x, b = i // (2 * nz), i % (2 * nz)
            self.s1[x, b] = (self.data[s.c, x, b].astype(f32) + self.r1[x, b].astype(f32)).astype(bf16)
            return c
        lax.fori_loop(0, 4 * nz, add, 0)
        self.to_y().start()

    def three(self):
        s, nz = self.s, self.s.nz
        self.to_y().wait_recv()

        def add(i, c):
            x, b = i // nz, i % nz
            self.s2[x, b] = (self.s1[x, s.y * nz + b].astype(f32) + self.r2[x, b].astype(f32)).astype(bf16)
            return c
        lax.fori_loop(0, 2 * nz, add, 0)
        for k in range(1, nz):
            self.to_z(k).start()

    def four(self):
        s, nz = self.s, self.s.nz
        for k in range(1, nz):
            self.from_z(k).wait_recv()
        for x in range(2):
            v = self.s2[x, s.z].astype(f32)
            for k in range(1, nz):
                v = v + self.r3[s.zk(k), x].astype(f32)
            self.s3[x] = v.astype(bf16)
        self.to_x().start()

    def five(self):
        s, nz = self.s, self.s.nz
        self.to_x().wait_recv()
        v = self.s3[s.x].astype(f32) + self.r4[0].astype(f32)
        self.total[s.c, s.y * s.nz + s.z] = v.astype(bf16)
        for k in range(1, nz):
            self.back_z(k).start()

    def six(self):
        for k in range(1, self.s.nz):
            self.from_back_z(k).wait_recv()
        self.back_y(self.s.y).start()

    def seven(self):
        self.back_y(1 - self.s.y).wait_recv()
        self.back_core(self.s.c).start()

    def end(self):
        s = self.s
        self.back_core(1 - s.c).wait_recv()
        out = pltpu.make_async_copy(self.total, self.result, self.out.at[0])
        out.start()
        out.wait()
        self.to_core().wait_send()
        self.to_x().wait_send()
        self.to_y().wait_send()
        for k in range(1, s.nz):
            self.to_z(k).wait_send()
            self.back_z(k).wait_send()
        self.back_y(s.y).wait_send()
        self.back_core(s.c).wait_send()

    def actions(self):
        return [(f,) for f in (self.one, self.two, self.three, self.four, self.five, self.six, self.seven, self.end)]


def any_specs(n):
    return [pl.BlockSpec(memory_space=pl.ANY)] * n


def gathered(nz, arrays):
    return [jax.ShapeDtypeStruct((8 * nz,) + a.shape, a.dtype) for a in arrays]


def finish_kernel(nz, g_ref, d_ref, total_ref, got_ref, *refs):
    spot = Spot(nz)
    spot.barrier()
    reduce = Reduce(spot, g_ref, total_ref, refs[:-1])
    sems = refs[-1]
    there = remote(d_ref.at[1 - spot.x], got_ref, sems.at[0], sems.at[1], spot.xn)
    reduce.one()
    there.start()
    for f in reduce.actions()[1:]:
        f[0]()
    there.wait()


def finish_call(nz, g, d):
    width = g.shape[-1]
    dma = pltpu.SemaphoreType.DMA
    return pl.pallas_call(
        partial(finish_kernel, nz),
        in_specs=[pl.BlockSpec(memory_space=pltpu.VMEM), pl.BlockSpec(memory_space=pl.ANY)],
        out_specs=any_specs(2),
        out_shape=[
            jax.ShapeDtypeStruct((2,) + g.shape[2:], bf16), jax.ShapeDtypeStruct(d.shape[1:], bf16)],
        scratch_shapes=Reduce.scratch(nz, width) + [dma((2,))],
        compiler_params=pltpu.CompilerParams(collective_id=5, has_side_effects=True, vmem_limit_bytes=40 * 2**20),
        name="finish",
    )(g, d)


class Steps:
    def __init__(self, actions):
        self.actions = list(actions)

    def take(self, count):
        out, self.actions = self.actions[:count], self.actions[count:]
        return out

    @staticmethod
    def do(actions):
        for action in actions:
            action[0](*action[1:])

    def step(self, count):
        self.do(self.take(count))

    def rest(self):
        self.step(len(self.actions))

    def until(self, part):
        ends = [k for k, action in enumerate(self.actions) if action[0].__name__ == "end" and action[1] == part]
        if ends:
            self.step(ends[0] + 1)

    def within(self, first, last, *counts):
        plan = [(t, [self.take(count) for count in counts]) for t in range(first, last)]

        def point(k):
            def run(i):
                for t, lists in plan:
                    if lists[k]:
                        pl.when(i == t)(partial(self.do, lists[k]))
            return run
        return [point(k) for k in range(len(counts))]


class Quiet:
    args = ()
    outs = ()
    steps = 1

    def split(self, refs, own):
        a, b = len(self.args), len(self.outs)
        return refs[:a], refs[a:a + own], refs[a + own:a + own + b], refs[a + own + b:]

    def in_specs(self):
        return any_specs(len(self.args))

    def out_specs(self):
        return any_specs(len(self.outs))

    def out_shape(self):
        return list(self.outs)

    def scratch(self):
        return []

    def params(self):
        return pltpu.CompilerParams(vmem_limit_bytes=VMEM)

    def run(self, step, ins, outs, refs):
        pass

    def close(self, step, ins, outs, refs):
        pass

    def begin(self, ins, outs, refs):
        return Steps([])


class Fetch(Quiet):
    def __init__(self, nz, shards, parts, cid, halves=None):
        self.nz, self.parts, self.cid, self.na = nz, parts, cid, len(shards)
        self.args = tuple(shards) + (() if halves is None else (halves,))
        self.outs = gathered(nz, shards) + ([] if halves is None else [jax.ShapeDtypeStruct(halves.shape, halves.dtype)])

    def scratch(self):
        return Gather.scratch(self.nz, len(self.parts)) + [pltpu.SemaphoreType.DMA((3,))]

    def params(self):
        return pltpu.CompilerParams(vmem_limit_bytes=VMEM, collective_id=self.cid, has_side_effects=True)

    def make(self, ins, outs, refs):
        spot = Spot(self.nz)
        gather = Gather(spot, self.parts, ins[:self.na], outs[:self.na], *refs[-5:-1])
        swap = Swap(spot, ins[-1], outs[-1], refs[-1]) if len(ins) > self.na else None
        return spot, gather, swap

    def begin(self, ins, outs, refs):
        spot, gather, _ = self.make(ins, outs, refs)
        spot.barrier()
        return Steps(gather.actions())

    def run(self, step, ins, outs, refs):
        spot, gather, swap = self.make(ins, outs, refs)

        @pl.when(step == 0)
        def _():
            spot.barrier()
            if swap:
                swap.start()
        run_actions(gather.actions()[:-4], step, self.steps)

    def close(self, step, ins, outs, refs):
        _, gather, swap = self.make(ins, outs, refs)

        @pl.when(step == self.steps - 1)
        def _():
            for action in gather.actions()[-4:]:
                action[0](*action[1:])
            if swap:
                swap.end()


class Settle(Quiet):
    def __init__(self, nz, g, halves, cid):
        self.nz, self.width, self.cid = nz, g.shape[-1], cid
        self.args = (g, halves)
        self.outs = [jax.ShapeDtypeStruct((2,) + g.shape[2:], bf16), jax.ShapeDtypeStruct(halves.shape, halves.dtype)]

    def in_specs(self):
        return [pl.BlockSpec(memory_space=pltpu.VMEM), pl.BlockSpec(memory_space=pl.ANY)]

    def scratch(self):
        return Reduce.scratch(self.nz, self.width) + [pltpu.SemaphoreType.DMA((3,))]

    def params(self):
        return pltpu.CompilerParams(vmem_limit_bytes=VMEM, collective_id=self.cid, has_side_effects=True)

    def make(self, ins, outs, refs):
        spot = Spot(self.nz)
        refs = refs[-12:]
        return spot, Reduce(spot, ins[0], outs[0], refs[:-1]), Swap(spot, ins[1], outs[1], refs[-1])

    def run(self, step, ins, outs, refs):
        spot, reduce, swap = self.make(ins, outs, refs)
        when = [0, 1, 4, 7, 9, 11, 13]

        @pl.when(step == 0)
        def _():
            spot.barrier()
        for (f,), t in zip(reduce.actions(), when):
            pl.when(step == t)(f)

        @pl.when(step == 4)
        def _():
            swap.start()

    def close(self, step, ins, outs, refs):
        _, reduce, swap = self.make(ins, outs, refs)

        @pl.when(step == self.steps - 1)
        def _():
            reduce.end()
            swap.end()


def qkv_kernel(nh, tm, x_ref, w_ref, at_ref, b_ref, bias_ref, vec_ref, aid_ref, pic_ref, out_ref, n1_ref, h_ref):
    p = pl.program_id(0)
    j = pl.program_id(1)
    tokens = x_ref.shape[0]

    @pl.when((p == 0) & (j == 0))
    def _():
        def norm_step(i, c):
            rows = pl.ds(i * tm, tm)
            nhat, _ = norm_parts(x_ref[rows, :].astype(f32))
            n1_ref[rows, :] = (nhat * vec_ref[4:5, :] + vec_ref[5:6, :]).astype(bf16)
            return c
        lax.fori_loop(0, tokens // tm, norm_step, 0)

    @pl.when(j == 0)
    def _():
        def hidden_step(i, c):
            rows = pl.ds(i * tm, tm)
            h = nt(n1_ref[rows, :], at_ref[0]) * column_mask(aid_ref[rows, :])
            h_ref[0, rows, :] = h.astype(bf16)
            return c
        lax.fori_loop(0, tokens // tm, hidden_step, 0)

    def step(i, c):
        rows = pl.ds(i * tm, tm)
        y = nn(n1_ref[rows, :], w_ref[0, 0])
        y = y + 0.5 * nn(h_ref[0, rows, :], b_ref[0, 0]) + bias_ref[0, 0]
        slot = lane_ids(tm) - HEAD_DIM
        pic = pic_ref[rows, :]
        same = slot == pic
        in_slots = (slot >= 0) & (slot < 16)
        q_aug = jnp.where(same, 1.0, 0.0)
        k_aug = jnp.where(in_slots & jnp.logical_not(same), -BIG, 0.0)
        v_aug = jnp.where((slot == 0) | (slot == 1), 1.0, 0.0)
        aug = jnp.where(p == 0, q_aug, jnp.where(p == 1, k_aug, v_aug))[:, HEAD_DIM:]
        for h in range(nh):
            head = y[:, h * HEAD_DIM:(h + 1) * HEAD_DIM]
            out_ref[0, h, rows, :HEAD_DIM] = head.astype(bf16)
            out_ref[0, h, rows, HEAD_DIM:] = aug.astype(bf16)
        return c
    lax.fori_loop(0, tokens // tm, step, 0)


def qkv_call(x, w, at, bq, bias, vec, aid, pic):
    tokens, d = x.shape
    s = w.shape[1]
    nh = HEADS // s
    tm = min(256, tokens)
    return pl.pallas_call(
        partial(qkv_kernel, nh, tm),
        grid=(3, s),
        in_specs=[
            pl.BlockSpec((tokens, d), lambda p, j: (0, 0)),
            pl.BlockSpec((1, 1, d, d // s), lambda p, j: (p, j, 0, 0)),
            pl.BlockSpec((1, LORA, d), lambda p, j: (p, 0, 0)),
            pl.BlockSpec((1, 1, LORA, nh * HEAD_DIM), lambda p, j: (p, j, 0, 0)),
            pl.BlockSpec((1, 1, 1, nh * HEAD_DIM), lambda p, j: (p, j, 0, 0)),
            pl.BlockSpec(vec.shape, lambda p, j: (0, 0)),
            pl.BlockSpec((tokens, 1), lambda p, j: (0, 0)),
            pl.BlockSpec((tokens, 1), lambda p, j: (0, 0)),
        ],
        out_specs=[
            pl.BlockSpec((1, nh, tokens, LANES), lambda p, j: (p, j, 0, 0)),
            pl.BlockSpec((tokens, d), lambda p, j: (0, 0)),
            pl.BlockSpec((1, tokens, LORA), lambda p, j: (p, 0, 0)),
        ],
        out_shape=[
            jax.ShapeDtypeStruct((3, HEADS, tokens, LANES), bf16),
            jax.ShapeDtypeStruct((tokens, d), bf16),
            jax.ShapeDtypeStruct((3, tokens, LORA), bf16),
        ],
        compiler_params=pltpu.CompilerParams(vmem_limit_bytes=VMEM),
        name="qkv",
    )(x, w, at, bq, bias, vec, aid, pic)


def attn_fwd_kernel(tq, comm, q_ref, k_ref, v_ref, *refs):
    ins, (p_ref, o_ref), outs, refs = comm.split(refs, 2)
    comm.run(pl.program_id(0), ins, outs, refs)

    for i in range(q_ref.shape[2] // tq):
        rows = pl.ds(i * tq, tq)
        s = nt(q_ref[0, 0, rows, :], k_ref[0, 0])
        top = jnp.max(s, axis=-1, keepdims=True)
        p = jnp.exp2((s - top) * (SCALE * LOG2E)).astype(bf16)
        o = nn(p, v_ref[0, 0])
        inv = 1.0 / o[:, HEAD_DIM:HEAD_DIM + 1]
        p_ref[0, rows, :] = (p.astype(f32) * inv).astype(bf16)
        o_ref[0, rows, :] = (o * inv).astype(bf16)
    comm.close(pl.program_id(0), ins, outs, refs)


def attn_fwd_call(qkv, kv, off, comm):
    tokens, keys = qkv.shape[2], kv.shape[2]
    tq = min(512, tokens)
    comm.steps = HEADS
    return pl.pallas_call(
        partial(attn_fwd_kernel, tq, comm),
        grid=(HEADS,),
        in_specs=[
            pl.BlockSpec((1, 1, tokens, LANES), lambda h: (0, h, 0, 0)),
            pl.BlockSpec((1, 1, keys, LANES), lambda h: (off, h, 0, 0)),
            pl.BlockSpec((1, 1, keys, LANES), lambda h: (off + 1, h, 0, 0)),
        ] + comm.in_specs(),
        out_specs=[
            pl.BlockSpec((1, tokens, keys), lambda h: (h, 0, 0)),
            pl.BlockSpec((1, tokens, LANES), lambda h: (h, 0, 0)),
        ] + comm.out_specs(),
        out_shape=[
            jax.ShapeDtypeStruct((HEADS, tokens, keys), bf16),
            jax.ShapeDtypeStruct((HEADS, tokens, LANES), bf16),
        ] + comm.out_shape(),
        scratch_shapes=comm.scratch(),
        compiler_params=comm.params(),
        name="attn_fwd",
    )(qkv, kv, kv, *comm.args)


def attn_bwd_kernel(tq, comm, q_ref, k_ref, v_ref, p_ref, o_ref, do_ref, *refs):
    ins, (dq_ref, dk_ref, dv_ref), outs, (ds_ref, da_ref, *refs) = comm.split(refs, 3)
    comm.run(pl.program_id(0), ins, outs, refs)

    for i in range(q_ref.shape[2] // tq):
        rows = pl.ds(i * tq, tq)
        lane = lane_ids(tq)
        do = jnp.where(lane < HEAD_DIM, do_ref[0, rows, :].astype(f32), 0.0)
        delta = jnp.sum(do * o_ref[0, rows, :].astype(f32), axis=-1, keepdims=True)
        hi = delta.astype(bf16).astype(f32)
        do = jnp.where(lane == HEAD_DIM, -hi, jnp.where(lane == HEAD_DIM + 1, hi - delta, do)).astype(bf16)
        da_ref[rows, :] = do
        dp = nt(do, v_ref[0, 0])
        ds = (p_ref[0, rows, :].astype(f32) * dp).astype(bf16)
        ds_ref[rows, :] = ds
        dq_ref[0, rows, :] = (nn(ds, k_ref[0, 0]) * SCALE).astype(bf16)
    dv_ref[0] = nn(da_ref[...].T, p_ref[0]).T.astype(bf16)
    dk_ref[0] = (nn(q_ref[0, 0].T, ds_ref[...]).T * SCALE).astype(bf16)
    comm.close(pl.program_id(0), ins, outs, refs)


def attn_bwd_call(qkv, kv, off, probs, out, d_out, comm):
    tokens, keys = qkv.shape[2], kv.shape[2]
    tq = min(256, tokens)
    comm.steps = HEADS
    return pl.pallas_call(
        partial(attn_bwd_kernel, tq, comm),
        grid=(HEADS,),
        in_specs=[
            pl.BlockSpec((1, 1, tokens, LANES), lambda h: (0, h, 0, 0)),
            pl.BlockSpec((1, 1, keys, LANES), lambda h: (off, h, 0, 0)),
            pl.BlockSpec((1, 1, keys, LANES), lambda h: (off + 1, h, 0, 0)),
            pl.BlockSpec((1, tokens, keys), lambda h: (h, 0, 0)),
            pl.BlockSpec((1, tokens, LANES), lambda h: (h, 0, 0)),
            pl.BlockSpec((1, tokens, LANES), lambda h: (h, 0, 0)),
        ] + comm.in_specs(),
        out_specs=[
            pl.BlockSpec((1, tokens, LANES), lambda h: (h, 0, 0)),
            pl.BlockSpec((1, keys, LANES), lambda h: (h, 0, 0)),
            pl.BlockSpec((1, keys, LANES), lambda h: (h, 0, 0)),
        ] + comm.out_specs(),
        out_shape=[
            jax.ShapeDtypeStruct((HEADS, tokens, LANES), bf16),
            jax.ShapeDtypeStruct((HEADS, keys, LANES), bf16),
            jax.ShapeDtypeStruct((HEADS, keys, LANES), bf16),
        ] + comm.out_shape(),
        scratch_shapes=[pltpu.VMEM((tokens, keys), bf16), pltpu.VMEM((tokens, LANES), bf16)] + comm.scratch(),
        compiler_params=comm.params(),
        name="attn_bwd",
    )(qkv, kv, kv, probs, out, d_out, *comm.args)


def gelu_parts(z):
    c = 0.7978845608028654
    z2 = z * z
    t = jnp.tanh(z * (c + (c * 0.044715) * z2))
    half = 0.5 * (1.0 + t)
    g = z * half
    dg = half + 0.5 * z * (1.0 - t * t) * (c + (3 * c * 0.044715) * z2)
    return g, dg


def mid_work(s, n, cuts, run, ready, part, weights, load, save, wo_load, bufs):
    (aid_ref, ab_ref, ff_ref, bup_ref, vec_ref, pack_ref, obuf, xbuf, cotbuf, dybuf, wobuf, ocat, n2buf, mid, acc, dn2,
     hidden, wofull, ubuf, dbuf, ga, gb, wsem, go) = bufs
    tokens, d = xbuf.shape
    ds = d // s
    bo, bd, gain2, shift2 = vec_ref[2:3, :], vec_ref[3:4, :], vec_ref[6:7, :], vec_ref[7:8, :]
    at_o, at_u, b_o, b_d = (ab_ref.at[k] for k in range(4))
    ta, tm = min(256, tokens), min(512, tokens)
    chunks = [(c, j) for c in range(len(cuts)) for j in range(s)]

    def fetch(k):
        c, j = chunks[k]
        w = cuts[c][1]
        for m, (ref, buf) in enumerate(((weights[2 * c], ubuf), (weights[2 * c + 1], dbuf))):
            dst = buf.at[k % 2] if w == buf.shape[3] else buf.at[k % 2, :, :, pl.ds(0, w)]
            yield pltpu.make_async_copy(ref.at[pl.ds(j * n, n)], dst, wsem.at[k % 2, m])

    for copy in wo_load:
        copy.start()
    for i in range(tokens // ta):
        for copy in load(i):
            copy.start()
    if ready:
        for copy in fetch(0):
            copy.start()
    for copy in wo_load:
        copy.wait()
    run.step(4)

    wofull[...] = jnp.concatenate([wobuf[j].reshape(d, ds) for j in range(s)], axis=1)

    [serve] = run.within(1, tokens // ta, 3)

    def before(i, carry):
        rows = pl.ds(i * ta, ta)
        serve(i)
        for copy in load(i):
            copy.wait()
        mask = column_mask(aid_ref[rows, :])
        for h in range(HEADS):
            ocat[rows, h * HEAD_DIM:(h + 1) * HEAD_DIM] = obuf[h, rows, :HEAD_DIM]
        o = ocat[rows, :]
        h_o = (nt(o, at_o[...]) * mask).astype(bf16)
        value = xbuf[rows, :].astype(f32) + nn(o, wofull[...]) + 0.5 * nn(h_o, b_o[...]) + bo
        mid[rows, :] = value
        nh2, _ = norm_parts(value)
        n2 = (nh2 * gain2 + shift2).astype(bf16)
        n2buf[rows, :d] = n2
        dy = jnp.where(aid_ref[rows, :] >= 0, cotbuf[rows, :], jnp.zeros((ta, d), bf16))
        dybuf[rows, :d] = dy
        hidden[rows, :] = h_o
        n2buf[rows, d:] = (0.5 * (nt(n2, at_u[...]) * mask).astype(bf16).astype(f32)).astype(bf16)
        dybuf[rows, d:] = (0.5 * nt(dy, b_d[...]) * mask).astype(bf16)
        return carry
    lax.fori_loop(0, tokens // ta, before, 0)

    for k, (c, j) in enumerate(chunks):
        start, w = cuts[c]
        if k == 0 and not ready:
            run.until(part(0))
            for copy in fetch(0):
                copy.start()
        late = k + 1 < len(chunks) and chunks[k + 1][0] >= ready and chunks[k + 1][1] == 0
        if k + 1 < len(chunks) and not late:
            for copy in fetch(k + 1):
                copy.start()
        for copy in fetch(k):
            copy.wait()
        cols = slice(start, start + w)

        [serve] = run.within(1, tokens // tm, 8)

        def chunk(i, carry, k=k, j=j, w=w, cols=cols, slot=k % 2, serve=serve):
            rows = pl.ds(i * tm, tm)
            serve(i)
            wu = jnp.concatenate([ubuf[slot, :, :, :w].reshape(d, w), ff_ref[1, j, :, cols]])
            wd = jnp.concatenate([dbuf[slot, :, :, :w].reshape(d, w), ff_ref[0, j, :, cols]])
            z = nn(n2buf[rows, :], wu) + bup_ref[j, :, cols]
            g, dgelu = gelu_parts(z)
            g = g.astype(bf16)
            dg = nn(dybuf[rows, :], wd).astype(bf16)
            dz = (dg.astype(f32) * dgelu).astype(bf16)
            if k == 0:
                acc[rows, :] = nt(g, wd)
                dn2[rows, :] = nt(dz, wu)
            else:
                acc[rows, :] += nt(g, wd)
                dn2[rows, :] += nt(dz, wu)
            more_a, more_b = tn(dybuf[rows, d:], g), tn(n2buf[rows, d:], dz)

            @pl.when(i == 0)
            def _():
                ga[:, :w] = more_a
                gb[:, :w] = more_b

            @pl.when(i > 0)
            def _():
                ga[:, :w] += more_a
                gb[:, :w] += more_b
            return carry
        lax.fori_loop(0, tokens // tm, chunk, 0)
        at = 2 * d + j * ff_ref.shape[3] + start
        pack_ref[0, :, at:at + w] = ga[:, :w].astype(bf16)
        pack_ref[1, :, at:at + w] = gb[:, :w].astype(bf16)
        run.step(8)
        if late:
            run.until(part(chunks[k + 1][0]))
            for copy in fetch(k + 1):
                copy.start()

    run.rest()

    go[...] = jnp.zeros_like(go)

    def after(i, carry):
        rows = pl.ds(i * ta, ta)
        mask = column_mask(aid_ref[rows, :])
        h_d = (acc[rows, d:] * mask).astype(bf16)
        xbuf[rows, :] = (mid[rows, :] + bd + acc[rows, :d] + 0.5 * nn(h_d, b_d[...])).astype(bf16)
        dh_u = (0.5 * dn2[rows, d:] * mask).astype(bf16)
        nh2, r2 = norm_parts(mid[rows, :])
        dy = dybuf[rows, :d]
        dmid = dy.astype(f32) + norm_back(dn2[rows, :d] + nn(dh_u, at_u[...]), gain2, nh2, r2)
        mid[rows, :] = dmid
        db = dmid.astype(bf16)
        dh_o = (0.5 * nt(db, b_o[...]) * mask).astype(bf16)
        do = (nt(db, wofull[...]) + nn(dh_o, at_o[...])).astype(bf16)
        go[0] += tn(dh_o, ocat[rows, :])
        go[1] += 0.5 * tn(hidden[rows, :], db)
        go[2] += tn(dh_u, n2buf[rows, :d])
        go[3] += 0.5 * tn(h_d, dy)
        for h in range(HEADS):
            obuf[h, rows, :HEAD_DIM] = do[:, h * HEAD_DIM:(h + 1) * HEAD_DIM]
        for copy in save(i):
            copy.start()
        return carry
    lax.fori_loop(0, tokens // ta, after, 0)
    for c, order in enumerate(((0, 2), (1, 3))):
        for k, which in enumerate(order):
            pack_ref[c, :, k * d:(k + 1) * d] = go[which].astype(bf16)
    for i in range(tokens // ta):
        for copy in save(i):
            copy.wait()


def mid_kernel(s, n, cuts, *refs):
    (oaug_ref, x_ref, cot_ref, aid_ref, wo_ref, ab_ref, ff_ref, bup_ref, vec_ref) = refs[:9]
    weights, refs = refs[9:9 + 2 * len(cuts)], refs[9 + 2 * len(cuts):]
    mixed_ref, dmid_ref, do_ref, pack_ref, obuf, xbuf, isem, osem, lsem, *bufs = refs
    cotbuf, mid = bufs[0], bufs[5]
    ta = min(256, xbuf.shape[0])

    def load(i):
        rows = pl.ds(i * ta, ta)
        for k, (src, dst) in enumerate(((oaug_ref.at[:, rows], obuf.at[:, rows]), (x_ref.at[rows], xbuf.at[rows]),
                                        (cot_ref.at[rows], cotbuf.at[rows]))):
            yield pltpu.make_async_copy(src, dst, isem.at[i, k])

    def save(i):
        rows = pl.ds(i * ta, ta)
        for k, (src, dst) in enumerate(((xbuf.at[rows], mixed_ref.at[rows]), (mid.at[rows], dmid_ref.at[rows]),
                                        (obuf.at[:, rows], do_ref.at[:, rows]))):
            yield pltpu.make_async_copy(src, dst, osem.at[i, k])

    mid_work(s, n, cuts, Steps([]), len(cuts), None, weights, load, save,
             [pltpu.make_async_copy(wo_ref, bufs[2], lsem.at[0])],
             [aid_ref, ab_ref, ff_ref, bup_ref, vec_ref, pack_ref, obuf, xbuf] + bufs)


def mid_bufs(s, pieces, tokens, d, widest):
    def v(*shape, dtype=bf16):
        return pltpu.VMEM(shape, dtype)

    return [
        v(tokens, d), v(tokens, d + LORA), v(s, d, d // s), v(tokens, d), v(tokens, d + LORA),
        v(tokens, d, dtype=f32), v(tokens, d + LORA, dtype=f32), v(tokens, d + LORA, dtype=f32),
        v(tokens, LORA), v(d, d), v(2, pieces, d // pieces, widest), v(2, pieces, d // pieces, widest),
        v(LORA, widest, dtype=f32), v(LORA, widest, dtype=f32), pltpu.SemaphoreType.DMA((2, 2)),
        v(4, LORA, d, dtype=f32),
    ]


def mid_call(oaug, x, cot, aid, wo, weights, cuts, ab, ff, bup, vec):
    tokens, d = x.shape
    s = wo.shape[0]
    pieces = weights[0].shape[0] // s
    tiles = tokens // min(256, tokens)
    full = pl.BlockSpec(memory_space=pltpu.VMEM)
    dma = pltpu.SemaphoreType.DMA
    return pl.pallas_call(
        partial(mid_kernel, s, pieces, cuts),
        in_specs=any_specs(3) + [full] + any_specs(1) + [full] * 4 + any_specs(len(weights)),
        out_specs=any_specs(3) + [full],
        out_shape=[
            jax.ShapeDtypeStruct((tokens, d), bf16),
            jax.ShapeDtypeStruct((tokens, d), f32),
            jax.ShapeDtypeStruct((HEADS, tokens, LANES), bf16),
            jax.ShapeDtypeStruct((2, LORA, 2 * d + s * ff.shape[3]), bf16),
        ],
        scratch_shapes=[
            pltpu.VMEM((HEADS, tokens, LANES), bf16), pltpu.VMEM((tokens, d), bf16),
            dma((tiles, 3)), dma((tiles, 3)), dma((1,)),
        ] + mid_bufs(s, pieces, tokens, d, max(w for _, w in cuts)),
        compiler_params=pltpu.CompilerParams(vmem_limit_bytes=VMEM),
        name="mid",
    )(oaug, x, cot, aid, wo, ab, ff, bup, vec, *weights)


def forward_kernel(nz, cuts, na, *refs):
    shards, (tokens, vec, cot, aid_ref, pic_ref), refs = refs[:na], refs[na:na + 5], refs[na + 5:]
    wholes, refs = refs[:na], refs[na:]
    (x_out, vec_out, qkv_out, n1_out, h_out, probs_out, o_out, cot_row, mixed_ref, dmid_ref, do_ref, pack_ref), refs = (
        refs[:12], refs[12:])
    (xbuf, vbuf, obuf, ab, ff, vecs, bups, sems, wsem, osem, psem, csems, isem, ssem, *gather_refs) = refs
    n, d = nz * 4, xbuf.shape[2]
    half = xbuf.shape[1]
    count, tm = 2 * half, 512
    ds, fslot = shards[1].shape[1], ff.shape[3]
    nh = ds // HEAD_DIM
    each = LORA // 2
    spot = Spot(nz)
    spot.barrier()
    gather = Gather(spot, [(k, 0, a.shape[1]) for k, a in enumerate(shards)], shards, wholes, *gather_refs)
    run = Steps(gather.actions())
    swap = Swap(spot, cot, cot_row, csems)
    vec_here = pltpu.make_async_copy(vec, vbuf.at[spot.x], sems.at[0])
    vec_there = remote(vec, vbuf.at[spot.x], sems.at[1], sems.at[2], spot.xn)
    row_here = pltpu.make_async_copy(tokens.at[spot.x], xbuf.at[spot.x], sems.at[3])
    row_there = remote(tokens.at[1 - spot.x], xbuf.at[spot.x], sems.at[4], sems.at[5], spot.xn)

    def first(nbuf, widebuf, wbuf, abuf, bbuf, n1, hbuf, heads, pbuf):
        vec_here.start()
        vec_there.start()
        run.step(2)
        row_here.start()
        row_there.start()
        run.step(13)
        vec_here.wait()
        got = vbuf.at[1 - spot.x]
        remote(got, got, sems.at[1], sems.at[2], spot.xn).wait_recv()
        row_here.wait()
        got = xbuf.at[1 - spot.x]
        remote(got, got, sems.at[4], sems.at[5], spot.xn).wait_recv()
        for j in range(2):
            vecs[:, j * ds:(j + 1) * ds] = vbuf[j, :8, :ds].astype(f32)
            bups[j] = vbuf[j, 8:9, :].astype(f32)
        gain, shift = vecs[4:5, :], vecs[5:6, :]
        keep = [pltpu.make_async_copy(xbuf, x_out, osem.at[0]), pltpu.make_async_copy(vbuf, vec_out, osem.at[1])]
        for copy in keep:
            copy.start()
        for part in range(2):
            def norm_step(i, carry, part=part):
                nhat, _ = norm_parts(xbuf[part, pl.ds(i * 256, 256), :].astype(f32))
                n1[pl.ds(part * half + i * 256, 256), :d] = (nhat * gain + shift).astype(bf16)
                return carry
            lax.fori_loop(0, half // 256, norm_step, 0)
            run.step(4)
        keep.append(pltpu.make_async_copy(n1.at[:, pl.ds(0, d)], n1_out, osem.at[2]))
        keep[-1].start()

        run.until(0)
        small = pltpu.make_async_copy(wholes[0], nbuf, sems.at[6])
        small.start()
        small.wait()
        for j in range(2):
            rows = slice(j * each, (j + 1) * each)
            one = nbuf[j * n:(j + 1) * n].reshape(10 * each, d)
            for m in range(3):
                abuf[m, rows, :] = one[m * each:(m + 1) * each]
                for i in range(2):
                    bbuf[m, i, rows, :] = one[(5 + m) * each:(6 + m) * each, i * ds:(i + 1) * ds]
            for k, m in enumerate((3, 4, 8, 9)):
                ab[k, rows, :] = one[m * each:(m + 1) * each]

        def fetch(p, j):
            return pltpu.make_async_copy(wholes[1 + p].at[pl.ds(j * n, n)], wbuf.at[j], wsem.at[j])

        for p in range(3):
            run.until(1 + p)
            for j in range(2):
                fetch(p, j).start()
            for i in range(count // tm):
                rows = pl.ds(i * tm, tm)
                h = (nt(n1[rows, :d], abuf[p]) * column_mask(aid_ref[rows, :])).astype(bf16)
                hbuf[p, rows, :] = h
                n1[rows, d:] = (0.5 * h.astype(f32)).astype(bf16)
            for j in range(2):
                fetch(p, j).wait()
                bias = vbuf[j, p // 2:p // 2 + 1, :ds].astype(f32) if p != 1 else 0.0

                [serve] = run.within(1, count // tm, 3)

                def step(i, carry, p=p, j=j, bias=bias, serve=serve):
                    rows = pl.ds(i * tm, tm)
                    serve(i)
                    w = jnp.concatenate([wbuf[j].reshape(d, ds), bbuf[p, j]])
                    y = (nn(n1[rows, :], w) + bias).astype(bf16)
                    place = lax.broadcasted_iota(jnp.int32, (tm, LANES), 1) - HEAD_DIM
                    same = place == pic_ref[rows, :]
                    if p == 0:
                        extra = jnp.where(same, 1.0, 0.0)
                    elif p == 1:
                        extra = jnp.where((place >= 0) & (place < 16) & jnp.logical_not(same), -BIG, 0.0)
                    else:
                        extra = jnp.where((place == 0) | (place == 1), 1.0, 0.0)
                    extra = extra.astype(bf16)[:, HEAD_DIM:]
                    for h in range(nh):
                        heads[p, j * nh + h, rows, :HEAD_DIM] = y[:, h * HEAD_DIM:(h + 1) * HEAD_DIM]
                        heads[p, j * nh + h, rows, HEAD_DIM:] = extra
                    return carry
                lax.fori_loop(0, count // tm, step, 0)
                which = pl.ds(j * nh, nh)
                keep.append(pltpu.make_async_copy(
                    heads.at[p, which], qkv_out.at[p, which], osem.at[4 + 2 * p + j]))
                keep[-1].start()
                run.step(3)
        keep.append(pltpu.make_async_copy(hbuf, h_out, osem.at[3]))
        keep[-1].start()
        swap.start()

        def probs_copy(h):
            return pltpu.make_async_copy(pbuf.at[h % 2], probs_out.at[h], psem.at[h % 2])

        serve, again = run.within(0, HEADS, 2, 1)

        def head(h, carry):
            serve(h)

            @pl.when(h >= 2)
            def _():
                probs_copy(h - 2).wait()
            for i in range(count // tm):
                rows = pl.ds(i * tm, tm)
                s = nt(heads[0, h, rows, :], heads[1, h])
                top = jnp.max(s, axis=-1, keepdims=True)
                p = jnp.exp2((s - top) * (SCALE * LOG2E)).astype(bf16)
                o = nn(p, heads[2, h])
                inv = 1.0 / o[:, HEAD_DIM:HEAD_DIM + 1]
                pbuf[h % 2, rows, :] = (p.astype(f32) * inv).astype(bf16)
                obuf[h, rows, :] = (o * inv).astype(bf16)
            again(h)
            probs_copy(h).start()
            return carry
        lax.fori_loop(0, HEADS, head, 0)
        keep.append(pltpu.make_async_copy(obuf, o_out, osem.at[10]))
        keep[-1].start()
        run.until(5)
        big = pltpu.make_async_copy(wholes[5], widebuf, sems.at[7])
        big.start()
        big.wait()
        for j in range(2):
            one = widebuf[j * n:(j + 1) * n].reshape(LORA, 2 * fslot)
            for m in range(2):
                for i in range(2):
                    ff[m, i, j * each:(j + 1) * each, :] = one[m * each:(m + 1) * each, i * fslot:(i + 1) * fslot]
        for h in range(HEADS - 2, HEADS):
            probs_copy(h).wait()
        for copy in keep:
            copy.wait()

    def v(*shape):
        return pltpu.VMEM(shape, bf16)

    pl.run_scoped(
        first, v(8 * nz, *shards[0].shape), v(8 * nz, *shards[5].shape), v(2, n, *shards[1].shape), v(3, LORA, d),
        v(3, 2, LORA, ds), v(count, d + LORA), v(3, count, LORA), v(3, HEADS, count, LANES), v(2, count, count))
    swap.end()

    def second(wobuf3, *bufs):
        cotbuf, mid = bufs[0], bufs[4]
        bufs = bufs[:2] + (wobuf3,) + bufs[2:]

        def load(i):
            yield pltpu.make_async_copy(cot_row.at[i * 256 // half, pl.ds(i * 256 % half, 256)],
                                        cotbuf.at[pl.ds(i * 256, 256)], isem.at[i, 0])

        def save(i):
            rows = pl.ds(i * 256, 256)
            inner = pl.ds(i * 256 % half, 256)
            for k, (src, dst) in enumerate((
                    (xrow.at[rows], mixed_ref.at[i * 256 // half, inner]), (mid.at[rows], dmid_ref.at[rows]),
                    (obuf.at[:, rows], do_ref.at[:, rows]))):
                yield pltpu.make_async_copy(src, dst, ssem.at[i, k])

        mid_work(2, n, cuts, run, 0, lambda c: 7 + 2 * c, wholes[6:], load, save,
                 [pltpu.make_async_copy(wholes[4].at[pl.ds(j * n, n)], wobuf3.at[j], isem.at[j, 1]) for j in range(2)],
                 [aid_ref, ab, ff, bups, vecs, pack_ref, obuf, xrow] + list(bufs))

    xrow = xbuf.reshape(count, d)
    bufs = mid_bufs(2, n, count, d, max(w for _, w in cuts))
    bufs[2] = v(2, n, d // n, ds)
    pl.run_scoped(second, bufs[2], *bufs[:2], *bufs[3:])
    vec_there.wait_send()
    row_there.wait_send()


def forward_call(nz, cuts, shards, tokens, vec, cot, aid, pic):
    na = len(shards)
    dma = pltpu.SemaphoreType.DMA
    half, d = tokens.shape[1], tokens.shape[2]
    count, fslot = 2 * half, shards[5].shape[1] // 2
    tiles = count // 256
    full = pl.BlockSpec(memory_space=pltpu.VMEM)

    def v(*shape, dtype=bf16):
        return pltpu.VMEM(shape, dtype)

    def out(*shape, dtype=bf16):
        return jax.ShapeDtypeStruct(shape, dtype)

    return pl.pallas_call(
        partial(forward_kernel, nz, cuts, na),
        in_specs=any_specs(na + 3) + [full, full],
        out_specs=any_specs(na + 11) + [full],
        out_shape=gathered(nz, shards) + [
            out(*tokens.shape), out(2, *vec.shape), out(3, HEADS, count, LANES), out(count, d), out(3, count, LORA),
            out(HEADS, count, count), out(HEADS, count, LANES), out(*tokens.shape), out(*tokens.shape),
            out(count, d, dtype=f32), out(HEADS, count, LANES), out(2, LORA, 2 * d + 2 * fslot)],
        scratch_shapes=[
            v(*tokens.shape), v(2, *vec.shape), v(HEADS, count, LANES), v(4, LORA, d), v(2, 2, LORA, fslot),
            v(8, d, dtype=f32), v(2, 1, fslot, dtype=f32), dma((8,)), dma((2,)), dma((11,)), dma((2,)), dma((3,)),
            dma((tiles, 2)), dma((tiles, 3))] + Gather.scratch(nz, na),
        compiler_params=pltpu.CompilerParams(collective_id=1, has_side_effects=True, vmem_limit_bytes=VMEM),
        name="forward",
    )(*shards, tokens, vec, cot, aid, pic)


def tail_kernel(s, dq_ref, dk_ref, dv_ref, x_ref, n1_ref, h_ref, dmid_ref, aid_ref,
                wq_ref, wk_ref, wv_ref, at_ref, b_ref, vec_ref, out_ref, low_ref, pack_ref, dy_ref, ga_ref, gb_ref):
    i = pl.program_id(0)
    tm, d = x_ref.shape
    nh = HEADS // s
    ds = d // s
    mask = column_mask(aid_ref[...])

    @pl.when(i == 0)
    def _():
        ga_ref[...] = jnp.zeros_like(ga_ref)
        gb_ref[...] = jnp.zeros_like(gb_ref)

    n1 = n1_ref[...]
    dn = jnp.zeros((tm, d), f32)
    for p, (src, w_ref) in enumerate(((dq_ref, wq_ref), (dk_ref, wk_ref), (dv_ref, wv_ref))):
        dh = jnp.zeros((tm, LORA), f32)
        for j in range(s):
            for h in range(nh):
                dy_ref[p, j, :, h * HEAD_DIM:(h + 1) * HEAD_DIM] = src[j * nh + h, :, :HEAD_DIM]
            dy = dy_ref[p, j]
            dh = dh + nt(dy, b_ref[p, j])
            dn = dn + nt(dy, w_ref[j])
            gb_ref[p, j] += 0.5 * tn(h_ref[p], dy)
        dh = (0.5 * dh * mask).astype(bf16)
        dn = dn + nn(dh, at_ref[p])
        ga_ref[p] += tn(dh, n1)
    nhat, r = norm_parts(x_ref[...].astype(f32))
    out = dmid_ref[...] + norm_back(dn, vec_ref[4:5, :], nhat, r)
    out_ref[...] = out
    low_ref[...] = out.astype(bf16)

    @pl.when(i == pl.num_programs(0) - 1)
    def _():
        for p in range(3):
            pack_ref[0, :, p * d:(p + 1) * d] = ga_ref[p].astype(bf16)
            for j in range(s):
                at = p * d + j * ds
                pack_ref[1, :, at:at + ds] = gb_ref[p, j].astype(bf16)


def tail_call(dq, dk, dv, x, n1, hid, dmid, aid, wq, wk, wv, at, bq, vec):
    tokens, d = x.shape
    s = wq.shape[0]
    tm = min(256, tokens)
    full = pl.BlockSpec(memory_space=pltpu.VMEM)
    tile = pl.BlockSpec((tm, d), lambda i: (i, 0))
    heads = pl.BlockSpec((HEADS, tm, LANES), lambda i: (0, i, 0))
    return pl.pallas_call(
        partial(tail_kernel, s),
        grid=(tokens // tm,),
        in_specs=[
            heads, heads, heads, tile, tile,
            pl.BlockSpec((3, tm, LORA), lambda i: (0, i, 0)),
            tile,
            pl.BlockSpec((tm, 1), lambda i: (i, 0)),
            full, full, full, full, full, full,
        ],
        out_specs=[tile, tile, full],
        out_shape=[
            jax.ShapeDtypeStruct((tokens, d), f32),
            jax.ShapeDtypeStruct((tokens, d), bf16),
            jax.ShapeDtypeStruct((2, LORA, 3 * d), bf16),
        ],
        scratch_shapes=[
            pltpu.VMEM((3, s, tm, d // s), bf16),
            pltpu.VMEM((3, LORA, d), f32),
            pltpu.VMEM((3, s, LORA, d // s), f32),
        ],
        compiler_params=pltpu.CompilerParams(vmem_limit_bytes=VMEM),
        name="tail",
    )(dq, dk, dv, x, n1, hid, dmid, aid, wq, wk, wv, at, bq, vec)


def rows_of_adapters(a):
    t = jnp.swapaxes(a, -1, -2)
    return t.reshape(*t.shape[:-3], t.shape[-3] * t.shape[-2], t.shape[-1])


def local(tokens, cotangent, lengths, adapter_ids, w_query, w_key, w_value, w_out, w_up, w_down,
          b_query, b_value, b_out, b_up, b_down, gain_one, shift_one, gain_two, shift_two,
          qkv_a, out_a, attn_b, up_a, up_b, down_a, down_b):
    seq = lax.axis_size("seq")
    rows, part_len, d = tokens.shape
    group = seq // rows
    count = rows * part_len
    ds, fs = w_query.shape[1], w_up.shape[1]
    me = lax.axis_index("seq")
    row, chunk = me // group, me % group

    def moves(j):
        return [(a, (a % rows + j) % rows * group + a // rows) for a in range(seq)]

    def send(piece, pairs):
        return piece if all(a == b for a, b in pairs) else lax.ppermute(piece, "seq", pairs)

    def to_row(t):
        out = jnp.zeros((rows, part_len, d), t.dtype)
        for j in range(rows):
            piece = lax.dynamic_index_in_dim(t, (me + j) % rows, 0, False)
            out = lax.dynamic_update_index_in_dim(out, send(piece, moves(j)), (row - j) % rows, 0)
        return out.reshape(count, d)

    def from_row(t, dtype):
        t = t.reshape(rows, part_len, d)
        out = jnp.zeros((rows, part_len, d), dtype)
        for j in range(rows):
            piece = lax.dynamic_index_in_dim(t, (row - j) % rows, 0, False)
            pairs = [(b, a) for a, b in moves(j)]
            if not all(a == b for a, b in pairs):
                piece = piece.astype(bf16)
            got = send(piece, pairs).astype(dtype)
            out = lax.dynamic_update_index_in_dim(out, got, (me + j) % rows, 0)
        return out

    dps = lax.axis_size("dp")
    nz = dps // 4
    fast = seq == 2 and rows == 2 and nz == 4
    slot, fslot = up128(ds), up128(fs)
    step = up128(-(-fslot // max(round(fslot / 768), 1)))
    cuts = [(a, min(step, fslot - a)) for a in range(0, fslot, step)]

    def wide_to(t, n):
        return jnp.pad(t, ((0, 0), (0, n - t.shape[1])))

    wu_part, wd_part = wide_to(w_up, fslot), wide_to(w_down.T, fslot)
    ff_parts = [t[:, a:a + n] for a, n in cuts for t in (wu_part, wd_part)]
    narrow = jnp.concatenate([
        rows_of_adapters(qkv_a), rows_of_adapters(out_a)[None], rows_of_adapters(up_a)[None],
        attn_b.reshape(4, -1, d), down_b.reshape(1, -1, d)])
    wide = jnp.stack([rows_of_adapters(down_a), up_b.reshape(-1, up_b.shape[-1])])
    vec_part = jnp.stack([b_query, b_value, b_out, b_down, gain_one, shift_one, gain_two, shift_two])
    teams = [[g * group + c for c in range(group)] for g in range(rows)]

    my_len = lax.dynamic_index_in_dim(lengths, row, 0, False)
    my_ids = lax.dynamic_index_in_dim(adapter_ids, row, 0, False)
    slots = jnp.arange(my_len.shape[0], dtype=jnp.int32)
    ends = jnp.sum(jnp.where(slots[None, :] <= slots[:, None], my_len[None, :], 0), axis=1)
    pos = chunk * count + jnp.arange(count, dtype=jnp.int32)
    pic = jnp.sum((pos[:, None] >= ends[None, :]).astype(jnp.int32), axis=1, keepdims=True)
    aid = jnp.sum(jnp.where(pic == slots[None, :], my_ids[None, :], 0), axis=1, keepdims=True)
    aid = jnp.where(pos[:, None] < ends[-1], aid, -1)

    def from_halves(t):
        return jnp.swapaxes(t, 0, 1).reshape(t.shape[1], -1, t.shape[3])

    if fast:
        me_dp = lax.axis_index("dp")

        def share(t):
            flat = t.reshape(-1, t.shape[-1])
            n = flat.shape[0] // dps
            return lax.dynamic_slice_in_dim(flat, me_dp * n, n, 0)

        def whole(t):
            return t.reshape(seq, d, t.shape[2])

        small = jnp.concatenate([wide_to(vec_part, fslot), wide_to(b_up[None], fslot), jnp.zeros((7, fslot), bf16)])
        wide = jnp.pad(wide.reshape(2, -1, seq, fs), ((0, 0), (0, 0), (0, 0), (0, fslot - fs)))
        wide = wide.reshape(2, -1, seq * fslot)
        narrow, wq, wk, wv, *got = forward_call(
            nz, cuts, [share(narrow), w_query, w_key, w_value, w_out, share(wide)] + ff_parts,
            tokens, small, cotangent, aid, pic)
        x, small, qkv, n1, hid, probs, oaug, _, mixed, dmid, d_out, g_mid = got[2 + len(ff_parts):]
        x = x.reshape(count, d)
        narrow = from_halves(narrow.reshape(seq, 10, LORA // seq, d))
        vec = jnp.concatenate([small[k, :8, :ds] for k in range(seq)], axis=1).astype(f32)
        wq, wk, wv = whole(wq), whole(wk), whole(wv)
    else:
        def gather_all(shard):
            full = lax.all_gather(shard, ("seq", "dp"), axis=0, tiled=True)
            return full.reshape(seq, d, shard.shape[1])

        wq, wk, wv, wo, *weights = (gather_all(t) for t in [w_query, w_key, w_value, w_out] + ff_parts)
        narrow = lax.all_gather(narrow, "seq", axis=1, tiled=True)
        wide = lax.all_gather(wide, "seq", axis=1, tiled=True)
        vec = lax.all_gather(vec_part, "seq", axis=1, tiled=True).astype(f32)
        bup = lax.all_gather(b_up[None], "seq", axis=0, tiled=True).astype(f32)[:, None]
        x = to_row(tokens)
        cot = to_row(cotangent)

    at, b = narrow[:5], narrow[5:]
    bq = jnp.swapaxes(b[:3].reshape(3, LORA, seq, ds), 1, 2)
    if group == 1:
        off = 1
    if not fast:
        bias = jnp.stack([vec[0], jnp.zeros_like(vec[0]), vec[1]]).reshape(3, seq, 1, ds)
        qkv, n1, hid = qkv_call(x, jnp.stack([wq, wk, wv]), at, bq, bias, vec, aid, pic)
    kv = qkv
    if group > 1:
        kv = lax.all_gather(qkv[1:], "seq", axis=2, tiled=True, axis_index_groups=teams)
        off = 0
    if not fast:
        probs, oaug = attn_fwd_call(qkv, kv, off, Quiet())
        more = ((0, 0), (0, 0), (0, 0), (0, fslot - fs))
        ff = jnp.pad(jnp.swapaxes(wide.reshape(2, LORA, seq, fs), 1, 2), more)
        mixed, dmid, d_out, g_mid = mid_call(
            oaug, x, cot, aid, wo, weights, cuts, jnp.concatenate([at[3:], b[3:]]), ff, jnp.pad(bup, more[1:]), vec)

    def blocks(t):
        return t.reshape(2, 2, 2 * nz, 8, t.shape[2])

    third_comm = Settle(nz, blocks(g_mid), mixed, 4) if fast else Quiet()
    dq, dk, dv, *got = attn_bwd_call(qkv, kv, off, probs, oaug, d_out, third_comm)
    if fast:
        g_mid, mixed = got[0].reshape(2, LORA // seq, -1), got[1]
    if group > 1:
        dk, dv = (lax.psum_scatter(t, "seq", scatter_dimension=1, axis_index_groups=teams, tiled=True)
                  for t in (dk, dv))
    d_in, d_low, g_qkv = tail_call(dq, dk, dv, x, n1, hid, dmid, aid, wq, wk, wv, at, bq, vec)
    if fast:
        g_qkv, other = finish_call(nz, blocks(g_qkv), d_low.reshape(rows, part_len, d))
        g_qkv = g_qkv.reshape(2, LORA // seq, -1)
        mine = lax.dynamic_index_in_dim(d_in.reshape(rows, part_len, d), me, 0, False)
        other = other.astype(f32)
        d_in = jnp.where(me == 0, jnp.stack([mine, other]), jnp.stack([other, mine]))
    else:
        def total(t):
            return lax.psum(lax.psum_scatter(t, "seq", scatter_dimension=1, tiled=True), "dp")

        g_mid, g_qkv = total(g_mid), total(g_qkv)
        mixed = from_row(mixed, bf16)
        d_in = from_row(d_in, f32)

    def down_form(t):
        return jnp.swapaxes(t.astype(f32).reshape(-1, RANK, t.shape[-1]), -1, -2)

    def up_form(t):
        return t.astype(f32).reshape(-1, RANK, t.shape[-1])

    def cut(t, k):
        return t[:, k * d:(k + 1) * d]

    def ff_of(t):
        return jnp.concatenate([t[:, 2 * d + j * fslot:2 * d + j * fslot + fs] for j in range(seq)], axis=1)

    a_mid, b_mid = g_mid
    a_qkv, b_qkv = g_qkv
    return (
        mixed,
        d_in,
        jnp.stack([down_form(cut(a_qkv, p)) for p in range(3)]),
        down_form(cut(a_mid, 0)),
        jnp.stack([up_form(cut(b_qkv, p)) for p in range(3)] + [up_form(cut(b_mid, 0))]),
        down_form(cut(a_mid, 1)),
        up_form(ff_of(b_mid)),
        down_form(ff_of(a_mid)),
        up_form(cut(b_mid, 1)),
    )


def solution(mesh):
    both = P("dp", "seq", None)
    lead = P("seq", None, None)
    second = P(None, "seq", None, None)
    return jax.shard_map(
        local,
        mesh=mesh,
        in_specs=(both, both, P("dp", None), P("dp", None))
        + (P("dp", "seq"),) * 5 + (P("seq", "dp"),) + (P("seq"),) * 9
        + (second, lead, second, lead, lead, lead, lead),
        out_specs=(both, both, second, lead, second, lead, lead, lead, lead),
        check_vma=False,
    )
```

```python
from functools import partial

import jax
import jax.numpy as jnp
from jax import lax
from jax.experimental import pallas as pl
from jax.experimental.pallas import tpu as pltpu
from jax.sharding import PartitionSpec as P

HEADS = 16
HEAD_DIM = 72
RANK = 16
ADAPTERS = 8
LORA = RANK * ADAPTERS
LANES = 128
EPS = 1e-06
SCALE = HEAD_DIM ** (-0.5)
BIG = 1e30
LOG2E = 1.4426950408889634
VMEM = 61 * 1024 * 1024

MESH = pl.DeviceIdType.MESH
bf16 = jnp.bfloat16
f32 = jnp.float32


def nn(a, b):
    return jnp.dot(a, b, preferred_element_type=f32)


def nt(a, b):
    return lax.dot_general(a, b, (((1,), (1,)), ((), ())), preferred_element_type=f32)


def tn(a, b):
    return lax.dot_general(a, b, (((0,), (0,)), ((), ())), preferred_element_type=f32)


def up128(n):
    return -(-n // LANES) * LANES


def lane_ids(rows):
    return lax.broadcasted_iota(jnp.int32, (rows, LANES), 1)


def norm_parts(x):
    center = jnp.mean(x, axis=-1, keepdims=True)
    xc = x - center
    r = lax.rsqrt(jnp.mean(xc * xc, axis=-1, keepdims=True) + EPS)
    return xc * r, r


def norm_back(dn, gain, nh, r):
    gh = dn * gain
    a = jnp.mean(gh, axis=-1, keepdims=True)
    b = jnp.mean(gh * nh, axis=-1, keepdims=True)
    return r * (gh - a - nh * b)


def column_mask(aid):
    return (lane_ids(aid.shape[0]) // RANK == aid).astype(f32)


class Spot:
    def __init__(self, nz):
        dp = lax.axis_index("dp")
        self.nz = nz
        self.x = lax.axis_index("seq")
        self.z, self.y, self.c = dp // 4, (dp // 2) % 2, dp % 2
        self.xn = self.device(1 - self.x, self.y, self.z, self.c)
        self.yn = self.device(self.x, 1 - self.y, self.z, self.c)
        self.sib = self.device(self.x, self.y, self.z, 1 - self.c)
        self.zs = [None] + [self.device(self.x, self.y, self.zk(k), self.c) for k in range(1, nz)]
        flip = self.z // 2
        self.inner = self.z + flip * (3 - 2 * self.z)
        self.zr = [m + flip * (3 - 2 * m) for m in (self.inner, 1 - self.inner, 2, 3)]
        self.zp = [self.device(self.x, self.y, z, self.c) for z in self.zr]

    def device(self, x, y, z, c):
        return ((z * 2 + y) * 2 + c, x)

    def shard(self, x, y, z):
        return (x * self.nz + z) * 4 + y * 2 + self.c

    def zk(self, k):
        return (self.z + k) % self.nz

    def barrier(self):
        peers = [self.xn, self.yn, self.sib] + self.zs[1:]
        sem = pltpu.get_barrier_semaphore()
        for peer in peers:
            pl.semaphore_signal(sem, inc=1, device_id=peer, device_id_type=MESH)
        pl.semaphore_wait(sem, len(peers))


def remote(src, dst, send, recv, device):
    return pltpu.make_async_remote_copy(
        src_ref=src, dst_ref=dst, send_sem=send, recv_sem=recv, device_id=device, device_id_type=MESH
    )


class Gather:
    kinds = [(kind, r) for r in range(4) for kind in "zxyd"]

    def __init__(self, spot, parts, ins, outs, send, recv, core, own):
        self.s, self.parts, self.ins, self.outs = spot, parts, ins, outs
        self.send, self.recv, self.core, self.own = send, recv, core, own
        every = [to for kind, r in self.kinds for to in self.targets(kind, r)]
        self.counts = sum(to[0] != "i" for to in every), sum(to[0] == "i" for to in every)

    @staticmethod
    def scratch(nz, count):
        dma = pltpu.SemaphoreType.DMA
        return [dma((count, 2)), dma((count, 4 * nz)), dma((count,)), dma((count,))]

    def targets(self, kind, r):
        if kind == "z":
            return (["z1", "z2", "z3"] if r == 0 else []) + ["x", "y", "s"]
        if kind == "x":
            return (["y"] if r in (0, 3) else []) + ["s"]
        if kind == "d":
            return {0: ["z1", "iz2"], 2: ["iz1"]}.get(r, []) + ["s"]
        return ["s"]

    def index(self, kind, r):
        s = self.s
        x = 1 - s.x if kind in "xd" else s.x
        y = 1 - s.y if kind in "yd" else s.y
        return s.shard(x, y, s.zr[r])

    def place(self, g, index):
        a, start, size = self.parts[g]
        if size == self.outs[a].shape[2]:
            return self.outs[a].at[index]
        return self.outs[a].at[index, :, pl.ds(start, size)]

    def source(self, g, kind, r):
        if (kind, r) != ("z", 0):
            return self.place(g, self.index(kind, r))
        a, start, size = self.parts[g]
        if size == self.ins[a].shape[1]:
            return self.ins[a]
        return self.ins[a].at[:, pl.ds(start, size)]

    def arrival(self, g, kind, r):
        return self.recv.at[g, "zxyd".index(kind) * 4 + r]

    def copy(self, g, kind, r, to):
        s = self.s
        if to == "s":
            recv, device = self.core.at[g], s.sib
        elif to == "x":
            recv, device = self.arrival(g, "x", r), s.xn
        elif to == "y":
            recv, device = self.arrival(g, "y" if kind == "z" else "d", r), s.yn
        else:
            i = int(to[-1])
            if kind == "z":
                there = i if i < 2 else 3 - s.inner
            else:
                there = 1 if to == "z1" else 2
            recv, device = self.arrival(g, kind, there), s.zp[i]
        send = self.send.at[g, int(to[0] == "i")]
        return remote(self.source(g, kind, r), self.place(g, self.index(kind, r)), send, recv, device)

    def local(self, g):
        return pltpu.make_async_copy(self.source(g, "z", 0), self.place(g, self.index("z", 0)), self.own.at[g])

    def arrive(self, g, kind, r):
        if (kind, r) == ("z", 0):
            self.local(g).start()
        else:
            ref = self.place(g, self.index(kind, r))
            remote(ref, ref, self.send.at[g, 0], self.arrival(g, kind, r), self.s.xn).wait_recv()
        for to in self.targets(kind, r):
            if to[0] == "i":
                pl.when(self.s.inner == 1)(self.copy(g, kind, r, to).start)
            else:
                self.copy(g, kind, r, to).start()

    def several(self, g, n, which=0):
        a, start, size = self.parts[g]
        ref = self.outs[a].at[pl.ds(0, n)]
        if size < self.outs[a].shape[2]:
            ref = self.outs[a].at[pl.ds(0, n), :, pl.ds(start, size)]
        return remote(ref, ref, self.send.at[g, which], self.core.at[g], self.s.sib)

    def end(self, g):
        self.several(g, self.outs[self.parts[g][0]].shape[0] // 2).wait_recv()
        self.local(g).wait()
        self.several(g, self.counts[0]).wait_send()

        @pl.when(self.s.inner == 1)
        def _():
            self.several(g, self.counts[1], 1).wait_send()

    def actions(self):
        n = len(self.parts)
        out = []
        for t in range(n + 4):
            if t < n:
                out.append((self.arrive, t, "z", 0))
            if 0 <= t - 1 < n:
                out += [(self.arrive, t - 1, "z", r) for r in (1, 2, 3)]
            if 0 <= t - 2 < n:
                out += [(self.arrive, t - 2, kind, r) for r in (0, 3, 1, 2) for kind in "xy"]
            if 0 <= t - 3 < n:
                out += [(self.arrive, t - 3, "d", r) for r in (0, 3, 2, 1)]
            if 0 <= t - 4 < n:
                out.append((self.end, t - 4))
        return out


class Swap:
    def __init__(self, spot, mine, got, sems, slot=None):
        self.s, self.mine, self.got, self.sems = spot, mine, got, sems
        self.slot = spot.x if slot is None else slot

    def copies(self):
        s = self.s
        here = pltpu.make_async_copy(self.mine.at[s.x], self.got.at[s.x], self.sems.at[0])
        there = remote(self.mine.at[1 - s.x], self.got.at[self.slot], self.sems.at[1], self.sems.at[2], s.xn)
        return here, there

    def start(self):
        for copy in self.copies():
            copy.start()

    def end(self):
        here, there = self.copies()
        here.wait()
        ref = self.got.at[1 - self.s.x]
        remote(ref, ref, self.sems.at[1], self.sems.at[2], self.s.xn).wait_recv()
        there.wait_send()


class Reduce:
    def __init__(self, spot, data, result, refs):
        self.s, self.data, self.result = spot, data, result
        self.r1, self.s1, self.r2, self.s2, self.r3, self.s3, self.r4, self.total = refs[:8]
        self.send, self.recv, self.out = refs[8:]

    @staticmethod
    def scratch(nz, width):
        def v(*dims):
            return pltpu.VMEM((*dims, 8, width), bf16)
        dma = pltpu.SemaphoreType.DMA
        n = 5 + 2 * (nz - 1)
        return [v(2, 2 * nz), v(2, 2 * nz), v(2, nz), v(2, nz), v(nz, 2), v(2), v(1), v(2, 2 * nz),
                dma((n,)), dma((n,)), dma((1,))]

    def pair(self, i, src, dst, device):
        return remote(src, dst, self.send.at[i], self.recv.at[i], device)

    def to_core(self):
        return self.pair(0, self.data.at[1 - self.s.c], self.r1, self.s.sib)

    def to_y(self):
        nz = self.s.nz
        return self.pair(1, self.s1.at[:, pl.ds((1 - self.s.y) * nz, nz)], self.r2, self.s.yn)

    def to_x(self):
        return self.pair(2, self.s3.at[1 - self.s.x], self.r4.at[0], self.s.xn)

    def to_z(self, k):
        s = self.s
        return self.pair(4 + k, self.s2.at[:, s.zk(k)], self.r3.at[s.z], s.zs[k])

    def from_z(self, k):
        s = self.s
        ref = self.r3.at[s.zk(k)]
        return remote(ref, ref, self.send.at[4 + s.nz - k], self.recv.at[4 + s.nz - k], s.zs[k])

    def back_z(self, k):
        s = self.s
        ref = self.total.at[s.c, s.y * s.nz + s.z]
        return self.pair(4 + s.nz - 1 + k, ref, ref, s.zs[k])

    def from_back_z(self, k):
        s = self.s
        i = 4 + s.nz - 1 + s.nz - k
        ref = self.total.at[s.c, s.y * s.nz + s.zk(k)]
        return remote(ref, ref, self.send.at[i], self.recv.at[i], s.zs[k])

    def back_y(self, y):
        s = self.s
        ref = self.total.at[s.c, pl.ds(y * s.nz, s.nz)]
        return self.pair(3, ref, ref, s.yn)

    def back_core(self, c):
        ref = self.total.at[c]
        return self.pair(4, ref, ref, self.s.sib)

    def one(self):
        self.to_core().start()

    def two(self):
        s, nz = self.s, self.s.nz
        self.to_core().wait_recv()

        def add(i, c):
            x, b = i // (2 * nz), i % (2 * nz)
            self.s1[x, b] = (self.data[s.c, x, b].astype(f32) + self.r1[x, b].astype(f32)).astype(bf16)
            return c
        lax.fori_loop(0, 4 * nz, add, 0)
        self.to_y().start()

    def three(self):
        s, nz = self.s, self.s.nz
        self.to_y().wait_recv()

        def add(i, c):
            x, b = i // nz, i % nz
            self.s2[x, b] = (self.s1[x, s.y * nz + b].astype(f32) + self.r2[x, b].astype(f32)).astype(bf16)
            return c
        lax.fori_loop(0, 2 * nz, add, 0)
        for k in range(1, nz):
            self.to_z(k).start()

    def four(self):
        s, nz = self.s, self.s.nz
        for k in range(1, nz):
            self.from_z(k).wait_recv()
        for x in range(2):
            v = self.s2[x, s.z].astype(f32)
            for k in range(1, nz):
                v = v + self.r3[s.zk(k), x].astype(f32)
            self.s3[x] = v.astype(bf16)
        self.to_x().start()

    def five(self):
        s, nz = self.s, self.s.nz
        self.to_x().wait_recv()
        v = self.s3[s.x].astype(f32) + self.r4[0].astype(f32)
        self.total[s.c, s.y * s.nz + s.z] = v.astype(bf16)
        for k in range(1, nz):
            self.back_z(k).start()

    def six(self):
        for k in range(1, self.s.nz):
            self.from_back_z(k).wait_recv()
        self.back_y(self.s.y).start()

    def seven(self):
        self.back_y(1 - self.s.y).wait_recv()
        self.back_core(self.s.c).start()

    def end(self):
        s = self.s
        self.back_core(1 - s.c).wait_recv()
        out = pltpu.make_async_copy(self.total, self.result, self.out.at[0])
        out.start()
        out.wait()
        self.to_core().wait_send()
        self.to_x().wait_send()
        self.to_y().wait_send()
        for k in range(1, s.nz):
            self.to_z(k).wait_send()
            self.back_z(k).wait_send()
        self.back_y(s.y).wait_send()
        self.back_core(s.c).wait_send()

    def actions(self):
        return [(f,) for f in (self.one, self.two, self.three, self.four, self.five, self.six, self.seven, self.end)]


def any_specs(n):
    return [pl.BlockSpec(memory_space=pl.ANY)] * n


def gathered(nz, arrays):
    return [jax.ShapeDtypeStruct((8 * nz,) + a.shape, a.dtype) for a in arrays]


class Steps:
    def __init__(self, actions):
        self.actions = list(actions)

    def take(self, count):
        out, self.actions = self.actions[:count], self.actions[count:]
        return out

    @staticmethod
    def do(actions):
        for action in actions:
            action[0](*action[1:])

    def step(self, count):
        self.do(self.take(count))

    def rest(self):
        self.step(len(self.actions))

    def until(self, part):
        ends = [k for k, action in enumerate(self.actions) if action[0].__name__ == "end" and action[1] == part]
        if ends:
            self.step(ends[0] + 1)

    def within(self, first, last, *counts):
        plan = [(t, [self.take(count) for count in counts]) for t in range(first, last)]

        def point(k):
            def run(i):
                for t, lists in plan:
                    if lists[k]:
                        pl.when(i == t)(partial(self.do, lists[k]))
            return run
        return [point(k) for k in range(len(counts))]


def qkv_kernel(nh, tm, x_ref, w_ref, at_ref, b_ref, bias_ref, vec_ref, aid_ref, pic_ref, out_ref, n1_ref, h_ref):
    p = pl.program_id(0)
    j = pl.program_id(1)
    tokens = x_ref.shape[0]

    @pl.when((p == 0) & (j == 0))
    def _():
        def norm_step(i, c):
            rows = pl.ds(i * tm, tm)
            nhat, _ = norm_parts(x_ref[rows, :].astype(f32))
            n1_ref[rows, :] = (nhat * vec_ref[4:5, :] + vec_ref[5:6, :]).astype(bf16)
            return c
        lax.fori_loop(0, tokens // tm, norm_step, 0)

    @pl.when(j == 0)
    def _():
        def hidden_step(i, c):
            rows = pl.ds(i * tm, tm)
            h = nt(n1_ref[rows, :], at_ref[0]) * column_mask(aid_ref[rows, :])
            h_ref[0, rows, :] = h.astype(bf16)
            return c
        lax.fori_loop(0, tokens // tm, hidden_step, 0)

    def step(i, c):
        rows = pl.ds(i * tm, tm)
        y = nn(n1_ref[rows, :], w_ref[0, 0])
        y = y + 0.5 * nn(h_ref[0, rows, :], b_ref[0, 0]) + bias_ref[0, 0]
        slot = lane_ids(tm) - HEAD_DIM
        pic = pic_ref[rows, :]
        same = slot == pic
        in_slots = (slot >= 0) & (slot < 16)
        q_aug = jnp.where(same, 1.0, 0.0)
        k_aug = jnp.where(in_slots & jnp.logical_not(same), -BIG, 0.0)
        v_aug = jnp.where((slot == 0) | (slot == 1), 1.0, 0.0)
        aug = jnp.where(p == 0, q_aug, jnp.where(p == 1, k_aug, v_aug))[:, HEAD_DIM:]
        for h in range(nh):
            head = y[:, h * HEAD_DIM:(h + 1) * HEAD_DIM]
            out_ref[0, h, rows, :HEAD_DIM] = head.astype(bf16)
            out_ref[0, h, rows, HEAD_DIM:] = aug.astype(bf16)
        return c
    lax.fori_loop(0, tokens // tm, step, 0)


def qkv_call(x, w, at, bq, bias, vec, aid, pic):
    tokens, d = x.shape
    s = w.shape[1]
    nh = HEADS // s
    tm = min(256, tokens)
    return pl.pallas_call(
        partial(qkv_kernel, nh, tm),
        grid=(3, s),
        in_specs=[
            pl.BlockSpec((tokens, d), lambda p, j: (0, 0)),
            pl.BlockSpec((1, 1, d, d // s), lambda p, j: (p, j, 0, 0)),
            pl.BlockSpec((1, LORA, d), lambda p, j: (p, 0, 0)),
            pl.BlockSpec((1, 1, LORA, nh * HEAD_DIM), lambda p, j: (p, j, 0, 0)),
            pl.BlockSpec((1, 1, 1, nh * HEAD_DIM), lambda p, j: (p, j, 0, 0)),
            pl.BlockSpec(vec.shape, lambda p, j: (0, 0)),
            pl.BlockSpec((tokens, 1), lambda p, j: (0, 0)),
            pl.BlockSpec((tokens, 1), lambda p, j: (0, 0)),
        ],
        out_specs=[
            pl.BlockSpec((1, nh, tokens, LANES), lambda p, j: (p, j, 0, 0)),
            pl.BlockSpec((tokens, d), lambda p, j: (0, 0)),
            pl.BlockSpec((1, tokens, LORA), lambda p, j: (p, 0, 0)),
        ],
        out_shape=[
            jax.ShapeDtypeStruct((3, HEADS, tokens, LANES), bf16),
            jax.ShapeDtypeStruct((tokens, d), bf16),
            jax.ShapeDtypeStruct((3, tokens, LORA), bf16),
        ],
        compiler_params=pltpu.CompilerParams(vmem_limit_bytes=VMEM),
        name="qkv",
    )(x, w, at, bq, bias, vec, aid, pic)


def attn_fwd_kernel(tq, q_ref, k_ref, v_ref, p_ref, o_ref):
    for i in range(q_ref.shape[2] // tq):
        rows = pl.ds(i * tq, tq)
        s = nt(q_ref[0, 0, rows, :], k_ref[0, 0])
        top = jnp.max(s, axis=-1, keepdims=True)
        p = jnp.exp2((s - top) * (SCALE * LOG2E)).astype(bf16)
        o = nn(p, v_ref[0, 0])
        inv = 1.0 / o[:, HEAD_DIM:HEAD_DIM + 1]
        p_ref[0, rows, :] = (p.astype(f32) * inv).astype(bf16)
        o_ref[0, rows, :] = (o * inv).astype(bf16)


def attn_fwd_call(qkv, kv, off):
    tokens, keys = qkv.shape[2], kv.shape[2]
    tq = min(512, tokens)
    return pl.pallas_call(
        partial(attn_fwd_kernel, tq),
        grid=(HEADS,),
        in_specs=[
            pl.BlockSpec((1, 1, tokens, LANES), lambda h: (0, h, 0, 0)),
            pl.BlockSpec((1, 1, keys, LANES), lambda h: (off, h, 0, 0)),
            pl.BlockSpec((1, 1, keys, LANES), lambda h: (off + 1, h, 0, 0)),
        ],
        out_specs=[
            pl.BlockSpec((1, tokens, keys), lambda h: (h, 0, 0)),
            pl.BlockSpec((1, tokens, LANES), lambda h: (h, 0, 0)),
        ],
        out_shape=[
            jax.ShapeDtypeStruct((HEADS, tokens, keys), bf16),
            jax.ShapeDtypeStruct((HEADS, tokens, LANES), bf16),
        ],
        compiler_params=pltpu.CompilerParams(vmem_limit_bytes=VMEM),
        name="attn_fwd",
    )(qkv, kv, kv)


def attn_bwd_kernel(tq, q_ref, k_ref, v_ref, p_ref, o_ref, do_ref, dq_ref, dk_ref, dv_ref, ds_ref, da_ref):
    for i in range(q_ref.shape[2] // tq):
        rows = pl.ds(i * tq, tq)
        lane = lane_ids(tq)
        do = jnp.where(lane < HEAD_DIM, do_ref[0, rows, :].astype(f32), 0.0)
        delta = jnp.sum(do * o_ref[0, rows, :].astype(f32), axis=-1, keepdims=True)
        hi = delta.astype(bf16).astype(f32)
        do = jnp.where(lane == HEAD_DIM, -hi, jnp.where(lane == HEAD_DIM + 1, hi - delta, do)).astype(bf16)
        da_ref[rows, :] = do
        dp = nt(do, v_ref[0, 0])
        ds = (p_ref[0, rows, :].astype(f32) * dp).astype(bf16)
        ds_ref[rows, :] = ds
        dq_ref[0, rows, :] = (nn(ds, k_ref[0, 0]) * SCALE).astype(bf16)
    dv_ref[0] = nn(da_ref[...].T, p_ref[0]).T.astype(bf16)
    dk_ref[0] = (nn(q_ref[0, 0].T, ds_ref[...]).T * SCALE).astype(bf16)


def attn_bwd_call(qkv, kv, off, probs, out, d_out):
    tokens, keys = qkv.shape[2], kv.shape[2]
    tq = min(256, tokens)
    return pl.pallas_call(
        partial(attn_bwd_kernel, tq),
        grid=(HEADS,),
        in_specs=[
            pl.BlockSpec((1, 1, tokens, LANES), lambda h: (0, h, 0, 0)),
            pl.BlockSpec((1, 1, keys, LANES), lambda h: (off, h, 0, 0)),
            pl.BlockSpec((1, 1, keys, LANES), lambda h: (off + 1, h, 0, 0)),
            pl.BlockSpec((1, tokens, keys), lambda h: (h, 0, 0)),
            pl.BlockSpec((1, tokens, LANES), lambda h: (h, 0, 0)),
            pl.BlockSpec((1, tokens, LANES), lambda h: (h, 0, 0)),
        ],
        out_specs=[
            pl.BlockSpec((1, tokens, LANES), lambda h: (h, 0, 0)),
            pl.BlockSpec((1, keys, LANES), lambda h: (h, 0, 0)),
            pl.BlockSpec((1, keys, LANES), lambda h: (h, 0, 0)),
        ],
        out_shape=[
            jax.ShapeDtypeStruct((HEADS, tokens, LANES), bf16),
            jax.ShapeDtypeStruct((HEADS, keys, LANES), bf16),
            jax.ShapeDtypeStruct((HEADS, keys, LANES), bf16),
        ],
        scratch_shapes=[pltpu.VMEM((tokens, keys), bf16), pltpu.VMEM((tokens, LANES), bf16)],
        compiler_params=pltpu.CompilerParams(vmem_limit_bytes=VMEM),
        name="attn_bwd",
    )(qkv, kv, kv, probs, out, d_out)


def gelu_parts(z):
    c = 0.7978845608028654
    z2 = z * z
    t = jnp.tanh(z * (c + (c * 0.044715) * z2))
    half = 0.5 * (1.0 + t)
    g = z * half
    dg = half + 0.5 * z * (1.0 - t * t) * (c + (3 * c * 0.044715) * z2)
    return g, dg


def mid_work(s, n, cuts, run, ready, part, weights, load, save, wo_load, bufs):
    (aid_ref, ab_ref, ff_ref, bup_ref, vec_ref, pack_ref, obuf, xbuf, cotbuf, dybuf, wobuf, ocat, n2buf, mid, acc, dn2,
     hidden, wofull, ubuf, dbuf, ga, gb, wsem, go) = bufs
    tokens, d = xbuf.shape
    ds = d // s
    bo, bd, gain2, shift2 = vec_ref[2:3, :], vec_ref[3:4, :], vec_ref[6:7, :], vec_ref[7:8, :]
    at_o, at_u, b_o, b_d = (ab_ref.at[k] for k in range(4))
    ta, tm = min(256, tokens), min(512, tokens)
    chunks = [(c, j) for c in range(len(cuts)) for j in range(s)]

    def fetch(k):
        c, j = chunks[k]
        w = cuts[c][1]
        for m, (ref, buf) in enumerate(((weights[2 * c], ubuf), (weights[2 * c + 1], dbuf))):
            dst = buf.at[k % 2] if w == buf.shape[3] else buf.at[k % 2, :, :, pl.ds(0, w)]
            yield pltpu.make_async_copy(ref.at[pl.ds(j * n, n)], dst, wsem.at[k % 2, m])

    for copy in wo_load:
        copy.start()
    for i in range(tokens // ta):
        for copy in load(i):
            copy.start()
    if ready:
        for copy in fetch(0):
            copy.start()
    for copy in wo_load:
        copy.wait()
    run.step(4)

    wofull[...] = jnp.concatenate([wobuf[j].reshape(d, ds) for j in range(s)], axis=1)

    [serve] = run.within(1, tokens // ta, 3)

    def before(i, carry):
        rows = pl.ds(i * ta, ta)
        serve(i)
        for copy in load(i):
            copy.wait()
        mask = column_mask(aid_ref[rows, :])
        for h in range(HEADS):
            ocat[rows, h * HEAD_DIM:(h + 1) * HEAD_DIM] = obuf[h, rows, :HEAD_DIM]
        o = ocat[rows, :]
        h_o = (nt(o, at_o[...]) * mask).astype(bf16)
        value = xbuf[rows, :].astype(f32) + nn(o, wofull[...]) + 0.5 * nn(h_o, b_o[...]) + bo
        mid[rows, :] = value
        nh2, _ = norm_parts(value)
        n2 = (nh2 * gain2 + shift2).astype(bf16)
        n2buf[rows, :d] = n2
        dy = jnp.where(aid_ref[rows, :] >= 0, cotbuf[rows, :], jnp.zeros((ta, d), bf16))
        dybuf[rows, :d] = dy
        hidden[rows, :] = h_o
        n2buf[rows, d:] = (0.5 * (nt(n2, at_u[...]) * mask).astype(bf16).astype(f32)).astype(bf16)
        dybuf[rows, d:] = (0.5 * nt(dy, b_d[...]) * mask).astype(bf16)
        return carry
    lax.fori_loop(0, tokens // ta, before, 0)

    for k, (c, j) in enumerate(chunks):
        start, w = cuts[c]
        if k == 0 and not ready:
            run.until(part(0))
            for copy in fetch(0):
                copy.start()
        late = k + 1 < len(chunks) and chunks[k + 1][0] >= ready and chunks[k + 1][1] == 0
        if k + 1 < len(chunks) and not late:
            for copy in fetch(k + 1):
                copy.start()
        for copy in fetch(k):
            copy.wait()
        cols = slice(start, start + w)

        [serve] = run.within(1, tokens // tm, 8)

        def chunk(i, carry, k=k, j=j, w=w, cols=cols, slot=k % 2, serve=serve):
            rows = pl.ds(i * tm, tm)
            serve(i)
            wu = jnp.concatenate([ubuf[slot, :, :, :w].reshape(d, w), ff_ref[1, j, :, cols]])
            wd = jnp.concatenate([dbuf[slot, :, :, :w].reshape(d, w), ff_ref[0, j, :, cols]])
            z = nn(n2buf[rows, :], wu) + bup_ref[j, :, cols]
            g, dgelu = gelu_parts(z)
            g = g.astype(bf16)
            dg = nn(dybuf[rows, :], wd).astype(bf16)
            dz = (dg.astype(f32) * dgelu).astype(bf16)
            if k == 0:
                acc[rows, :] = nt(g, wd)
                dn2[rows, :] = nt(dz, wu)
            else:
                acc[rows, :] += nt(g, wd)
                dn2[rows, :] += nt(dz, wu)
            more_a, more_b = tn(dybuf[rows, d:], g), tn(n2buf[rows, d:], dz)

            @pl.when(i == 0)
            def _():
                ga[:, :w] = more_a
                gb[:, :w] = more_b

            @pl.when(i > 0)
            def _():
                ga[:, :w] += more_a
                gb[:, :w] += more_b
            return carry
        lax.fori_loop(0, tokens // tm, chunk, 0)
        at = 2 * d + j * ff_ref.shape[3] + start
        pack_ref[0, :, at:at + w] = ga[:, :w].astype(bf16)
        pack_ref[1, :, at:at + w] = gb[:, :w].astype(bf16)
        run.step(8)
        if late:
            run.until(part(chunks[k + 1][0]))
            for copy in fetch(k + 1):
                copy.start()

    run.rest()

    go[...] = jnp.zeros_like(go)

    def after(i, carry):
        rows = pl.ds(i * ta, ta)
        mask = column_mask(aid_ref[rows, :])
        h_d = (acc[rows, d:] * mask).astype(bf16)
        xbuf[rows, :] = (mid[rows, :] + bd + acc[rows, :d] + 0.5 * nn(h_d, b_d[...])).astype(bf16)
        dh_u = (0.5 * dn2[rows, d:] * mask).astype(bf16)
        nh2, r2 = norm_parts(mid[rows, :])
        dy = dybuf[rows, :d]
        dmid = dy.astype(f32) + norm_back(dn2[rows, :d] + nn(dh_u, at_u[...]), gain2, nh2, r2)
        mid[rows, :] = dmid
        db = dmid.astype(bf16)
        dh_o = (0.5 * nt(db, b_o[...]) * mask).astype(bf16)
        do = (nt(db, wofull[...]) + nn(dh_o, at_o[...])).astype(bf16)
        go[0] += tn(dh_o, ocat[rows, :])
        go[1] += 0.5 * tn(hidden[rows, :], db)
        go[2] += tn(dh_u, n2buf[rows, :d])
        go[3] += 0.5 * tn(h_d, dy)
        for h in range(HEADS):
            obuf[h, rows, :HEAD_DIM] = do[:, h * HEAD_DIM:(h + 1) * HEAD_DIM]
        for copy in save(i):
            copy.start()
        return carry
    lax.fori_loop(0, tokens // ta, after, 0)
    for c, order in enumerate(((0, 2), (1, 3))):
        for k, which in enumerate(order):
            pack_ref[c, :, k * d:(k + 1) * d] = go[which].astype(bf16)
    for i in range(tokens // ta):
        for copy in save(i):
            copy.wait()


def mid_kernel(s, n, cuts, *refs):
    (oaug_ref, x_ref, cot_ref, aid_ref, wo_ref, ab_ref, ff_ref, bup_ref, vec_ref) = refs[:9]
    weights, refs = refs[9:9 + 2 * len(cuts)], refs[9 + 2 * len(cuts):]
    mixed_ref, dmid_ref, do_ref, pack_ref, obuf, xbuf, isem, osem, lsem, *bufs = refs
    cotbuf, mid = bufs[0], bufs[5]
    ta = min(256, xbuf.shape[0])

    def load(i):
        rows = pl.ds(i * ta, ta)
        for k, (src, dst) in enumerate(((oaug_ref.at[:, rows], obuf.at[:, rows]), (x_ref.at[rows], xbuf.at[rows]),
                                        (cot_ref.at[rows], cotbuf.at[rows]))):
            yield pltpu.make_async_copy(src, dst, isem.at[i, k])

    def save(i):
        rows = pl.ds(i * ta, ta)
        for k, (src, dst) in enumerate(((xbuf.at[rows], mixed_ref.at[rows]), (mid.at[rows], dmid_ref.at[rows]),
                                        (obuf.at[:, rows], do_ref.at[:, rows]))):
            yield pltpu.make_async_copy(src, dst, osem.at[i, k])

    mid_work(s, n, cuts, Steps([]), len(cuts), None, weights, load, save,
             [pltpu.make_async_copy(wo_ref, bufs[2], lsem.at[0])],
             [aid_ref, ab_ref, ff_ref, bup_ref, vec_ref, pack_ref, obuf, xbuf] + bufs)


def mid_bufs(s, pieces, tokens, d, widest):
    def v(*shape, dtype=bf16):
        return pltpu.VMEM(shape, dtype)

    return [
        v(tokens, d), v(tokens, d + LORA), v(s, d, d // s), v(tokens, d), v(tokens, d + LORA),
        v(tokens, d, dtype=f32), v(tokens, d + LORA, dtype=f32), v(tokens, d + LORA, dtype=f32),
        v(tokens, LORA), v(d, d), v(2, pieces, d // pieces, widest), v(2, pieces, d // pieces, widest),
        v(LORA, widest, dtype=f32), v(LORA, widest, dtype=f32), pltpu.SemaphoreType.DMA((2, 2)),
        v(4, LORA, d, dtype=f32),
    ]


def mid_call(oaug, x, cot, aid, wo, weights, cuts, ab, ff, bup, vec):
    tokens, d = x.shape
    s = wo.shape[0]
    pieces = weights[0].shape[0] // s
    tiles = tokens // min(256, tokens)
    full = pl.BlockSpec(memory_space=pltpu.VMEM)
    dma = pltpu.SemaphoreType.DMA
    return pl.pallas_call(
        partial(mid_kernel, s, pieces, cuts),
        in_specs=any_specs(3) + [full] + any_specs(1) + [full] * 4 + any_specs(len(weights)),
        out_specs=any_specs(3) + [full],
        out_shape=[
            jax.ShapeDtypeStruct((tokens, d), bf16),
            jax.ShapeDtypeStruct((tokens, d), f32),
            jax.ShapeDtypeStruct((HEADS, tokens, LANES), bf16),
            jax.ShapeDtypeStruct((2, LORA, 2 * d + s * ff.shape[3]), bf16),
        ],
        scratch_shapes=[
            pltpu.VMEM((HEADS, tokens, LANES), bf16), pltpu.VMEM((tokens, d), bf16),
            dma((tiles, 3)), dma((tiles, 3)), dma((1,)),
        ] + mid_bufs(s, pieces, tokens, d, max(w for _, w in cuts)),
        compiler_params=pltpu.CompilerParams(vmem_limit_bytes=VMEM),
        name="mid",
    )(oaug, x, cot, aid, wo, ab, ff, bup, vec, *weights)


def forward_kernel(nz, cuts, na, *refs):
    shards, (tokens, vec, cot, aid_ref, pic_ref), refs = refs[:na], refs[na:na + 5], refs[na + 5:]
    wholes, refs = refs[:na], refs[na:]
    (x_out, vec_out, a_out, b_out, qkv_out, n1_out, h_out, probs_out, o_out, cot_row, mixed_ref, dmid_ref, do_ref,
     pack_ref), refs = refs[:14], refs[14:]
    (xbuf, vbuf, obuf, ab, ff, vecs, bups, sems, wsem, osem, psem, csems, isem, ssem, *gather_refs) = refs
    n, d = nz * 4, xbuf.shape[2]
    half = xbuf.shape[1]
    count, tm = 2 * half, 512
    ds, fslot = shards[1].shape[1], ff.shape[3]
    nh = ds // HEAD_DIM
    each = LORA // 2
    spot = Spot(nz)
    spot.barrier()
    gather = Gather(spot, [(k, 0, a.shape[1]) for k, a in enumerate(shards)], shards, wholes, *gather_refs)
    run = Steps(gather.actions())
    swap = Swap(spot, cot, cot_row, csems)
    vec_here = pltpu.make_async_copy(vec, vbuf.at[spot.x], sems.at[0])
    vec_there = remote(vec, vbuf.at[spot.x], sems.at[1], sems.at[2], spot.xn)
    row_here = pltpu.make_async_copy(tokens.at[spot.x], xbuf.at[spot.x], sems.at[3])
    row_there = remote(tokens.at[1 - spot.x], xbuf.at[spot.x], sems.at[4], sems.at[5], spot.xn)

    def first(nbuf, widebuf, wbuf, abuf, bbuf, n1, hbuf, heads, pbuf):
        vec_here.start()
        vec_there.start()
        run.step(2)
        row_here.start()
        row_there.start()
        run.step(13)
        vec_here.wait()
        got = vbuf.at[1 - spot.x]
        remote(got, got, sems.at[1], sems.at[2], spot.xn).wait_recv()
        row_here.wait()
        got = xbuf.at[1 - spot.x]
        remote(got, got, sems.at[4], sems.at[5], spot.xn).wait_recv()
        for j in range(2):
            vecs[:, j * ds:(j + 1) * ds] = vbuf[j, :8, :ds].astype(f32)
            bups[j] = vbuf[j, 8:9, :].astype(f32)
        gain, shift = vecs[4:5, :], vecs[5:6, :]
        keep = [pltpu.make_async_copy(xbuf, x_out, osem.at[0]), pltpu.make_async_copy(vecs, vec_out, osem.at[1])]
        for copy in keep:
            copy.start()
        for part in range(2):
            def norm_step(i, carry, part=part):
                nhat, _ = norm_parts(xbuf[part, pl.ds(i * 256, 256), :].astype(f32))
                n1[pl.ds(part * half + i * 256, 256), :d] = (nhat * gain + shift).astype(bf16)
                return carry
            lax.fori_loop(0, half // 256, norm_step, 0)
            run.step(4)
        keep.append(pltpu.make_async_copy(n1.at[:, pl.ds(0, d)], n1_out, osem.at[2]))
        keep[-1].start()

        run.until(0)
        small = pltpu.make_async_copy(wholes[0], nbuf, sems.at[6])
        small.start()
        small.wait()
        for j in range(2):
            rows = slice(j * each, (j + 1) * each)
            one = nbuf[j * n:(j + 1) * n].reshape(10 * each, d)
            for m in range(3):
                abuf[m, rows, :] = one[m * each:(m + 1) * each]
                for i in range(2):
                    bbuf[m, i, rows, :] = one[(5 + m) * each:(6 + m) * each, i * ds:(i + 1) * ds]
            for k, m in enumerate((3, 4, 8, 9)):
                ab[k, rows, :] = one[m * each:(m + 1) * each]

        for copy in (pltpu.make_async_copy(abuf, a_out, osem.at[11]), pltpu.make_async_copy(bbuf, b_out, osem.at[12])):
            keep.append(copy)
            copy.start()

        def fetch(p, j):
            return pltpu.make_async_copy(wholes[1 + p].at[pl.ds(j * n, n)], wbuf.at[j], wsem.at[j])

        for p in range(3):
            run.until(1 + p)
            for j in range(2):
                fetch(p, j).start()
            for i in range(count // tm):
                rows = pl.ds(i * tm, tm)
                h = (nt(n1[rows, :d], abuf[p]) * column_mask(aid_ref[rows, :])).astype(bf16)
                hbuf[p, rows, :] = h
                n1[rows, d:] = (0.5 * h.astype(f32)).astype(bf16)
            for j in range(2):
                fetch(p, j).wait()
                bias = vbuf[j, p // 2:p // 2 + 1, :ds].astype(f32) if p != 1 else 0.0

                [serve] = run.within(1, count // tm, 3)

                def step(i, carry, p=p, j=j, bias=bias, serve=serve):
                    rows = pl.ds(i * tm, tm)
                    serve(i)
                    w = jnp.concatenate([wbuf[j].reshape(d, ds), bbuf[p, j]])
                    y = (nn(n1[rows, :], w) + bias).astype(bf16)
                    place = lax.broadcasted_iota(jnp.int32, (tm, LANES), 1) - HEAD_DIM
                    same = place == pic_ref[rows, :]
                    if p == 0:
                        extra = jnp.where(same, 1.0, 0.0)
                    elif p == 1:
                        extra = jnp.where((place >= 0) & (place < 16) & jnp.logical_not(same), -BIG, 0.0)
                    else:
                        extra = jnp.where((place == 0) | (place == 1), 1.0, 0.0)
                    extra = extra.astype(bf16)[:, HEAD_DIM:]
                    for h in range(nh):
                        heads[p, j * nh + h, rows, :HEAD_DIM] = y[:, h * HEAD_DIM:(h + 1) * HEAD_DIM]
                        heads[p, j * nh + h, rows, HEAD_DIM:] = extra
                    return carry
                lax.fori_loop(0, count // tm, step, 0)
                which = pl.ds(j * nh, nh)
                keep.append(pltpu.make_async_copy(
                    heads.at[p, which], qkv_out.at[p, which], osem.at[4 + 2 * p + j]))
                keep[-1].start()
                run.step(3)
        keep.append(pltpu.make_async_copy(hbuf, h_out, osem.at[3]))
        keep[-1].start()
        swap.start()

        def probs_copy(h):
            return pltpu.make_async_copy(pbuf.at[h % 2], probs_out.at[h], psem.at[h % 2])

        serve, again = run.within(0, HEADS, 2, 1)

        def head(h, carry):
            serve(h)

            @pl.when(h >= 2)
            def _():
                probs_copy(h - 2).wait()
            for i in range(count // tm):
                rows = pl.ds(i * tm, tm)
                s = nt(heads[0, h, rows, :], heads[1, h])
                top = jnp.max(s, axis=-1, keepdims=True)
                p = jnp.exp2((s - top) * (SCALE * LOG2E)).astype(bf16)
                o = nn(p, heads[2, h])
                inv = 1.0 / o[:, HEAD_DIM:HEAD_DIM + 1]
                pbuf[h % 2, rows, :] = (p.astype(f32) * inv).astype(bf16)
                obuf[h, rows, :] = (o * inv).astype(bf16)
            again(h)
            probs_copy(h).start()
            return carry
        lax.fori_loop(0, HEADS, head, 0)
        keep.append(pltpu.make_async_copy(obuf, o_out, osem.at[10]))
        keep[-1].start()
        run.until(5)
        big = pltpu.make_async_copy(wholes[5], widebuf, sems.at[7])
        big.start()
        big.wait()
        for j in range(2):
            one = widebuf[j * n:(j + 1) * n].reshape(LORA, 2 * fslot)
            for m in range(2):
                for i in range(2):
                    ff[m, i, j * each:(j + 1) * each, :] = one[m * each:(m + 1) * each, i * fslot:(i + 1) * fslot]
        for h in range(HEADS - 2, HEADS):
            probs_copy(h).wait()
        for copy in keep:
            copy.wait()

    def v(*shape):
        return pltpu.VMEM(shape, bf16)

    pl.run_scoped(
        first, v(8 * nz, *shards[0].shape), v(8 * nz, *shards[5].shape), v(2, n, *shards[1].shape), v(3, LORA, d),
        v(3, 2, LORA, ds), v(count, d + LORA), v(3, count, LORA), v(3, HEADS, count, LANES), v(2, count, count))
    swap.end()

    def second(wobuf3, *bufs):
        cotbuf, mid = bufs[0], bufs[4]
        bufs = bufs[:2] + (wobuf3,) + bufs[2:]

        def load(i):
            yield pltpu.make_async_copy(cot_row.at[i * 256 // half, pl.ds(i * 256 % half, 256)],
                                        cotbuf.at[pl.ds(i * 256, 256)], isem.at[i, 0])

        def save(i):
            rows = pl.ds(i * 256, 256)
            inner = pl.ds(i * 256 % half, 256)
            for k, (src, dst) in enumerate((
                    (xrow.at[rows], mixed_ref.at[i * 256 // half, inner]), (mid.at[rows], dmid_ref.at[rows]),
                    (obuf.at[:, rows], do_ref.at[:, rows]))):
                yield pltpu.make_async_copy(src, dst, ssem.at[i, k])

        mid_work(2, n, cuts, run, 0, lambda c: 7 + 2 * c, wholes[6:], load, save,
                 [pltpu.make_async_copy(wholes[4].at[pl.ds(j * n, n)], wobuf3.at[j], isem.at[j, 1]) for j in range(2)],
                 [aid_ref, ab, ff, bups, vecs, pack_ref, obuf, xrow] + list(bufs))

    xrow = xbuf.reshape(count, d)
    bufs = mid_bufs(2, n, count, d, max(w for _, w in cuts))
    bufs[2] = v(2, n, d // n, ds)
    pl.run_scoped(second, bufs[2], *bufs[:2], *bufs[3:])
    vec_there.wait_send()
    row_there.wait_send()


def forward_call(nz, cuts, shards, tokens, vec, cot, aid, pic):
    na = len(shards)
    dma = pltpu.SemaphoreType.DMA
    half, d = tokens.shape[1], tokens.shape[2]
    count, fslot = 2 * half, shards[5].shape[1] // 2
    tiles = count // 256
    full = pl.BlockSpec(memory_space=pltpu.VMEM)

    def v(*shape, dtype=bf16):
        return pltpu.VMEM(shape, dtype)

    def out(*shape, dtype=bf16):
        return jax.ShapeDtypeStruct(shape, dtype)

    return pl.pallas_call(
        partial(forward_kernel, nz, cuts, na),
        in_specs=any_specs(na + 3) + [full, full],
        out_specs=any_specs(na + 13) + [full],
        out_shape=gathered(nz, shards) + [
            out(*tokens.shape), out(8, d, dtype=f32), out(3, LORA, d), out(3, 2, LORA, shards[1].shape[1]),
            out(3, HEADS, count, LANES), out(count, d), out(3, count, LORA), out(HEADS, count, count), out(HEADS, count, LANES), out(*tokens.shape), out(*tokens.shape),
            out(count, d, dtype=f32), out(HEADS, count, LANES), out(2, LORA, 2 * d + 2 * fslot)],
        scratch_shapes=[
            v(*tokens.shape), v(2, *vec.shape), v(HEADS, count, LANES), v(4, LORA, d), v(2, 2, LORA, fslot),
            v(8, d, dtype=f32), v(2, 1, fslot, dtype=f32), dma((8,)), dma((2,)), dma((13,)), dma((2,)), dma((3,)),
            dma((tiles, 2)), dma((tiles, 3))] + Gather.scratch(nz, na),
        compiler_params=pltpu.CompilerParams(collective_id=1, has_side_effects=True, vmem_limit_bytes=VMEM),
        name="forward",
    )(*shards, tokens, vec, cot, aid, pic)


def tail_kernel(s, dq_ref, dk_ref, dv_ref, x_ref, n1_ref, h_ref, dmid_ref, aid_ref,
                wq_ref, wk_ref, wv_ref, at_ref, b_ref, vec_ref, out_ref, pack_ref, dy_ref, ga_ref, gb_ref):
    i = pl.program_id(0)
    tm, d = x_ref.shape
    nh = HEADS // s
    ds = d // s
    mask = column_mask(aid_ref[...])

    @pl.when(i == 0)
    def _():
        ga_ref[...] = jnp.zeros_like(ga_ref)
        gb_ref[...] = jnp.zeros_like(gb_ref)

    n1 = n1_ref[...]
    dn = jnp.zeros((tm, d), f32)
    for p, (src, w_ref) in enumerate(((dq_ref, wq_ref), (dk_ref, wk_ref), (dv_ref, wv_ref))):
        dh = jnp.zeros((tm, LORA), f32)
        for j in range(s):
            for h in range(nh):
                dy_ref[p, j, :, h * HEAD_DIM:(h + 1) * HEAD_DIM] = src[j * nh + h, :, :HEAD_DIM]
            dy = dy_ref[p, j]
            dh = dh + nt(dy, b_ref[p, j])
            dn = dn + nt(dy, w_ref[j])
            gb_ref[p, j] += 0.5 * tn(h_ref[p], dy)
        dh = (0.5 * dh * mask).astype(bf16)
        dn = dn + nn(dh, at_ref[p])
        ga_ref[p] += tn(dh, n1)
    nhat, r = norm_parts(x_ref[...].astype(f32))
    out_ref[...] = dmid_ref[...] + norm_back(dn, vec_ref[4:5, :], nhat, r)

    @pl.when(i == pl.num_programs(0) - 1)
    def _():
        for p in range(3):
            pack_ref[0, :, p * d:(p + 1) * d] = ga_ref[p].astype(bf16)
            for j in range(s):
                at = p * d + j * ds
                pack_ref[1, :, at:at + ds] = gb_ref[p, j].astype(bf16)


def tail_call(dq, dk, dv, x, n1, hid, dmid, aid, wq, wk, wv, at, bq, vec):
    tokens, d = x.shape
    s = wq.shape[0]
    tm = min(256, tokens)
    full = pl.BlockSpec(memory_space=pltpu.VMEM)
    tile = pl.BlockSpec((tm, d), lambda i: (i, 0))
    heads = pl.BlockSpec((HEADS, tm, LANES), lambda i: (0, i, 0))
    return pl.pallas_call(
        partial(tail_kernel, s),
        grid=(tokens // tm,),
        in_specs=[
            heads, heads, heads, tile, tile,
            pl.BlockSpec((3, tm, LORA), lambda i: (0, i, 0)),
            tile,
            pl.BlockSpec((tm, 1), lambda i: (i, 0)),
            full, full, full, full, full, full,
        ],
        out_specs=[tile, full],
        out_shape=[
            jax.ShapeDtypeStruct((tokens, d), f32),
            jax.ShapeDtypeStruct((2, LORA, 3 * d), bf16),
        ],
        scratch_shapes=[
            pltpu.VMEM((3, s, tm, d // s), bf16),
            pltpu.VMEM((3, LORA, d), f32),
            pltpu.VMEM((3, s, LORA, d // s), f32),
        ],
        compiler_params=pltpu.CompilerParams(vmem_limit_bytes=VMEM),
        name="tail",
    )(dq, dk, dv, x, n1, hid, dmid, aid, wq, wk, wv, at, bq, vec)


def backward_kernel(nz, *refs):
    (qkv, probs, o, d_out, x, n1, hid, dmid, wq, wk, wv, mixed, g_mid, a_ref, b_ref, vec_ref, aid_ref) = refs[:17]
    (own_out, got, mid_total, qkv_total, mixed_out), refs = refs[17:22], refs[22:]
    (dy, dh, w, g_qkv, low, wsem, msem, dsem, lsem, psem, tsem, csem, *sums) = refs
    n, d = 4 * nz, x.shape[2]
    half = x.shape[1]
    count, ds = 2 * half, dy.shape[3]
    nh = HEADS // 2
    spot = Spot(nz)
    spot.barrier()
    per = len(sums) // 3
    width = g_mid.shape[4] // 2
    one, two = (Reduce(spot, g_mid.at[:, :, :, :, pl.ds(k * width, width)], mid_total.at[:, :, :, pl.ds(k * width, width)],
                       sums[k * per:(k + 1) * per]) for k in range(2))
    last = Reduce(spot, g_qkv, qkv_total, sums[2 * per:])
    swap = Swap(spot, mixed, mixed_out, msem)
    weights = [pltpu.make_async_copy(src.at[pl.ds(j * n, n)], w.at[p, j], wsem.at[p, j])
               for p, src in enumerate((wq, wk, wv)) for j in range(2)]

    one.one()
    two.one()
    swap.start()
    serve = {1: [one.two], 2: [two.two], 6: [one.three], 10: [two.three], 12: [one.four, one.five], 15: [two.four]}

    def first(heads):
        def attention(small, pbuf, dsbuf, dabuf):
            srcs = [qkv.at[0], qkv.at[1], qkv.at[2], o, d_out]

            def loads(h):
                for k, src in enumerate(srcs):
                    yield pltpu.make_async_copy(src.at[h], small.at[h % 2, k], lsem.at[h % 2, k])
                yield pltpu.make_async_copy(probs.at[h], pbuf.at[h % 2], psem.at[h % 2])

            for copy in loads(0):
                copy.start()
            lane = lane_ids(256)

            def head(h, carry):
                for t, acts in serve.items():
                    @pl.when(h == t)
                    def _(acts=acts):
                        for act in acts:
                            act()

                @pl.when(h + 1 < HEADS)
                def _():
                    for copy in loads(h + 1):
                        copy.start()
                for copy in loads(h):
                    copy.wait()
                m = h % 2
                for i in range(count // 256):
                    rows = pl.ds(i * 256, 256)
                    do = jnp.where(lane < HEAD_DIM, small[m, 4, rows, :].astype(f32), 0.0)
                    delta = jnp.sum(do * small[m, 3, rows, :].astype(f32), axis=-1, keepdims=True)
                    hi = delta.astype(bf16).astype(f32)
                    do = jnp.where(lane == HEAD_DIM, -hi, jnp.where(lane == HEAD_DIM + 1, hi - delta, do)).astype(bf16)
                    dabuf[rows, :] = do
                    dp = nt(do, small[m, 2])
                    part = (pbuf[m, rows, :].astype(f32) * dp).astype(bf16)
                    dsbuf[rows, :] = part
                    heads[0, h, rows, :] = (nn(part, small[m, 1]) * SCALE).astype(bf16)
                heads[2, h] = nn(dabuf[...].T, pbuf[m]).T.astype(bf16)
                heads[1, h] = (nn(small[m, 0].T, dsbuf[...]).T * SCALE).astype(bf16)
                return carry
            lax.fori_loop(0, HEADS, head, 0)

        pl.run_scoped(attention, pltpu.VMEM((2, 5, count, LANES), bf16), pltpu.VMEM((2, count, count), bf16),
                      pltpu.VMEM((count, count), bf16), pltpu.VMEM((count, LANES), bf16))

        def adapters(nbuf, hbuf, ga, gb):
            here = [pltpu.make_async_copy(n1, nbuf, csem.at[0]), pltpu.make_async_copy(hid, hbuf, csem.at[1])]
            for copy in here + weights:
                copy.start()
            for copy in here:
                copy.wait()
            later = [[one.six, two.five], [one.seven, two.six], [two.seven]]
            for p in range(3):
                def tile(i, carry, p=p):
                    rows = pl.ds(i * 512, 512)
                    total = jnp.zeros((512, LORA), f32)
                    for j in range(2):
                        for h in range(nh):
                            dy[p, j, rows, h * HEAD_DIM:(h + 1) * HEAD_DIM] = heads[p, j * nh + h, rows, :HEAD_DIM]
                        part = dy[p, j, rows, :]
                        total = total + nt(part, b_ref[p, j])
                        more = 0.5 * tn(hbuf[p, rows, :], part)

                        @pl.when(i == 0)
                        def _(j=j, more=more):
                            gb[j] = more

                        @pl.when(i > 0)
                        def _(j=j, more=more):
                            gb[j] += more
                    grad = (0.5 * total * column_mask(aid_ref[rows, :])).astype(bf16)
                    dh[p, rows, :] = grad
                    more = tn(grad, nbuf[rows, :])

                    @pl.when(i == 0)
                    def _():
                        ga[...] = more

                    @pl.when(i > 0)
                    def _():
                        ga[...] += more
                    return carry
                lax.fori_loop(0, count // 512, tile, 0)
                cols = slice(p * d, (p + 1) * d)
                g_qkv[0, :, :, :, cols] = ga[...].reshape(2, 2 * nz, 8, d).astype(bf16)
                for j in range(2):
                    cols = slice(p * d + j * ds, p * d + (j + 1) * ds)
                    g_qkv[1, :, :, :, cols] = gb[j].reshape(2, 2 * nz, 8, ds).astype(bf16)
                for act in later[p]:
                    act()

        pl.run_scoped(adapters, pltpu.VMEM((count, d), bf16), pltpu.VMEM((3, count, LORA), bf16),
                      pltpu.VMEM((LORA, d), f32), pltpu.VMEM((2, LORA, ds), f32))

    pl.run_scoped(first, pltpu.VMEM((3, HEADS, count, LANES), bf16))
    last.one()

    def second(xbuf, mbuf, obuf):
        def spots(t):
            side = 1 - spot.x if t < 2 else spot.x
            return side, t % 2 * 256

        def loads(t):
            side, inner = spots(t)
            rows = pl.ds(pl.multiple_of(side * half + inner, 256), 256)
            return (pltpu.make_async_copy(x.at[side, pl.ds(inner, 256)], xbuf.at[t % 2], dsem.at[t, 0]),
                    pltpu.make_async_copy(dmid.at[rows], mbuf.at[t % 2], dsem.at[t, 1]))

        def there(t):
            return remote(low.at[t], got.at[pl.ds(t * 256, 256)], tsem.at[t, 0], tsem.at[t, 1], spot.xn)

        def keep(t):
            return pltpu.make_async_copy(obuf.at[t - 2], own_out.at[pl.ds((t - 2) * 256, 256)], tsem.at[t, 0])

        for t in range(2):
            for copy in loads(t):
                copy.start()
        for copy in weights:
            copy.wait()
        serve = [[], [last.two], [], [last.three]]
        for t in range(4):
            side, inner = spots(t)
            rows = pl.ds(pl.multiple_of(side * half + inner, 256), 256)
            dn = jnp.zeros((256, d), f32)
            for p in range(3):
                for j in range(2):
                    dn = dn + nt(dy[p, j, rows, :], w[p, j].reshape(d, ds))
                dn = dn + nn(dh[p, rows, :], a_ref[p])
            for copy in loads(t):
                copy.wait()
            nhat, r = norm_parts(xbuf[t % 2].astype(f32))
            value = mbuf[t % 2] + norm_back(dn, vec_ref[4:5, :], nhat, r)
            if t < 2:
                low[t] = value.astype(bf16)
                there(t).start()
                for copy in loads(t + 2):
                    copy.start()
            else:
                obuf[t - 2] = value
                keep(t).start()
            for act in serve[t]:
                act()
        last.four()
        last.five()
        last.six()
        last.seven()
        for t in range(2):
            there(t).wait()
        for t in range(2, 4):
            keep(t).wait()

    pl.run_scoped(second, pltpu.VMEM((2, 256, d), bf16), pltpu.VMEM((2, 256, d), f32), pltpu.VMEM((2, 256, d), f32))
    for reduce in (one, two, last):
        reduce.end()
    swap.end()


def backward_call(nz, qkv, probs, o, d_out, x, n1, hid, dmid, wq, wk, wv, mixed, g_mid, at, bq, vec, aid):
    dma = pltpu.SemaphoreType.DMA
    half, d = x.shape[1], x.shape[2]
    count, ds = 2 * half, wq.shape[2]
    full = pl.BlockSpec(memory_space=pltpu.VMEM)

    def v(*shape, dtype=bf16):
        return pltpu.VMEM(shape, dtype)

    def out(*shape, dtype=bf16):
        return jax.ShapeDtypeStruct(shape, dtype)

    return pl.pallas_call(
        partial(backward_kernel, nz),
        in_specs=any_specs(12) + [full] * 5,
        out_specs=any_specs(5),
        out_shape=[out(half, d, dtype=f32), out(half, d), out(2, 2 * nz, 8, g_mid.shape[4]), out(2, 2 * nz, 8, 3 * d),
                   out(*mixed.shape)],
        scratch_shapes=[
            v(3, 2, count, ds), v(3, count, LORA), v(3, 2, 4 * nz, d // (4 * nz), ds), v(2, 2, 2 * nz, 8, 3 * d),
            v(2, 256, d), dma((3, 2)), dma((3,)), dma((4, 2)), dma((2, 5)), dma((2,)), dma((4, 2)), dma((2,))]
        + Reduce.scratch(nz, g_mid.shape[4] // 2) * 2 + Reduce.scratch(nz, 3 * d),
        compiler_params=pltpu.CompilerParams(collective_id=4, has_side_effects=True, vmem_limit_bytes=VMEM),
        name="backward",
    )(qkv, probs, o, d_out, x, n1, hid, dmid, wq, wk, wv, mixed, g_mid, at, bq, vec, aid)


def rows_of_adapters(a):
    t = jnp.swapaxes(a, -1, -2)
    return t.reshape(*t.shape[:-3], t.shape[-3] * t.shape[-2], t.shape[-1])


def local(tokens, cotangent, lengths, adapter_ids, w_query, w_key, w_value, w_out, w_up, w_down,
          b_query, b_value, b_out, b_up, b_down, gain_one, shift_one, gain_two, shift_two,
          qkv_a, out_a, attn_b, up_a, up_b, down_a, down_b):
    seq = lax.axis_size("seq")
    rows, part_len, d = tokens.shape
    group = seq // rows
    count = rows * part_len
    ds, fs = w_query.shape[1], w_up.shape[1]
    me = lax.axis_index("seq")
    row, chunk = me // group, me % group

    def moves(j):
        return [(a, (a % rows + j) % rows * group + a // rows) for a in range(seq)]

    def send(piece, pairs):
        return piece if all(a == b for a, b in pairs) else lax.ppermute(piece, "seq", pairs)

    def to_row(t):
        out = jnp.zeros((rows, part_len, d), t.dtype)
        for j in range(rows):
            piece = lax.dynamic_index_in_dim(t, (me + j) % rows, 0, False)
            out = lax.dynamic_update_index_in_dim(out, send(piece, moves(j)), (row - j) % rows, 0)
        return out.reshape(count, d)

    def from_row(t, dtype):
        t = t.reshape(rows, part_len, d)
        out = jnp.zeros((rows, part_len, d), dtype)
        for j in range(rows):
            piece = lax.dynamic_index_in_dim(t, (row - j) % rows, 0, False)
            pairs = [(b, a) for a, b in moves(j)]
            if not all(a == b for a, b in pairs):
                piece = piece.astype(bf16)
            got = send(piece, pairs).astype(dtype)
            out = lax.dynamic_update_index_in_dim(out, got, (me + j) % rows, 0)
        return out

    dps = lax.axis_size("dp")
    nz = dps // 4
    fast = seq == 2 and rows == 2 and nz == 4
    slot, fslot = up128(ds), up128(fs)
    step = up128(-(-fslot // max(round(fslot / 768), 1)))
    cuts = [(a, min(step, fslot - a)) for a in range(0, fslot, step)]

    def wide_to(t, n):
        return jnp.pad(t, ((0, 0), (0, n - t.shape[1])))

    wu_part, wd_part = wide_to(w_up, fslot), wide_to(w_down.T, fslot)
    ff_parts = [t[:, a:a + n] for a, n in cuts for t in (wu_part, wd_part)]
    narrow = jnp.concatenate([
        rows_of_adapters(qkv_a), rows_of_adapters(out_a)[None], rows_of_adapters(up_a)[None],
        attn_b.reshape(4, -1, d), down_b.reshape(1, -1, d)])
    wide = jnp.stack([rows_of_adapters(down_a), up_b.reshape(-1, up_b.shape[-1])])
    vec_part = jnp.stack([b_query, b_value, b_out, b_down, gain_one, shift_one, gain_two, shift_two])
    teams = [[g * group + c for c in range(group)] for g in range(rows)]

    my_len = lax.dynamic_index_in_dim(lengths, row, 0, False)
    my_ids = lax.dynamic_index_in_dim(adapter_ids, row, 0, False)
    slots = jnp.arange(my_len.shape[0], dtype=jnp.int32)
    ends = jnp.sum(jnp.where(slots[None, :] <= slots[:, None], my_len[None, :], 0), axis=1)
    pos = chunk * count + jnp.arange(count, dtype=jnp.int32)
    pic = jnp.sum((pos[:, None] >= ends[None, :]).astype(jnp.int32), axis=1, keepdims=True)
    aid = jnp.sum(jnp.where(pic == slots[None, :], my_ids[None, :], 0), axis=1, keepdims=True)
    aid = jnp.where(pos[:, None] < ends[-1], aid, -1)

    def from_halves(t):
        return jnp.swapaxes(t, 0, 1).reshape(t.shape[1], -1, t.shape[3])

    if fast:
        me_dp = lax.axis_index("dp")

        def share(t):
            flat = t.reshape(-1, t.shape[-1])
            n = flat.shape[0] // dps
            return lax.dynamic_slice_in_dim(flat, me_dp * n, n, 0)

        def whole(t):
            return t.reshape(seq, d, t.shape[2])

        small = jnp.concatenate([wide_to(vec_part, fslot), wide_to(b_up[None], fslot), jnp.zeros((7, fslot), bf16)])
        wide = jnp.pad(wide.reshape(2, -1, seq, fs), ((0, 0), (0, 0), (0, 0), (0, fslot - fs)))
        wide = wide.reshape(2, -1, seq * fslot)
        narrow, wq, wk, wv, *got = forward_call(
            nz, cuts, [share(narrow), w_query, w_key, w_value, w_out, share(wide)] + ff_parts,
            tokens, small, cotangent, aid, pic)
        x, vec, at, bq, qkv, n1, hid, probs, oaug, _, mixed, dmid, d_out, g_mid = got[2 + len(ff_parts):]
    else:
        def gather_all(shard):
            full = lax.all_gather(shard, ("seq", "dp"), axis=0, tiled=True)
            return full.reshape(seq, d, shard.shape[1])

        wq, wk, wv, wo, *weights = (gather_all(t) for t in [w_query, w_key, w_value, w_out] + ff_parts)
        narrow = lax.all_gather(narrow, "seq", axis=1, tiled=True)
        wide = lax.all_gather(wide, "seq", axis=1, tiled=True)
        vec = lax.all_gather(vec_part, "seq", axis=1, tiled=True).astype(f32)
        bup = lax.all_gather(b_up[None], "seq", axis=0, tiled=True).astype(f32)[:, None]
        x = to_row(tokens)
        cot = to_row(cotangent)

    if fast:
        mine, other, g_mid, g_qkv, mixed = backward_call(
            nz, qkv, probs, oaug, d_out, x, n1, hid, dmid, wq, wk, wv, mixed,
            g_mid.reshape(2, 2, 2 * nz, 8, g_mid.shape[2]), at, bq, vec, aid)
        g_mid, g_qkv = (t.reshape(2, LORA // seq, -1) for t in (g_mid, g_qkv))
        other = other.astype(f32)
        d_in = jnp.where(me == 0, jnp.stack([mine, other]), jnp.stack([other, mine]))
    else:
        at, b = narrow[:5], narrow[5:]
        bq = jnp.swapaxes(b[:3].reshape(3, LORA, seq, ds), 1, 2)
        bias = jnp.stack([vec[0], jnp.zeros_like(vec[0]), vec[1]]).reshape(3, seq, 1, ds)
        qkv, n1, hid = qkv_call(x, jnp.stack([wq, wk, wv]), at, bq, bias, vec, aid, pic)
        kv, off = qkv, 1
        if group > 1:
            kv = lax.all_gather(qkv[1:], "seq", axis=2, tiled=True, axis_index_groups=teams)
            off = 0
        probs, oaug = attn_fwd_call(qkv, kv, off)
        more = ((0, 0), (0, 0), (0, 0), (0, fslot - fs))
        ff = jnp.pad(jnp.swapaxes(wide.reshape(2, LORA, seq, fs), 1, 2), more)
        mixed, dmid, d_out, g_mid = mid_call(
            oaug, x, cot, aid, wo, weights, cuts, jnp.concatenate([at[3:], b[3:]]), ff, jnp.pad(bup, more[1:]), vec)
        dq, dk, dv = attn_bwd_call(qkv, kv, off, probs, oaug, d_out)
        if group > 1:
            dk, dv = (lax.psum_scatter(t, "seq", scatter_dimension=1, axis_index_groups=teams, tiled=True)
                      for t in (dk, dv))
        d_in, g_qkv = tail_call(dq, dk, dv, x, n1, hid, dmid, aid, wq, wk, wv, at, bq, vec)

        def total(t):
            return lax.psum(lax.psum_scatter(t, "seq", scatter_dimension=1, tiled=True), "dp")

        g_mid, g_qkv = total(g_mid), total(g_qkv)
        mixed = from_row(mixed, bf16)
        d_in = from_row(d_in, f32)

    def down_form(t):
        return jnp.swapaxes(t.astype(f32).reshape(-1, RANK, t.shape[-1]), -1, -2)

    def up_form(t):
        return t.astype(f32).reshape(-1, RANK, t.shape[-1])

    def cut(t, k):
        return t[:, k * d:(k + 1) * d]

    def ff_of(t):
        return jnp.concatenate([t[:, 2 * d + j * fslot:2 * d + j * fslot + fs] for j in range(seq)], axis=1)

    a_mid, b_mid = g_mid
    a_qkv, b_qkv = g_qkv
    return (
        mixed,
        d_in,
        jnp.stack([down_form(cut(a_qkv, p)) for p in range(3)]),
        down_form(cut(a_mid, 0)),
        jnp.stack([up_form(cut(b_qkv, p)) for p in range(3)] + [up_form(cut(b_mid, 0))]),
        down_form(cut(a_mid, 1)),
        up_form(ff_of(b_mid)),
        down_form(ff_of(a_mid)),
        up_form(cut(b_mid, 1)),
    )


def solution(mesh):
    both = P("dp", "seq", None)
    lead = P("seq", None, None)
    second = P(None, "seq", None, None)
    return jax.shard_map(
        local,
        mesh=mesh,
        in_specs=(both, both, P("dp", None), P("dp", None))
        + (P("dp", "seq"),) * 5 + (P("seq", "dp"),) + (P("seq"),) * 9
        + (second, lead, second, lead, lead, lead, lead),
        out_specs=(both, both, second, lead, second, lead, lead, lead, lead),
        check_vma=False,
    )
```

```python
from functools import partial

import jax
import jax.numpy as jnp
from jax import lax
from jax.experimental import pallas as pl
from jax.experimental.pallas import tpu as pltpu
from jax.sharding import PartitionSpec as P

HEADS = 16
HEAD_DIM = 72
RANK = 16
ADAPTERS = 8
LORA = RANK * ADAPTERS
LANES = 128
EPS = 1e-06
SCALE = HEAD_DIM ** (-0.5)
BIG = 1e30
LOG2E = 1.4426950408889634
VMEM = 61 * 1024 * 1024
HEAD, BEFORE, CHUNK = (1, 0), 1, 3

MESH = pl.DeviceIdType.MESH
bf16 = jnp.bfloat16
f32 = jnp.float32


def nn(a, b):
    return jnp.dot(a, b, preferred_element_type=f32)


def nt(a, b):
    return lax.dot_general(a, b, (((1,), (1,)), ((), ())), preferred_element_type=f32)


def tn(a, b):
    return lax.dot_general(a, b, (((0,), (0,)), ((), ())), preferred_element_type=f32)


def up128(n):
    return -(-n // LANES) * LANES


def lane_ids(rows):
    return lax.broadcasted_iota(jnp.int32, (rows, LANES), 1)


def norm_parts(x):
    center = jnp.mean(x, axis=-1, keepdims=True)
    xc = x - center
    r = lax.rsqrt(jnp.mean(xc * xc, axis=-1, keepdims=True) + EPS)
    return xc * r, r


def norm_back(dn, gain, nh, r):
    gh = dn * gain
    a = jnp.mean(gh, axis=-1, keepdims=True)
    b = jnp.mean(gh * nh, axis=-1, keepdims=True)
    return r * (gh - a - nh * b)


def column_mask(aid):
    return (lane_ids(aid.shape[0]) // RANK == aid).astype(f32)


class Spot:
    def __init__(self, nz):
        dp = lax.axis_index("dp")
        self.nz = nz
        self.x = lax.axis_index("seq")
        self.z, self.y, self.c = dp // 4, (dp // 2) % 2, dp % 2
        self.xn = self.device(1 - self.x, self.y, self.z, self.c)
        self.yn = self.device(self.x, 1 - self.y, self.z, self.c)
        self.sib = self.device(self.x, self.y, self.z, 1 - self.c)
        self.zs = [None] + [self.device(self.x, self.y, self.zk(k), self.c) for k in range(1, nz)]
        flip = self.z // 2
        self.inner = self.z + flip * (3 - 2 * self.z)
        self.zr = [m + flip * (3 - 2 * m) for m in (self.inner, 1 - self.inner, 2, 3)]
        self.zp = [self.device(self.x, self.y, z, self.c) for z in self.zr]

    def device(self, x, y, z, c):
        return ((z * 2 + y) * 2 + c, x)

    def zk(self, k):
        return (self.z + k) % self.nz

    def barrier(self):
        peers = [self.xn, self.yn, self.sib] + self.zs[1:]
        sem = pltpu.get_barrier_semaphore()
        for peer in peers:
            pl.semaphore_signal(sem, inc=1, device_id=peer, device_id_type=MESH)
        pl.semaphore_wait(sem, len(peers))


def remote(src, dst, send, recv, device):
    return pltpu.make_async_remote_copy(
        src_ref=src, dst_ref=dst, send_sem=send, recv_sem=recv, device_id=device, device_id_type=MESH
    )


class Gather:
    def __init__(self, spot, ins, outs, send, recv, own):
        self.s, self.ins, self.outs, self.send, self.recv, self.own = spot, ins, outs, send, recv, own

    @staticmethod
    def scratch(nz, count):
        dma = pltpu.SemaphoreType.DMA
        return [dma((count, 14)), dma((count, 8)), dma((count,))]

    def column(self, g, x, y):
        return self.outs[g].at[self.s.c, x, y]

    def shard(self, g, x, y, r):
        return self.outs[g].at[self.s.c, x, y, self.s.zr[r]]

    def sends(self, g):
        s = self.s
        here, over = self.column(g, s.x, s.y), self.column(g, 1 - s.x, s.y)
        side, far = self.column(g, s.x, 1 - s.y), self.column(g, 1 - s.x, 1 - s.y)
        mine = self.shard(g, s.x, s.y, 0)
        first, third = self.shard(g, 1 - s.x, s.y, 0), self.shard(g, 1 - s.x, s.y, 3)
        diagonal, other = self.shard(g, 1 - s.x, 1 - s.y, 0), self.shard(g, 1 - s.x, 1 - s.y, 2)
        return {
            "z1": (self.ins[g], mine, 0, s.zp[1]), "z2": (self.ins[g], mine, 0, s.zp[2]),
            "z3": (self.ins[g], mine, 0, s.zp[3]),
            "x": (here, here, 1, s.xn), "y": (here, here, 2, s.yn), "s": (here, here, 7, s.sib),
            "xy0": (first, first, 3, s.yn), "xy3": (third, third, 6, s.yn), "xs": (over, over, 7, s.sib),
            "ys": (side, side, 7, s.sib),
            "d1": (diagonal, diagonal, 4, s.zp[1]), "i2": (diagonal, diagonal, 5, s.zp[2]),
            "i1": (other, other, 5, s.zp[1]), "ds": (far, far, 7, s.sib),
        }

    def copy(self, g, name):
        table = self.sends(g)
        src, dst, arrival, device = table[name]
        return remote(src, dst, self.send.at[g, list(table).index(name)], self.recv.at[g, arrival], device)

    def start(self, g, *names):
        for name in names:
            if name[0] == "i":
                pl.when(self.s.inner == 1)(self.copy(g, name).start)
            else:
                self.copy(g, name).start()

    def await_(self, g, arrival, ref):
        remote(ref, ref, self.send.at[g, 0], self.recv.at[g, arrival], self.s.xn).wait_recv()

    def local(self, g):
        return pltpu.make_async_copy(self.ins[g], self.shard(g, self.s.x, self.s.y, 0), self.own.at[g])

    def begin(self, g):
        self.local(g).start()
        self.start(g, "z1", "z2", "z3")

    def spread(self, g):
        s = self.s
        self.local(g).wait()
        self.await_(g, 0, self.outs[g].at[s.c, s.x, s.y, pl.ds(0, s.nz - 1)])
        self.start(g, "x", "y", "s")

    def over_x(self, g):
        self.await_(g, 1, self.column(g, 1 - self.s.x, self.s.y))
        self.start(g, "xy0", "xy3", "xs")

    def over_y(self, g):
        self.await_(g, 2, self.column(g, self.s.x, 1 - self.s.y))
        self.start(g, "ys")

    def far(self, g, r):
        s = self.s
        self.await_(g, 3 + r, self.shard(g, 1 - s.x, 1 - s.y, r))
        self.start(g, *{0: ["d1", "i2"], 2: ["i1"], 1: ["ds"]}.get(r, []))

    def end(self, g):
        self.await_(g, 7, self.outs[g].at[1 - self.s.c])
        for name in self.sends(g):
            if name[0] == "i":
                pl.when(self.s.inner == 1)(self.copy(g, name).wait_send)
            else:
                self.copy(g, name).wait_send()

    def actions(self):
        n = len(self.ins)
        out = []
        for t in range(n + 4):
            if t < n:
                out.append((self.begin, t))
            if 0 <= t - 1 < n:
                out.append((self.spread, t - 1))
            if 0 <= t - 2 < n:
                out += [(self.over_x, t - 2), (self.over_y, t - 2)]
            if 0 <= t - 3 < n:
                out += [(self.far, t - 3, r) for r in (0, 3, 2, 1)]
            if 0 <= t - 4 < n:
                out.append((self.end, t - 4))
        return out


def pull(nz, src, j, dst, sem):
    def start():
        for c in range(2):
            for y in range(2):
                pltpu.make_async_copy(src.at[c, j, y], dst.at[:, y, c], sem).start()

    return start, lambda: pltpu.make_async_copy(dst, dst, sem).wait()


class Swap:
    def __init__(self, spot, mine, got, sems, slot=None):
        self.s, self.mine, self.got, self.sems = spot, mine, got, sems
        self.slot = spot.x if slot is None else slot

    def copies(self):
        s = self.s
        here = pltpu.make_async_copy(self.mine.at[s.x], self.got.at[s.x], self.sems.at[0])
        there = remote(self.mine.at[1 - s.x], self.got.at[self.slot], self.sems.at[1], self.sems.at[2], s.xn)
        return here, there

    def start(self):
        for copy in self.copies():
            copy.start()

    def end(self):
        here, there = self.copies()
        here.wait()
        ref = self.got.at[1 - self.s.x]
        remote(ref, ref, self.sems.at[1], self.sems.at[2], self.s.xn).wait_recv()
        there.wait_send()


class Reduce:
    def __init__(self, spot, data, result, refs):
        self.s, self.data, self.result = spot, data, result
        self.r1, self.s1, self.r2, self.s2, self.r3, self.s3, self.r4, self.total = refs[:8]
        self.send, self.recv, self.out = refs[8:]

    @staticmethod
    def scratch(nz, width):
        def v(*dims):
            return pltpu.VMEM((*dims, 8, width), bf16)
        dma = pltpu.SemaphoreType.DMA
        n = 5 + 2 * (nz - 1)
        return [v(2, 2 * nz), v(2, 2 * nz), v(2, nz), v(2, nz), v(nz, 2), v(2), v(1), v(2, 2 * nz),
                dma((n,)), dma((n,)), dma((1,))]

    def pair(self, i, src, dst, device):
        return remote(src, dst, self.send.at[i], self.recv.at[i], device)

    def to_core(self):
        return self.pair(0, self.data.at[1 - self.s.c], self.r1, self.s.sib)

    def to_y(self):
        nz = self.s.nz
        return self.pair(1, self.s1.at[:, pl.ds((1 - self.s.y) * nz, nz)], self.r2, self.s.yn)

    def to_x(self):
        return self.pair(2, self.s3.at[1 - self.s.x], self.r4.at[0], self.s.xn)

    def to_z(self, k):
        s = self.s
        return self.pair(4 + k, self.s2.at[:, s.zk(k)], self.r3.at[s.z], s.zs[k])

    def from_z(self, k):
        s = self.s
        ref = self.r3.at[s.zk(k)]
        return remote(ref, ref, self.send.at[4 + s.nz - k], self.recv.at[4 + s.nz - k], s.zs[k])

    def back_z(self, k):
        s = self.s
        ref = self.total.at[s.c, s.y * s.nz + s.z]
        return self.pair(4 + s.nz - 1 + k, ref, ref, s.zs[k])

    def from_back_z(self, k):
        s = self.s
        i = 4 + s.nz - 1 + s.nz - k
        ref = self.total.at[s.c, s.y * s.nz + s.zk(k)]
        return remote(ref, ref, self.send.at[i], self.recv.at[i], s.zs[k])

    def back_y(self, y):
        s = self.s
        ref = self.total.at[s.c, pl.ds(y * s.nz, s.nz)]
        return self.pair(3, ref, ref, s.yn)

    def back_core(self, c):
        ref = self.total.at[c]
        return self.pair(4, ref, ref, self.s.sib)

    def one(self):
        self.to_core().start()

    def two(self):
        s, nz = self.s, self.s.nz
        self.to_core().wait_recv()

        def add(i, c):
            x, b = i // (2 * nz), i % (2 * nz)
            self.s1[x, b] = (self.data[s.c, x, b].astype(f32) + self.r1[x, b].astype(f32)).astype(bf16)
            return c
        lax.fori_loop(0, 4 * nz, add, 0)
        self.to_y().start()

    def three(self):
        s, nz = self.s, self.s.nz
        self.to_y().wait_recv()

        def add(i, c):
            x, b = i // nz, i % nz
            self.s2[x, b] = (self.s1[x, s.y * nz + b].astype(f32) + self.r2[x, b].astype(f32)).astype(bf16)
            return c
        lax.fori_loop(0, 2 * nz, add, 0)
        for k in range(1, nz):
            self.to_z(k).start()

    def four(self):
        s, nz = self.s, self.s.nz
        for k in range(1, nz):
            self.from_z(k).wait_recv()
        for x in range(2):
            v = self.s2[x, s.z].astype(f32)
            for k in range(1, nz):
                v = v + self.r3[s.zk(k), x].astype(f32)
            self.s3[x] = v.astype(bf16)
        self.to_x().start()

    def five(self):
        s, nz = self.s, self.s.nz
        self.to_x().wait_recv()
        v = self.s3[s.x].astype(f32) + self.r4[0].astype(f32)
        self.total[s.c, s.y * s.nz + s.z] = v.astype(bf16)
        for k in range(1, nz):
            self.back_z(k).start()

    def six(self):
        for k in range(1, self.s.nz):
            self.from_back_z(k).wait_recv()
        self.back_y(self.s.y).start()

    def seven(self):
        self.back_y(1 - self.s.y).wait_recv()
        self.back_core(self.s.c).start()

    def end(self):
        s = self.s
        self.back_core(1 - s.c).wait_recv()
        out = pltpu.make_async_copy(self.total, self.result, self.out.at[0])
        out.start()
        out.wait()
        self.to_core().wait_send()
        self.to_x().wait_send()
        self.to_y().wait_send()
        for k in range(1, s.nz):
            self.to_z(k).wait_send()
            self.back_z(k).wait_send()
        self.back_y(s.y).wait_send()
        self.back_core(s.c).wait_send()

    def actions(self):
        return [(f,) for f in (self.one, self.two, self.three, self.four, self.five, self.six, self.seven, self.end)]


def any_specs(n):
    return [pl.BlockSpec(memory_space=pl.ANY)] * n


def gathered(nz, arrays):
    return [jax.ShapeDtypeStruct((2, 2, 2, nz) + a.shape, a.dtype) for a in arrays]


class Steps:
    def __init__(self, actions):
        self.actions = list(actions)

    def take(self, count):
        out, self.actions = self.actions[:count], self.actions[count:]
        return out

    @staticmethod
    def do(actions):
        for action in actions:
            action[0](*action[1:])

    def step(self, count):
        self.do(self.take(count))

    def rest(self):
        self.step(len(self.actions))

    def until(self, part):
        ends = [k for k, action in enumerate(self.actions) if action[0].__name__ == "end" and action[1] == part]
        if ends:
            self.step(ends[0] + 1)

    def within(self, first, last, *counts):
        plan = [(t, [self.take(count) for count in counts]) for t in range(first, last)]

        def point(k):
            def run(i):
                for t, lists in plan:
                    if lists[k]:
                        pl.when(i == t)(partial(self.do, lists[k]))
            return run
        return [point(k) for k in range(len(counts))]


def qkv_kernel(nh, tm, x_ref, w_ref, at_ref, b_ref, bias_ref, vec_ref, aid_ref, pic_ref, out_ref, n1_ref, h_ref):
    p = pl.program_id(0)
    j = pl.program_id(1)
    tokens = x_ref.shape[0]

    @pl.when((p == 0) & (j == 0))
    def _():
        def norm_step(i, c):
            rows = pl.ds(i * tm, tm)
            nhat, _ = norm_parts(x_ref[rows, :].astype(f32))
            n1_ref[rows, :] = (nhat * vec_ref[4:5, :] + vec_ref[5:6, :]).astype(bf16)
            return c
        lax.fori_loop(0, tokens // tm, norm_step, 0)

    @pl.when(j == 0)
    def _():
        def hidden_step(i, c):
            rows = pl.ds(i * tm, tm)
            h = nt(n1_ref[rows, :], at_ref[0]) * column_mask(aid_ref[rows, :])
            h_ref[0, rows, :] = h.astype(bf16)
            return c
        lax.fori_loop(0, tokens // tm, hidden_step, 0)

    def step(i, c):
        rows = pl.ds(i * tm, tm)
        y = nn(n1_ref[rows, :], w_ref[0, 0])
        y = y + 0.5 * nn(h_ref[0, rows, :], b_ref[0, 0]) + bias_ref[0, 0]
        slot = lane_ids(tm) - HEAD_DIM
        pic = pic_ref[rows, :]
        same = slot == pic
        in_slots = (slot >= 0) & (slot < 16)
        q_aug = jnp.where(same, 1.0, 0.0)
        k_aug = jnp.where(in_slots & jnp.logical_not(same), -BIG, 0.0)
        v_aug = jnp.where((slot == 0) | (slot == 1), 1.0, 0.0)
        aug = jnp.where(p == 0, q_aug, jnp.where(p == 1, k_aug, v_aug))[:, HEAD_DIM:]
        for h in range(nh):
            head = y[:, h * HEAD_DIM:(h + 1) * HEAD_DIM]
            out_ref[0, h, rows, :HEAD_DIM] = head.astype(bf16)
            out_ref[0, h, rows, HEAD_DIM:] = aug.astype(bf16)
        return c
    lax.fori_loop(0, tokens // tm, step, 0)


def qkv_call(x, w, at, bq, bias, vec, aid, pic):
    tokens, d = x.shape
    s = w.shape[1]
    nh = HEADS // s
    tm = min(256, tokens)
    return pl.pallas_call(
        partial(qkv_kernel, nh, tm),
        grid=(3, s),
        in_specs=[
            pl.BlockSpec((tokens, d), lambda p, j: (0, 0)),
            pl.BlockSpec((1, 1, d, d // s), lambda p, j: (p, j, 0, 0)),
            pl.BlockSpec((1, LORA, d), lambda p, j: (p, 0, 0)),
            pl.BlockSpec((1, 1, LORA, nh * HEAD_DIM), lambda p, j: (p, j, 0, 0)),
            pl.BlockSpec((1, 1, 1, nh * HEAD_DIM), lambda p, j: (p, j, 0, 0)),
            pl.BlockSpec(vec.shape, lambda p, j: (0, 0)),
            pl.BlockSpec((tokens, 1), lambda p, j: (0, 0)),
            pl.BlockSpec((tokens, 1), lambda p, j: (0, 0)),
        ],
        out_specs=[
            pl.BlockSpec((1, nh, tokens, LANES), lambda p, j: (p, j, 0, 0)),
            pl.BlockSpec((tokens, d), lambda p, j: (0, 0)),
            pl.BlockSpec((1, tokens, LORA), lambda p, j: (p, 0, 0)),
        ],
        out_shape=[
            jax.ShapeDtypeStruct((3, HEADS, tokens, LANES), bf16),
            jax.ShapeDtypeStruct((tokens, d), bf16),
            jax.ShapeDtypeStruct((3, tokens, LORA), bf16),
        ],
        compiler_params=pltpu.CompilerParams(vmem_limit_bytes=VMEM),
        name="qkv",
    )(x, w, at, bq, bias, vec, aid, pic)


def attn_fwd_kernel(tq, q_ref, k_ref, v_ref, p_ref, o_ref):
    for i in range(q_ref.shape[2] // tq):
        rows = pl.ds(i * tq, tq)
        s = nt(q_ref[0, 0, rows, :], k_ref[0, 0])
        top = jnp.max(s, axis=-1, keepdims=True)
        p = jnp.exp2((s - top) * (SCALE * LOG2E)).astype(bf16)
        o = nn(p, v_ref[0, 0])
        inv = 1.0 / o[:, HEAD_DIM:HEAD_DIM + 1]
        p_ref[0, rows, :] = (p.astype(f32) * inv).astype(bf16)
        o_ref[0, rows, :] = (o * inv).astype(bf16)


def attn_fwd_call(qkv, kv, off):
    tokens, keys = qkv.shape[2], kv.shape[2]
    tq = min(512, tokens)
    return pl.pallas_call(
        partial(attn_fwd_kernel, tq),
        grid=(HEADS,),
        in_specs=[
            pl.BlockSpec((1, 1, tokens, LANES), lambda h: (0, h, 0, 0)),
            pl.BlockSpec((1, 1, keys, LANES), lambda h: (off, h, 0, 0)),
            pl.BlockSpec((1, 1, keys, LANES), lambda h: (off + 1, h, 0, 0)),
        ],
        out_specs=[
            pl.BlockSpec((1, tokens, keys), lambda h: (h, 0, 0)),
            pl.BlockSpec((1, tokens, LANES), lambda h: (h, 0, 0)),
        ],
        out_shape=[
            jax.ShapeDtypeStruct((HEADS, tokens, keys), bf16),
            jax.ShapeDtypeStruct((HEADS, tokens, LANES), bf16),
        ],
        compiler_params=pltpu.CompilerParams(vmem_limit_bytes=VMEM),
        name="attn_fwd",
    )(qkv, kv, kv)


def attn_bwd_kernel(tq, q_ref, k_ref, v_ref, p_ref, o_ref, do_ref, dq_ref, dk_ref, dv_ref, ds_ref, da_ref):
    for i in range(q_ref.shape[2] // tq):
        rows = pl.ds(i * tq, tq)
        lane = lane_ids(tq)
        do = jnp.where(lane < HEAD_DIM, do_ref[0, rows, :].astype(f32), 0.0)
        delta = jnp.sum(do * o_ref[0, rows, :].astype(f32), axis=-1, keepdims=True)
        hi = delta.astype(bf16).astype(f32)
        do = jnp.where(lane == HEAD_DIM, -hi, jnp.where(lane == HEAD_DIM + 1, hi - delta, do)).astype(bf16)
        da_ref[rows, :] = do
        dp = nt(do, v_ref[0, 0])
        ds = (p_ref[0, rows, :].astype(f32) * dp).astype(bf16)
        ds_ref[rows, :] = ds
        dq_ref[0, rows, :] = (nn(ds, k_ref[0, 0]) * SCALE).astype(bf16)
    dv_ref[0] = nn(da_ref[...].T, p_ref[0]).T.astype(bf16)
    dk_ref[0] = (nn(q_ref[0, 0].T, ds_ref[...]).T * SCALE).astype(bf16)


def attn_bwd_call(qkv, kv, off, probs, out, d_out):
    tokens, keys = qkv.shape[2], kv.shape[2]
    tq = min(256, tokens)
    return pl.pallas_call(
        partial(attn_bwd_kernel, tq),
        grid=(HEADS,),
        in_specs=[
            pl.BlockSpec((1, 1, tokens, LANES), lambda h: (0, h, 0, 0)),
            pl.BlockSpec((1, 1, keys, LANES), lambda h: (off, h, 0, 0)),
            pl.BlockSpec((1, 1, keys, LANES), lambda h: (off + 1, h, 0, 0)),
            pl.BlockSpec((1, tokens, keys), lambda h: (h, 0, 0)),
            pl.BlockSpec((1, tokens, LANES), lambda h: (h, 0, 0)),
            pl.BlockSpec((1, tokens, LANES), lambda h: (h, 0, 0)),
        ],
        out_specs=[
            pl.BlockSpec((1, tokens, LANES), lambda h: (h, 0, 0)),
            pl.BlockSpec((1, keys, LANES), lambda h: (h, 0, 0)),
            pl.BlockSpec((1, keys, LANES), lambda h: (h, 0, 0)),
        ],
        out_shape=[
            jax.ShapeDtypeStruct((HEADS, tokens, LANES), bf16),
            jax.ShapeDtypeStruct((HEADS, keys, LANES), bf16),
            jax.ShapeDtypeStruct((HEADS, keys, LANES), bf16),
        ],
        scratch_shapes=[pltpu.VMEM((tokens, keys), bf16), pltpu.VMEM((tokens, LANES), bf16)],
        compiler_params=pltpu.CompilerParams(vmem_limit_bytes=VMEM),
        name="attn_bwd",
    )(qkv, kv, kv, probs, out, d_out)


def gelu_parts(z):
    c = 0.7978845608028654
    z2 = z * z
    t = jnp.tanh(z * (c + (c * 0.044715) * z2))
    half = 0.5 * (1.0 + t)
    g = z * half
    dg = half + 0.5 * z * (1.0 - t * t) * (c + (3 * c * 0.044715) * z2)
    return g, dg


def mid_work(s, cuts, run, ready, part, take, weights, load, save, wo_load, bufs):
    (aid_ref, ab_ref, ff_ref, bup_ref, vec_ref, pack_ref, obuf, xbuf, cotbuf, dybuf, wobuf, ocat, n2buf, mid, acc, dn2,
     hidden, wofull, ubuf, dbuf, ga, gb, wsem, go) = bufs
    tokens, d = xbuf.shape
    ds = d // s
    bo, bd, gain2, shift2 = vec_ref[2:3, :], vec_ref[3:4, :], vec_ref[6:7, :], vec_ref[7:8, :]
    at_o, at_u, b_o, b_d = (ab_ref.at[k] for k in range(4))
    ta, tm = min(256, tokens), min(512, tokens)
    chunks = [(c, j) for c in range(len(cuts)) for j in range(s)]

    def slot_of(buf, k, w):
        return buf.at[(k % 2,) + (slice(None),) * (len(buf.shape) - 2) + (pl.ds(0, w),)] if w < buf.shape[-1] else buf.at[k % 2]

    def fetch(k):
        c, j = chunks[k]
        for m, (ref, buf) in enumerate(((weights[2 * c], ubuf), (weights[2 * c + 1], dbuf))):
            yield take(ref, j, slot_of(buf, k, cuts[c][1]), wsem.at[k % 2, m])

    def begin(k):
        for start, _ in fetch(k):
            start()

    for start, _ in wo_load:
        start()
    for i in range(tokens // ta):
        for copy in load(i):
            copy.start()
    if ready:
        begin(0)
    for _, done in wo_load:
        done()
    run.step(2)

    wofull[...] = jnp.concatenate([wobuf[j].reshape(d, ds) for j in range(s)], axis=1)

    [serve] = run.within(1, tokens // ta, BEFORE)

    def before(i, carry):
        rows = pl.ds(i * ta, ta)
        serve(i)
        for copy in load(i):
            copy.wait()
        mask = column_mask(aid_ref[rows, :])
        for h in range(HEADS):
            ocat[rows, h * HEAD_DIM:(h + 1) * HEAD_DIM] = obuf[h, rows, :HEAD_DIM]
        o = ocat[rows, :]
        h_o = (nt(o, at_o[...]) * mask).astype(bf16)
        value = xbuf[rows, :].astype(f32) + nn(o, wofull[...]) + 0.5 * nn(h_o, b_o[...]) + bo
        mid[rows, :] = value
        nh2, _ = norm_parts(value)
        n2 = (nh2 * gain2 + shift2).astype(bf16)
        n2buf[rows, :d] = n2
        dy = jnp.where(aid_ref[rows, :] >= 0, cotbuf[rows, :], jnp.zeros((ta, d), bf16))
        dybuf[rows, :d] = dy
        hidden[rows, :] = h_o
        n2buf[rows, d:] = (0.5 * (nt(n2, at_u[...]) * mask).astype(bf16).astype(f32)).astype(bf16)
        dybuf[rows, d:] = (0.5 * nt(dy, b_d[...]) * mask).astype(bf16)
        return carry
    lax.fori_loop(0, tokens // ta, before, 0)

    for k, (c, j) in enumerate(chunks):
        start, w = cuts[c]
        if k == 0 and not ready:
            run.until(part(0))
            begin(0)
        late = k + 1 < len(chunks) and chunks[k + 1][0] >= ready and chunks[k + 1][1] == 0
        if k + 1 < len(chunks) and not late:
            begin(k + 1)
        for _, done in fetch(k):
            done()
        cols = slice(start, start + w)

        [serve] = run.within(1, tokens // tm, CHUNK)

        def chunk(i, carry, k=k, j=j, w=w, cols=cols, slot=k % 2, serve=serve):
            rows = pl.ds(i * tm, tm)
            serve(i)
            wu = jnp.concatenate([slot_of(ubuf, slot, w)[...].reshape(d, w), ff_ref[1, j, :, cols]])
            wd = jnp.concatenate([slot_of(dbuf, slot, w)[...].reshape(d, w), ff_ref[0, j, :, cols]])
            z = nn(n2buf[rows, :], wu) + bup_ref[j, :, cols]
            g, dgelu = gelu_parts(z)
            g = g.astype(bf16)
            dg = nn(dybuf[rows, :], wd).astype(bf16)
            dz = (dg.astype(f32) * dgelu).astype(bf16)
            if k == 0:
                acc[rows, :] = nt(g, wd)
                dn2[rows, :] = nt(dz, wu)
            else:
                acc[rows, :] += nt(g, wd)
                dn2[rows, :] += nt(dz, wu)
            more_a, more_b = tn(dybuf[rows, d:], g), tn(n2buf[rows, d:], dz)

            @pl.when(i == 0)
            def _():
                ga[:, :w] = more_a
                gb[:, :w] = more_b

            @pl.when(i > 0)
            def _():
                ga[:, :w] += more_a
                gb[:, :w] += more_b
            return carry
        lax.fori_loop(0, tokens // tm, chunk, 0)
        at = 2 * d + j * ff_ref.shape[3] + start
        pack_ref[0, :, at:at + w] = ga[:, :w].astype(bf16)
        pack_ref[1, :, at:at + w] = gb[:, :w].astype(bf16)
        run.step(CHUNK)
        if late:
            run.until(part(chunks[k + 1][0]))
            begin(k + 1)

    run.rest()

    go[...] = jnp.zeros_like(go)

    def after(i, carry):
        rows = pl.ds(i * ta, ta)
        mask = column_mask(aid_ref[rows, :])
        h_d = (acc[rows, d:] * mask).astype(bf16)
        xbuf[rows, :] = (mid[rows, :] + bd + acc[rows, :d] + 0.5 * nn(h_d, b_d[...])).astype(bf16)
        dh_u = (0.5 * dn2[rows, d:] * mask).astype(bf16)
        nh2, r2 = norm_parts(mid[rows, :])
        dy = dybuf[rows, :d]
        dmid = dy.astype(f32) + norm_back(dn2[rows, :d] + nn(dh_u, at_u[...]), gain2, nh2, r2)
        mid[rows, :] = dmid
        db = dmid.astype(bf16)
        dh_o = (0.5 * nt(db, b_o[...]) * mask).astype(bf16)
        do = (nt(db, wofull[...]) + nn(dh_o, at_o[...])).astype(bf16)
        go[0] += tn(dh_o, ocat[rows, :])
        go[1] += 0.5 * tn(hidden[rows, :], db)
        go[2] += tn(dh_u, n2buf[rows, :d])
        go[3] += 0.5 * tn(h_d, dy)
        for h in range(HEADS):
            obuf[h, rows, :HEAD_DIM] = do[:, h * HEAD_DIM:(h + 1) * HEAD_DIM]
        for copy in save(i):
            copy.start()
        return carry
    lax.fori_loop(0, tokens // ta, after, 0)
    for c, order in enumerate(((0, 2), (1, 3))):
        for k, which in enumerate(order):
            pack_ref[c, :, k * d:(k + 1) * d] = go[which].astype(bf16)
    for i in range(tokens // ta):
        for copy in save(i):
            copy.wait()


def mid_kernel(s, n, cuts, *refs):
    (oaug_ref, x_ref, cot_ref, aid_ref, wo_ref, ab_ref, ff_ref, bup_ref, vec_ref) = refs[:9]
    weights, refs = refs[9:9 + 2 * len(cuts)], refs[9 + 2 * len(cuts):]
    mixed_ref, dmid_ref, do_ref, pack_ref, obuf, xbuf, isem, osem, lsem, *bufs = refs
    cotbuf, mid = bufs[0], bufs[5]
    ta = min(256, xbuf.shape[0])

    def load(i):
        rows = pl.ds(i * ta, ta)
        for k, (src, dst) in enumerate(((oaug_ref.at[:, rows], obuf.at[:, rows]), (x_ref.at[rows], xbuf.at[rows]),
                                        (cot_ref.at[rows], cotbuf.at[rows]))):
            yield pltpu.make_async_copy(src, dst, isem.at[i, k])

    def save(i):
        rows = pl.ds(i * ta, ta)
        for k, (src, dst) in enumerate(((xbuf.at[rows], mixed_ref.at[rows]), (mid.at[rows], dmid_ref.at[rows]),
                                        (obuf.at[:, rows], do_ref.at[:, rows]))):
            yield pltpu.make_async_copy(src, dst, osem.at[i, k])

    def take(ref, j, dst, sem):
        return one(ref.at[pl.ds(j * n, n)], dst, sem)

    def one(src, dst, sem):
        return (lambda: pltpu.make_async_copy(src, dst, sem).start(),
                lambda: pltpu.make_async_copy(src, dst, sem).wait())

    mid_work(s, cuts, Steps([]), len(cuts), None, take, weights, load, save, [one(wo_ref, bufs[2], lsem.at[0])],
             [aid_ref, ab_ref, ff_ref, bup_ref, vec_ref, pack_ref, obuf, xbuf] + bufs)


def mid_bufs(s, pieces, tokens, d, widest):
    def v(*shape, dtype=bf16):
        return pltpu.VMEM(shape, dtype)

    return [
        v(tokens, d), v(tokens, d + LORA), v(s, d, d // s), v(tokens, d), v(tokens, d + LORA),
        v(tokens, d, dtype=f32), v(tokens, d + LORA, dtype=f32), v(tokens, d + LORA, dtype=f32),
        v(tokens, LORA), v(d, d), v(2, pieces, d // pieces, widest), v(2, pieces, d // pieces, widest),
        v(LORA, widest, dtype=f32), v(LORA, widest, dtype=f32), pltpu.SemaphoreType.DMA((2, 2)),
        v(4, LORA, d, dtype=f32),
    ]


def mid_call(oaug, x, cot, aid, wo, weights, cuts, ab, ff, bup, vec):
    tokens, d = x.shape
    s = wo.shape[0]
    pieces = weights[0].shape[0] // s
    tiles = tokens // min(256, tokens)
    full = pl.BlockSpec(memory_space=pltpu.VMEM)
    dma = pltpu.SemaphoreType.DMA
    return pl.pallas_call(
        partial(mid_kernel, s, pieces, cuts),
        in_specs=any_specs(3) + [full] + any_specs(1) + [full] * 4 + any_specs(len(weights)),
        out_specs=any_specs(3) + [full],
        out_shape=[
            jax.ShapeDtypeStruct((tokens, d), bf16),
            jax.ShapeDtypeStruct((tokens, d), f32),
            jax.ShapeDtypeStruct((HEADS, tokens, LANES), bf16),
            jax.ShapeDtypeStruct((2, LORA, 2 * d + s * ff.shape[3]), bf16),
        ],
        scratch_shapes=[
            pltpu.VMEM((HEADS, tokens, LANES), bf16), pltpu.VMEM((tokens, d), bf16),
            dma((tiles, 3)), dma((tiles, 3)), dma((1,)),
        ] + mid_bufs(s, pieces, tokens, d, max(w for _, w in cuts)),
        compiler_params=pltpu.CompilerParams(vmem_limit_bytes=VMEM),
        name="mid",
    )(oaug, x, cot, aid, wo, ab, ff, bup, vec, *weights)


def forward_kernel(nz, cuts, na, *refs):
    shards, (tokens, vec, cot, aid_ref, pic_ref), refs = refs[:na], refs[na:na + 5], refs[na + 5:]
    wholes, refs = refs[:na], refs[na:]
    (x_out, vec_out, a_out, b_out, qkv_out, n1_out, h_out, probs_out, o_out, cot_row, mixed_ref, dmid_ref, do_ref,
     pack_ref), refs = refs[:14], refs[14:]
    (xbuf, vbuf, obuf, ab, ff, vecs, bups, sems, wsem, osem, psem, csems, isem, ssem, *gather_refs) = refs
    n, d = nz * 4, xbuf.shape[2]
    half = xbuf.shape[1]
    count, tm = 2 * half, 512
    ds, fslot = shards[1].shape[1], ff.shape[3]
    nh = ds // HEAD_DIM
    each = LORA // 2
    spot = Spot(nz)
    spot.barrier()
    gather = Gather(spot, shards, wholes, *gather_refs)
    run = Steps(gather.actions())
    swap = Swap(spot, cot, cot_row, csems)
    vec_here = pltpu.make_async_copy(vec, vbuf.at[spot.x], sems.at[0])
    vec_there = remote(vec, vbuf.at[spot.x], sems.at[1], sems.at[2], spot.xn)
    row_here = pltpu.make_async_copy(tokens.at[spot.x], xbuf.at[spot.x], sems.at[3])
    row_there = remote(tokens.at[1 - spot.x], xbuf.at[spot.x], sems.at[4], sems.at[5], spot.xn)

    def first(nbuf, widebuf, wbuf, abuf, bbuf, n1, hbuf, heads, pbuf):
        vec_here.start()
        vec_there.start()
        run.step(2)
        row_here.start()
        row_there.start()
        run.step(6)
        vec_here.wait()
        got = vbuf.at[1 - spot.x]
        remote(got, got, sems.at[1], sems.at[2], spot.xn).wait_recv()
        row_here.wait()
        got = xbuf.at[1 - spot.x]
        remote(got, got, sems.at[4], sems.at[5], spot.xn).wait_recv()
        for j in range(2):
            vecs[:, j * ds:(j + 1) * ds] = vbuf[j, :8, :ds].astype(f32)
            bups[j] = vbuf[j, 8:9, :].astype(f32)
        gain, shift = vecs[4:5, :], vecs[5:6, :]
        keep = [pltpu.make_async_copy(xbuf, x_out, osem.at[0]), pltpu.make_async_copy(vecs, vec_out, osem.at[1])]
        for copy in keep:
            copy.start()
        for part in range(2):
            def norm_step(i, carry, part=part):
                nhat, _ = norm_parts(xbuf[part, pl.ds(i * 256, 256), :].astype(f32))
                n1[pl.ds(part * half + i * 256, 256), :d] = (nhat * gain + shift).astype(bf16)
                return carry
            lax.fori_loop(0, half // 256, norm_step, 0)
            run.step(2)
        keep.append(pltpu.make_async_copy(n1.at[:, pl.ds(0, d)], n1_out, osem.at[2]))
        keep[-1].start()

        run.until(0)
        for c in range(2):
            pltpu.make_async_copy(wholes[0].at[c], nbuf.at[:, c], sems.at[6]).start()
        pltpu.make_async_copy(nbuf, nbuf, sems.at[6]).wait()
        for j in range(2):
            rows = slice(j * each, (j + 1) * each)
            one = nbuf[j].reshape(10 * each, d)
            for m in range(3):
                abuf[m, rows, :] = one[m * each:(m + 1) * each]
                for i in range(2):
                    bbuf[m, i, rows, :] = one[(5 + m) * each:(6 + m) * each, i * ds:(i + 1) * ds]
            for k, m in enumerate((3, 4, 8, 9)):
                ab[k, rows, :] = one[m * each:(m + 1) * each]

        for copy in (pltpu.make_async_copy(abuf, a_out, osem.at[11]), pltpu.make_async_copy(bbuf, b_out, osem.at[12])):
            keep.append(copy)
            copy.start()

        def fetch(p, j):
            return pull(nz, wholes[1 + p], j, wbuf.at[j], wsem.at[j])

        for p in range(3):
            run.until(1 + p)
            for j in range(2):
                fetch(p, j)[0]()
            for i in range(count // tm):
                rows = pl.ds(i * tm, tm)
                h = (nt(n1[rows, :d], abuf[p]) * column_mask(aid_ref[rows, :])).astype(bf16)
                hbuf[p, rows, :] = h
                n1[rows, d:] = (0.5 * h.astype(f32)).astype(bf16)
            for j in range(2):
                fetch(p, j)[1]()
                bias = vbuf[j, p // 2:p // 2 + 1, :ds].astype(f32) if p != 1 else 0.0

                [serve] = run.within(1, count // tm, 2)

                def step(i, carry, p=p, j=j, bias=bias, serve=serve):
                    rows = pl.ds(i * tm, tm)
                    serve(i)
                    w = jnp.concatenate([wbuf[j].reshape(d, ds), bbuf[p, j]])
                    y = (nn(n1[rows, :], w) + bias).astype(bf16)
                    place = lax.broadcasted_iota(jnp.int32, (tm, LANES), 1) - HEAD_DIM
                    same = place == pic_ref[rows, :]
                    if p == 0:
                        extra = jnp.where(same, 1.0, 0.0)
                    elif p == 1:
                        extra = jnp.where((place >= 0) & (place < 16) & jnp.logical_not(same), -BIG, 0.0)
                    else:
                        extra = jnp.where((place == 0) | (place == 1), 1.0, 0.0)
                    extra = extra.astype(bf16)[:, HEAD_DIM:]
                    for h in range(nh):
                        heads[p, j * nh + h, rows, :HEAD_DIM] = y[:, h * HEAD_DIM:(h + 1) * HEAD_DIM]
                        heads[p, j * nh + h, rows, HEAD_DIM:] = extra
                    return carry
                lax.fori_loop(0, count // tm, step, 0)
                which = pl.ds(j * nh, nh)
                keep.append(pltpu.make_async_copy(
                    heads.at[p, which], qkv_out.at[p, which], osem.at[4 + 2 * p + j]))
                keep[-1].start()
                run.step(1)
        keep.append(pltpu.make_async_copy(hbuf, h_out, osem.at[3]))
        keep[-1].start()
        swap.start()

        def probs_copy(h):
            return pltpu.make_async_copy(pbuf.at[h % 2], probs_out.at[h], psem.at[h % 2])

        serve, again = run.within(0, HEADS, *HEAD)

        def head(h, carry):
            serve(h)

            @pl.when(h >= 2)
            def _():
                probs_copy(h - 2).wait()
            for i in range(count // tm):
                rows = pl.ds(i * tm, tm)
                s = nt(heads[0, h, rows, :], heads[1, h])
                top = jnp.max(s, axis=-1, keepdims=True)
                p = jnp.exp2((s - top) * (SCALE * LOG2E)).astype(bf16)
                o = nn(p, heads[2, h])
                inv = 1.0 / o[:, HEAD_DIM:HEAD_DIM + 1]
                pbuf[h % 2, rows, :] = (p.astype(f32) * inv).astype(bf16)
                obuf[h, rows, :] = (o * inv).astype(bf16)
            again(h)
            probs_copy(h).start()
            return carry
        lax.fori_loop(0, HEADS, head, 0)
        keep.append(pltpu.make_async_copy(obuf, o_out, osem.at[10]))
        keep[-1].start()
        run.until(5)
        for c in range(2):
            pltpu.make_async_copy(wholes[5].at[c], widebuf.at[:, c], sems.at[7]).start()
        pltpu.make_async_copy(widebuf, widebuf, sems.at[7]).wait()
        for j in range(2):
            one = widebuf[j].reshape(LORA, 2 * fslot)
            for m in range(2):
                for i in range(2):
                    ff[m, i, j * each:(j + 1) * each, :] = one[m * each:(m + 1) * each, i * fslot:(i + 1) * fslot]
        for h in range(HEADS - 2, HEADS):
            probs_copy(h).wait()
        for copy in keep:
            copy.wait()

    def v(*shape):
        return pltpu.VMEM(shape, bf16)

    pl.run_scoped(
        first, v(2, 2, 2, nz, *shards[0].shape), v(2, 2, 2, nz, *shards[5].shape), v(2, nz, 2, 2, *shards[1].shape),
        v(3, LORA, d),
        v(3, 2, LORA, ds), v(count, d + LORA), v(3, count, LORA), v(3, HEADS, count, LANES), v(2, count, count))
    swap.end()

    def second(wobuf3, *bufs):
        cotbuf, mid = bufs[0], bufs[4]
        bufs = bufs[:2] + (wobuf3,) + bufs[2:]

        def load(i):
            yield pltpu.make_async_copy(cot_row.at[i * 256 // half, pl.ds(i * 256 % half, 256)],
                                        cotbuf.at[pl.ds(i * 256, 256)], isem.at[i, 0])

        def save(i):
            rows = pl.ds(i * 256, 256)
            inner = pl.ds(i * 256 % half, 256)
            for k, (src, dst) in enumerate((
                    (xrow.at[rows], mixed_ref.at[i * 256 // half, inner]), (mid.at[rows], dmid_ref.at[rows]),
                    (obuf.at[:, rows], do_ref.at[:, rows]))):
                yield pltpu.make_async_copy(src, dst, ssem.at[i, k])

        mid_work(2, cuts, run, 0, lambda c: 7 + 2 * c, partial(pull, nz), wholes[6:], load, save,
                 [pull(nz, wholes[4], j, wobuf3.at[j], isem.at[j, 1]) for j in range(2)],
                 [aid_ref, ab, ff, bups, vecs, pack_ref, obuf, xrow] + list(bufs))

    xrow = xbuf.reshape(count, d)
    bufs = mid_bufs(2, n, count, d, max(w for _, w in cuts))
    bufs[2] = v(2, nz, 2, 2, d // n, ds)
    bufs[10] = bufs[11] = v(2, nz, 2, 2, d // n, max(w for _, w in cuts))
    pl.run_scoped(second, bufs[2], *bufs[:2], *bufs[3:])
    vec_there.wait_send()
    row_there.wait_send()


def forward_call(nz, cuts, shards, tokens, vec, cot, aid, pic):
    na = len(shards)
    dma = pltpu.SemaphoreType.DMA
    half, d = tokens.shape[1], tokens.shape[2]
    count, fslot = 2 * half, shards[5].shape[1] // 2
    tiles = count // 256
    full = pl.BlockSpec(memory_space=pltpu.VMEM)

    def v(*shape, dtype=bf16):
        return pltpu.VMEM(shape, dtype)

    def out(*shape, dtype=bf16):
        return jax.ShapeDtypeStruct(shape, dtype)

    return pl.pallas_call(
        partial(forward_kernel, nz, cuts, na),
        in_specs=any_specs(na + 3) + [full, full],
        out_specs=any_specs(na + 13) + [full],
        out_shape=gathered(nz, shards) + [
            out(*tokens.shape), out(8, d, dtype=f32), out(3, LORA, d), out(3, 2, LORA, shards[1].shape[1]),
            out(3, HEADS, count, LANES), out(count, d), out(3, count, LORA), out(HEADS, count, count), out(HEADS, count, LANES), out(*tokens.shape), out(*tokens.shape),
            out(count, d, dtype=f32), out(HEADS, count, LANES), out(2, LORA, 2 * d + 2 * fslot)],
        scratch_shapes=[
            v(*tokens.shape), v(2, *vec.shape), v(HEADS, count, LANES), v(4, LORA, d), v(2, 2, LORA, fslot),
            v(8, d, dtype=f32), v(2, 1, fslot, dtype=f32), dma((8,)), dma((2,)), dma((13,)), dma((2,)), dma((3,)),
            dma((tiles, 2)), dma((tiles, 3))] + Gather.scratch(nz, na),
        compiler_params=pltpu.CompilerParams(collective_id=1, has_side_effects=True, vmem_limit_bytes=VMEM),
        name="forward",
    )(*shards, tokens, vec, cot, aid, pic)


def tail_kernel(s, dq_ref, dk_ref, dv_ref, x_ref, n1_ref, h_ref, dmid_ref, aid_ref,
                wq_ref, wk_ref, wv_ref, at_ref, b_ref, vec_ref, out_ref, pack_ref, dy_ref, ga_ref, gb_ref):
    i = pl.program_id(0)
    tm, d = x_ref.shape
    nh = HEADS // s
    ds = d // s
    mask = column_mask(aid_ref[...])

    @pl.when(i == 0)
    def _():
        ga_ref[...] = jnp.zeros_like(ga_ref)
        gb_ref[...] = jnp.zeros_like(gb_ref)

    n1 = n1_ref[...]
    dn = jnp.zeros((tm, d), f32)
    for p, (src, w_ref) in enumerate(((dq_ref, wq_ref), (dk_ref, wk_ref), (dv_ref, wv_ref))):
        dh = jnp.zeros((tm, LORA), f32)
        for j in range(s):
            for h in range(nh):
                dy_ref[p, j, :, h * HEAD_DIM:(h + 1) * HEAD_DIM] = src[j * nh + h, :, :HEAD_DIM]
            dy = dy_ref[p, j]
            dh = dh + nt(dy, b_ref[p, j])
            dn = dn + nt(dy, w_ref[j])
            gb_ref[p, j] += 0.5 * tn(h_ref[p], dy)
        dh = (0.5 * dh * mask).astype(bf16)
        dn = dn + nn(dh, at_ref[p])
        ga_ref[p] += tn(dh, n1)
    nhat, r = norm_parts(x_ref[...].astype(f32))
    out_ref[...] = dmid_ref[...] + norm_back(dn, vec_ref[4:5, :], nhat, r)

    @pl.when(i == pl.num_programs(0) - 1)
    def _():
        for p in range(3):
            pack_ref[0, :, p * d:(p + 1) * d] = ga_ref[p].astype(bf16)
            for j in range(s):
                at = p * d + j * ds
                pack_ref[1, :, at:at + ds] = gb_ref[p, j].astype(bf16)


def tail_call(dq, dk, dv, x, n1, hid, dmid, aid, wq, wk, wv, at, bq, vec):
    tokens, d = x.shape
    s = wq.shape[0]
    tm = min(256, tokens)
    full = pl.BlockSpec(memory_space=pltpu.VMEM)
    tile = pl.BlockSpec((tm, d), lambda i: (i, 0))
    heads = pl.BlockSpec((HEADS, tm, LANES), lambda i: (0, i, 0))
    return pl.pallas_call(
        partial(tail_kernel, s),
        grid=(tokens // tm,),
        in_specs=[
            heads, heads, heads, tile, tile,
            pl.BlockSpec((3, tm, LORA), lambda i: (0, i, 0)),
            tile,
            pl.BlockSpec((tm, 1), lambda i: (i, 0)),
            full, full, full, full, full, full,
        ],
        out_specs=[tile, full],
        out_shape=[
            jax.ShapeDtypeStruct((tokens, d), f32),
            jax.ShapeDtypeStruct((2, LORA, 3 * d), bf16),
        ],
        scratch_shapes=[
            pltpu.VMEM((3, s, tm, d // s), bf16),
            pltpu.VMEM((3, LORA, d), f32),
            pltpu.VMEM((3, s, LORA, d // s), f32),
        ],
        compiler_params=pltpu.CompilerParams(vmem_limit_bytes=VMEM),
        name="tail",
    )(dq, dk, dv, x, n1, hid, dmid, aid, wq, wk, wv, at, bq, vec)


def backward_kernel(nz, *refs):
    (qkv, probs, o, d_out, x, n1, hid, dmid, wq, wk, wv, mixed, g_mid, a_ref, b_ref, vec_ref, aid_ref) = refs[:17]
    (own_out, got, mid_total, qkv_total, mixed_out), refs = refs[17:22], refs[22:]
    (dy, dh, w, g_qkv, low, wsem, msem, dsem, lsem, psem, tsem, csem, *sums) = refs
    n, d = 4 * nz, x.shape[2]
    half = x.shape[1]
    count, ds = 2 * half, dy.shape[3]
    nh = HEADS // 2
    spot = Spot(nz)
    spot.barrier()
    per = len(sums) // 3
    width = g_mid.shape[4] // 2
    one, two = (Reduce(spot, g_mid.at[:, :, :, :, pl.ds(k * width, width)], mid_total.at[:, :, :, pl.ds(k * width, width)],
                       sums[k * per:(k + 1) * per]) for k in range(2))
    last = Reduce(spot, g_qkv, qkv_total, sums[2 * per:])
    swap = Swap(spot, mixed, mixed_out, msem)
    weights = [pull(nz, src, j, w.at[p, j], wsem.at[p, j])
               for p, src in enumerate((wq, wk, wv)) for j in range(2)]

    one.one()
    two.one()
    swap.start()
    serve = {1: [one.two], 2: [two.two], 6: [one.three], 10: [two.three], 12: [one.four, one.five], 15: [two.four]}

    def first(heads):
        def attention(small, pbuf, dsbuf, dabuf):
            srcs = [qkv.at[0], qkv.at[1], qkv.at[2], o, d_out]

            def loads(h):
                for k, src in enumerate(srcs):
                    yield pltpu.make_async_copy(src.at[h], small.at[h % 2, k], lsem.at[h % 2, k])
                yield pltpu.make_async_copy(probs.at[h], pbuf.at[h % 2], psem.at[h % 2])

            for copy in loads(0):
                copy.start()
            lane = lane_ids(256)

            def head(h, carry):
                for t, acts in serve.items():
                    @pl.when(h == t)
                    def _(acts=acts):
                        for act in acts:
                            act()

                @pl.when(h + 1 < HEADS)
                def _():
                    for copy in loads(h + 1):
                        copy.start()
                for copy in loads(h):
                    copy.wait()
                m = h % 2
                for i in range(count // 256):
                    rows = pl.ds(i * 256, 256)
                    do = jnp.where(lane < HEAD_DIM, small[m, 4, rows, :].astype(f32), 0.0)
                    delta = jnp.sum(do * small[m, 3, rows, :].astype(f32), axis=-1, keepdims=True)
                    hi = delta.astype(bf16).astype(f32)
                    do = jnp.where(lane == HEAD_DIM, -hi, jnp.where(lane == HEAD_DIM + 1, hi - delta, do)).astype(bf16)
                    dabuf[rows, :] = do
                    dp = nt(do, small[m, 2])
                    part = (pbuf[m, rows, :].astype(f32) * dp).astype(bf16)
                    dsbuf[rows, :] = part
                    heads[0, h, rows, :] = (nn(part, small[m, 1]) * SCALE).astype(bf16)
                heads[2, h] = nn(dabuf[...].T, pbuf[m]).T.astype(bf16)
                heads[1, h] = (nn(small[m, 0].T, dsbuf[...]).T * SCALE).astype(bf16)
                return carry
            lax.fori_loop(0, HEADS, head, 0)

        pl.run_scoped(attention, pltpu.VMEM((2, 5, count, LANES), bf16), pltpu.VMEM((2, count, count), bf16),
                      pltpu.VMEM((count, count), bf16), pltpu.VMEM((count, LANES), bf16))

        def adapters(nbuf, hbuf, ga, gb):
            here = [pltpu.make_async_copy(n1, nbuf, csem.at[0]), pltpu.make_async_copy(hid, hbuf, csem.at[1])]
            for copy in here:
                copy.start()
            for start, _ in weights:
                start()
            for copy in here:
                copy.wait()
            later = [[one.six, two.five], [one.seven, two.six], [two.seven]]
            for p in range(3):
                def tile(i, carry, p=p):
                    rows = pl.ds(i * 512, 512)
                    total = jnp.zeros((512, LORA), f32)
                    for j in range(2):
                        for h in range(nh):
                            dy[p, j, rows, h * HEAD_DIM:(h + 1) * HEAD_DIM] = heads[p, j * nh + h, rows, :HEAD_DIM]
                        part = dy[p, j, rows, :]
                        total = total + nt(part, b_ref[p, j])
                        more = 0.5 * tn(hbuf[p, rows, :], part)

                        @pl.when(i == 0)
                        def _(j=j, more=more):
                            gb[j] = more

                        @pl.when(i > 0)
                        def _(j=j, more=more):
                            gb[j] += more
                    grad = (0.5 * total * column_mask(aid_ref[rows, :])).astype(bf16)
                    dh[p, rows, :] = grad
                    more = tn(grad, nbuf[rows, :])

                    @pl.when(i == 0)
                    def _():
                        ga[...] = more

                    @pl.when(i > 0)
                    def _():
                        ga[...] += more
                    return carry
                lax.fori_loop(0, count // 512, tile, 0)
                cols = slice(p * d, (p + 1) * d)
                g_qkv[0, :, :, :, cols] = ga[...].reshape(2, 2 * nz, 8, d).astype(bf16)
                for j in range(2):
                    cols = slice(p * d + j * ds, p * d + (j + 1) * ds)
                    g_qkv[1, :, :, :, cols] = gb[j].reshape(2, 2 * nz, 8, ds).astype(bf16)
                for act in later[p]:
                    act()

        pl.run_scoped(adapters, pltpu.VMEM((count, d), bf16), pltpu.VMEM((3, count, LORA), bf16),
                      pltpu.VMEM((LORA, d), f32), pltpu.VMEM((2, LORA, ds), f32))

    pl.run_scoped(first, pltpu.VMEM((3, HEADS, count, LANES), bf16))
    last.one()

    def second(xbuf, mbuf, obuf):
        def spots(t):
            side = 1 - spot.x if t < 2 else spot.x
            return side, t % 2 * 256

        def loads(t):
            side, inner = spots(t)
            rows = pl.ds(pl.multiple_of(side * half + inner, 256), 256)
            return (pltpu.make_async_copy(x.at[side, pl.ds(inner, 256)], xbuf.at[t % 2], dsem.at[t, 0]),
                    pltpu.make_async_copy(dmid.at[rows], mbuf.at[t % 2], dsem.at[t, 1]))

        def there(t):
            return remote(low.at[t], got.at[pl.ds(t * 256, 256)], tsem.at[t, 0], tsem.at[t, 1], spot.xn)

        def keep(t):
            return pltpu.make_async_copy(obuf.at[t - 2], own_out.at[pl.ds((t - 2) * 256, 256)], tsem.at[t, 0])

        for t in range(2):
            for copy in loads(t):
                copy.start()
        for _, done in weights:
            done()
        serve = [[], [last.two], [], [last.three]]
        for t in range(4):
            side, inner = spots(t)
            rows = pl.ds(pl.multiple_of(side * half + inner, 256), 256)
            dn = jnp.zeros((256, d), f32)
            for p in range(3):
                for j in range(2):
                    dn = dn + nt(dy[p, j, rows, :], w[p, j].reshape(d, ds))
                dn = dn + nn(dh[p, rows, :], a_ref[p])
            for copy in loads(t):
                copy.wait()
            nhat, r = norm_parts(xbuf[t % 2].astype(f32))
            value = mbuf[t % 2] + norm_back(dn, vec_ref[4:5, :], nhat, r)
            if t < 2:
                low[t] = value.astype(bf16)
                there(t).start()
                for copy in loads(t + 2):
                    copy.start()
            else:
                obuf[t - 2] = value
                keep(t).start()
            for act in serve[t]:
                act()
        last.four()
        last.five()
        last.six()
        last.seven()
        for t in range(2):
            there(t).wait()
        for t in range(2, 4):
            keep(t).wait()

    pl.run_scoped(second, pltpu.VMEM((2, 256, d), bf16), pltpu.VMEM((2, 256, d), f32), pltpu.VMEM((2, 256, d), f32))
    for reduce in (one, two, last):
        reduce.end()
    swap.end()


def backward_call(nz, qkv, probs, o, d_out, x, n1, hid, dmid, wq, wk, wv, mixed, g_mid, at, bq, vec, aid):
    dma = pltpu.SemaphoreType.DMA
    half, d = x.shape[1], x.shape[2]
    count, ds = 2 * half, wq.shape[-1]
    full = pl.BlockSpec(memory_space=pltpu.VMEM)

    def v(*shape, dtype=bf16):
        return pltpu.VMEM(shape, dtype)

    def out(*shape, dtype=bf16):
        return jax.ShapeDtypeStruct(shape, dtype)

    return pl.pallas_call(
        partial(backward_kernel, nz),
        in_specs=any_specs(12) + [full] * 5,
        out_specs=any_specs(5),
        out_shape=[out(half, d, dtype=f32), out(half, d), out(2, 2 * nz, 8, g_mid.shape[4]), out(2, 2 * nz, 8, 3 * d),
                   out(*mixed.shape)],
        scratch_shapes=[
            v(3, 2, count, ds), v(3, count, LORA), v(3, 2, nz, 2, 2, d // (4 * nz), ds), v(2, 2, 2 * nz, 8, 3 * d),
            v(2, 256, d), dma((3, 2)), dma((3,)), dma((4, 2)), dma((2, 5)), dma((2,)), dma((4, 2)), dma((2,))]
        + Reduce.scratch(nz, g_mid.shape[4] // 2) * 2 + Reduce.scratch(nz, 3 * d),
        compiler_params=pltpu.CompilerParams(collective_id=4, has_side_effects=True, vmem_limit_bytes=VMEM),
        name="backward",
    )(qkv, probs, o, d_out, x, n1, hid, dmid, wq, wk, wv, mixed, g_mid, at, bq, vec, aid)


def rows_of_adapters(a):
    t = jnp.swapaxes(a, -1, -2)
    return t.reshape(*t.shape[:-3], t.shape[-3] * t.shape[-2], t.shape[-1])


def local(tokens, cotangent, lengths, adapter_ids, w_query, w_key, w_value, w_out, w_up, w_down,
          b_query, b_value, b_out, b_up, b_down, gain_one, shift_one, gain_two, shift_two,
          qkv_a, out_a, attn_b, up_a, up_b, down_a, down_b):
    seq = lax.axis_size("seq")
    rows, part_len, d = tokens.shape
    group = seq // rows
    count = rows * part_len
    ds, fs = w_query.shape[1], w_up.shape[1]
    me = lax.axis_index("seq")
    row, chunk = me // group, me % group

    def moves(j):
        return [(a, (a % rows + j) % rows * group + a // rows) for a in range(seq)]

    def send(piece, pairs):
        return piece if all(a == b for a, b in pairs) else lax.ppermute(piece, "seq", pairs)

    def to_row(t):
        out = jnp.zeros((rows, part_len, d), t.dtype)
        for j in range(rows):
            piece = lax.dynamic_index_in_dim(t, (me + j) % rows, 0, False)
            out = lax.dynamic_update_index_in_dim(out, send(piece, moves(j)), (row - j) % rows, 0)
        return out.reshape(count, d)

    def from_row(t, dtype):
        t = t.reshape(rows, part_len, d)
        out = jnp.zeros((rows, part_len, d), dtype)
        for j in range(rows):
            piece = lax.dynamic_index_in_dim(t, (row - j) % rows, 0, False)
            pairs = [(b, a) for a, b in moves(j)]
            if not all(a == b for a, b in pairs):
                piece = piece.astype(bf16)
            got = send(piece, pairs).astype(dtype)
            out = lax.dynamic_update_index_in_dim(out, got, (me + j) % rows, 0)
        return out

    dps = lax.axis_size("dp")
    nz = dps // 4
    fast = seq == 2 and rows == 2 and nz == 4
    slot, fslot = up128(ds), up128(fs)
    step = up128(-(-fslot // max(round(fslot / 768), 1)))
    cuts = [(a, min(step, fslot - a)) for a in range(0, fslot, step)]

    def wide_to(t, n):
        return jnp.pad(t, ((0, 0), (0, n - t.shape[1])))

    wu_part, wd_part = wide_to(w_up, fslot), wide_to(w_down.T, fslot)
    ff_parts = [t[:, a:a + n] for a, n in cuts for t in (wu_part, wd_part)]
    narrow = jnp.concatenate([
        rows_of_adapters(qkv_a), rows_of_adapters(out_a)[None], rows_of_adapters(up_a)[None],
        attn_b.reshape(4, -1, d), down_b.reshape(1, -1, d)])
    wide = jnp.stack([rows_of_adapters(down_a), up_b.reshape(-1, up_b.shape[-1])])
    vec_part = jnp.stack([b_query, b_value, b_out, b_down, gain_one, shift_one, gain_two, shift_two])
    teams = [[g * group + c for c in range(group)] for g in range(rows)]

    my_len = lax.dynamic_index_in_dim(lengths, row, 0, False)
    my_ids = lax.dynamic_index_in_dim(adapter_ids, row, 0, False)
    slots = jnp.arange(my_len.shape[0], dtype=jnp.int32)
    ends = jnp.sum(jnp.where(slots[None, :] <= slots[:, None], my_len[None, :], 0), axis=1)
    pos = chunk * count + jnp.arange(count, dtype=jnp.int32)
    pic = jnp.sum((pos[:, None] >= ends[None, :]).astype(jnp.int32), axis=1, keepdims=True)
    aid = jnp.sum(jnp.where(pic == slots[None, :], my_ids[None, :], 0), axis=1, keepdims=True)
    aid = jnp.where(pos[:, None] < ends[-1], aid, -1)

    def from_halves(t):
        return jnp.swapaxes(t, 0, 1).reshape(t.shape[1], -1, t.shape[3])

    if fast:
        me_dp = lax.axis_index("dp")
        place = (me_dp % 2 * 2 + me_dp // 2 % 2) * nz + me_dp // 4

        def share(t):
            flat = t.reshape(-1, t.shape[-1])
            n = flat.shape[0] // dps
            return lax.dynamic_slice_in_dim(flat, place * n, n, 0)

        small = jnp.concatenate([wide_to(vec_part, fslot), wide_to(b_up[None], fslot), jnp.zeros((7, fslot), bf16)])
        wide = jnp.pad(wide.reshape(2, -1, seq, fs), ((0, 0), (0, 0), (0, 0), (0, fslot - fs)))
        wide = wide.reshape(2, -1, seq * fslot)
        narrow, wq, wk, wv, *got = forward_call(
            nz, cuts, [share(narrow), w_query, w_key, w_value, w_out, share(wide)] + ff_parts,
            tokens, small, cotangent, aid, pic)
        x, vec, at, bq, qkv, n1, hid, probs, oaug, _, mixed, dmid, d_out, g_mid = got[2 + len(ff_parts):]
    else:
        def gather_all(shard):
            full = lax.all_gather(shard, ("seq", "dp"), axis=0, tiled=True)
            return full.reshape(seq, d, shard.shape[1])

        wq, wk, wv, wo, *weights = (gather_all(t) for t in [w_query, w_key, w_value, w_out] + ff_parts)
        narrow = lax.all_gather(narrow, "seq", axis=1, tiled=True)
        wide = lax.all_gather(wide, "seq", axis=1, tiled=True)
        vec = lax.all_gather(vec_part, "seq", axis=1, tiled=True).astype(f32)
        bup = lax.all_gather(b_up[None], "seq", axis=0, tiled=True).astype(f32)[:, None]
        x = to_row(tokens)
        cot = to_row(cotangent)

    if fast:
        mine, other, g_mid, g_qkv, mixed = backward_call(
            nz, qkv, probs, oaug, d_out, x, n1, hid, dmid, wq, wk, wv, mixed,
            g_mid.reshape(2, 2, 2 * nz, 8, g_mid.shape[2]), at, bq, vec, aid)
        g_mid, g_qkv = (t.reshape(2, LORA // seq, -1) for t in (g_mid, g_qkv))
        other = other.astype(f32)
        d_in = jnp.where(me == 0, jnp.stack([mine, other]), jnp.stack([other, mine]))
    else:
        at, b = narrow[:5], narrow[5:]
        bq = jnp.swapaxes(b[:3].reshape(3, LORA, seq, ds), 1, 2)
        bias = jnp.stack([vec[0], jnp.zeros_like(vec[0]), vec[1]]).reshape(3, seq, 1, ds)
        qkv, n1, hid = qkv_call(x, jnp.stack([wq, wk, wv]), at, bq, bias, vec, aid, pic)
        kv, off = qkv, 1
        if group > 1:
            kv = lax.all_gather(qkv[1:], "seq", axis=2, tiled=True, axis_index_groups=teams)
            off = 0
        probs, oaug = attn_fwd_call(qkv, kv, off)
        more = ((0, 0), (0, 0), (0, 0), (0, fslot - fs))
        ff = jnp.pad(jnp.swapaxes(wide.reshape(2, LORA, seq, fs), 1, 2), more)
        mixed, dmid, d_out, g_mid = mid_call(
            oaug, x, cot, aid, wo, weights, cuts, jnp.concatenate([at[3:], b[3:]]), ff, jnp.pad(bup, more[1:]), vec)
        dq, dk, dv = attn_bwd_call(qkv, kv, off, probs, oaug, d_out)
        if group > 1:
            dk, dv = (lax.psum_scatter(t, "seq", scatter_dimension=1, axis_index_groups=teams, tiled=True)
                      for t in (dk, dv))
        d_in, g_qkv = tail_call(dq, dk, dv, x, n1, hid, dmid, aid, wq, wk, wv, at, bq, vec)

        def total(t):
            return lax.psum(lax.psum_scatter(t, "seq", scatter_dimension=1, tiled=True), "dp")

        g_mid, g_qkv = total(g_mid), total(g_qkv)
        mixed = from_row(mixed, bf16)
        d_in = from_row(d_in, f32)

    def down_form(t):
        return jnp.swapaxes(t.astype(f32).reshape(-1, RANK, t.shape[-1]), -1, -2)

    def up_form(t):
        return t.astype(f32).reshape(-1, RANK, t.shape[-1])

    def cut(t, k):
        return t[:, k * d:(k + 1) * d]

    def ff_of(t):
        return jnp.concatenate([t[:, 2 * d + j * fslot:2 * d + j * fslot + fs] for j in range(seq)], axis=1)

    a_mid, b_mid = g_mid
    a_qkv, b_qkv = g_qkv
    return (
        mixed,
        d_in,
        jnp.stack([down_form(cut(a_qkv, p)) for p in range(3)]),
        down_form(cut(a_mid, 0)),
        jnp.stack([up_form(cut(b_qkv, p)) for p in range(3)] + [up_form(cut(b_mid, 0))]),
        down_form(cut(a_mid, 1)),
        up_form(ff_of(b_mid)),
        down_form(ff_of(a_mid)),
        up_form(cut(b_mid, 1)),
    )


def solution(mesh):
    both = P("dp", "seq", None)
    lead = P("seq", None, None)
    second = P(None, "seq", None, None)
    return jax.shard_map(
        local,
        mesh=mesh,
        in_specs=(both, both, P("dp", None), P("dp", None))
        + (P("dp", "seq"),) * 5 + (P("seq", "dp"),) + (P("seq"),) * 9
        + (second, lead, second, lead, lead, lead, lead),
        out_specs=(both, both, second, lead, second, lead, lead, lead, lead),
        check_vma=False,
    )
```

```python
from functools import partial

import jax
import jax.numpy as jnp
from jax import lax
from jax.experimental import pallas as pl
from jax.experimental.pallas import tpu as pltpu
from jax.sharding import PartitionSpec as P

HEADS = 16
HEAD_DIM = 72
RANK = 16
ADAPTERS = 8
LORA = RANK * ADAPTERS
LANES = 128
EPS = 1e-06
SCALE = HEAD_DIM ** (-0.5)
BIG = 1e30
LOG2E = 1.4426950408889634
VMEM = 61 * 1024 * 1024
HEAD, BEFORE, CHUNK = (1, 0), 1, 3

MESH = pl.DeviceIdType.MESH
bf16 = jnp.bfloat16
f32 = jnp.float32


def nn(a, b):
    return jnp.dot(a, b, preferred_element_type=f32)


def nt(a, b):
    return lax.dot_general(a, b, (((1,), (1,)), ((), ())), preferred_element_type=f32)


def tn(a, b):
    return lax.dot_general(a, b, (((0,), (0,)), ((), ())), preferred_element_type=f32)


def up128(n):
    return -(-n // LANES) * LANES


def lane_ids(rows):
    return lax.broadcasted_iota(jnp.int32, (rows, LANES), 1)


def norm_parts(x):
    center = jnp.mean(x, axis=-1, keepdims=True)
    xc = x - center
    r = lax.rsqrt(jnp.mean(xc * xc, axis=-1, keepdims=True) + EPS)
    return xc * r, r


def norm_back(dn, gain, nh, r):
    gh = dn * gain
    a = jnp.mean(gh, axis=-1, keepdims=True)
    b = jnp.mean(gh * nh, axis=-1, keepdims=True)
    return r * (gh - a - nh * b)


def column_mask(aid):
    return (lane_ids(aid.shape[0]) // RANK == aid).astype(f32)


class Spot:
    def __init__(self, nz):
        dp = lax.axis_index("dp")
        self.nz = nz
        self.x = lax.axis_index("seq")
        self.z, self.y, self.c = dp // 4, (dp // 2) % 2, dp % 2
        self.xn = self.device(1 - self.x, self.y, self.z, self.c)
        self.yn = self.device(self.x, 1 - self.y, self.z, self.c)
        self.sib = self.device(self.x, self.y, self.z, 1 - self.c)
        self.zs = [None] + [self.device(self.x, self.y, self.zk(k), self.c) for k in range(1, nz)]
        flip = self.z // 2
        self.inner = self.z + flip * (3 - 2 * self.z)
        self.zr = [m + flip * (3 - 2 * m) for m in (self.inner, 1 - self.inner, 2, 3)]
        self.zp = [self.device(self.x, self.y, z, self.c) for z in self.zr]

    def device(self, x, y, z, c):
        return ((z * 2 + y) * 2 + c, x)

    def zk(self, k):
        return (self.z + k) % self.nz

    def barrier(self):
        peers = [self.xn, self.yn, self.sib] + self.zs[1:]
        sem = pltpu.get_barrier_semaphore()
        for peer in peers:
            pl.semaphore_signal(sem, inc=1, device_id=peer, device_id_type=MESH)
        pl.semaphore_wait(sem, len(peers))


def remote(src, dst, send, recv, device):
    return pltpu.make_async_remote_copy(
        src_ref=src, dst_ref=dst, send_sem=send, recv_sem=recv, device_id=device, device_id_type=MESH
    )


class Gather:
    def __init__(self, spot, ins, outs, send, recv, own):
        self.s, self.ins, self.outs, self.send, self.recv, self.own = spot, ins, outs, send, recv, own

    @staticmethod
    def scratch(nz, count):
        dma = pltpu.SemaphoreType.DMA
        return [dma((count, 14)), dma((count, 8)), dma((count,))]

    def column(self, g, x, y):
        return self.outs[g].at[self.s.c, x, y]

    def shard(self, g, x, y, r):
        return self.outs[g].at[self.s.c, x, y, self.s.zr[r]]

    def sends(self, g):
        s = self.s
        here, over = self.column(g, s.x, s.y), self.column(g, 1 - s.x, s.y)
        side, far = self.column(g, s.x, 1 - s.y), self.column(g, 1 - s.x, 1 - s.y)
        mine = self.shard(g, s.x, s.y, 0)
        first, third = self.shard(g, 1 - s.x, s.y, 0), self.shard(g, 1 - s.x, s.y, 3)
        diagonal, other = self.shard(g, 1 - s.x, 1 - s.y, 0), self.shard(g, 1 - s.x, 1 - s.y, 2)
        return {
            "z1": (self.ins[g], mine, 0, s.zp[1]), "z2": (self.ins[g], mine, 0, s.zp[2]),
            "z3": (self.ins[g], mine, 0, s.zp[3]),
            "x": (here, here, 1, s.xn), "y": (here, here, 2, s.yn), "s": (here, here, 7, s.sib),
            "xy0": (first, first, 3, s.yn), "xy3": (third, third, 6, s.yn), "xs": (over, over, 7, s.sib),
            "ys": (side, side, 7, s.sib),
            "d1": (diagonal, diagonal, 4, s.zp[1]), "i2": (diagonal, diagonal, 5, s.zp[2]),
            "i1": (other, other, 5, s.zp[1]), "ds": (far, far, 7, s.sib),
        }

    def copy(self, g, name):
        table = self.sends(g)
        src, dst, arrival, device = table[name]
        return remote(src, dst, self.send.at[g, list(table).index(name)], self.recv.at[g, arrival], device)

    def start(self, g, *names):
        for name in names:
            if name[0] == "i":
                pl.when(self.s.inner == 1)(self.copy(g, name).start)
            else:
                self.copy(g, name).start()

    def await_(self, g, arrival, ref):
        remote(ref, ref, self.send.at[g, 0], self.recv.at[g, arrival], self.s.xn).wait_recv()

    def local(self, g):
        return pltpu.make_async_copy(self.ins[g], self.shard(g, self.s.x, self.s.y, 0), self.own.at[g])

    def begin(self, g):
        self.local(g).start()
        self.start(g, "z1", "z2", "z3")

    def spread(self, g):
        s = self.s
        self.local(g).wait()
        self.await_(g, 0, self.outs[g].at[s.c, s.x, s.y, pl.ds(0, s.nz - 1)])
        self.start(g, "x", "y", "s")

    def over_x(self, g):
        self.await_(g, 1, self.column(g, 1 - self.s.x, self.s.y))
        self.start(g, "xy0", "xy3", "xs")

    def over_y(self, g):
        self.await_(g, 2, self.column(g, self.s.x, 1 - self.s.y))
        self.start(g, "ys")

    def far(self, g, r):
        s = self.s
        self.await_(g, 3 + r, self.shard(g, 1 - s.x, 1 - s.y, r))
        self.start(g, *{0: ["d1", "i2"], 2: ["i1"], 1: ["ds"]}.get(r, []))

    def end(self, g):
        self.await_(g, 7, self.outs[g].at[1 - self.s.c])
        for name in self.sends(g):
            if name[0] == "i":
                pl.when(self.s.inner == 1)(self.copy(g, name).wait_send)
            else:
                self.copy(g, name).wait_send()

    def actions(self):
        n = len(self.ins)
        out = [(self.begin, 0)]
        for t in range(n + 4):
            if t + 1 < n:
                out.append((self.begin, t + 1))
            if 0 <= t - 1 < n:
                out.append((self.spread, t - 1))
            if 0 <= t - 2 < n:
                out += [(self.over_x, t - 2), (self.over_y, t - 2)]
            if 0 <= t - 3 < n:
                out += [(self.far, t - 3, r) for r in (0, 3, 2, 1)]
            if 0 <= t - 4 < n:
                out.append((self.end, t - 4))
        return out


def pull(nz, src, j, dst, sem):
    def start():
        for c in range(2):
            for y in range(2):
                pltpu.make_async_copy(src.at[c, j, y], dst.at[:, y, c], sem).start()

    return start, lambda: pltpu.make_async_copy(dst, dst, sem).wait()


class Swap:
    def __init__(self, spot, mine, got, sems, slot=None):
        self.s, self.mine, self.got, self.sems = spot, mine, got, sems
        self.slot = spot.x if slot is None else slot

    def copies(self):
        s = self.s
        here = pltpu.make_async_copy(self.mine.at[s.x], self.got.at[s.x], self.sems.at[0])
        there = remote(self.mine.at[1 - s.x], self.got.at[self.slot], self.sems.at[1], self.sems.at[2], s.xn)
        return here, there

    def start(self):
        for copy in self.copies():
            copy.start()

    def end(self):
        here, there = self.copies()
        here.wait()
        ref = self.got.at[1 - self.s.x]
        remote(ref, ref, self.sems.at[1], self.sems.at[2], self.s.xn).wait_recv()
        there.wait_send()


class Reduce:
    def __init__(self, spot, data, result, refs):
        self.s, self.data, self.result = spot, data, result
        self.r1, self.s1, self.r2, self.s2, self.r3, self.s3, self.r4, self.total = refs[:8]
        self.send, self.recv, self.out = refs[8:]

    @staticmethod
    def scratch(nz, width):
        def v(*dims):
            return pltpu.VMEM((*dims, 8, width), bf16)
        dma = pltpu.SemaphoreType.DMA
        n = 5 + 2 * (nz - 1)
        return [v(2, 2 * nz), v(2, 2 * nz), v(2, nz), v(2, nz), v(nz, 2), v(2), v(1), v(2, 2 * nz),
                dma((n,)), dma((n,)), dma((1,))]

    def pair(self, i, src, dst, device):
        return remote(src, dst, self.send.at[i], self.recv.at[i], device)

    def to_core(self):
        return self.pair(0, self.data.at[1 - self.s.c], self.r1, self.s.sib)

    def to_y(self):
        nz = self.s.nz
        return self.pair(1, self.s1.at[:, pl.ds((1 - self.s.y) * nz, nz)], self.r2, self.s.yn)

    def to_x(self):
        return self.pair(2, self.s3.at[1 - self.s.x], self.r4.at[0], self.s.xn)

    def to_z(self, k):
        s = self.s
        return self.pair(4 + k, self.s2.at[:, s.zk(k)], self.r3.at[s.z], s.zs[k])

    def from_z(self, k):
        s = self.s
        ref = self.r3.at[s.zk(k)]
        return remote(ref, ref, self.send.at[4 + s.nz - k], self.recv.at[4 + s.nz - k], s.zs[k])

    def back_z(self, k):
        s = self.s
        ref = self.total.at[s.c, s.y * s.nz + s.z]
        return self.pair(4 + s.nz - 1 + k, ref, ref, s.zs[k])

    def from_back_z(self, k):
        s = self.s
        i = 4 + s.nz - 1 + s.nz - k
        ref = self.total.at[s.c, s.y * s.nz + s.zk(k)]
        return remote(ref, ref, self.send.at[i], self.recv.at[i], s.zs[k])

    def back_y(self, y):
        s = self.s
        ref = self.total.at[s.c, pl.ds(y * s.nz, s.nz)]
        return self.pair(3, ref, ref, s.yn)

    def back_core(self, c):
        ref = self.total.at[c]
        return self.pair(4, ref, ref, self.s.sib)

    def one(self):
        self.to_core().start()

    def two(self):
        s, nz = self.s, self.s.nz
        self.to_core().wait_recv()

        def add(i, c):
            x, b = i // (2 * nz), i % (2 * nz)
            self.s1[x, b] = (self.data[s.c, x, b].astype(f32) + self.r1[x, b].astype(f32)).astype(bf16)
            return c
        lax.fori_loop(0, 4 * nz, add, 0)
        self.to_y().start()

    def three(self):
        s, nz = self.s, self.s.nz
        self.to_y().wait_recv()

        def add(i, c):
            x, b = i // nz, i % nz
            self.s2[x, b] = (self.s1[x, s.y * nz + b].astype(f32) + self.r2[x, b].astype(f32)).astype(bf16)
            return c
        lax.fori_loop(0, 2 * nz, add, 0)
        for k in range(1, nz):
            self.to_z(k).start()

    def four(self):
        s, nz = self.s, self.s.nz
        for k in range(1, nz):
            self.from_z(k).wait_recv()
        for x in range(2):
            v = self.s2[x, s.z].astype(f32)
            for k in range(1, nz):
                v = v + self.r3[s.zk(k), x].astype(f32)
            self.s3[x] = v.astype(bf16)
        self.to_x().start()

    def five(self):
        s, nz = self.s, self.s.nz
        self.to_x().wait_recv()
        v = self.s3[s.x].astype(f32) + self.r4[0].astype(f32)
        self.total[s.c, s.y * s.nz + s.z] = v.astype(bf16)
        for k in range(1, nz):
            self.back_z(k).start()

    def six(self):
        for k in range(1, self.s.nz):
            self.from_back_z(k).wait_recv()
        self.back_y(self.s.y).start()

    def seven(self):
        self.back_y(1 - self.s.y).wait_recv()
        self.back_core(self.s.c).start()

    def end(self):
        s = self.s
        self.back_core(1 - s.c).wait_recv()
        out = pltpu.make_async_copy(self.total, self.result, self.out.at[0])
        out.start()
        out.wait()
        self.to_core().wait_send()
        self.to_x().wait_send()
        self.to_y().wait_send()
        for k in range(1, s.nz):
            self.to_z(k).wait_send()
            self.back_z(k).wait_send()
        self.back_y(s.y).wait_send()
        self.back_core(s.c).wait_send()

    def actions(self):
        return [(f,) for f in (self.one, self.two, self.three, self.four, self.five, self.six, self.seven, self.end)]


def any_specs(n):
    return [pl.BlockSpec(memory_space=pl.ANY)] * n


def gathered(nz, arrays):
    return [jax.ShapeDtypeStruct((2, 2, 2, nz) + a.shape, a.dtype) for a in arrays]


class Steps:
    def __init__(self, actions):
        self.actions = list(actions)

    def take(self, count):
        out, self.actions = self.actions[:count], self.actions[count:]
        return out

    @staticmethod
    def do(actions):
        for action in actions:
            action[0](*action[1:])

    def step(self, count):
        self.do(self.take(count))

    def rest(self):
        self.step(len(self.actions))

    def until(self, part):
        ends = [k for k, action in enumerate(self.actions) if action[0].__name__ == "end" and action[1] == part]
        if ends:
            self.step(ends[0] + 1)

    def within(self, first, last, *counts):
        plan = [(t, [self.take(count) for count in counts]) for t in range(first, last)]

        def point(k):
            def run(i):
                for t, lists in plan:
                    if lists[k]:
                        pl.when(i == t)(partial(self.do, lists[k]))
            return run
        return [point(k) for k in range(len(counts))]


def qkv_kernel(nh, tm, x_ref, w_ref, at_ref, b_ref, bias_ref, vec_ref, aid_ref, pic_ref, out_ref, n1_ref, h_ref):
    p = pl.program_id(0)
    j = pl.program_id(1)
    tokens = x_ref.shape[0]

    @pl.when((p == 0) & (j == 0))
    def _():
        def norm_step(i, c):
            rows = pl.ds(i * tm, tm)
            nhat, _ = norm_parts(x_ref[rows, :].astype(f32))
            n1_ref[rows, :] = (nhat * vec_ref[4:5, :] + vec_ref[5:6, :]).astype(bf16)
            return c
        lax.fori_loop(0, tokens // tm, norm_step, 0)

    @pl.when(j == 0)
    def _():
        def hidden_step(i, c):
            rows = pl.ds(i * tm, tm)
            h = nt(n1_ref[rows, :], at_ref[0]) * column_mask(aid_ref[rows, :])
            h_ref[0, rows, :] = h.astype(bf16)
            return c
        lax.fori_loop(0, tokens // tm, hidden_step, 0)

    def step(i, c):
        rows = pl.ds(i * tm, tm)
        y = nn(n1_ref[rows, :], w_ref[0, 0])
        y = y + 0.5 * nn(h_ref[0, rows, :], b_ref[0, 0]) + bias_ref[0, 0]
        slot = lane_ids(tm) - HEAD_DIM
        pic = pic_ref[rows, :]
        same = slot == pic
        in_slots = (slot >= 0) & (slot < 16)
        q_aug = jnp.where(same, 1.0, 0.0)
        k_aug = jnp.where(in_slots & jnp.logical_not(same), -BIG, 0.0)
        v_aug = jnp.where((slot == 0) | (slot == 1), 1.0, 0.0)
        aug = jnp.where(p == 0, q_aug, jnp.where(p == 1, k_aug, v_aug))[:, HEAD_DIM:]
        for h in range(nh):
            head = y[:, h * HEAD_DIM:(h + 1) * HEAD_DIM]
            out_ref[0, h, rows, :HEAD_DIM] = head.astype(bf16)
            out_ref[0, h, rows, HEAD_DIM:] = aug.astype(bf16)
        return c
    lax.fori_loop(0, tokens // tm, step, 0)


def qkv_call(x, w, at, bq, bias, vec, aid, pic):
    tokens, d = x.shape
    s = w.shape[1]
    nh = HEADS // s
    tm = min(256, tokens)
    return pl.pallas_call(
        partial(qkv_kernel, nh, tm),
        grid=(3, s),
        in_specs=[
            pl.BlockSpec((tokens, d), lambda p, j: (0, 0)),
            pl.BlockSpec((1, 1, d, d // s), lambda p, j: (p, j, 0, 0)),
            pl.BlockSpec((1, LORA, d), lambda p, j: (p, 0, 0)),
            pl.BlockSpec((1, 1, LORA, nh * HEAD_DIM), lambda p, j: (p, j, 0, 0)),
            pl.BlockSpec((1, 1, 1, nh * HEAD_DIM), lambda p, j: (p, j, 0, 0)),
            pl.BlockSpec(vec.shape, lambda p, j: (0, 0)),
            pl.BlockSpec((tokens, 1), lambda p, j: (0, 0)),
            pl.BlockSpec((tokens, 1), lambda p, j: (0, 0)),
        ],
        out_specs=[
            pl.BlockSpec((1, nh, tokens, LANES), lambda p, j: (p, j, 0, 0)),
            pl.BlockSpec((tokens, d), lambda p, j: (0, 0)),
            pl.BlockSpec((1, tokens, LORA), lambda p, j: (p, 0, 0)),
        ],
        out_shape=[
            jax.ShapeDtypeStruct((3, HEADS, tokens, LANES), bf16),
            jax.ShapeDtypeStruct((tokens, d), bf16),
            jax.ShapeDtypeStruct((3, tokens, LORA), bf16),
        ],
        compiler_params=pltpu.CompilerParams(vmem_limit_bytes=VMEM),
        name="qkv",
    )(x, w, at, bq, bias, vec, aid, pic)


def attn_fwd_kernel(tq, q_ref, k_ref, v_ref, p_ref, o_ref):
    for i in range(q_ref.shape[2] // tq):
        rows = pl.ds(i * tq, tq)
        s = nt(q_ref[0, 0, rows, :], k_ref[0, 0])
        top = jnp.max(s, axis=-1, keepdims=True)
        p = jnp.exp2((s - top) * (SCALE * LOG2E)).astype(bf16)
        o = nn(p, v_ref[0, 0])
        inv = 1.0 / o[:, HEAD_DIM:HEAD_DIM + 1]
        p_ref[0, rows, :] = (p.astype(f32) * inv).astype(bf16)
        o_ref[0, rows, :] = (o * inv).astype(bf16)


def attn_fwd_call(qkv, kv, off):
    tokens, keys = qkv.shape[2], kv.shape[2]
    tq = min(512, tokens)
    return pl.pallas_call(
        partial(attn_fwd_kernel, tq),
        grid=(HEADS,),
        in_specs=[
            pl.BlockSpec((1, 1, tokens, LANES), lambda h: (0, h, 0, 0)),
            pl.BlockSpec((1, 1, keys, LANES), lambda h: (off, h, 0, 0)),
            pl.BlockSpec((1, 1, keys, LANES), lambda h: (off + 1, h, 0, 0)),
        ],
        out_specs=[
            pl.BlockSpec((1, tokens, keys), lambda h: (h, 0, 0)),
            pl.BlockSpec((1, tokens, LANES), lambda h: (h, 0, 0)),
        ],
        out_shape=[
            jax.ShapeDtypeStruct((HEADS, tokens, keys), bf16),
            jax.ShapeDtypeStruct((HEADS, tokens, LANES), bf16),
        ],
        compiler_params=pltpu.CompilerParams(vmem_limit_bytes=VMEM),
        name="attn_fwd",
    )(qkv, kv, kv)


def attn_bwd_kernel(tq, q_ref, k_ref, v_ref, p_ref, o_ref, do_ref, dq_ref, dk_ref, dv_ref, ds_ref, da_ref):
    for i in range(q_ref.shape[2] // tq):
        rows = pl.ds(i * tq, tq)
        lane = lane_ids(tq)
        do = jnp.where(lane < HEAD_DIM, do_ref[0, rows, :].astype(f32), 0.0)
        delta = jnp.sum(do * o_ref[0, rows, :].astype(f32), axis=-1, keepdims=True)
        hi = delta.astype(bf16).astype(f32)
        do = jnp.where(lane == HEAD_DIM, -hi, jnp.where(lane == HEAD_DIM + 1, hi - delta, do)).astype(bf16)
        da_ref[rows, :] = do
        dp = nt(do, v_ref[0, 0])
        ds = (p_ref[0, rows, :].astype(f32) * dp).astype(bf16)
        ds_ref[rows, :] = ds
        dq_ref[0, rows, :] = (nn(ds, k_ref[0, 0]) * SCALE).astype(bf16)
    dv_ref[0] = nn(da_ref[...].T, p_ref[0]).T.astype(bf16)
    dk_ref[0] = (nn(q_ref[0, 0].T, ds_ref[...]).T * SCALE).astype(bf16)


def attn_bwd_call(qkv, kv, off, probs, out, d_out):
    tokens, keys = qkv.shape[2], kv.shape[2]
    tq = min(256, tokens)
    return pl.pallas_call(
        partial(attn_bwd_kernel, tq),
        grid=(HEADS,),
        in_specs=[
            pl.BlockSpec((1, 1, tokens, LANES), lambda h: (0, h, 0, 0)),
            pl.BlockSpec((1, 1, keys, LANES), lambda h: (off, h, 0, 0)),
            pl.BlockSpec((1, 1, keys, LANES), lambda h: (off + 1, h, 0, 0)),
            pl.BlockSpec((1, tokens, keys), lambda h: (h, 0, 0)),
            pl.BlockSpec((1, tokens, LANES), lambda h: (h, 0, 0)),
            pl.BlockSpec((1, tokens, LANES), lambda h: (h, 0, 0)),
        ],
        out_specs=[
            pl.BlockSpec((1, tokens, LANES), lambda h: (h, 0, 0)),
            pl.BlockSpec((1, keys, LANES), lambda h: (h, 0, 0)),
            pl.BlockSpec((1, keys, LANES), lambda h: (h, 0, 0)),
        ],
        out_shape=[
            jax.ShapeDtypeStruct((HEADS, tokens, LANES), bf16),
            jax.ShapeDtypeStruct((HEADS, keys, LANES), bf16),
            jax.ShapeDtypeStruct((HEADS, keys, LANES), bf16),
        ],
        scratch_shapes=[pltpu.VMEM((tokens, keys), bf16), pltpu.VMEM((tokens, LANES), bf16)],
        compiler_params=pltpu.CompilerParams(vmem_limit_bytes=VMEM),
        name="attn_bwd",
    )(qkv, kv, kv, probs, out, d_out)


def gelu_parts(z):
    c = 0.7978845608028654
    z2 = z * z
    t = jnp.tanh(z * (c + (c * 0.044715) * z2))
    half = 0.5 * (1.0 + t)
    g = z * half
    dg = half + 0.5 * z * (1.0 - t * t) * (c + (3 * c * 0.044715) * z2)
    return g, dg


def mid_work(s, cuts, run, ready, part, take, weights, load, save, wo_load, bufs):
    (aid_ref, ab_ref, ff_ref, bup_ref, vec_ref, pack_ref, obuf, xbuf, cotbuf, dybuf, wobuf, ocat, n2buf, mid, acc, dn2,
     hidden, wofull, ubuf, dbuf, ga, gb, wsem, go) = bufs
    tokens, d = xbuf.shape
    ds = d // s
    bo, bd, gain2, shift2 = vec_ref[2:3, :], vec_ref[3:4, :], vec_ref[6:7, :], vec_ref[7:8, :]
    at_o, at_u, b_o, b_d = (ab_ref.at[k] for k in range(4))
    ta, tm = min(256, tokens), min(512, tokens)
    chunks = [(c, j) for c in range(len(cuts)) for j in range(s)]

    def slot_of(buf, k, w):
        return buf.at[(k % 2,) + (slice(None),) * (len(buf.shape) - 2) + (pl.ds(0, w),)] if w < buf.shape[-1] else buf.at[k % 2]

    def fetch(k):
        c, j = chunks[k]
        for m, (ref, buf) in enumerate(((weights[2 * c], ubuf), (weights[2 * c + 1], dbuf))):
            yield take(ref, j, slot_of(buf, k, cuts[c][1]), wsem.at[k % 2, m])

    def begin(k):
        for start, _ in fetch(k):
            start()

    for start, _ in wo_load:
        start()
    for i in range(tokens // ta):
        for copy in load(i):
            copy.start()
    if ready:
        begin(0)
    for _, done in wo_load:
        done()
    run.step(2)

    wofull[...] = jnp.concatenate([wobuf[j].reshape(d, ds) for j in range(s)], axis=1)

    [serve] = run.within(1, tokens // ta, BEFORE)

    def before(i, carry):
        rows = pl.ds(i * ta, ta)
        serve(i)
        for copy in load(i):
            copy.wait()
        mask = column_mask(aid_ref[rows, :])
        for h in range(HEADS):
            ocat[rows, h * HEAD_DIM:(h + 1) * HEAD_DIM] = obuf[h, rows, :HEAD_DIM]
        o = ocat[rows, :]
        h_o = (nt(o, at_o[...]) * mask).astype(bf16)
        value = xbuf[rows, :].astype(f32) + nn(o, wofull[...]) + 0.5 * nn(h_o, b_o[...]) + bo
        mid[rows, :] = value
        nh2, _ = norm_parts(value)
        n2 = (nh2 * gain2 + shift2).astype(bf16)
        n2buf[rows, :d] = n2
        dy = jnp.where(aid_ref[rows, :] >= 0, cotbuf[rows, :], jnp.zeros((ta, d), bf16))
        dybuf[rows, :d] = dy
        hidden[rows, :] = h_o
        n2buf[rows, d:] = (0.5 * (nt(n2, at_u[...]) * mask).astype(bf16).astype(f32)).astype(bf16)
        dybuf[rows, d:] = (0.5 * nt(dy, b_d[...]) * mask).astype(bf16)
        return carry
    lax.fori_loop(0, tokens // ta, before, 0)

    for k, (c, j) in enumerate(chunks):
        start, w = cuts[c]
        if k == 0 and not ready:
            run.until(part(0))
            begin(0)
        late = k + 1 < len(chunks) and chunks[k + 1][0] >= ready and chunks[k + 1][1] == 0
        if k + 1 < len(chunks) and not late:
            begin(k + 1)
        for _, done in fetch(k):
            done()
        cols = slice(start, start + w)

        [serve] = run.within(1, tokens // tm, CHUNK)

        def chunk(i, carry, k=k, j=j, w=w, cols=cols, slot=k % 2, serve=serve):
            rows = pl.ds(i * tm, tm)
            serve(i)
            wu = jnp.concatenate([slot_of(ubuf, slot, w)[...].reshape(d, w), ff_ref[1, j, :, cols]])
            wd = jnp.concatenate([slot_of(dbuf, slot, w)[...].reshape(d, w), ff_ref[0, j, :, cols]])
            z = nn(n2buf[rows, :], wu) + bup_ref[j, :, cols]
            g, dgelu = gelu_parts(z)
            g = g.astype(bf16)
            dg = nn(dybuf[rows, :], wd).astype(bf16)
            dz = (dg.astype(f32) * dgelu).astype(bf16)
            if k == 0:
                acc[rows, :] = nt(g, wd)
                dn2[rows, :] = nt(dz, wu)
            else:
                acc[rows, :] += nt(g, wd)
                dn2[rows, :] += nt(dz, wu)
            more_a, more_b = tn(dybuf[rows, d:], g), tn(n2buf[rows, d:], dz)

            @pl.when(i == 0)
            def _():
                ga[:, :w] = more_a
                gb[:, :w] = more_b

            @pl.when(i > 0)
            def _():
                ga[:, :w] += more_a
                gb[:, :w] += more_b
            return carry
        lax.fori_loop(0, tokens // tm, chunk, 0)
        at = 2 * d + j * ff_ref.shape[3] + start
        pack_ref[0, :, at:at + w] = ga[:, :w].astype(bf16)
        pack_ref[1, :, at:at + w] = gb[:, :w].astype(bf16)
        run.step(CHUNK)
        if late:
            run.until(part(chunks[k + 1][0]))
            begin(k + 1)

    run.rest()

    go[...] = jnp.zeros_like(go)

    def after(i, carry):
        rows = pl.ds(i * ta, ta)
        mask = column_mask(aid_ref[rows, :])
        h_d = (acc[rows, d:] * mask).astype(bf16)
        xbuf[rows, :] = (mid[rows, :] + bd + acc[rows, :d] + 0.5 * nn(h_d, b_d[...])).astype(bf16)
        dh_u = (0.5 * dn2[rows, d:] * mask).astype(bf16)
        nh2, r2 = norm_parts(mid[rows, :])
        dy = dybuf[rows, :d]
        dmid = dy.astype(f32) + norm_back(dn2[rows, :d] + nn(dh_u, at_u[...]), gain2, nh2, r2)
        mid[rows, :] = dmid
        db = dmid.astype(bf16)
        dh_o = (0.5 * nt(db, b_o[...]) * mask).astype(bf16)
        do = (nt(db, wofull[...]) + nn(dh_o, at_o[...])).astype(bf16)
        go[0] += tn(dh_o, ocat[rows, :])
        go[1] += 0.5 * tn(hidden[rows, :], db)
        go[2] += tn(dh_u, n2buf[rows, :d])
        go[3] += 0.5 * tn(h_d, dy)
        for h in range(HEADS):
            obuf[h, rows, :HEAD_DIM] = do[:, h * HEAD_DIM:(h + 1) * HEAD_DIM]
        for copy in save(i):
            copy.start()
        return carry
    lax.fori_loop(0, tokens // ta, after, 0)
    for c, order in enumerate(((0, 2), (1, 3))):
        for k, which in enumerate(order):
            pack_ref[c, :, k * d:(k + 1) * d] = go[which].astype(bf16)
    for i in range(tokens // ta):
        for copy in save(i):
            copy.wait()


def mid_kernel(s, n, cuts, *refs):
    (oaug_ref, x_ref, cot_ref, aid_ref, wo_ref, ab_ref, ff_ref, bup_ref, vec_ref) = refs[:9]
    weights, refs = refs[9:9 + 2 * len(cuts)], refs[9 + 2 * len(cuts):]
    mixed_ref, dmid_ref, do_ref, pack_ref, obuf, xbuf, isem, osem, lsem, *bufs = refs
    cotbuf, mid = bufs[0], bufs[5]
    ta = min(256, xbuf.shape[0])

    def load(i):
        rows = pl.ds(i * ta, ta)
        for k, (src, dst) in enumerate(((oaug_ref.at[:, rows], obuf.at[:, rows]), (x_ref.at[rows], xbuf.at[rows]),
                                        (cot_ref.at[rows], cotbuf.at[rows]))):
            yield pltpu.make_async_copy(src, dst, isem.at[i, k])

    def save(i):
        rows = pl.ds(i * ta, ta)
        for k, (src, dst) in enumerate(((xbuf.at[rows], mixed_ref.at[rows]), (mid.at[rows], dmid_ref.at[rows]),
                                        (obuf.at[:, rows], do_ref.at[:, rows]))):
            yield pltpu.make_async_copy(src, dst, osem.at[i, k])

    def take(ref, j, dst, sem):
        return one(ref.at[pl.ds(j * n, n)], dst, sem)

    def one(src, dst, sem):
        return (lambda: pltpu.make_async_copy(src, dst, sem).start(),
                lambda: pltpu.make_async_copy(src, dst, sem).wait())

    mid_work(s, cuts, Steps([]), len(cuts), None, take, weights, load, save, [one(wo_ref, bufs[2], lsem.at[0])],
             [aid_ref, ab_ref, ff_ref, bup_ref, vec_ref, pack_ref, obuf, xbuf] + bufs)


def mid_bufs(s, pieces, tokens, d, widest):
    def v(*shape, dtype=bf16):
        return pltpu.VMEM(shape, dtype)

    return [
        v(tokens, d), v(tokens, d + LORA), v(s, d, d // s), v(tokens, d), v(tokens, d + LORA),
        v(tokens, d, dtype=f32), v(tokens, d + LORA, dtype=f32), v(tokens, d + LORA, dtype=f32),
        v(tokens, LORA), v(d, d), v(2, pieces, d // pieces, widest), v(2, pieces, d // pieces, widest),
        v(LORA, widest, dtype=f32), v(LORA, widest, dtype=f32), pltpu.SemaphoreType.DMA((2, 2)),
        v(4, LORA, d, dtype=f32),
    ]


def mid_call(oaug, x, cot, aid, wo, weights, cuts, ab, ff, bup, vec):
    tokens, d = x.shape
    s = wo.shape[0]
    pieces = weights[0].shape[0] // s
    tiles = tokens // min(256, tokens)
    full = pl.BlockSpec(memory_space=pltpu.VMEM)
    dma = pltpu.SemaphoreType.DMA
    return pl.pallas_call(
        partial(mid_kernel, s, pieces, cuts),
        in_specs=any_specs(3) + [full] + any_specs(1) + [full] * 4 + any_specs(len(weights)),
        out_specs=any_specs(3) + [full],
        out_shape=[
            jax.ShapeDtypeStruct((tokens, d), bf16),
            jax.ShapeDtypeStruct((tokens, d), f32),
            jax.ShapeDtypeStruct((HEADS, tokens, LANES), bf16),
            jax.ShapeDtypeStruct((2, LORA, 2 * d + s * ff.shape[3]), bf16),
        ],
        scratch_shapes=[
            pltpu.VMEM((HEADS, tokens, LANES), bf16), pltpu.VMEM((tokens, d), bf16),
            dma((tiles, 3)), dma((tiles, 3)), dma((1,)),
        ] + mid_bufs(s, pieces, tokens, d, max(w for _, w in cuts)),
        compiler_params=pltpu.CompilerParams(vmem_limit_bytes=VMEM),
        name="mid",
    )(oaug, x, cot, aid, wo, ab, ff, bup, vec, *weights)


def forward_kernel(nz, cuts, na, *refs):
    shards, (tokens, vec, cot, aid_ref, pic_ref), refs = refs[:na], refs[na:na + 5], refs[na + 5:]
    wholes, refs = refs[:na], refs[na:]
    (x_out, vec_out, a_out, b_out, qkv_out, n1_out, h_out, probs_out, o_out, cot_row, mixed_ref, dmid_ref, do_ref,
     pack_ref), refs = refs[:14], refs[14:]
    (xbuf, vbuf, obuf, ab, ff, vecs, bups, sems, wsem, osem, psem, csems, isem, ssem, *gather_refs) = refs
    n, d = nz * 4, xbuf.shape[2]
    half = xbuf.shape[1]
    count, tm = 2 * half, 512
    ds, fslot = shards[1].shape[1], ff.shape[3]
    nh = ds // HEAD_DIM
    each = LORA // 2
    spot = Spot(nz)
    spot.barrier()
    gather = Gather(spot, shards, wholes, *gather_refs)
    run = Steps(gather.actions())
    swap = Swap(spot, cot, cot_row, csems)
    vec_here = pltpu.make_async_copy(vec, vbuf.at[spot.x], sems.at[0])
    vec_there = remote(vec, vbuf.at[spot.x], sems.at[1], sems.at[2], spot.xn)
    row_here = pltpu.make_async_copy(tokens.at[spot.x], xbuf.at[spot.x], sems.at[3])
    row_there = remote(tokens.at[1 - spot.x], xbuf.at[spot.x], sems.at[4], sems.at[5], spot.xn)

    def first(nbuf, widebuf, wbuf, abuf, bbuf, n1, hbuf, heads, pbuf):
        vec_here.start()
        vec_there.start()
        run.step(2)
        row_here.start()
        row_there.start()
        run.step(6)
        vec_here.wait()
        got = vbuf.at[1 - spot.x]
        remote(got, got, sems.at[1], sems.at[2], spot.xn).wait_recv()
        row_here.wait()
        got = xbuf.at[1 - spot.x]
        remote(got, got, sems.at[4], sems.at[5], spot.xn).wait_recv()
        for j in range(2):
            vecs[:, j * ds:(j + 1) * ds] = vbuf[j, :8, :ds].astype(f32)
            bups[j] = vbuf[j, 8:9, :].astype(f32)
        gain, shift = vecs[4:5, :], vecs[5:6, :]
        keep = [pltpu.make_async_copy(xbuf, x_out, osem.at[0]), pltpu.make_async_copy(vecs, vec_out, osem.at[1])]
        for copy in keep:
            copy.start()
        for part in range(2):
            def norm_step(i, carry, part=part):
                nhat, _ = norm_parts(xbuf[part, pl.ds(i * 256, 256), :].astype(f32))
                n1[pl.ds(part * half + i * 256, 256), :d] = (nhat * gain + shift).astype(bf16)
                return carry
            lax.fori_loop(0, half // 256, norm_step, 0)
            run.step(2)
        keep.append(pltpu.make_async_copy(n1.at[:, pl.ds(0, d)], n1_out, osem.at[2]))
        keep[-1].start()

        run.until(0)
        for c in range(2):
            pltpu.make_async_copy(wholes[0].at[c], nbuf.at[:, c], sems.at[6]).start()
        pltpu.make_async_copy(nbuf, nbuf, sems.at[6]).wait()
        for j in range(2):
            rows = slice(j * each, (j + 1) * each)
            one = nbuf[j].reshape(10 * each, d)
            for m in range(3):
                abuf[m, rows, :] = one[m * each:(m + 1) * each]
                for i in range(2):
                    bbuf[m, i, rows, :] = one[(5 + m) * each:(6 + m) * each, i * ds:(i + 1) * ds]
            for k, m in enumerate((3, 4, 8, 9)):
                ab[k, rows, :] = one[m * each:(m + 1) * each]

        for copy in (pltpu.make_async_copy(abuf, a_out, osem.at[11]), pltpu.make_async_copy(bbuf, b_out, osem.at[12])):
            keep.append(copy)
            copy.start()

        def fetch(p, j):
            return pull(nz, wholes[1 + p], j, wbuf.at[j], wsem.at[j])

        for p in range(3):
            run.until(1 + p)
            for j in range(2):
                fetch(p, j)[0]()
            for i in range(count // tm):
                rows = pl.ds(i * tm, tm)
                h = (nt(n1[rows, :d], abuf[p]) * column_mask(aid_ref[rows, :])).astype(bf16)
                hbuf[p, rows, :] = h
                n1[rows, d:] = (0.5 * h.astype(f32)).astype(bf16)
            for j in range(2):
                fetch(p, j)[1]()
                bias = vbuf[j, p // 2:p // 2 + 1, :ds].astype(f32) if p != 1 else 0.0

                [serve] = run.within(1, count // tm, 2)

                def step(i, carry, p=p, j=j, bias=bias, serve=serve):
                    rows = pl.ds(i * tm, tm)
                    serve(i)
                    w = jnp.concatenate([wbuf[j].reshape(d, ds), bbuf[p, j]])
                    y = (nn(n1[rows, :], w) + bias).astype(bf16)
                    place = lax.broadcasted_iota(jnp.int32, (tm, LANES), 1) - HEAD_DIM
                    same = place == pic_ref[rows, :]
                    if p == 0:
                        extra = jnp.where(same, 1.0, 0.0)
                    elif p == 1:
                        extra = jnp.where((place >= 0) & (place < 16) & jnp.logical_not(same), -BIG, 0.0)
                    else:
                        extra = jnp.where((place == 0) | (place == 1), 1.0, 0.0)
                    extra = extra.astype(bf16)[:, HEAD_DIM:]
                    for h in range(nh):
                        heads[p, j * nh + h, rows, :HEAD_DIM] = y[:, h * HEAD_DIM:(h + 1) * HEAD_DIM]
                        heads[p, j * nh + h, rows, HEAD_DIM:] = extra
                    return carry
                lax.fori_loop(0, count // tm, step, 0)
                which = pl.ds(j * nh, nh)
                keep.append(pltpu.make_async_copy(
                    heads.at[p, which], qkv_out.at[p, which], osem.at[4 + 2 * p + j]))
                keep[-1].start()
                run.step(1)
        keep.append(pltpu.make_async_copy(hbuf, h_out, osem.at[3]))
        keep[-1].start()
        swap.start()

        def probs_copy(h):
            return pltpu.make_async_copy(pbuf.at[h % 2], probs_out.at[h], psem.at[h % 2])

        serve, again = run.within(0, HEADS, *HEAD)

        def head(h, carry):
            serve(h)

            @pl.when(h >= 2)
            def _():
                probs_copy(h - 2).wait()
            for i in range(count // tm):
                rows = pl.ds(i * tm, tm)
                s = nt(heads[0, h, rows, :], heads[1, h])
                top = jnp.max(s, axis=-1, keepdims=True)
                p = jnp.exp2((s - top) * (SCALE * LOG2E)).astype(bf16)
                o = nn(p, heads[2, h])
                inv = 1.0 / o[:, HEAD_DIM:HEAD_DIM + 1]
                pbuf[h % 2, rows, :] = (p.astype(f32) * inv).astype(bf16)
                obuf[h, rows, :] = (o * inv).astype(bf16)
            again(h)
            probs_copy(h).start()
            return carry
        lax.fori_loop(0, HEADS, head, 0)
        keep.append(pltpu.make_async_copy(obuf, o_out, osem.at[10]))
        keep[-1].start()
        run.until(5)
        for c in range(2):
            pltpu.make_async_copy(wholes[5].at[c], widebuf.at[:, c], sems.at[7]).start()
        pltpu.make_async_copy(widebuf, widebuf, sems.at[7]).wait()
        for j in range(2):
            one = widebuf[j].reshape(LORA, 2 * fslot)
            for m in range(2):
                for i in range(2):
                    ff[m, i, j * each:(j + 1) * each, :] = one[m * each:(m + 1) * each, i * fslot:(i + 1) * fslot]
        for h in range(HEADS - 2, HEADS):
            probs_copy(h).wait()
        for copy in keep:
            copy.wait()

    def v(*shape):
        return pltpu.VMEM(shape, bf16)

    pl.run_scoped(
        first, v(2, 2, 2, nz, *shards[0].shape), v(2, 2, 2, nz, *shards[5].shape), v(2, nz, 2, 2, *shards[1].shape),
        v(3, LORA, d),
        v(3, 2, LORA, ds), v(count, d + LORA), v(3, count, LORA), v(3, HEADS, count, LANES), v(2, count, count))
    swap.end()

    def second(wobuf3, *bufs):
        cotbuf, mid = bufs[0], bufs[4]
        bufs = bufs[:2] + (wobuf3,) + bufs[2:]

        def load(i):
            yield pltpu.make_async_copy(cot_row.at[i * 256 // half, pl.ds(i * 256 % half, 256)],
                                        cotbuf.at[pl.ds(i * 256, 256)], isem.at[i, 0])

        def save(i):
            rows = pl.ds(i * 256, 256)
            inner = pl.ds(i * 256 % half, 256)
            for k, (src, dst) in enumerate((
                    (xrow.at[rows], mixed_ref.at[i * 256 // half, inner]), (mid.at[rows], dmid_ref.at[rows]),
                    (obuf.at[:, rows], do_ref.at[:, rows]))):
                yield pltpu.make_async_copy(src, dst, ssem.at[i, k])

        mid_work(2, cuts, run, 0, lambda c: 7 + 2 * c, partial(pull, nz), wholes[6:], load, save,
                 [pull(nz, wholes[4], j, wobuf3.at[j], isem.at[j, 1]) for j in range(2)],
                 [aid_ref, ab, ff, bups, vecs, pack_ref, obuf, xrow] + list(bufs))

    xrow = xbuf.reshape(count, d)
    bufs = mid_bufs(2, n, count, d, max(w for _, w in cuts))
    bufs[2] = v(2, nz, 2, 2, d // n, ds)
    bufs[10] = bufs[11] = v(2, nz, 2, 2, d // n, max(w for _, w in cuts))
    pl.run_scoped(second, bufs[2], *bufs[:2], *bufs[3:])
    vec_there.wait_send()
    row_there.wait_send()


def forward_call(nz, cuts, shards, tokens, vec, cot, aid, pic):
    na = len(shards)
    dma = pltpu.SemaphoreType.DMA
    half, d = tokens.shape[1], tokens.shape[2]
    count, fslot = 2 * half, shards[5].shape[1] // 2
    tiles = count // 256
    full = pl.BlockSpec(memory_space=pltpu.VMEM)

    def v(*shape, dtype=bf16):
        return pltpu.VMEM(shape, dtype)

    def out(*shape, dtype=bf16):
        return jax.ShapeDtypeStruct(shape, dtype)

    return pl.pallas_call(
        partial(forward_kernel, nz, cuts, na),
        in_specs=any_specs(na + 3) + [full, full],
        out_specs=any_specs(na + 13) + [full],
        out_shape=gathered(nz, shards) + [
            out(*tokens.shape), out(8, d, dtype=f32), out(3, LORA, d), out(3, 2, LORA, shards[1].shape[1]),
            out(3, HEADS, count, LANES), out(count, d), out(3, count, LORA), out(HEADS, count, count), out(HEADS, count, LANES), out(*tokens.shape), out(*tokens.shape),
            out(count, d, dtype=f32), out(HEADS, count, LANES), out(2, LORA, 2 * d + 2 * fslot)],
        scratch_shapes=[
            v(*tokens.shape), v(2, *vec.shape), v(HEADS, count, LANES), v(4, LORA, d), v(2, 2, LORA, fslot),
            v(8, d, dtype=f32), v(2, 1, fslot, dtype=f32), dma((8,)), dma((2,)), dma((13,)), dma((2,)), dma((3,)),
            dma((tiles, 2)), dma((tiles, 3))] + Gather.scratch(nz, na),
        compiler_params=pltpu.CompilerParams(collective_id=1, has_side_effects=True, vmem_limit_bytes=VMEM),
        name="forward",
    )(*shards, tokens, vec, cot, aid, pic)


def tail_kernel(s, dq_ref, dk_ref, dv_ref, x_ref, n1_ref, h_ref, dmid_ref, aid_ref,
                wq_ref, wk_ref, wv_ref, at_ref, b_ref, vec_ref, out_ref, pack_ref, dy_ref, ga_ref, gb_ref):
    i = pl.program_id(0)
    tm, d = x_ref.shape
    nh = HEADS // s
    ds = d // s
    mask = column_mask(aid_ref[...])

    @pl.when(i == 0)
    def _():
        ga_ref[...] = jnp.zeros_like(ga_ref)
        gb_ref[...] = jnp.zeros_like(gb_ref)

    n1 = n1_ref[...]
    dn = jnp.zeros((tm, d), f32)
    for p, (src, w_ref) in enumerate(((dq_ref, wq_ref), (dk_ref, wk_ref), (dv_ref, wv_ref))):
        dh = jnp.zeros((tm, LORA), f32)
        for j in range(s):
            for h in range(nh):
                dy_ref[p, j, :, h * HEAD_DIM:(h + 1) * HEAD_DIM] = src[j * nh + h, :, :HEAD_DIM]
            dy = dy_ref[p, j]
            dh = dh + nt(dy, b_ref[p, j])
            dn = dn + nt(dy, w_ref[j])
            gb_ref[p, j] += 0.5 * tn(h_ref[p], dy)
        dh = (0.5 * dh * mask).astype(bf16)
        dn = dn + nn(dh, at_ref[p])
        ga_ref[p] += tn(dh, n1)
    nhat, r = norm_parts(x_ref[...].astype(f32))
    out_ref[...] = dmid_ref[...] + norm_back(dn, vec_ref[4:5, :], nhat, r)

    @pl.when(i == pl.num_programs(0) - 1)
    def _():
        for p in range(3):
            pack_ref[0, :, p * d:(p + 1) * d] = ga_ref[p].astype(bf16)
            for j in range(s):
                at = p * d + j * ds
                pack_ref[1, :, at:at + ds] = gb_ref[p, j].astype(bf16)


def tail_call(dq, dk, dv, x, n1, hid, dmid, aid, wq, wk, wv, at, bq, vec):
    tokens, d = x.shape
    s = wq.shape[0]
    tm = min(256, tokens)
    full = pl.BlockSpec(memory_space=pltpu.VMEM)
    tile = pl.BlockSpec((tm, d), lambda i: (i, 0))
    heads = pl.BlockSpec((HEADS, tm, LANES), lambda i: (0, i, 0))
    return pl.pallas_call(
        partial(tail_kernel, s),
        grid=(tokens // tm,),
        in_specs=[
            heads, heads, heads, tile, tile,
            pl.BlockSpec((3, tm, LORA), lambda i: (0, i, 0)),
            tile,
            pl.BlockSpec((tm, 1), lambda i: (i, 0)),
            full, full, full, full, full, full,
        ],
        out_specs=[tile, full],
        out_shape=[
            jax.ShapeDtypeStruct((tokens, d), f32),
            jax.ShapeDtypeStruct((2, LORA, 3 * d), bf16),
        ],
        scratch_shapes=[
            pltpu.VMEM((3, s, tm, d // s), bf16),
            pltpu.VMEM((3, LORA, d), f32),
            pltpu.VMEM((3, s, LORA, d // s), f32),
        ],
        compiler_params=pltpu.CompilerParams(vmem_limit_bytes=VMEM),
        name="tail",
    )(dq, dk, dv, x, n1, hid, dmid, aid, wq, wk, wv, at, bq, vec)


def backward_kernel(nz, *refs):
    (qkv, probs, o, d_out, x, n1, hid, dmid, wq, wk, wv, mixed, g_mid, a_ref, b_ref, vec_ref, aid_ref) = refs[:17]
    (own_out, got, mid_total, qkv_total, mixed_out), refs = refs[17:22], refs[22:]
    (dy, dh, w, g_qkv, low, wsem, msem, dsem, lsem, psem, tsem, csem, *sums) = refs
    n, d = 4 * nz, x.shape[2]
    half = x.shape[1]
    count, ds = 2 * half, dy.shape[3]
    nh = HEADS // 2
    spot = Spot(nz)
    spot.barrier()
    per = len(sums) // 3
    width = g_mid.shape[4] // 2
    one, two = (Reduce(spot, g_mid.at[:, :, :, :, pl.ds(k * width, width)], mid_total.at[:, :, :, pl.ds(k * width, width)],
                       sums[k * per:(k + 1) * per]) for k in range(2))
    last = Reduce(spot, g_qkv, qkv_total, sums[2 * per:])
    swap = Swap(spot, mixed, mixed_out, msem)
    weights = [pull(nz, src, j, w.at[p, j], wsem.at[p, j])
               for p, src in enumerate((wq, wk, wv)) for j in range(2)]

    one.one()
    two.one()
    swap.start()
    serve = {1: [one.two], 2: [two.two], 6: [one.three], 10: [two.three], 12: [one.four, one.five], 15: [two.four]}

    def first(heads):
        def attention(small, pbuf, dsbuf, dabuf):
            srcs = [qkv.at[0], qkv.at[1], qkv.at[2], o, d_out]

            def loads(h):
                for k, src in enumerate(srcs):
                    yield pltpu.make_async_copy(src.at[h], small.at[h % 2, k], lsem.at[h % 2, k])
                yield pltpu.make_async_copy(probs.at[h], pbuf.at[h % 2], psem.at[h % 2])

            for copy in loads(0):
                copy.start()
            lane = lane_ids(256)

            def head(h, carry):
                for t, acts in serve.items():
                    @pl.when(h == t)
                    def _(acts=acts):
                        for act in acts:
                            act()

                @pl.when(h + 1 < HEADS)
                def _():
                    for copy in loads(h + 1):
                        copy.start()
                for copy in loads(h):
                    copy.wait()
                m = h % 2
                for i in range(count // 256):
                    rows = pl.ds(i * 256, 256)
                    do = jnp.where(lane < HEAD_DIM, small[m, 4, rows, :].astype(f32), 0.0)
                    delta = jnp.sum(do * small[m, 3, rows, :].astype(f32), axis=-1, keepdims=True)
                    hi = delta.astype(bf16).astype(f32)
                    do = jnp.where(lane == HEAD_DIM, -hi, jnp.where(lane == HEAD_DIM + 1, hi - delta, do)).astype(bf16)
                    dabuf[rows, :] = do
                    dp = nt(do, small[m, 2])
                    part = (pbuf[m, rows, :].astype(f32) * dp).astype(bf16)
                    dsbuf[rows, :] = part
                    heads[0, h, rows, :] = (nn(part, small[m, 1]) * SCALE).astype(bf16)
                heads[2, h] = nn(dabuf[...].T, pbuf[m]).T.astype(bf16)
                heads[1, h] = (nn(small[m, 0].T, dsbuf[...]).T * SCALE).astype(bf16)
                return carry
            lax.fori_loop(0, HEADS, head, 0)

        pl.run_scoped(attention, pltpu.VMEM((2, 5, count, LANES), bf16), pltpu.VMEM((2, count, count), bf16),
                      pltpu.VMEM((count, count), bf16), pltpu.VMEM((count, LANES), bf16))

        def adapters(nbuf, hbuf, ga, gb):
            here = [pltpu.make_async_copy(n1, nbuf, csem.at[0]), pltpu.make_async_copy(hid, hbuf, csem.at[1])]
            for copy in here:
                copy.start()
            for start, _ in weights:
                start()
            for copy in here:
                copy.wait()
            later = [[one.six, two.five], [one.seven, two.six], [two.seven]]
            for p in range(3):
                def tile(i, carry, p=p):
                    rows = pl.ds(i * 512, 512)
                    total = jnp.zeros((512, LORA), f32)
                    for j in range(2):
                        for h in range(nh):
                            dy[p, j, rows, h * HEAD_DIM:(h + 1) * HEAD_DIM] = heads[p, j * nh + h, rows, :HEAD_DIM]
                        part = dy[p, j, rows, :]
                        total = total + nt(part, b_ref[p, j])
                        more = 0.5 * tn(hbuf[p, rows, :], part)

                        @pl.when(i == 0)
                        def _(j=j, more=more):
                            gb[j] = more

                        @pl.when(i > 0)
                        def _(j=j, more=more):
                            gb[j] += more
                    grad = (0.5 * total * column_mask(aid_ref[rows, :])).astype(bf16)
                    dh[p, rows, :] = grad
                    more = tn(grad, nbuf[rows, :])

                    @pl.when(i == 0)
                    def _():
                        ga[...] = more

                    @pl.when(i > 0)
                    def _():
                        ga[...] += more
                    return carry
                lax.fori_loop(0, count // 512, tile, 0)
                cols = slice(p * d, (p + 1) * d)
                g_qkv[0, :, :, :, cols] = ga[...].reshape(2, 2 * nz, 8, d).astype(bf16)
                for j in range(2):
                    cols = slice(p * d + j * ds, p * d + (j + 1) * ds)
                    g_qkv[1, :, :, :, cols] = gb[j].reshape(2, 2 * nz, 8, ds).astype(bf16)
                for act in later[p]:
                    act()

        pl.run_scoped(adapters, pltpu.VMEM((count, d), bf16), pltpu.VMEM((3, count, LORA), bf16),
                      pltpu.VMEM((LORA, d), f32), pltpu.VMEM((2, LORA, ds), f32))

    pl.run_scoped(first, pltpu.VMEM((3, HEADS, count, LANES), bf16))
    last.one()

    def second(xbuf, mbuf, obuf):
        def spots(t):
            side = 1 - spot.x if t < 2 else spot.x
            return side, t % 2 * 256

        def loads(t):
            side, inner = spots(t)
            rows = pl.ds(pl.multiple_of(side * half + inner, 256), 256)
            return (pltpu.make_async_copy(x.at[side, pl.ds(inner, 256)], xbuf.at[t % 2], dsem.at[t, 0]),
                    pltpu.make_async_copy(dmid.at[rows], mbuf.at[t % 2], dsem.at[t, 1]))

        def there(t):
            return remote(low.at[t], got.at[pl.ds(t * 256, 256)], tsem.at[t, 0], tsem.at[t, 1], spot.xn)

        def keep(t):
            return pltpu.make_async_copy(obuf.at[t - 2], own_out.at[pl.ds((t - 2) * 256, 256)], tsem.at[t, 0])

        for t in range(2):
            for copy in loads(t):
                copy.start()
        for _, done in weights:
            done()
        serve = [[], [last.two], [], [last.three]]
        for t in range(4):
            side, inner = spots(t)
            rows = pl.ds(pl.multiple_of(side * half + inner, 256), 256)
            dn = jnp.zeros((256, d), f32)
            for p in range(3):
                for j in range(2):
                    dn = dn + nt(dy[p, j, rows, :], w[p, j].reshape(d, ds))
                dn = dn + nn(dh[p, rows, :], a_ref[p])
            for copy in loads(t):
                copy.wait()
            nhat, r = norm_parts(xbuf[t % 2].astype(f32))
            value = mbuf[t % 2] + norm_back(dn, vec_ref[4:5, :], nhat, r)
            if t < 2:
                low[t] = value.astype(bf16)
                there(t).start()
                for copy in loads(t + 2):
                    copy.start()
            else:
                obuf[t - 2] = value
                keep(t).start()
            for act in serve[t]:
                act()
        last.four()
        last.five()
        last.six()
        last.seven()
        for t in range(2):
            there(t).wait()
        for t in range(2, 4):
            keep(t).wait()

    pl.run_scoped(second, pltpu.VMEM((2, 256, d), bf16), pltpu.VMEM((2, 256, d), f32), pltpu.VMEM((2, 256, d), f32))
    for reduce in (one, two, last):
        reduce.end()
    swap.end()


def backward_call(nz, qkv, probs, o, d_out, x, n1, hid, dmid, wq, wk, wv, mixed, g_mid, at, bq, vec, aid):
    dma = pltpu.SemaphoreType.DMA
    half, d = x.shape[1], x.shape[2]
    count, ds = 2 * half, wq.shape[-1]
    full = pl.BlockSpec(memory_space=pltpu.VMEM)

    def v(*shape, dtype=bf16):
        return pltpu.VMEM(shape, dtype)

    def out(*shape, dtype=bf16):
        return jax.ShapeDtypeStruct(shape, dtype)

    return pl.pallas_call(
        partial(backward_kernel, nz),
        in_specs=any_specs(12) + [full] * 5,
        out_specs=any_specs(5),
        out_shape=[out(half, d, dtype=f32), out(half, d), out(2, 2 * nz, 8, g_mid.shape[4]), out(2, 2 * nz, 8, 3 * d),
                   out(*mixed.shape)],
        scratch_shapes=[
            v(3, 2, count, ds), v(3, count, LORA), v(3, 2, nz, 2, 2, d // (4 * nz), ds), v(2, 2, 2 * nz, 8, 3 * d),
            v(2, 256, d), dma((3, 2)), dma((3,)), dma((4, 2)), dma((2, 5)), dma((2,)), dma((4, 2)), dma((2,))]
        + Reduce.scratch(nz, g_mid.shape[4] // 2) * 2 + Reduce.scratch(nz, 3 * d),
        compiler_params=pltpu.CompilerParams(collective_id=4, has_side_effects=True, vmem_limit_bytes=VMEM),
        name="backward",
    )(qkv, probs, o, d_out, x, n1, hid, dmid, wq, wk, wv, mixed, g_mid, at, bq, vec, aid)


def rows_of_adapters(a):
    t = jnp.swapaxes(a, -1, -2)
    return t.reshape(*t.shape[:-3], t.shape[-3] * t.shape[-2], t.shape[-1])


def local(tokens, cotangent, lengths, adapter_ids, w_query, w_key, w_value, w_out, w_up, w_down,
          b_query, b_value, b_out, b_up, b_down, gain_one, shift_one, gain_two, shift_two,
          qkv_a, out_a, attn_b, up_a, up_b, down_a, down_b):
    seq = lax.axis_size("seq")
    rows, part_len, d = tokens.shape
    group = seq // rows
    count = rows * part_len
    ds, fs = w_query.shape[1], w_up.shape[1]
    me = lax.axis_index("seq")
    row, chunk = me // group, me % group

    def moves(j):
        return [(a, (a % rows + j) % rows * group + a // rows) for a in range(seq)]

    def send(piece, pairs):
        return piece if all(a == b for a, b in pairs) else lax.ppermute(piece, "seq", pairs)

    def to_row(t):
        out = jnp.zeros((rows, part_len, d), t.dtype)
        for j in range(rows):
            piece = lax.dynamic_index_in_dim(t, (me + j) % rows, 0, False)
            out = lax.dynamic_update_index_in_dim(out, send(piece, moves(j)), (row - j) % rows, 0)
        return out.reshape(count, d)

    def from_row(t, dtype):
        t = t.reshape(rows, part_len, d)
        out = jnp.zeros((rows, part_len, d), dtype)
        for j in range(rows):
            piece = lax.dynamic_index_in_dim(t, (row - j) % rows, 0, False)
            pairs = [(b, a) for a, b in moves(j)]
            if not all(a == b for a, b in pairs):
                piece = piece.astype(bf16)
            got = send(piece, pairs).astype(dtype)
            out = lax.dynamic_update_index_in_dim(out, got, (me + j) % rows, 0)
        return out

    dps = lax.axis_size("dp")
    nz = dps // 4
    fast = seq == 2 and rows == 2 and nz == 4
    slot, fslot = up128(ds), up128(fs)
    step = up128(-(-fslot // max(round(fslot / 768), 1)))
    cuts = [(a, min(step, fslot - a)) for a in range(0, fslot, step)]

    def wide_to(t, n):
        return jnp.pad(t, ((0, 0), (0, n - t.shape[1])))

    wu_part, wd_part = wide_to(w_up, fslot), wide_to(w_down.T, fslot)
    ff_parts = [t[:, a:a + n] for a, n in cuts for t in (wu_part, wd_part)]
    narrow = jnp.concatenate([
        rows_of_adapters(qkv_a), rows_of_adapters(out_a)[None], rows_of_adapters(up_a)[None],
        attn_b.reshape(4, -1, d), down_b.reshape(1, -1, d)])
    wide = jnp.stack([rows_of_adapters(down_a), up_b.reshape(-1, up_b.shape[-1])])
    vec_part = jnp.stack([b_query, b_value, b_out, b_down, gain_one, shift_one, gain_two, shift_two])
    teams = [[g * group + c for c in range(group)] for g in range(rows)]

    my_len = lax.dynamic_index_in_dim(lengths, row, 0, False)
    my_ids = lax.dynamic_index_in_dim(adapter_ids, row, 0, False)
    slots = jnp.arange(my_len.shape[0], dtype=jnp.int32)
    ends = jnp.sum(jnp.where(slots[None, :] <= slots[:, None], my_len[None, :], 0), axis=1)
    pos = chunk * count + jnp.arange(count, dtype=jnp.int32)
    pic = jnp.sum((pos[:, None] >= ends[None, :]).astype(jnp.int32), axis=1, keepdims=True)
    aid = jnp.sum(jnp.where(pic == slots[None, :], my_ids[None, :], 0), axis=1, keepdims=True)
    aid = jnp.where(pos[:, None] < ends[-1], aid, -1)

    def from_halves(t):
        return jnp.swapaxes(t, 0, 1).reshape(t.shape[1], -1, t.shape[3])

    if fast:
        me_dp = lax.axis_index("dp")
        place = (me_dp % 2 * 2 + me_dp // 2 % 2) * nz + me_dp // 4

        def share(t):
            flat = t.reshape(-1, t.shape[-1])
            n = flat.shape[0] // dps
            return lax.dynamic_slice_in_dim(flat, place * n, n, 0)

        small = jnp.concatenate([wide_to(vec_part, fslot), wide_to(b_up[None], fslot), jnp.zeros((7, fslot), bf16)])
        wide = jnp.pad(wide.reshape(2, -1, seq, fs), ((0, 0), (0, 0), (0, 0), (0, fslot - fs)))
        wide = wide.reshape(2, -1, seq * fslot)
        narrow, wq, wk, wv, *got = forward_call(
            nz, cuts, [share(narrow), w_query, w_key, w_value, w_out, share(wide)] + ff_parts,
            tokens, small, cotangent, aid, pic)
        x, vec, at, bq, qkv, n1, hid, probs, oaug, _, mixed, dmid, d_out, g_mid = got[2 + len(ff_parts):]
    else:
        def gather_all(shard):
            full = lax.all_gather(shard, ("seq", "dp"), axis=0, tiled=True)
            return full.reshape(seq, d, shard.shape[1])

        wq, wk, wv, wo, *weights = (gather_all(t) for t in [w_query, w_key, w_value, w_out] + ff_parts)
        narrow = lax.all_gather(narrow, "seq", axis=1, tiled=True)
        wide = lax.all_gather(wide, "seq", axis=1, tiled=True)
        vec = lax.all_gather(vec_part, "seq", axis=1, tiled=True).astype(f32)
        bup = lax.all_gather(b_up[None], "seq", axis=0, tiled=True).astype(f32)[:, None]
        x = to_row(tokens)
        cot = to_row(cotangent)

    if fast:
        mine, other, g_mid, g_qkv, mixed = backward_call(
            nz, qkv, probs, oaug, d_out, x, n1, hid, dmid, wq, wk, wv, mixed,
            g_mid.reshape(2, 2, 2 * nz, 8, g_mid.shape[2]), at, bq, vec, aid)
        g_mid, g_qkv = (t.reshape(2, LORA // seq, -1) for t in (g_mid, g_qkv))
        other = other.astype(f32)
        d_in = jnp.where(me == 0, jnp.stack([mine, other]), jnp.stack([other, mine]))
    else:
        at, b = narrow[:5], narrow[5:]
        bq = jnp.swapaxes(b[:3].reshape(3, LORA, seq, ds), 1, 2)
        bias = jnp.stack([vec[0], jnp.zeros_like(vec[0]), vec[1]]).reshape(3, seq, 1, ds)
        qkv, n1, hid = qkv_call(x, jnp.stack([wq, wk, wv]), at, bq, bias, vec, aid, pic)
        kv, off = qkv, 1
        if group > 1:
            kv = lax.all_gather(qkv[1:], "seq", axis=2, tiled=True, axis_index_groups=teams)
            off = 0
        probs, oaug = attn_fwd_call(qkv, kv, off)
        more = ((0, 0), (0, 0), (0, 0), (0, fslot - fs))
        ff = jnp.pad(jnp.swapaxes(wide.reshape(2, LORA, seq, fs), 1, 2), more)
        mixed, dmid, d_out, g_mid = mid_call(
            oaug, x, cot, aid, wo, weights, cuts, jnp.concatenate([at[3:], b[3:]]), ff, jnp.pad(bup, more[1:]), vec)
        dq, dk, dv = attn_bwd_call(qkv, kv, off, probs, oaug, d_out)
        if group > 1:
            dk, dv = (lax.psum_scatter(t, "seq", scatter_dimension=1, axis_index_groups=teams, tiled=True)
                      for t in (dk, dv))
        d_in, g_qkv = tail_call(dq, dk, dv, x, n1, hid, dmid, aid, wq, wk, wv, at, bq, vec)

        def total(t):
            return lax.psum(lax.psum_scatter(t, "seq", scatter_dimension=1, tiled=True), "dp")

        g_mid, g_qkv = total(g_mid), total(g_qkv)
        mixed = from_row(mixed, bf16)
        d_in = from_row(d_in, f32)

    def down_form(t):
        return jnp.swapaxes(t.astype(f32).reshape(-1, RANK, t.shape[-1]), -1, -2)

    def up_form(t):
        return t.astype(f32).reshape(-1, RANK, t.shape[-1])

    def cut(t, k):
        return t[:, k * d:(k + 1) * d]

    def ff_of(t):
        return jnp.concatenate([t[:, 2 * d + j * fslot:2 * d + j * fslot + fs] for j in range(seq)], axis=1)

    a_mid, b_mid = g_mid
    a_qkv, b_qkv = g_qkv
    return (
        mixed,
        d_in,
        jnp.stack([down_form(cut(a_qkv, p)) for p in range(3)]),
        down_form(cut(a_mid, 0)),
        jnp.stack([up_form(cut(b_qkv, p)) for p in range(3)] + [up_form(cut(b_mid, 0))]),
        down_form(cut(a_mid, 1)),
        up_form(ff_of(b_mid)),
        down_form(ff_of(a_mid)),
        up_form(cut(b_mid, 1)),
    )


def solution(mesh):
    both = P("dp", "seq", None)
    lead = P("seq", None, None)
    second = P(None, "seq", None, None)
    return jax.shard_map(
        local,
        mesh=mesh,
        in_specs=(both, both, P("dp", None), P("dp", None))
        + (P("dp", "seq"),) * 5 + (P("seq", "dp"),) + (P("seq"),) * 9
        + (second, lead, second, lead, lead, lead, lead),
        out_specs=(both, both, second, lead, second, lead, lead, lead, lead),
        check_vma=False,
    )
```
